32 devices in a mesh: rows: 4 (over y, x), cols: 8 (over z, core).
Axes of the slice: x: 2, y: 2, z: 4, core: 2. Of those that a mesh axis runs over, the one named last changes fastest.
Arguments:
- layer_in: bfloat16 [1, 4096, 2560], P(None, 'cols', 'rows'), may hold values from -6 to 6
- norm1_gain: bfloat16 [2560], P('cols'), may hold values from 0.25 to 1.75
- w_query: bfloat16 [2560, 2560], P('cols', 'rows'), may hold values from -0.125 to 0.125
- key_matrix: bfloat16 [2560, 512], P('cols', 'rows'), may hold values from -0.125 to 0.125
- value_matrix: bfloat16 [2560, 512], P('cols', 'rows'), may hold values from -0.125 to 0.125
- w_out: bfloat16 [2560, 2560], P('rows', 'cols'), may hold values from -2 to 2
- norm2_gain: bfloat16 [2560], P('cols'), may hold values from 0.25 to 1.75
- w_router: bfloat16 [2560, 16], P('cols'), may hold values from -0.0625 to 0.0625
- shared_gate: bfloat16 [2560, 3072], P('cols', 'rows'), may hold values from -0.125 to 0.125
- shared_up: bfloat16 [2560, 3072], P('cols', 'rows'), may hold values from -0.125 to 0.125
- shared_down: bfloat16 [3072, 2560], P('rows', 'cols'), may hold values from -0.109375 to 0.109375
- expert_gate: bfloat16 [32, 2560, 768], P(('rows', 'cols')), may hold values from -0.125 to 0.125
- expert_up: bfloat16 [32, 2560, 768], P(('rows', 'cols')), may hold values from -0.125 to 0.125
- expert_down: bfloat16 [32, 768, 2560], P(('rows', 'cols')), may hold values from -0.3125 to 0.3125
- routes: int32 [8, 4, 128, 6], P('cols', 'rows'), may hold values from 0 to 15, all different within a row; in each aligned block of 128 rows (0 to 127, 128 to 255, ..., all dimensions but the last counted through in order) at most 60 rows name the same one
- cotangent: bfloat16 [1, 4096, 2560], P(None, 'cols', 'rows'), may hold values from -6 to 6
Outputs:
- layer_out: bfloat16 [1, 4096, 2560], P(None, 'cols', 'rows')
- grad_in: float32 [1, 4096, 2560], P(None, 'cols', 'rows')
- grad_norm1_gain: float32 [2560], P('cols')
- grad_w_query: float32 [2560, 2560], P('cols', 'rows')
- grad_w_key: float32 [2560, 512], P('cols', 'rows')
- grad_w_value: float32 [2560, 512], P('cols', 'rows')
- grad_w_out: float32 [2560, 2560], P('rows', 'cols')
- grad_norm2_gain: float32 [2560], P('cols')
- grad_w_router: float32 [2560, 16], P('cols')
- grad_shared_gate: float32 [2560, 3072], P('cols', 'rows')
- grad_shared_up: float32 [2560, 3072], P('cols', 'rows')
- grad_shared_down: float32 [3072, 2560], P('rows', 'cols')
- grad_expert_gate: float32 [32, 2560, 768], P(('rows', 'cols'))
- grad_expert_up: float32 [32, 2560, 768], P(('rows', 'cols'))
- grad_expert_down: float32 [32, 768, 2560], P(('rows', 'cols'))
The draws below stay inside these ranges and needn't reach their ends.
Inputs may be any that keep to these rules, and one draw needn't show every extreme that they name: The 6 experts of a token differ. Among the 128 tokens of one device's block of routes no expert is named more than 60 times, and in every draw some expert is named exactly 60 times in some block.
All inputs are finite; a program needn't handle non-finite values.
Results may differ from the reference program's by a relative error of at most 0.03.
Values may be sent and summed in bfloat16 or wider, within the bound.
A program may use at most 320 MiB of HBM per device.

```python
import math
import jax
import jax.numpy as jnp
import numpy as np
from jax import lax

MODEL_DIM = 2560
HQ = 20
KEY_VALUE_HEADS = 4
HEAD_DIM = 128
FS = 3072
EF = 1536
TOPK = 6
LENGTH = 4096
EXPERTS = 16
EF_HALF = 768
SEQS = 1
ROWS_DEV = 128
CAP = 60
N_ROWS = 4
N_COLS = 8


def shard_levels(own_key, extent, pieces, smallest, high):
    level, own = 1.0, jax.random.fold_in(own_key, 6)
    for position, shards_of in pieces:
        steps = jnp.exp(jax.random.uniform(jax.random.fold_in(own, position), (shards_of,), jnp.float32, smallest / len(pieces), high / len(pieces)))
        level = level * jnp.repeat(steps, extent[position] // shards_of).reshape([-1 if axis == position else 1 for axis in range(len(extent))])
    return level


def assign_block(key, own, number, rows, amount, top, most, skew):
    sequence = jax.random.permutation(key, amount)
    crowded, usual = portions_of(amount, rows * top, most, skew, True), portions_of(amount, rows * top, most, skew, False)
    places = jnp.arange(amount)

    def named(lengths, turn):
        used = int((lengths > 0).sum())
        fixed = max(1, used // 4)
        moved = fixed + (places - fixed + turn * (used - fixed)) % max(1, amount - fixed)
        return jnp.zeros((amount,), jnp.int32).at[sequence[jnp.where(places < fixed, places, moved)]].set(jnp.asarray(lengths, jnp.int32))

    lengths = jnp.where(number % 4 == 0, named(crowded, number // 4), named(usual, number - number // 4 - 1))
    mixed = jax.random.permutation(jax.random.fold_in(own, 3), amount)
    donor, sink = mixed[0:amount // 2 * 2:2], mixed[1:amount // 2 * 2:2]
    slack = jnp.minimum(lengths[donor] - 1, most - lengths[sink]) // 2
    slack = jnp.where((donor == sequence[0]) | (sink == sequence[0]) | (lengths[sink] == 0), 0, jnp.maximum(slack, 0))
    moved = jax.random.randint(jax.random.fold_in(own, 4), (amount // 2,), 0, 1 << 20) % (slack + 1)
    lengths = lengths.at[donor].add(-moved).at[sink].add(moved)
    items = jnp.searchsorted(jnp.cumsum(lengths), jnp.arange(rows * top), side="right").astype(jnp.int32)
    listing = items.reshape(top, rows).T
    listing = listing[jax.random.permutation(jax.random.fold_in(own, 1), rows)]
    turn = jax.random.randint(jax.random.fold_in(own, 2), (rows, 1), 0, top)
    return jnp.take_along_axis(listing, (jnp.arange(top)[None, :] + turn) % top, axis=1)


def portions_of(number_of, total, most, slope, full):
    portions = [(1 << 20) // math.isqrt(standing ** slope) + 1 for standing in range(1, number_of + 1)]
    largest = most if full else min(most, max(-(-total // number_of), total * portions[0] // sum(portions)))
    least = 1 if total - largest >= number_of - 1 else 0
    given, spare = [largest] + [least] * (number_of - 1), total - largest - least * (number_of - 1)
    while spare > 0:
        movable = [i for i in range(1, number_of) if given[i] < largest] or [i for i in range(1, number_of) if given[i] < most]
        whole, remaining = sum([portions[i] for i in movable]), spare
        for i in movable:
            more = min(most - given[i], max(1, remaining * portions[i] // whole), spare)
            given[i] = given[i] + more
            spare = spare - more
    return np.array(given)


def bell_draw(stream_key, extent, spread, bound, shards=(), kind=jnp.bfloat16):
    values = spread * jax.random.normal(stream_key, extent, jnp.float32)
    if shards:
        values = values * shard_levels(stream_key, extent, shards, -0.22, 0.18)
    return jnp.clip(values, -bound, bound).astype(kind)


def setup_inputs(seed: int = 0) -> dict:
    key_list = jax.random.split(jax.random.key(seed), 17)
    layer_in = bell_draw(key_list[0], (SEQS, LENGTH, MODEL_DIM), 1.0, 6.0, ((1, 8), (2, 4)))
    norm1_gain = jnp.clip(1.0 + 0.15 * jax.random.normal(key_list[1], (MODEL_DIM,), jnp.float32), 0.25, 1.75).astype(jnp.bfloat16)
    w_query = bell_draw(key_list[2], (MODEL_DIM, HQ * HEAD_DIM), MODEL_DIM ** -0.5, 0.125, ((0, 8), (1, 4)))
    key_matrix = bell_draw(key_list[3], (MODEL_DIM, KEY_VALUE_HEADS * HEAD_DIM), MODEL_DIM ** -0.5, 0.125, ((0, 8), (1, 4)))
    value_matrix = bell_draw(key_list[4], (MODEL_DIM, KEY_VALUE_HEADS * HEAD_DIM), MODEL_DIM ** -0.5, 0.125, ((0, 8), (1, 4)))
    w_out = bell_draw(key_list[5], (HQ * HEAD_DIM, MODEL_DIM), 8 ** -0.5, 2.0, ((0, 4), (1, 8)))
    norm2_gain = jnp.clip(1.0 + 0.15 * jax.random.normal(key_list[6], (MODEL_DIM,), jnp.float32), 0.25, 1.75).astype(jnp.bfloat16)
    w_router = bell_draw(key_list[7], (MODEL_DIM, EXPERTS), (4 * MODEL_DIM) ** -0.5, 0.0625, ((0, 8),))
    shared_gate = bell_draw(key_list[8], (MODEL_DIM, FS), MODEL_DIM ** -0.5, 0.125, ((0, 8), (1, 4)))
    shared_up = bell_draw(key_list[9], (MODEL_DIM, FS), MODEL_DIM ** -0.5, 0.125, ((0, 8), (1, 4)))
    shared_down = bell_draw(key_list[10], (FS, MODEL_DIM), FS ** -0.5, 0.109375, ((0, 4), (1, 8)))
    expert_gate = bell_draw(key_list[11], (2 * EXPERTS, MODEL_DIM, EF_HALF), MODEL_DIM ** -0.5, 0.125, ((0, 32),))
    expert_up = bell_draw(key_list[12], (2 * EXPERTS, MODEL_DIM, EF_HALF), MODEL_DIM ** -0.5, 0.125, ((0, 32),))
    expert_down = bell_draw(key_list[13], (2 * EXPERTS, EF_HALF, MODEL_DIM), (EF // 4) ** -0.5, 0.3125, ((0, 32),))
    routes_keys = jax.random.split(jax.random.fold_in(key_list[14], 1), N_COLS * N_ROWS * ROWS_DEV // ROWS_DEV)
    routes_turns = jax.random.permutation(jax.random.fold_in(key_list[14], 3), N_COLS * N_ROWS * ROWS_DEV // ROWS_DEV)
    routes = jax.vmap(lambda own, number: assign_block(jax.random.fold_in(key_list[14], 2), own, number, ROWS_DEV, EXPERTS, TOPK, CAP, 1))(routes_keys, routes_turns).reshape((N_COLS, N_ROWS, ROWS_DEV, TOPK))
    cotangent = bell_draw(key_list[15], (SEQS, LENGTH, MODEL_DIM), 1.0, 6.0, ((1, 8), (2, 4)))
    return dict(layer_in=layer_in, norm1_gain=norm1_gain, w_query=w_query, key_matrix=key_matrix, value_matrix=value_matrix, w_out=w_out, norm2_gain=norm2_gain, w_router=w_router, shared_gate=shared_gate, shared_up=shared_up, shared_down=shared_down, expert_gate=expert_gate, expert_up=expert_up, expert_down=expert_down, routes=routes, cotangent=cotangent)


NORM_EPS = 1e-05
ROPE_BASE = 500000.0
NEG_LARGE = -1e+30
PRECISE = lax.Precision.HIGHEST

@jax.custom_vjp
def reduced_copy(v):
    return lax.optimization_barrier(v.astype(jnp.bfloat16)).astype(jnp.float32)

@jax.custom_vjp
def reduced_return(v):
    return v

def low_keep(v):
    return (reduced_copy(v), None)

def low_pass(kept, grad):
    return (grad,)

def back_keep(v):
    return (v, None)

def back_low(kept, grad):
    return (reduced_copy(grad),)
reduced_copy.defvjp(low_keep, low_pass)
reduced_return.defvjp(back_keep, back_low)

def matmul(left_op, right_op):
    return jnp.dot(left_op, right_op, precision=PRECISE, preferred_element_type=jnp.float32)

def rms_norm(values, scales):
    return values * lax.rsqrt(lax.optimization_barrier(jnp.mean(values * values, -1, keepdims=True)) + NORM_EPS) * scales

def rope_tables(positions, head_size):
    half_size = head_size // 2
    inv_freq = ROPE_BASE ** (-(2.0 * jnp.arange(half_size, dtype=jnp.float32)) / head_size)
    angles = positions.astype(jnp.float32)[:, None] * inv_freq[None, :]
    return (jnp.cos(angles), jnp.sin(angles))

def apply_rotary(values, cosine_table, sine_table):
    half_size = values.shape[-1] // 2
    first_half = values[..., :half_size]
    second = values[..., half_size:]
    cos_b = cosine_table[:, None, :]
    sin_b = sine_table[:, None, :]
    return jnp.concatenate([first_half * cos_b - second * sin_b, second * cos_b + first_half * sin_b], -1)

def attention_core(rotated_queries, rotated_keys, value_all):
    sequence_count, token_length, head_count, head_size = rotated_queries.shape
    kv_heads = rotated_keys.shape[2]
    group_size = head_count // kv_heads
    q_block = min(512, token_length)
    n_blocks = token_length // q_block
    score_scale = 1.0 / math.sqrt(head_size)
    key_pos = jnp.arange(token_length, dtype=jnp.int32)

    def query_block(packed):
        q_part, q_start = packed
        q_grouped = q_part.reshape(sequence_count, q_block, kv_heads, group_size, head_size)
        scores = jnp.einsum('sqkgd,slkd->skgql', q_grouped, rotated_keys, precision=PRECISE) * score_scale
        scores = reduced_return(scores)
        q_pos = q_start + jnp.arange(q_block, dtype=jnp.int32)
        causal = q_pos[:, None] >= key_pos[None, :]
        scores = jnp.where(causal, scores, NEG_LARGE)
        prob_vals = jax.nn.softmax(scores, -1)
        result = jnp.einsum('skgql,slkd->sqkgd', reduced_copy(prob_vals), value_all, precision=PRECISE)
        return result.reshape(sequence_count, q_block, head_count, head_size)
    blocked = jnp.transpose(rotated_queries.reshape(sequence_count, n_blocks, q_block, head_count, head_size), (1, 0, 2, 3, 4))
    starts = (jnp.arange(n_blocks, dtype=jnp.int32) * q_block).astype(jnp.int32)
    outputs = lax.map(jax.checkpoint(query_block), (blocked, starts))
    return jnp.transpose(outputs, (1, 0, 2, 3, 4)).reshape(sequence_count, token_length, head_count, head_size)

def whole_layer(layer_in, gain_one, w_query, key_matrix, value_matrix, w_out, gain_two, w_router, shared_gate, shared_up, shared_down, expert_gate, expert_up, expert_down, tables):
    route_token, inverse_perm, route_expert, slot_table, slot_valid, assign_index = tables
    sequence_count, token_length, model_width = layer_in.shape
    tokens = layer_in.reshape(sequence_count * token_length, model_width)
    first_normed = reduced_copy(rms_norm(tokens, gain_one))
    q_pre = reduced_return(matmul(first_normed, w_query))
    key_unrotated = reduced_return(matmul(first_normed, key_matrix))
    value_projected = reduced_return(reduced_copy(matmul(first_normed, value_matrix)))
    cosine_table, sine_table = rope_tables(jnp.arange(token_length, dtype=jnp.int32), HEAD_DIM)
    rotated_queries = reduced_copy(apply_rotary(q_pre.reshape(sequence_count, token_length, HQ, HEAD_DIM), cosine_table, sine_table))
    rotated_keys = reduced_copy(apply_rotary(key_unrotated.reshape(sequence_count, token_length, KEY_VALUE_HEADS, HEAD_DIM), cosine_table, sine_table))
    head_outputs = reduced_return(reduced_copy(attention_core(rotated_queries, rotated_keys, value_projected.reshape(sequence_count, token_length, KEY_VALUE_HEADS, HEAD_DIM))))
    attn_proj = reduced_return(matmul(head_outputs.reshape(sequence_count * token_length, HQ * HEAD_DIM), w_out))
    residual_stream = tokens + attn_proj
    second_normed = reduced_copy(rms_norm(residual_stream, gain_two))
    gate_pre = reduced_return(matmul(second_normed, shared_gate))
    up_pre = reduced_return(matmul(second_normed, shared_up))
    shared_act = reduced_copy(jax.nn.silu(gate_pre) * up_pre)
    shared_out = matmul(shared_act, shared_down)
    normed_route = second_normed[route_token]
    logits = matmul(normed_route, w_router)
    chosen_hot = (route_expert[:, :, None] == jnp.arange(EXPERTS, dtype=jnp.int32)[None, None, :]).astype(jnp.float32)
    gate_probs = jax.nn.softmax(lax.optimization_barrier(jnp.sum(chosen_hot * logits[:, None, :], -1)), -1)
    gate_four = expert_gate.reshape(EXPERTS, 2, model_width, EF_HALF)
    up_four = expert_up.reshape(EXPERTS, 2, model_width, EF_HALF)
    down_four = expert_down.reshape(EXPERTS, 2, EF_HALF, model_width)

    def expert(packed):
        row_index, is_valid, w_gate, w_up, w_down = packed
        rows_all = jnp.where(is_valid[:, None] > 0, second_normed[row_index], 0.0)
        rows_shared = reduced_return(rows_all)
        summed = jnp.zeros((row_index.shape[0], model_width), jnp.float32)
        for half_index in range(2):
            rows_in = reduced_return(rows_shared)
            e_gate = reduced_return(matmul(rows_in, w_gate[half_index]))
            e_up = reduced_return(matmul(rows_in, w_up[half_index]))
            e_act = reduced_copy(jax.nn.silu(e_gate) * e_up)
            summed = summed + reduced_return(reduced_copy(matmul(e_act, w_down[half_index])))
        return reduced_copy(summed)
    expert_out = lax.map(jax.checkpoint(expert), (slot_table, slot_valid, gate_four, up_four, down_four))
    picked = expert_out.reshape(-1, model_width)[assign_index]
    routed = lax.optimization_barrier(jnp.sum(gate_probs[:, :, None] * picked, 1))[inverse_perm]
    return (residual_stream + shared_out + routed).reshape(sequence_count, token_length, model_width)

def reference(layer_in, norm1_gain, w_query, key_matrix, value_matrix, w_out, norm2_gain, w_router, shared_gate, shared_up, shared_down, expert_gate, expert_up, expert_down, routes, cotangent):
    len_dev = LENGTH // N_COLS
    block_count = N_COLS * N_ROWS
    total_tokens = SEQS * LENGTH
    flat_routes = routes.reshape(block_count, ROWS_DEV * TOPK).astype(jnp.int32)
    expert_hot = (flat_routes[:, :, None] == jnp.arange(EXPERTS, dtype=jnp.int32)[None, None, :]).astype(jnp.int32)
    rank_in = lax.optimization_barrier(jnp.sum((jnp.cumsum(expert_hot, 1) - expert_hot) * expert_hot, -1))
    block_ids = jnp.arange(block_count, dtype=jnp.int32)[:, None]
    slot_flat = (block_ids * CAP + rank_in).reshape(-1).astype(jnp.int32)
    expert_flat = flat_routes.reshape(-1)
    route_index = jnp.arange(total_tokens, dtype=jnp.int32)
    col_of = route_index // (N_ROWS * ROWS_DEV)
    within = route_index % (N_ROWS * ROWS_DEV)
    seq_of = within // len_dev
    pos_of = col_of * len_dev + within % len_dev
    route_token = (seq_of * LENGTH + pos_of).astype(jnp.int32)
    inverse_perm = jnp.zeros((total_tokens,), jnp.int32).at[route_token].set(route_index)
    token_of_assign = jnp.repeat(route_token, TOPK)
    slot_table = jnp.zeros((EXPERTS, block_count * CAP), jnp.int32).at[expert_flat, slot_flat].set(token_of_assign)
    slot_valid = jnp.zeros((EXPERTS, block_count * CAP), jnp.int32).at[expert_flat, slot_flat].set(1)
    assign_index = (expert_flat * (block_count * CAP) + slot_flat).reshape(total_tokens, TOPK).astype(jnp.int32)
    route_expert = flat_routes.reshape(total_tokens, TOPK)
    tables = (route_token, inverse_perm, route_expert, slot_table, slot_valid, assign_index)
    params = tuple((item.astype(jnp.float32) for item in (layer_in, norm1_gain, w_query, key_matrix, value_matrix, w_out, norm2_gain, w_router, shared_gate, shared_up, shared_down, expert_gate, expert_up, expert_down)))

    def forward(*weights):
        return whole_layer(*weights, tables)
    result, pullback = jax.vjp(forward, *params)
    grads = pullback(cotangent.astype(jnp.float32))
    return (result.astype(jnp.bfloat16), grads[0], grads[1], grads[2], grads[3], grads[4], grads[5], grads[6], grads[7], grads[8], grads[9], grads[10], grads[11], grads[12], grads[13])
```

```python
import math

import jax
import jax.numpy as jnp
from jax import lax
from jax.experimental import pallas as pl
from jax.experimental.pallas import tpu as pltpu
from jax.sharding import PartitionSpec as P

HEAD_DIM = 128


NORM_EPS = 1e-05
ROPE_BASE = 500000.0
NEG_LARGE = -1e30
PRECISE = lax.Precision.HIGHEST


def rope_tables(positions, head_size):
    half_size = head_size // 2
    inv_freq = ROPE_BASE ** (-(2.0 * jnp.arange(half_size, dtype=jnp.float32)) / head_size)
    angles = positions.astype(jnp.float32)[:, None] * inv_freq[None, :]
    return (jnp.cos(angles), jnp.sin(angles))


def apply_rotary(values, cosine_table, sine_table):
    half_size = values.shape[-1] // 2
    first_half = values[..., :half_size]
    second = values[..., half_size:]
    cos_b = cosine_table[:, None, :]
    sin_b = sine_table[:, None, :]
    return jnp.concatenate(
        [first_half * cos_b - second * sin_b, second * cos_b + first_half * sin_b], -1
    )


def matmul(left_op, right_op):
    return jnp.dot(left_op, right_op, preferred_element_type=jnp.float32)


def matmul_tn(left_op, right_op):
    return lax.dot_general(
        left_op, right_op, (((0,), (0,)), ((), ())), preferred_element_type=jnp.float32
    )


def matmul_nt(left_op, right_op):
    return lax.dot_general(
        left_op, right_op, (((1,), (1,)), ((), ())), preferred_element_type=jnp.float32
    )


def silu_parts(pre_act):
    sigma = jax.nn.sigmoid(pre_act)
    return (pre_act * sigma, sigma * (1.0 + pre_act * (1.0 - sigma)))


def keep_same(carry_in):
    return carry_in


def routed_layer(
    layer_in,
    norm1_gain,
    w_query,
    key_matrix,
    value_matrix,
    w_out,
    norm2_gain,
    w_router,
    shared_gate,
    shared_up,
    shared_down,
    expert_gate,
    expert_up,
    expert_down,
    routes,
    cotangent,
):
    n_rows = lax.axis_size("rows")
    n_cols = lax.axis_size("cols")
    row_idx = lax.axis_index("rows")
    col_idx = lax.axis_index("cols")
    sequence_count, len_dev, row_width = layer_in.shape
    tok_dev = sequence_count * len_dev
    rows_dev = routes.shape[2]
    top_k = routes.shape[3]
    experts = w_router.shape[1]
    devices = n_rows * n_cols
    capacity = 2 * max(1, 5 * rows_dev * top_k // (8 * experts))
    full_in = lax.all_gather(layer_in, "rows", axis=2, tiled=True)
    (
        gain_one,
        wq_full,
        wk_full,
        wv_full,
        wo_full,
        gain_two,
        router_full,
        sg_full,
        su_full,
        sd_full,
    ) = (
        lax.all_gather(norm1_gain, "cols", axis=0, tiled=True),
        lax.all_gather(w_query, "cols", axis=0, tiled=True),
        lax.all_gather(key_matrix, "cols", axis=0, tiled=True),
        lax.all_gather(value_matrix, "cols", axis=0, tiled=True),
        lax.all_gather(w_out, "cols", axis=1, tiled=True),
        lax.all_gather(norm2_gain, "cols", axis=0, tiled=True),
        lax.all_gather(w_router, "cols", axis=0, tiled=True),
        lax.all_gather(shared_gate, "cols", axis=0, tiled=True),
        lax.all_gather(shared_up, "cols", axis=0, tiled=True),
        lax.all_gather(shared_down, "cols", axis=1, tiled=True),
    )
    model_width = full_in.shape[2]
    token_input = full_in.reshape(tok_dev, model_width).astype(jnp.float32)
    first_inverse_deviation = lax.rsqrt(
        jnp.mean(token_input * token_input, -1, keepdims=True) + NORM_EPS
    )
    first_unit_rows = token_input * first_inverse_deviation
    first_gain_float = gain_one.astype(jnp.float32)
    first_normed = (first_unit_rows * first_gain_float).astype(jnp.bfloat16)
    q_pre = matmul(first_normed, wq_full)
    key_unrotated = matmul(first_normed, wk_full)
    value_projected = matmul(first_normed, wv_full).astype(jnp.bfloat16)
    q_heads = q_pre.shape[1] // HEAD_DIM
    positions = col_idx * len_dev + jnp.arange(len_dev, dtype=jnp.int32)
    cosine_table, sine_table = rope_tables(positions, HEAD_DIM)
    rotated_queries = apply_rotary(
        q_pre.reshape(sequence_count, len_dev, q_heads, HEAD_DIM), cosine_table, sine_table
    ).astype(jnp.bfloat16)
    rotated_keys = apply_rotary(
        key_unrotated.reshape(sequence_count, len_dev, 1, HEAD_DIM), cosine_table, sine_table
    ).astype(jnp.bfloat16)
    kv_local = jnp.concatenate(
        [
            rotated_keys.reshape(sequence_count, len_dev, HEAD_DIM),
            value_projected.reshape(sequence_count, len_dev, HEAD_DIM),
        ],
        -1,
    )
    kv_local = jnp.swapaxes(kv_local, 0, 1)
    query_t = jnp.transpose(rotated_queries, (0, 2, 1, 3))
    score_scale = 1.0 / math.sqrt(HEAD_DIM)
    q_last = col_idx * len_dev + len_dev - 1

    def online_update(carry_in, key_part, k_start):
        run_max, run_sum, run_acc = carry_in
        block_len = key_part.shape[0]
        scores = (
            jnp.einsum(
                "shqd,bsd->shqb",
                query_t,
                key_part[:, :, :HEAD_DIM],
                preferred_element_type=jnp.float32,
            )
            * score_scale
        )
        key_pos = k_start + jnp.arange(block_len, dtype=jnp.int32)
        causal = positions[:, None] >= key_pos[None, :]
        scores = jnp.where(causal, scores, NEG_LARGE)
        new_max = jnp.maximum(run_max, jnp.max(scores, -1))
        prob_vals = jnp.where(causal, jnp.exp(scores - new_max[..., None]), 0.0)
        rescale = jnp.exp(run_max - new_max)
        run_sum = run_sum * rescale + jnp.sum(prob_vals, -1)
        run_acc = run_acc * rescale[..., None] + jnp.einsum(
            "shqb,bsd->shqd",
            prob_vals.astype(jnp.bfloat16),
            key_part[:, :, HEAD_DIM:],
            preferred_element_type=jnp.float32,
        )
        return (new_max, run_sum, run_acc)

    fold_start = (
        jnp.full((sequence_count, q_heads, len_dev), NEG_LARGE, jnp.float32),
        jnp.zeros((sequence_count, q_heads, len_dev), jnp.float32),
        jnp.zeros((sequence_count, q_heads, len_dev, HEAD_DIM), jnp.float32),
    )
    carry_in = fold_start
    piece = lax.all_gather(kv_local, "cols", axis=0, tiled=True)
    start = jnp.int32(0)
    piece_len = piece.shape[0]
    step_len = min(512, piece_len)
    for offset in range(0, piece_len, step_len):
        key_part = piece[offset : offset + step_len]
        k_start = start + offset

        def updated(state_in, key_part=key_part, k_start=k_start):
            return online_update(state_in, key_part, k_start)

        carry_in = lax.cond(k_start <= q_last, updated, keep_same, carry_in)
    run_max, run_sum, run_acc = carry_in
    attn_f32 = run_acc / run_sum[..., None]
    log_total = run_max + jnp.log(run_sum)
    attn_bf = attn_f32.astype(jnp.bfloat16)
    attn_rows = jnp.transpose(attn_bf, (0, 2, 1, 3)).reshape(tok_dev, q_heads * HEAD_DIM)
    attn_proj = lax.psum(matmul(attn_rows, wo_full).astype(jnp.bfloat16), "rows").astype(
        jnp.float32
    )
    residual_stream = token_input + attn_proj
    second_inverse_deviation = lax.rsqrt(
        jnp.mean(residual_stream * residual_stream, -1, keepdims=True) + NORM_EPS
    )
    second_unit_rows = residual_stream * second_inverse_deviation
    second_gain_float = gain_two.astype(jnp.float32)
    second_normed = (second_unit_rows * second_gain_float).astype(jnp.bfloat16)
    gate_pre = matmul(second_normed, sg_full)
    up_pre = matmul(second_normed, su_full)
    silu_gate, silu_slope = silu_parts(gate_pre)
    shared_act = (silu_gate * up_pre).astype(jnp.bfloat16)
    ffn_part = matmul(shared_act, sd_full)
    my_rows = row_idx * rows_dev
    normed_mine = lax.dynamic_slice_in_dim(second_normed, my_rows, rows_dev, 0)
    route_mine = routes.reshape(rows_dev, top_k)
    logits = matmul(normed_mine, router_full)
    expert_ids = jnp.arange(experts, dtype=jnp.int32)
    chosen_hot = (route_mine[:, :, None] == expert_ids[None, None, :]).astype(jnp.float32)
    chosen = jnp.sum(chosen_hot * logits[:, None, :], -1)
    gate_probs = jax.nn.softmax(chosen, -1)
    assign_count = rows_dev * top_k
    flat_routes = route_mine.reshape(assign_count)
    assign_hot = (flat_routes[:, None] == expert_ids[None, :]).astype(jnp.int32)
    rank_in = jnp.sum((jnp.cumsum(assign_hot, 0) - assign_hot) * assign_hot, 1)
    slot_of = flat_routes * capacity + rank_in
    assign_of_slot = (
        jnp.zeros((experts * capacity,), jnp.int32)
        .at[slot_of]
        .set(jnp.arange(assign_count, dtype=jnp.int32))
    )
    slot_used = jnp.zeros((experts * capacity,), jnp.int32).at[slot_of].set(1)
    slot_row = assign_of_slot // top_k

    def send_rows(slot_vals):
        slot_vals = slot_vals.reshape(experts, capacity, model_width)
        outgoing = jnp.broadcast_to(
            slot_vals[:, None], (experts, 2, capacity, model_width)
        ).reshape(devices, capacity, model_width)
        received = lax.all_to_all(
            outgoing, ("rows", "cols"), split_axis=0, concat_axis=0, tiled=True
        )
        return received.reshape(devices * capacity, model_width)

    def return_rows(slot_vals):
        returned = lax.all_to_all(
            slot_vals.reshape(devices, capacity, model_width),
            ("rows", "cols"),
            split_axis=0,
            concat_axis=0,
            tiled=True,
        )
        returned = returned.reshape(experts, 2, capacity, model_width).astype(jnp.float32)
        summed = (returned[:, 0] + returned[:, 1]).astype(jnp.bfloat16)
        return summed.reshape(experts * capacity, model_width).astype(jnp.float32)

    slot_inputs = jnp.where(slot_used[:, None] > 0, normed_mine[slot_row], 0)
    expert_rows = send_rows(slot_inputs)
    eg_mat = expert_gate.reshape(model_width, -1)
    eu_mat = expert_up.reshape(model_width, -1)
    ed_mat = expert_down.reshape(-1, model_width)
    e_gate = matmul(expert_rows, eg_mat)
    e_up = matmul(expert_rows, eu_mat)
    e_silu, e_slope = silu_parts(e_gate)
    e_act = (e_silu * e_up).astype(jnp.bfloat16)
    e_out = matmul(e_act, ed_mat).astype(jnp.bfloat16)
    expert_sum = return_rows(e_out)
    picked = expert_sum[slot_of].reshape(rows_dev, top_k, model_width)
    routed = jnp.sum(gate_probs[:, :, None] * picked, 1)
    ffn_full = lax.dynamic_update_slice_in_dim(
        ffn_part, lax.dynamic_slice_in_dim(ffn_part, my_rows, rows_dev, 0) + routed, my_rows, 0
    )
    ffn_mine = lax.psum_scatter(
        ffn_full.reshape(sequence_count, len_dev, model_width).astype(jnp.bfloat16),
        "rows",
        scatter_dimension=2,
        tiled=True,
    ).astype(jnp.float32)
    resid_mine = lax.dynamic_slice_in_dim(
        residual_stream.reshape(sequence_count, len_dev, model_width),
        row_idx * row_width,
        row_width,
        2,
    )
    layer_out = (resid_mine + ffn_mine).astype(jnp.bfloat16)
    grad_full = lax.all_gather(cotangent, "rows", axis=2, tiled=True).reshape(tok_dev, model_width)
    d_shared_act = matmul_nt(grad_full, sd_full)
    grad_sd = matmul_tn(shared_act, grad_full)
    d_gate_pre = (d_shared_act * up_pre * silu_slope).astype(jnp.bfloat16)
    d_up_pre = (d_shared_act * silu_gate).astype(jnp.bfloat16)
    grad_sg = matmul_tn(second_normed, d_gate_pre)
    grad_su = matmul_tn(second_normed, d_up_pre)
    grad_second_normed = matmul_nt(d_gate_pre, sg_full) + matmul_nt(d_up_pre, su_full)
    grad_mine = lax.dynamic_slice_in_dim(grad_full, my_rows, rows_dev, 0).astype(jnp.float32)
    d_gates = jnp.sum(grad_mine[:, None, :] * picked, -1)
    to_experts = (
        (gate_probs[:, :, None] * grad_mine[:, None, :])
        .reshape(assign_count, model_width)
        .astype(jnp.bfloat16)
    )
    slot_grads = jnp.where(slot_used[:, None] > 0, to_experts[assign_of_slot], 0)
    d_expert_out = send_rows(slot_grads)
    grad_ed = matmul_tn(e_act, d_expert_out)
    d_e_act = matmul_nt(d_expert_out, ed_mat)
    d_e_gate = (d_e_act * e_up * e_slope).astype(jnp.bfloat16)
    d_e_up = (d_e_act * e_silu).astype(jnp.bfloat16)
    grad_eg = matmul_tn(expert_rows, d_e_gate)
    grad_eu = matmul_tn(expert_rows, d_e_up)
    d_rows = (matmul_nt(d_e_gate, eg_mat) + matmul_nt(d_e_up, eu_mat)).astype(jnp.bfloat16)
    d_assign = return_rows(d_rows)[slot_of].reshape(rows_dev, top_k, model_width)
    d_routed_in = jnp.sum(d_assign, 1)
    d_chosen = gate_probs * (d_gates - jnp.sum(gate_probs * d_gates, -1, keepdims=True))
    d_logits = jnp.sum(chosen_hot * d_chosen[:, :, None], 1)
    router_f = router_full.astype(jnp.float32)
    grad_router_part = jnp.dot(normed_mine.astype(jnp.float32).T, d_logits, precision=PRECISE)
    d_router_in = jnp.dot(d_logits, router_f.T, precision=PRECISE)
    d_mine = (
        lax.dynamic_slice_in_dim(grad_second_normed, my_rows, rows_dev, 0)
        + d_routed_in
        + d_router_in
    )
    grad_second_normed = lax.dynamic_update_slice_in_dim(grad_second_normed, d_mine, my_rows, 0)
    grad_second_normed, grad_router = (
        lax.psum(grad_second_normed.astype(jnp.bfloat16), "rows").astype(jnp.float32),
        lax.psum(grad_router_part.astype(jnp.bfloat16), "rows").astype(jnp.float32),
    )
    grad_second_unit = grad_second_normed * second_gain_float
    second_gain_gradient = jnp.sum(grad_second_normed * second_unit_rows, 0)
    d_resid = grad_full.astype(jnp.float32) + second_inverse_deviation * (
        grad_second_unit
        - second_unit_rows * jnp.mean(grad_second_unit * second_unit_rows, -1, keepdims=True)
    )
    d_attn = d_resid.astype(jnp.bfloat16)
    grad_wo = matmul_tn(attn_rows, d_attn)
    d_heads = matmul_nt(d_attn, wo_full).astype(jnp.bfloat16)
    d_heads_t = jnp.transpose(
        d_heads.reshape(sequence_count, len_dev, q_heads, HEAD_DIM), (0, 2, 1, 3)
    )
    delta_rows = jnp.sum(d_heads_t.astype(jnp.float32) * attn_f32, -1)
    kv_all = lax.all_gather(kv_local, "cols", axis=0, tiled=True)
    seq_len = kv_all.shape[0]
    key_block = min(512, seq_len)

    def key_step(block_no, carry_in):
        k_start = block_no * key_block
        key_part = lax.dynamic_slice_in_dim(kv_all, k_start, key_block, 0)

        def contribute(state_in):
            d_query_in, d_kv_in = state_in
            keys_bf = key_part[:, :, :HEAD_DIM]
            values_bf = key_part[:, :, HEAD_DIM:]
            scores = (
                jnp.einsum("shqd,bsd->shqb", query_t, keys_bf, preferred_element_type=jnp.float32)
                * score_scale
            )
            key_pos = k_start + jnp.arange(key_block, dtype=jnp.int32)
            causal = positions[:, None] >= key_pos[None, :]
            prob_vals = jnp.where(causal, jnp.exp(scores - log_total[..., None]), 0.0)
            d_prob = jnp.einsum(
                "shqd,bsd->shqb", d_heads_t, values_bf, preferred_element_type=jnp.float32
            )
            d_scores = (prob_vals * (d_prob - delta_rows[..., None])).astype(jnp.bfloat16)
            d_query_in = (
                d_query_in
                + jnp.einsum(
                    "shqb,bsd->shqd", d_scores, keys_bf, preferred_element_type=jnp.float32
                )
                * score_scale
            )
            d_key = (
                jnp.einsum("shqb,shqd->bsd", d_scores, query_t, preferred_element_type=jnp.float32)
                * score_scale
            )
            d_value = jnp.einsum(
                "shqb,shqd->bsd",
                prob_vals.astype(jnp.bfloat16),
                d_heads_t,
                preferred_element_type=jnp.float32,
            )
            d_kv_in = lax.dynamic_update_slice_in_dim(
                d_kv_in, jnp.concatenate([d_key, d_value], -1), k_start, 0
            )
            return (d_query_in, d_kv_in)

        return lax.cond(k_start <= q_last, contribute, keep_same, carry_in)

    grad_start = (
        jnp.zeros((sequence_count, q_heads, len_dev, HEAD_DIM), jnp.float32),
        jnp.zeros((seq_len, sequence_count, 2 * HEAD_DIM), jnp.float32),
    )
    d_query, d_kv_all = lax.fori_loop(0, seq_len // key_block, key_step, grad_start)
    d_kv = lax.psum_scatter(
        d_kv_all.astype(jnp.bfloat16), "cols", scatter_dimension=0, tiled=True
    ).astype(jnp.float32)
    d_query_rows = (
        apply_rotary(jnp.transpose(d_query, (0, 2, 1, 3)), cosine_table, -sine_table)
        .reshape(tok_dev, q_heads * HEAD_DIM)
        .astype(jnp.bfloat16)
    )
    d_kv_t = jnp.swapaxes(d_kv, 0, 1)
    d_key_rows = (
        apply_rotary(
            d_kv_t[:, :, :HEAD_DIM].reshape(sequence_count, len_dev, 1, HEAD_DIM),
            cosine_table,
            -sine_table,
        )
        .reshape(tok_dev, HEAD_DIM)
        .astype(jnp.bfloat16)
    )
    d_value_rows = d_kv_t[:, :, HEAD_DIM:].reshape(tok_dev, HEAD_DIM).astype(jnp.bfloat16)
    grad_wq = matmul_tn(first_normed, d_query_rows)
    grad_wk = matmul_tn(first_normed, d_key_rows)
    grad_wv = matmul_tn(first_normed, d_value_rows)
    grad_first_normed = (
        matmul_nt(d_query_rows, wq_full)
        + matmul_nt(d_key_rows, wk_full)
        + matmul_nt(d_value_rows, wv_full)
    )
    grad_first_normed = lax.psum(grad_first_normed.astype(jnp.bfloat16), "rows").astype(jnp.float32)
    grad_first_unit = grad_first_normed * first_gain_float
    first_gain_gradient = jnp.sum(grad_first_normed * first_unit_rows, 0)
    d_input = d_resid + first_inverse_deviation * (
        grad_first_unit
        - first_unit_rows * jnp.mean(grad_first_unit * first_unit_rows, -1, keepdims=True)
    )
    grad_in = lax.dynamic_slice_in_dim(
        d_input.reshape(sequence_count, len_dev, model_width), row_idx * row_width, row_width, 2
    )
    g_gain_one, g_wq, g_wk, g_wv, g_wo, g_gain_two, g_router, g_sg, g_su, g_sd = (
        lax.psum_scatter(
            first_gain_gradient.astype(jnp.bfloat16), "cols", scatter_dimension=0, tiled=True
        ).astype(jnp.float32),
        lax.psum_scatter(
            grad_wq.astype(jnp.bfloat16), "cols", scatter_dimension=0, tiled=True
        ).astype(jnp.float32),
        lax.psum_scatter(
            grad_wk.astype(jnp.bfloat16), "cols", scatter_dimension=0, tiled=True
        ).astype(jnp.float32),
        lax.psum_scatter(
            grad_wv.astype(jnp.bfloat16), "cols", scatter_dimension=0, tiled=True
        ).astype(jnp.float32),
        lax.psum_scatter(
            grad_wo.astype(jnp.bfloat16), "cols", scatter_dimension=1, tiled=True
        ).astype(jnp.float32),
        lax.psum_scatter(
            second_gain_gradient.astype(jnp.bfloat16), "cols", scatter_dimension=0, tiled=True
        ).astype(jnp.float32),
        lax.psum_scatter(
            grad_router.astype(jnp.bfloat16), "cols", scatter_dimension=0, tiled=True
        ).astype(jnp.float32),
        lax.psum_scatter(
            grad_sg.astype(jnp.bfloat16), "cols", scatter_dimension=0, tiled=True
        ).astype(jnp.float32),
        lax.psum_scatter(
            grad_su.astype(jnp.bfloat16), "cols", scatter_dimension=0, tiled=True
        ).astype(jnp.float32),
        lax.psum_scatter(
            grad_sd.astype(jnp.bfloat16), "cols", scatter_dimension=1, tiled=True
        ).astype(jnp.float32),
    )
    return (
        layer_out,
        grad_in,
        g_gain_one,
        g_wq,
        g_wk,
        g_wv,
        g_wo,
        g_gain_two,
        g_router,
        g_sg,
        g_su,
        g_sd,
        grad_eg.reshape(expert_gate.shape),
        grad_eu.reshape(expert_up.shape),
        grad_ed.reshape(expert_down.shape),
    )


def scores_of(keys, queries, scale):
    return matmul_nt(keys, queries) * scale


def causal_mask(scores):
    key_pos = lax.broadcasted_iota(jnp.int32, scores.shape, 0)
    query_pos = lax.broadcasted_iota(jnp.int32, scores.shape, 1)
    return query_pos >= key_pos


def attention_forward_kernel(
    scale, block_ref, q_ref, k_ref, vt_ref, out_ref, lse_ref, top, total, acc
):
    length = q_ref.shape[0]
    own = block_ref[0]
    queries = q_ref[...]

    def part(block):
        start = pl.multiple_of(block * length, length)
        scores = scores_of(k_ref[pl.ds(start, length), :], queries, scale)
        return scores, vt_ref[:, pl.ds(start, length)]

    scores, values_t = part(own)
    scores = jnp.where(causal_mask(scores), scores, NEG_LARGE)
    high = jnp.max(scores, 0, keepdims=True)
    probs = jnp.exp(scores - high)
    top[...] = high
    total[...] = jnp.sum(probs, 0, keepdims=True)
    acc[...] = matmul(values_t, probs.astype(jnp.bfloat16))

    @pl.loop(0, own)
    def _(block):
        scores, values_t = part(block)
        high = jnp.maximum(top[...], jnp.max(scores, 0, keepdims=True))
        probs = jnp.exp(scores - high)
        shrink = jnp.exp(top[...] - high)
        top[...] = high
        total[...] = total[...] * shrink + jnp.sum(probs, 0, keepdims=True)
        acc[...] = acc[...] * shrink + matmul(values_t, probs.astype(jnp.bfloat16))

    out_ref[...] = (acc[...] / total[...]).T
    lse_ref[0] = top[...] + jnp.log(total[...])


def attention_forward(block, queries, keys, values_t):
    length, width = queries.shape
    heads = width // HEAD_DIM
    whole = keys.shape[0]
    return pl.pallas_call(
        lambda *refs: attention_forward_kernel(1.0 / math.sqrt(HEAD_DIM), *refs),
        grid_spec=pltpu.PrefetchScalarGridSpec(
            num_scalar_prefetch=1,
            grid=(heads,),
            in_specs=[
                pl.BlockSpec((length, HEAD_DIM), lambda h, s: (0, h)),
                pl.BlockSpec((whole, HEAD_DIM), lambda h, s: (0, 0)),
                pl.BlockSpec((HEAD_DIM, whole), lambda h, s: (0, 0)),
            ],
            out_specs=[
                pl.BlockSpec((length, HEAD_DIM), lambda h, s: (0, h)),
                pl.BlockSpec((1, 1, length), lambda h, s: (h, 0, 0)),
            ],
            scratch_shapes=[
                pltpu.VMEM((1, length), jnp.float32),
                pltpu.VMEM((1, length), jnp.float32),
                pltpu.VMEM((HEAD_DIM, length), jnp.float32),
            ],
        ),
        out_shape=[
            jax.ShapeDtypeStruct((length, width), jnp.float32),
            jax.ShapeDtypeStruct((heads, 1, length), jnp.float32),
        ],
        compiler_params=pltpu.CompilerParams(vmem_limit_bytes=48 * 1024 * 1024),
        cost_estimate=pl.CostEstimate(
            flops=4 * length * width * whole,
            bytes_accessed=2 * whole * HEAD_DIM * 2 + length * width * 6,
            transcendentals=length * heads * whole,
        ),
        name="attention_forward",
    )(block, queries, keys, values_t)


def attention_backward_kernel(
    scale, block_ref, q_ref, k_ref, kt_ref, v_ref, go_ref, lse_ref, delta_ref, dq_ref, dkv_ref, dqt
):
    length, width = q_ref.shape
    heads = width // HEAD_DIM
    step = pl.program_id(0)
    own = block_ref[0]

    @pl.when(step == 0)
    def _():
        dqt[...] = jnp.zeros_like(dqt)

    def one_block(masked):
        keys = k_ref[...]
        keys_t = kt_ref[...]
        values = v_ref[...]
        d_key = jnp.zeros((length, HEAD_DIM), jnp.float32)
        d_value = jnp.zeros((length, HEAD_DIM), jnp.float32)
        for head in range(heads):
            columns = slice(head * HEAD_DIM, (head + 1) * HEAD_DIM)
            queries = q_ref[:, columns]
            grads = go_ref[:, columns]
            probs = jnp.exp(scores_of(keys, queries, scale) - lse_ref[head])
            if masked:
                probs = jnp.where(causal_mask(probs), probs, 0.0)
            d_probs = matmul_nt(values, grads)
            d_scores = (probs * (d_probs - delta_ref[head])).astype(jnp.bfloat16)
            d_value = d_value + matmul(probs.astype(jnp.bfloat16), grads)
            d_key = d_key + matmul(d_scores, queries)
            dqt[head] = dqt[head] + matmul(keys_t, d_scores)
        dkv_ref[:, :HEAD_DIM] = (d_key * scale).astype(dkv_ref.dtype)
        dkv_ref[:, HEAD_DIM:] = d_value.astype(dkv_ref.dtype)

    @pl.when(step < own)
    def _():
        one_block(False)

    @pl.when(step == own)
    def _():
        one_block(True)

    @pl.when(step > own)
    def _():
        dkv_ref[...] = jnp.zeros_like(dkv_ref)

    @pl.when(step == pl.num_programs(0) - 1)
    def _():
        for head in range(heads):
            dq_ref[:, head * HEAD_DIM : (head + 1) * HEAD_DIM] = (dqt[head] * scale).T


def attention_backward(block, queries, keys, keys_t, values, grads, lse, delta):
    length, width = queries.shape
    heads = width // HEAD_DIM
    whole = keys.shape[0]
    fixed = lambda b, s: (0, 0)
    fixed_three = lambda b, s: (0, 0, 0)
    return pl.pallas_call(
        lambda *refs: attention_backward_kernel(1.0 / math.sqrt(HEAD_DIM), *refs),
        grid_spec=pltpu.PrefetchScalarGridSpec(
            num_scalar_prefetch=1,
            grid=(whole // length,),
            in_specs=[
                pl.BlockSpec((length, width), fixed),
                pl.BlockSpec((length, HEAD_DIM), lambda b, s: (jnp.minimum(b, s[0]), 0)),
                pl.BlockSpec((HEAD_DIM, length), lambda b, s: (0, jnp.minimum(b, s[0]))),
                pl.BlockSpec((length, HEAD_DIM), lambda b, s: (jnp.minimum(b, s[0]), 0)),
                pl.BlockSpec((length, width), fixed),
                pl.BlockSpec((heads, 1, length), fixed_three),
                pl.BlockSpec((heads, 1, length), fixed_three),
            ],
            out_specs=[
                pl.BlockSpec((length, width), fixed),
                pl.BlockSpec((length, 2 * HEAD_DIM), lambda b, s: (b, 0)),
            ],
            scratch_shapes=[pltpu.VMEM((heads, HEAD_DIM, length), jnp.float32)],
        ),
        out_shape=[
            jax.ShapeDtypeStruct((length, width), jnp.float32),
            jax.ShapeDtypeStruct((whole, 2 * HEAD_DIM), jnp.bfloat16),
        ],
        compiler_params=pltpu.CompilerParams(vmem_limit_bytes=48 * 1024 * 1024),
        cost_estimate=pl.CostEstimate(
            flops=10 * length * width * whole,
            bytes_accessed=6 * whole * HEAD_DIM * 2 + length * width * 8,
            transcendentals=length * heads * whole,
        ),
        name="attention_backward",
    )(block, queries, keys, keys_t, values, grads, lse, delta)


def add_bf16(left, right):
    return (left.astype(jnp.float32) + right.astype(jnp.float32)).astype(jnp.bfloat16)


class Exchange:
    def __init__(self):
        self.n_rows = lax.axis_size("rows")
        self.n_cols = lax.axis_size("cols")
        self.ring = self.n_cols // 2
        self.r = lax.axis_index("rows")
        self.c = lax.axis_index("cols")
        self.z = self.c // 2
        self.k = self.c % 2

    def move(self, values, target):
        pairs = []
        for r in range(self.n_rows):
            for c in range(self.n_cols):
                to_r, to_c = target(r, c)
                pairs.append((r * self.n_cols + c, to_r * self.n_cols + to_c))
        return lax.ppermute(values, ("rows", "cols"), pairs)

    def along_x(self, values):
        return self.move(values, lambda r, c: (r ^ 1, c))

    def along_y(self, values):
        return self.move(values, lambda r, c: (r ^ 2, c))

    def along_z(self, values, hops=1):
        return self.move(values, lambda r, c: (r, (c + 2 * hops) % self.n_cols))

    def across_z(self, values, bit):
        return self.move(values, lambda r, c: (r, c ^ (2 * bit)))

    def sibling(self, values):
        return self.move(values, lambda r, c: (r, c ^ 1))

    def chip(self, hops):
        return (self.z - hops + self.ring) % self.ring

    def place(self, hops):
        return self.r ^ self.chip(hops)

    def mixed(self, values, axis):
        width = values.shape[axis] // self.n_rows

        def branch(row):
            return lambda whole: jnp.concatenate(
                [
                    lax.slice_in_dim(whole, (row ^ j) * width, ((row ^ j) + 1) * width, axis=axis)
                    for j in range(self.n_rows)
                ],
                axis,
            )

        return lax.switch(self.r, [branch(row) for row in range(self.n_rows)], values)

    def rows_gather(self, block):
        half = block.shape[0] // 2
        from_x = self.along_x(block)
        from_y = self.along_y(block)
        first = self.along_y(from_x[:half])
        second = self.along_x(from_y[half:])
        return [block, from_x, from_y, jnp.concatenate([first, second], 0)]

    def rows_scatter(self, blocks):
        half = blocks[0].shape[0] // 2
        upper = [block[:half] for block in blocks]
        lower = [block[half:] for block in blocks]
        sent = self.along_x(jnp.stack([upper[1], upper[3]]))
        forward = add_bf16(upper[2], sent[1])
        upper_sum = upper[0].astype(jnp.float32) + sent[0].astype(jnp.float32)
        upper_sum = upper_sum + self.along_y(forward).astype(jnp.float32)
        sent = self.along_y(jnp.stack([lower[2], lower[3]]))
        forward = add_bf16(lower[1], sent[1])
        lower_sum = lower[0].astype(jnp.float32) + sent[0].astype(jnp.float32)
        lower_sum = lower_sum + self.along_x(forward).astype(jnp.float32)
        return jnp.concatenate([upper_sum, lower_sum], 0)

    def cols_gather(self, block, place):
        shape = (self.ring, 2) + block.shape
        whole = jnp.zeros(shape, block.dtype)
        rest = (0,) * block.ndim
        for hops in range(self.ring):
            twin = self.sibling(block)
            spot = place(hops)
            whole = lax.dynamic_update_slice(whole, block[None, None], (spot, self.k) + rest)
            whole = lax.dynamic_update_slice(whole, twin[None, None], (spot, 1 - self.k) + rest)
            if hops < self.ring - 1:
                block = self.along_z(block)
        return whole

    def pair_sum(self, parts):
        mine = lax.dynamic_index_in_dim(parts, self.k, 1, False)
        other = lax.dynamic_index_in_dim(parts, 1 - self.k, 1, False)
        return add_bf16(mine, self.sibling(other))

    def cols_scatter(self, parts, place):
        summed = self.pair_sum(parts)
        pick = lambda hops: lax.dynamic_index_in_dim(summed, place(hops), 0, False)
        run = pick(1)
        for hops in range(2, self.ring):
            run = add_bf16(self.along_z(run), pick(hops))
        return self.along_z(run).astype(jnp.float32) + pick(0).astype(jnp.float32)


def split_terms(values):
    high = lax.reduce_precision(values, 8, 7)
    return high.astype(jnp.bfloat16), (values - high).astype(jnp.bfloat16)


def gathered_layer(
    layer_in,
    norm1_gain,
    w_query,
    key_matrix,
    value_matrix,
    w_out,
    norm2_gain,
    w_router,
    shared_gate,
    shared_up,
    shared_down,
    expert_gate,
    expert_up,
    expert_down,
    routes,
    cotangent,
):
    net = Exchange()
    n_rows, ring = net.n_rows, net.ring
    r, c, z, k = net.r, net.c, net.z, net.k
    length, row_width = layer_in.shape[1:]
    rows_dev, top_k = routes.shape[2:]
    experts = w_router.shape[1]
    model_width = row_width * n_rows
    col_width = w_query.shape[0]
    q_width = w_query.shape[1]
    q_heads = q_width // HEAD_DIM
    kv_width = key_matrix.shape[1]
    shared_hidden = shared_gate.shape[1] // ring
    half_hidden = expert_gate.shape[2]
    slots = -(-2 * max(1, 5 * rows_dev * top_k // (8 * experts)) // 16) * 16
    index = lax.dynamic_index_in_dim

    expert_ids = jnp.arange(experts, dtype=jnp.int32)
    hot = jnp.sum(
        (routes.reshape(rows_dev, top_k)[:, :, None] == expert_ids).astype(jnp.float32), 1
    )
    earlier = jnp.tril(jnp.ones((rows_dev, rows_dev), jnp.float32), -1)
    rank = jnp.dot(earlier, hot, precision=PRECISE)
    slot_map = jnp.where(hot > 0, rank, -1.0).T
    slot_maps = lax.all_gather(slot_map, ("cols", "rows"), axis=0, tiled=False)
    slot_maps = slot_maps.reshape(ring, 2, n_rows, experts, rows_dev)
    slot_maps = index(slot_maps, k, 1, False)

    small = jnp.concatenate([w_router, norm1_gain[:, None], norm2_gain[:, None]], 1)
    small = jnp.pad(small, ((0, 0), (0, 128 - small.shape[1])))
    small = net.mixed(lax.all_gather(small, "cols", axis=0, tiled=True), 0)
    router_full = small[:, :experts]
    gains = small[:, experts : experts + 2].astype(jnp.float32).T
    first_gain, second_gain = gains[0][None], gains[1][None]

    token_input = jnp.concatenate(net.rows_gather(layer_in[0]), 1).astype(jnp.float32)
    weights_in = net.cols_gather(
        jnp.concatenate([w_query, key_matrix, value_matrix], 1), net.place
    ).reshape(model_width, -1)
    weights_out_t = net.cols_gather(w_out.T, net.place).reshape(model_width, -1)
    first_inverse = lax.rsqrt(jnp.mean(token_input * token_input, -1, keepdims=True) + NORM_EPS)
    first_unit = token_input * first_inverse
    first_normed = (first_unit * first_gain).astype(jnp.bfloat16)
    projected = matmul(first_normed, weights_in)
    positions = c * length + jnp.arange(length, dtype=jnp.int32)
    cosine_table, sine_table = rope_tables(positions, HEAD_DIM)
    rotated = apply_rotary(
        projected[:, : q_width + kv_width].reshape(length, -1, HEAD_DIM), cosine_table, sine_table
    ).astype(jnp.bfloat16)
    queries = rotated[:, :q_heads].reshape(length, q_width)
    kv_local = jnp.concatenate(
        [rotated[:, q_heads], projected[:, q_width + kv_width :].astype(jnp.bfloat16)], 1
    )
    kv_all = net.cols_gather(kv_local, net.chip).reshape(-1, 2 * HEAD_DIM)
    keys_all, values_all = kv_all[:, :HEAD_DIM], kv_all[:, HEAD_DIM:]
    block_no = c.astype(jnp.int32)[None]
    attn_f32, log_total = attention_forward(block_no, queries, keys_all, values_all.T)
    attn_rows = attn_f32.astype(jnp.bfloat16)
    proj = matmul_nt(attn_rows, weights_out_t).astype(jnp.bfloat16)
    blocks_of = lambda whole: [
        whole[:, j * row_width : (j + 1) * row_width] for j in range(n_rows)
    ]
    proj_mine = net.rows_scatter(blocks_of(proj)).astype(jnp.bfloat16)
    attn_proj = jnp.concatenate(net.rows_gather(proj_mine), 1).astype(jnp.float32)
    residual = token_input + attn_proj
    second_inverse = lax.rsqrt(jnp.mean(residual * residual, -1, keepdims=True) + NORM_EPS)
    second_unit = residual * second_inverse
    second_normed = (second_unit * second_gain).astype(jnp.bfloat16)

    pair = lambda own, axis: jnp.concatenate([own, net.sibling(own)], axis)
    e_gate_w = net.mixed(pair(expert_gate[0], 1), 0)
    e_up_w = net.mixed(pair(expert_up[0], 1), 0)
    e_down_w = net.mixed(pair(expert_down[0], 0), 1)
    packed = jnp.concatenate(
        [
            shared_gate.reshape(col_width, ring, shared_hidden),
            shared_up.reshape(col_width, ring, shared_hidden),
            shared_down.T.reshape(col_width, ring, shared_hidden),
        ],
        2,
    )
    packed = jnp.swapaxes(packed, 0, 1)
    shared_w = jnp.zeros((ring, 2) + packed.shape[1:], jnp.bfloat16)
    for hops in range(ring):
        piece = index(packed, net.chip(-hops), 0, False)
        piece = net.along_z(piece, hops) if hops else piece
        twin = net.sibling(piece)
        spot = net.place(hops)
        shared_w = lax.dynamic_update_slice(shared_w, piece[None, None], (spot, k, 0, 0))
        shared_w = lax.dynamic_update_slice(shared_w, twin[None, None], (spot, 1 - k, 0, 0))
    shared_w = shared_w.reshape(model_width, 3 * shared_hidden)
    shared_in, shared_down_t = shared_w[:, : 2 * shared_hidden], shared_w[:, 2 * shared_hidden :]
    token_w = jnp.concatenate([shared_in, router_full], 1)

    my_expert = r * ring + z
    mine_hot = (expert_ids == my_expert).astype(jnp.float32)
    slot_ids = jnp.arange(slots, dtype=jnp.float32)

    def routing(hops):
        maps = index(slot_maps, net.chip(hops), 0, False)
        my_map = index(maps, my_expert, 1, False)
        pick = my_map[:, None, :] == slot_ids[None, :, None]
        chosen = jnp.swapaxes(maps >= 0, 1, 2).reshape(length, experts)
        return pick, chosen

    def take(pick, rows):
        return jnp.einsum(
            "bst,btd->bsd",
            pick.astype(jnp.bfloat16),
            rows.reshape(n_rows, rows_dev, model_width),
            preferred_element_type=jnp.float32,
        ).astype(jnp.bfloat16).reshape(n_rows * slots, model_width)

    def spread(pick, rows):
        return jnp.einsum(
            "bst,bsd->btd",
            pick.astype(jnp.bfloat16),
            rows.reshape(n_rows, slots, model_width),
            preferred_element_type=jnp.float32,
        ).reshape(length, model_width)

    grad_block = cotangent[0]
    early = []
    for hops in range(ring):
        grad_rows = jnp.concatenate(net.rows_gather(grad_block), 1)
        if hops < ring - 1:
            grad_block = net.along_z(grad_block)
        pick, chosen = routing(hops)
        slot_grads = take(pick, grad_rows)
        through = matmul_nt(slot_grads, e_down_w)
        shared_through = matmul(grad_rows, shared_down_t)
        early.append((pick, chosen, grad_rows, slot_grads, through, shared_through))

    normed_block = second_normed[:, :row_width]
    done = []
    for hops in range(ring):
        pick, chosen, grad_rows, slot_grads, through, shared_through = early[hops]
        if hops == 0:
            rows = second_normed
        else:
            normed_block = net.along_z(normed_block)
            rows = jnp.concatenate(net.rows_gather(normed_block), 1)
        from_tokens = matmul(rows, token_w)
        s_gate = from_tokens[:, :shared_hidden]
        s_up = from_tokens[:, shared_hidden : 2 * shared_hidden]
        logits = from_tokens[:, 2 * shared_hidden :]
        gate_probs = jax.nn.softmax(jnp.where(chosen, logits, NEG_LARGE), -1)
        my_gate = jnp.sum(gate_probs * mine_hot, -1).reshape(n_rows, 1, rows_dev)
        slot_gate = jnp.sum(jnp.where(pick, my_gate, 0.0), -1).reshape(-1, 1)
        slot_rows = take(pick, rows)
        e_gate = matmul(slot_rows, e_gate_w)
        e_up = matmul(slot_rows, e_up_w)
        e_silu, e_slope = silu_parts(e_gate)
        e_act_f = e_silu * e_up
        e_act = e_act_f.astype(jnp.bfloat16)
        d_gate_slot = jnp.sum(e_act_f * through, -1).reshape(n_rows, slots, 1)
        d_gate_token = jnp.sum(jnp.where(pick, d_gate_slot, 0.0), 1).reshape(1, length)
        d_e_act = through * slot_gate
        d_e_gate = (d_e_act * e_up * e_slope).astype(jnp.bfloat16)
        d_e_up = (d_e_act * e_silu).astype(jnp.bfloat16)
        d_part = (slot_grads.astype(jnp.float32) * slot_gate).astype(jnp.bfloat16)
        s_silu, s_slope = silu_parts(s_gate)
        s_act = (s_silu * s_up).astype(jnp.bfloat16)
        d_s_gate = (shared_through * s_up * s_slope).astype(jnp.bfloat16)
        d_s_up = (shared_through * s_silu).astype(jnp.bfloat16)
        d_shared = jnp.concatenate([d_s_gate, d_s_up], 1)
        d_slot_rows = (matmul_nt(d_e_gate, e_gate_w) + matmul_nt(d_e_up, e_up_w)).astype(
            jnp.bfloat16
        )
        d_rows = (spread(pick, d_slot_rows) + matmul_nt(d_shared, shared_in)).astype(jnp.bfloat16)
        part = (matmul(e_act, e_down_w) * slot_gate).astype(jnp.bfloat16)
        out_rows = (spread(pick, part) + matmul_nt(s_act, shared_down_t)).astype(jnp.bfloat16)
        done.append(
            dict(
                rows=rows, slot_rows=slot_rows, e_act=e_act, d_e_gate=d_e_gate, d_e_up=d_e_up,
                d_part=d_part, s_act=s_act, d_shared=d_shared, d_rows=d_rows, out_rows=out_rows,
                gate_probs=gate_probs, d_gate_token=d_gate_token, grad_rows=grad_rows,
            )
        )

    def ring_scatter(name):
        run = None
        for hops in list(range(1, ring)) + [0]:
            here = net.rows_scatter(blocks_of(done[hops][name]))
            if run is not None:
                here = here + net.along_z(run).astype(jnp.float32)
            run = here.astype(jnp.bfloat16)
        return here

    d_gate_all = jnp.zeros((ring, length), jnp.float32)
    for hops in range(ring):
        d_gate_all = lax.dynamic_update_slice(
            d_gate_all, done[hops]["d_gate_token"], (net.chip(hops), 0)
        )
    d_gate_all = lax.all_gather(d_gate_all, ("rows", "cols"), axis=0, tiled=False)
    d_gate_all = index(d_gate_all.reshape(experts, 2, ring, length), k, 1, False)
    grad_router = jnp.zeros((row_width, experts), jnp.float32)
    d_logits_own = None
    for hops in range(ring):
        gate_probs = done[hops]["gate_probs"]
        d_gates = index(d_gate_all, net.chip(hops), 1, False).T
        d_logits = gate_probs * (d_gates - jnp.sum(gate_probs * d_gates, -1, keepdims=True))
        if hops == 0:
            d_logits_own = d_logits
        quarter = lax.dynamic_slice_in_dim(done[hops]["rows"], r * rows_dev, rows_dev, 0)
        quarter = lax.switch(
            r ^ z,
            [
                lambda rows, j=j: rows[:, j * row_width : (j + 1) * row_width]
                for j in range(n_rows)
            ],
            quarter,
        )
        d_quarter = lax.dynamic_slice_in_dim(d_logits, r * rows_dev, rows_dev, 0)
        high, low = split_terms(d_quarter)
        both = matmul_tn(quarter, jnp.concatenate([high, low], 1))
        grad_router = grad_router + both[:, :experts] + both[:, experts:]
    grad_router = grad_router.reshape(2, col_width, experts)
    g_router = index(grad_router, k, 0, False) + net.sibling(index(grad_router, 1 - k, 0, False))
    g_router = g_router + net.along_x(g_router)
    g_router = g_router + net.along_y(g_router)
    high, low = split_terms(d_logits_own)
    d_router_in = matmul_nt(
        jnp.concatenate([high, low], 1), jnp.concatenate([router_full, router_full], 1)
    )

    d_second_mine = ring_scatter("d_rows").astype(jnp.bfloat16)
    d_second = jnp.concatenate(net.rows_gather(d_second_mine), 1).astype(jnp.float32)
    d_second = d_second + d_router_in
    d_second_unit = d_second * second_gain
    second_gain_grad = jnp.sum((d_second * second_unit)[:, :row_width], 0)
    d_resid = done[0]["grad_rows"].astype(jnp.float32) + second_inverse * (
        d_second_unit
        - second_unit * jnp.mean(d_second_unit * second_unit, -1, keepdims=True)
    )
    d_attn = d_resid.astype(jnp.bfloat16)

    d_heads = matmul(d_attn, weights_out_t).astype(jnp.bfloat16)
    delta = jnp.sum(
        (d_heads.astype(jnp.float32) * attn_f32).reshape(length, q_heads, HEAD_DIM), -1
    ).T[:, None, :]
    d_query, d_kv_all = attention_backward(
        block_no, queries, keys_all, keys_all.T, values_all, d_heads, log_total, delta
    )
    d_kv = net.cols_scatter(d_kv_all.reshape(ring, 2, length, 2 * HEAD_DIM), net.chip)
    d_rotated = jnp.concatenate([d_query, d_kv[:, :HEAD_DIM]], 1).reshape(length, -1, HEAD_DIM)
    d_rotated = apply_rotary(d_rotated, cosine_table, -sine_table).reshape(length, -1)
    d_projected = jnp.concatenate([d_rotated, d_kv[:, HEAD_DIM:]], 1).astype(jnp.bfloat16)
    d_first = matmul_nt(d_projected, weights_in).astype(jnp.bfloat16)
    d_first = net.rows_scatter(blocks_of(d_first))
    unit_mine = first_unit[:, :row_width]
    d_first_unit = d_first * first_gain[:, :row_width]
    moment = jnp.sum(d_first_unit * unit_mine, -1).reshape(-1, 128)
    moment = moment + net.along_x(moment)
    moment = moment + net.along_y(moment)
    moment = moment.reshape(length, 1) / model_width
    grad_in = d_resid[:, :row_width] + first_inverse * (d_first_unit - unit_mine * moment)
    first_gain_grad = jnp.sum(d_first * unit_mine, 0)
    gain_grads = jnp.stack([first_gain_grad, second_gain_grad])
    gain_grads = gain_grads + net.sibling(gain_grads)
    bit = 1
    while bit < ring:
        gain_grads = gain_grads + net.across_z(gain_grads, bit)
        bit *= 2
    gain_grads = jnp.stack([gain_grads, net.along_x(gain_grads)])
    gain_grads = jnp.concatenate([gain_grads, net.along_y(gain_grads)])
    gain_grads = index(gain_grads, r ^ z, 0, False).reshape(2, 2, col_width)
    gain_grads = index(gain_grads, k, 1, False)

    column_parts = lambda whole: whole.astype(jnp.bfloat16).reshape(ring, 2, col_width, -1)
    g_in = net.cols_scatter(column_parts(matmul_tn(first_normed, d_projected)), net.place)
    g_out = net.cols_scatter(column_parts(matmul_tn(d_attn, attn_rows)), net.place).T
    joined = lambda name: jnp.concatenate([part[name] for part in done], 0)
    slot_rows, e_act = joined("slot_rows"), joined("e_act")
    d_e_gate, d_e_up, d_part = joined("d_e_gate"), joined("d_e_up"), joined("d_part")

    def halves(left, right, axis):
        whole_width = half_hidden
        own = lambda v: v[:, :whole_width]
        other = lambda v: v[:, whole_width:]
        if axis == 0:
            mine = matmul_tn(left, own(right))
            sent = matmul_tn(left, other(right)).astype(jnp.bfloat16)
        else:
            mine = matmul_tn(own(left), right)
            sent = matmul_tn(other(left), right).astype(jnp.bfloat16)
        return net.mixed(mine + net.sibling(sent).astype(jnp.float32), axis)[None]

    g_expert_gate = halves(slot_rows, d_e_gate, 0)
    g_expert_up = halves(slot_rows, d_e_up, 0)
    g_expert_down = halves(e_act, d_part, 1)

    rows_all, grads_all = joined("rows"), joined("grad_rows")
    shared_parts = jnp.concatenate(
        [matmul_tn(rows_all, joined("d_shared")), matmul_tn(grads_all, joined("s_act"))], 1
    )
    shared_parts = net.pair_sum(column_parts(shared_parts))
    g_shared = jnp.zeros(shared_parts.shape, jnp.bfloat16)
    for hops in range(ring):
        piece = index(shared_parts, net.place(-hops), 0, False)
        piece = net.along_z(piece, hops) if hops else piece
        g_shared = lax.dynamic_update_slice(g_shared, piece[None], (net.chip(hops), 0, 0))
    g_shared = g_shared.astype(jnp.float32)
    shared_cols = lambda n: jnp.swapaxes(
        g_shared[:, :, n * shared_hidden : (n + 1) * shared_hidden], 0, 1
    ).reshape(col_width, -1)

    out_mine = ring_scatter("out_rows")
    layer_out = (residual[:, :row_width] + out_mine).astype(jnp.bfloat16)
    return (
        layer_out[None],
        grad_in[None],
        gain_grads[0],
        g_in[:, :q_width],
        g_in[:, q_width : q_width + kv_width],
        g_in[:, q_width + kv_width :],
        g_out,
        gain_grads[1],
        g_router,
        shared_cols(0),
        shared_cols(1),
        shared_cols(2).T,
        g_expert_gate,
        g_expert_up,
        g_expert_down,
    )


def per_device(layer_in, *others):
    routes = others[13]
    w_router = others[6]
    n_rows, n_cols = lax.axis_size("rows"), lax.axis_size("cols")
    experts, top_k = w_router.shape[1], routes.shape[3]
    gathers = (
        experts <= 4 * top_k
        and layer_in.shape[0] == 1
        and n_rows == 4
        and n_cols == 2 * n_rows
        and 2 * experts == n_rows * n_cols
    )
    return (gathered_layer if gathers else routed_layer)(layer_in, *others)


def solution(mesh):
    placed = (
        P(None, "cols", "rows"),
        P("cols"),
        P("cols", "rows"),
        P("cols", "rows"),
        P("cols", "rows"),
        P("rows", "cols"),
        P("cols"),
        P("cols", None),
        P("cols", "rows"),
        P("cols", "rows"),
        P("rows", "cols"),
        P(("rows", "cols"), None, None),
        P(("rows", "cols"), None, None),
        P(("rows", "cols"), None, None),
        P("cols", "rows", None, None),
        P(None, "cols", "rows"),
    )
    return jax.shard_map(
        per_device,
        mesh=mesh,
        in_specs=placed,
        out_specs=(
            P(None, "cols", "rows"),
            P(None, "cols", "rows"),
            P("cols"),
            P("cols", "rows"),
            P("cols", "rows"),
            P("cols", "rows"),
            P("rows", "cols"),
            P("cols"),
            P("cols", None),
            P("cols", "rows"),
            P("cols", "rows"),
            P("rows", "cols"),
            P(("rows", "cols"), None, None),
            P(("rows", "cols"), None, None),
            P(("rows", "cols"), None, None),
        ),
        check_vma=False,
    )
```

```python
import math

import jax
import jax.numpy as jnp
from jax import lax
from jax.experimental import pallas as pl
from jax.experimental.pallas import tpu as pltpu
from jax.sharding import PartitionSpec as P

HEAD_DIM = 128


NORM_EPS = 1e-05
ROPE_BASE = 500000.0
NEG_LARGE = -1e30
PRECISE = lax.Precision.HIGHEST


def rope_tables(positions, head_size):
    half_size = head_size // 2
    inv_freq = ROPE_BASE ** (-(2.0 * jnp.arange(half_size, dtype=jnp.float32)) / head_size)
    angles = positions.astype(jnp.float32)[:, None] * inv_freq[None, :]
    return (jnp.cos(angles), jnp.sin(angles))


def apply_rotary(values, cosine_table, sine_table):
    half_size = values.shape[-1] // 2
    first_half = values[..., :half_size]
    second = values[..., half_size:]
    cos_b = cosine_table[:, None, :]
    sin_b = sine_table[:, None, :]
    return jnp.concatenate(
        [first_half * cos_b - second * sin_b, second * cos_b + first_half * sin_b], -1
    )


def matmul(left_op, right_op):
    return jnp.dot(left_op, right_op, preferred_element_type=jnp.float32)


def matmul_tn(left_op, right_op):
    return lax.dot_general(
        left_op, right_op, (((0,), (0,)), ((), ())), preferred_element_type=jnp.float32
    )


def matmul_nt(left_op, right_op):
    return lax.dot_general(
        left_op, right_op, (((1,), (1,)), ((), ())), preferred_element_type=jnp.float32
    )


def silu_parts(pre_act):
    sigma = jax.nn.sigmoid(pre_act)
    return (pre_act * sigma, sigma * (1.0 + pre_act * (1.0 - sigma)))


def keep_same(carry_in):
    return carry_in


def routed_layer(
    layer_in,
    norm1_gain,
    w_query,
    key_matrix,
    value_matrix,
    w_out,
    norm2_gain,
    w_router,
    shared_gate,
    shared_up,
    shared_down,
    expert_gate,
    expert_up,
    expert_down,
    routes,
    cotangent,
):
    n_rows = lax.axis_size("rows")
    n_cols = lax.axis_size("cols")
    row_idx = lax.axis_index("rows")
    col_idx = lax.axis_index("cols")
    sequence_count, len_dev, row_width = layer_in.shape
    tok_dev = sequence_count * len_dev
    rows_dev = routes.shape[2]
    top_k = routes.shape[3]
    experts = w_router.shape[1]
    devices = n_rows * n_cols
    capacity = 2 * max(1, 5 * rows_dev * top_k // (8 * experts))
    full_in = lax.all_gather(layer_in, "rows", axis=2, tiled=True)
    (
        gain_one,
        wq_full,
        wk_full,
        wv_full,
        wo_full,
        gain_two,
        router_full,
        sg_full,
        su_full,
        sd_full,
    ) = (
        lax.all_gather(norm1_gain, "cols", axis=0, tiled=True),
        lax.all_gather(w_query, "cols", axis=0, tiled=True),
        lax.all_gather(key_matrix, "cols", axis=0, tiled=True),
        lax.all_gather(value_matrix, "cols", axis=0, tiled=True),
        lax.all_gather(w_out, "cols", axis=1, tiled=True),
        lax.all_gather(norm2_gain, "cols", axis=0, tiled=True),
        lax.all_gather(w_router, "cols", axis=0, tiled=True),
        lax.all_gather(shared_gate, "cols", axis=0, tiled=True),
        lax.all_gather(shared_up, "cols", axis=0, tiled=True),
        lax.all_gather(shared_down, "cols", axis=1, tiled=True),
    )
    model_width = full_in.shape[2]
    token_input = full_in.reshape(tok_dev, model_width).astype(jnp.float32)
    first_inverse_deviation = lax.rsqrt(
        jnp.mean(token_input * token_input, -1, keepdims=True) + NORM_EPS
    )
    first_unit_rows = token_input * first_inverse_deviation
    first_gain_float = gain_one.astype(jnp.float32)
    first_normed = (first_unit_rows * first_gain_float).astype(jnp.bfloat16)
    q_pre = matmul(first_normed, wq_full)
    key_unrotated = matmul(first_normed, wk_full)
    value_projected = matmul(first_normed, wv_full).astype(jnp.bfloat16)
    q_heads = q_pre.shape[1] // HEAD_DIM
    positions = col_idx * len_dev + jnp.arange(len_dev, dtype=jnp.int32)
    cosine_table, sine_table = rope_tables(positions, HEAD_DIM)
    rotated_queries = apply_rotary(
        q_pre.reshape(sequence_count, len_dev, q_heads, HEAD_DIM), cosine_table, sine_table
    ).astype(jnp.bfloat16)
    rotated_keys = apply_rotary(
        key_unrotated.reshape(sequence_count, len_dev, 1, HEAD_DIM), cosine_table, sine_table
    ).astype(jnp.bfloat16)
    kv_local = jnp.concatenate(
        [
            rotated_keys.reshape(sequence_count, len_dev, HEAD_DIM),
            value_projected.reshape(sequence_count, len_dev, HEAD_DIM),
        ],
        -1,
    )
    kv_local = jnp.swapaxes(kv_local, 0, 1)
    query_t = jnp.transpose(rotated_queries, (0, 2, 1, 3))
    score_scale = 1.0 / math.sqrt(HEAD_DIM)
    q_last = col_idx * len_dev + len_dev - 1

    def online_update(carry_in, key_part, k_start):
        run_max, run_sum, run_acc = carry_in
        block_len = key_part.shape[0]
        scores = (
            jnp.einsum(
                "shqd,bsd->shqb",
                query_t,
                key_part[:, :, :HEAD_DIM],
                preferred_element_type=jnp.float32,
            )
            * score_scale
        )
        key_pos = k_start + jnp.arange(block_len, dtype=jnp.int32)
        causal = positions[:, None] >= key_pos[None, :]
        scores = jnp.where(causal, scores, NEG_LARGE)
        new_max = jnp.maximum(run_max, jnp.max(scores, -1))
        prob_vals = jnp.where(causal, jnp.exp(scores - new_max[..., None]), 0.0)
        rescale = jnp.exp(run_max - new_max)
        run_sum = run_sum * rescale + jnp.sum(prob_vals, -1)
        run_acc = run_acc * rescale[..., None] + jnp.einsum(
            "shqb,bsd->shqd",
            prob_vals.astype(jnp.bfloat16),
            key_part[:, :, HEAD_DIM:],
            preferred_element_type=jnp.float32,
        )
        return (new_max, run_sum, run_acc)

    fold_start = (
        jnp.full((sequence_count, q_heads, len_dev), NEG_LARGE, jnp.float32),
        jnp.zeros((sequence_count, q_heads, len_dev), jnp.float32),
        jnp.zeros((sequence_count, q_heads, len_dev, HEAD_DIM), jnp.float32),
    )
    carry_in = fold_start
    piece = lax.all_gather(kv_local, "cols", axis=0, tiled=True)
    start = jnp.int32(0)
    piece_len = piece.shape[0]
    step_len = min(512, piece_len)
    for offset in range(0, piece_len, step_len):
        key_part = piece[offset : offset + step_len]
        k_start = start + offset

        def updated(state_in, key_part=key_part, k_start=k_start):
            return online_update(state_in, key_part, k_start)

        carry_in = lax.cond(k_start <= q_last, updated, keep_same, carry_in)
    run_max, run_sum, run_acc = carry_in
    attn_f32 = run_acc / run_sum[..., None]
    log_total = run_max + jnp.log(run_sum)
    attn_bf = attn_f32.astype(jnp.bfloat16)
    attn_rows = jnp.transpose(attn_bf, (0, 2, 1, 3)).reshape(tok_dev, q_heads * HEAD_DIM)
    attn_proj = lax.psum(matmul(attn_rows, wo_full).astype(jnp.bfloat16), "rows").astype(
        jnp.float32
    )
    residual_stream = token_input + attn_proj
    second_inverse_deviation = lax.rsqrt(
        jnp.mean(residual_stream * residual_stream, -1, keepdims=True) + NORM_EPS
    )
    second_unit_rows = residual_stream * second_inverse_deviation
    second_gain_float = gain_two.astype(jnp.float32)
    second_normed = (second_unit_rows * second_gain_float).astype(jnp.bfloat16)
    gate_pre = matmul(second_normed, sg_full)
    up_pre = matmul(second_normed, su_full)
    silu_gate, silu_slope = silu_parts(gate_pre)
    shared_act = (silu_gate * up_pre).astype(jnp.bfloat16)
    ffn_part = matmul(shared_act, sd_full)
    my_rows = row_idx * rows_dev
    normed_mine = lax.dynamic_slice_in_dim(second_normed, my_rows, rows_dev, 0)
    route_mine = routes.reshape(rows_dev, top_k)
    logits = matmul(normed_mine, router_full)
    expert_ids = jnp.arange(experts, dtype=jnp.int32)
    chosen_hot = (route_mine[:, :, None] == expert_ids[None, None, :]).astype(jnp.float32)
    chosen = jnp.sum(chosen_hot * logits[:, None, :], -1)
    gate_probs = jax.nn.softmax(chosen, -1)
    assign_count = rows_dev * top_k
    flat_routes = route_mine.reshape(assign_count)
    assign_hot = (flat_routes[:, None] == expert_ids[None, :]).astype(jnp.int32)
    rank_in = jnp.sum((jnp.cumsum(assign_hot, 0) - assign_hot) * assign_hot, 1)
    slot_of = flat_routes * capacity + rank_in
    assign_of_slot = (
        jnp.zeros((experts * capacity,), jnp.int32)
        .at[slot_of]
        .set(jnp.arange(assign_count, dtype=jnp.int32))
    )
    slot_used = jnp.zeros((experts * capacity,), jnp.int32).at[slot_of].set(1)
    slot_row = assign_of_slot // top_k

    def send_rows(slot_vals):
        slot_vals = slot_vals.reshape(experts, capacity, model_width)
        outgoing = jnp.broadcast_to(
            slot_vals[:, None], (experts, 2, capacity, model_width)
        ).reshape(devices, capacity, model_width)
        received = lax.all_to_all(
            outgoing, ("rows", "cols"), split_axis=0, concat_axis=0, tiled=True
        )
        return received.reshape(devices * capacity, model_width)

    def return_rows(slot_vals):
        returned = lax.all_to_all(
            slot_vals.reshape(devices, capacity, model_width),
            ("rows", "cols"),
            split_axis=0,
            concat_axis=0,
            tiled=True,
        )
        returned = returned.reshape(experts, 2, capacity, model_width).astype(jnp.float32)
        summed = (returned[:, 0] + returned[:, 1]).astype(jnp.bfloat16)
        return summed.reshape(experts * capacity, model_width).astype(jnp.float32)

    slot_inputs = jnp.where(slot_used[:, None] > 0, normed_mine[slot_row], 0)
    expert_rows = send_rows(slot_inputs)
    eg_mat = expert_gate.reshape(model_width, -1)
    eu_mat = expert_up.reshape(model_width, -1)
    ed_mat = expert_down.reshape(-1, model_width)
    e_gate = matmul(expert_rows, eg_mat)
    e_up = matmul(expert_rows, eu_mat)
    e_silu, e_slope = silu_parts(e_gate)
    e_act = (e_silu * e_up).astype(jnp.bfloat16)
    e_out = matmul(e_act, ed_mat).astype(jnp.bfloat16)
    expert_sum = return_rows(e_out)
    picked = expert_sum[slot_of].reshape(rows_dev, top_k, model_width)
    routed = jnp.sum(gate_probs[:, :, None] * picked, 1)
    ffn_full = lax.dynamic_update_slice_in_dim(
        ffn_part, lax.dynamic_slice_in_dim(ffn_part, my_rows, rows_dev, 0) + routed, my_rows, 0
    )
    ffn_mine = lax.psum_scatter(
        ffn_full.reshape(sequence_count, len_dev, model_width).astype(jnp.bfloat16),
        "rows",
        scatter_dimension=2,
        tiled=True,
    ).astype(jnp.float32)
    resid_mine = lax.dynamic_slice_in_dim(
        residual_stream.reshape(sequence_count, len_dev, model_width),
        row_idx * row_width,
        row_width,
        2,
    )
    layer_out = (resid_mine + ffn_mine).astype(jnp.bfloat16)
    grad_full = lax.all_gather(cotangent, "rows", axis=2, tiled=True).reshape(tok_dev, model_width)
    d_shared_act = matmul_nt(grad_full, sd_full)
    grad_sd = matmul_tn(shared_act, grad_full)
    d_gate_pre = (d_shared_act * up_pre * silu_slope).astype(jnp.bfloat16)
    d_up_pre = (d_shared_act * silu_gate).astype(jnp.bfloat16)
    grad_sg = matmul_tn(second_normed, d_gate_pre)
    grad_su = matmul_tn(second_normed, d_up_pre)
    grad_second_normed = matmul_nt(d_gate_pre, sg_full) + matmul_nt(d_up_pre, su_full)
    grad_mine = lax.dynamic_slice_in_dim(grad_full, my_rows, rows_dev, 0).astype(jnp.float32)
    d_gates = jnp.sum(grad_mine[:, None, :] * picked, -1)
    to_experts = (
        (gate_probs[:, :, None] * grad_mine[:, None, :])
        .reshape(assign_count, model_width)
        .astype(jnp.bfloat16)
    )
    slot_grads = jnp.where(slot_used[:, None] > 0, to_experts[assign_of_slot], 0)
    d_expert_out = send_rows(slot_grads)
    grad_ed = matmul_tn(e_act, d_expert_out)
    d_e_act = matmul_nt(d_expert_out, ed_mat)
    d_e_gate = (d_e_act * e_up * e_slope).astype(jnp.bfloat16)
    d_e_up = (d_e_act * e_silu).astype(jnp.bfloat16)
    grad_eg = matmul_tn(expert_rows, d_e_gate)
    grad_eu = matmul_tn(expert_rows, d_e_up)
    d_rows = (matmul_nt(d_e_gate, eg_mat) + matmul_nt(d_e_up, eu_mat)).astype(jnp.bfloat16)
    d_assign = return_rows(d_rows)[slot_of].reshape(rows_dev, top_k, model_width)
    d_routed_in = jnp.sum(d_assign, 1)
    d_chosen = gate_probs * (d_gates - jnp.sum(gate_probs * d_gates, -1, keepdims=True))
    d_logits = jnp.sum(chosen_hot * d_chosen[:, :, None], 1)
    router_f = router_full.astype(jnp.float32)
    grad_router_part = jnp.dot(normed_mine.astype(jnp.float32).T, d_logits, precision=PRECISE)
    d_router_in = jnp.dot(d_logits, router_f.T, precision=PRECISE)
    d_mine = (
        lax.dynamic_slice_in_dim(grad_second_normed, my_rows, rows_dev, 0)
        + d_routed_in
        + d_router_in
    )
    grad_second_normed = lax.dynamic_update_slice_in_dim(grad_second_normed, d_mine, my_rows, 0)
    grad_second_normed, grad_router = (
        lax.psum(grad_second_normed.astype(jnp.bfloat16), "rows").astype(jnp.float32),
        lax.psum(grad_router_part.astype(jnp.bfloat16), "rows").astype(jnp.float32),
    )
    grad_second_unit = grad_second_normed * second_gain_float
    second_gain_gradient = jnp.sum(grad_second_normed * second_unit_rows, 0)
    d_resid = grad_full.astype(jnp.float32) + second_inverse_deviation * (
        grad_second_unit
        - second_unit_rows * jnp.mean(grad_second_unit * second_unit_rows, -1, keepdims=True)
    )
    d_attn = d_resid.astype(jnp.bfloat16)
    grad_wo = matmul_tn(attn_rows, d_attn)
    d_heads = matmul_nt(d_attn, wo_full).astype(jnp.bfloat16)
    d_heads_t = jnp.transpose(
        d_heads.reshape(sequence_count, len_dev, q_heads, HEAD_DIM), (0, 2, 1, 3)
    )
    delta_rows = jnp.sum(d_heads_t.astype(jnp.float32) * attn_f32, -1)
    kv_all = lax.all_gather(kv_local, "cols", axis=0, tiled=True)
    seq_len = kv_all.shape[0]
    key_block = min(512, seq_len)

    def key_step(block_no, carry_in):
        k_start = block_no * key_block
        key_part = lax.dynamic_slice_in_dim(kv_all, k_start, key_block, 0)

        def contribute(state_in):
            d_query_in, d_kv_in = state_in
            keys_bf = key_part[:, :, :HEAD_DIM]
            values_bf = key_part[:, :, HEAD_DIM:]
            scores = (
                jnp.einsum("shqd,bsd->shqb", query_t, keys_bf, preferred_element_type=jnp.float32)
                * score_scale
            )
            key_pos = k_start + jnp.arange(key_block, dtype=jnp.int32)
            causal = positions[:, None] >= key_pos[None, :]
            prob_vals = jnp.where(causal, jnp.exp(scores - log_total[..., None]), 0.0)
            d_prob = jnp.einsum(
                "shqd,bsd->shqb", d_heads_t, values_bf, preferred_element_type=jnp.float32
            )
            d_scores = (prob_vals * (d_prob - delta_rows[..., None])).astype(jnp.bfloat16)
            d_query_in = (
                d_query_in
                + jnp.einsum(
                    "shqb,bsd->shqd", d_scores, keys_bf, preferred_element_type=jnp.float32
                )
                * score_scale
            )
            d_key = (
                jnp.einsum("shqb,shqd->bsd", d_scores, query_t, preferred_element_type=jnp.float32)
                * score_scale
            )
            d_value = jnp.einsum(
                "shqb,shqd->bsd",
                prob_vals.astype(jnp.bfloat16),
                d_heads_t,
                preferred_element_type=jnp.float32,
            )
            d_kv_in = lax.dynamic_update_slice_in_dim(
                d_kv_in, jnp.concatenate([d_key, d_value], -1), k_start, 0
            )
            return (d_query_in, d_kv_in)

        return lax.cond(k_start <= q_last, contribute, keep_same, carry_in)

    grad_start = (
        jnp.zeros((sequence_count, q_heads, len_dev, HEAD_DIM), jnp.float32),
        jnp.zeros((seq_len, sequence_count, 2 * HEAD_DIM), jnp.float32),
    )
    d_query, d_kv_all = lax.fori_loop(0, seq_len // key_block, key_step, grad_start)
    d_kv = lax.psum_scatter(
        d_kv_all.astype(jnp.bfloat16), "cols", scatter_dimension=0, tiled=True
    ).astype(jnp.float32)
    d_query_rows = (
        apply_rotary(jnp.transpose(d_query, (0, 2, 1, 3)), cosine_table, -sine_table)
        .reshape(tok_dev, q_heads * HEAD_DIM)
        .astype(jnp.bfloat16)
    )
    d_kv_t = jnp.swapaxes(d_kv, 0, 1)
    d_key_rows = (
        apply_rotary(
            d_kv_t[:, :, :HEAD_DIM].reshape(sequence_count, len_dev, 1, HEAD_DIM),
            cosine_table,
            -sine_table,
        )
        .reshape(tok_dev, HEAD_DIM)
        .astype(jnp.bfloat16)
    )
    d_value_rows = d_kv_t[:, :, HEAD_DIM:].reshape(tok_dev, HEAD_DIM).astype(jnp.bfloat16)
    grad_wq = matmul_tn(first_normed, d_query_rows)
    grad_wk = matmul_tn(first_normed, d_key_rows)
    grad_wv = matmul_tn(first_normed, d_value_rows)
    grad_first_normed = (
        matmul_nt(d_query_rows, wq_full)
        + matmul_nt(d_key_rows, wk_full)
        + matmul_nt(d_value_rows, wv_full)
    )
    grad_first_normed = lax.psum(grad_first_normed.astype(jnp.bfloat16), "rows").astype(jnp.float32)
    grad_first_unit = grad_first_normed * first_gain_float
    first_gain_gradient = jnp.sum(grad_first_normed * first_unit_rows, 0)
    d_input = d_resid + first_inverse_deviation * (
        grad_first_unit
        - first_unit_rows * jnp.mean(grad_first_unit * first_unit_rows, -1, keepdims=True)
    )
    grad_in = lax.dynamic_slice_in_dim(
        d_input.reshape(sequence_count, len_dev, model_width), row_idx * row_width, row_width, 2
    )
    g_gain_one, g_wq, g_wk, g_wv, g_wo, g_gain_two, g_router, g_sg, g_su, g_sd = (
        lax.psum_scatter(
            first_gain_gradient.astype(jnp.bfloat16), "cols", scatter_dimension=0, tiled=True
        ).astype(jnp.float32),
        lax.psum_scatter(
            grad_wq.astype(jnp.bfloat16), "cols", scatter_dimension=0, tiled=True
        ).astype(jnp.float32),
        lax.psum_scatter(
            grad_wk.astype(jnp.bfloat16), "cols", scatter_dimension=0, tiled=True
        ).astype(jnp.float32),
        lax.psum_scatter(
            grad_wv.astype(jnp.bfloat16), "cols", scatter_dimension=0, tiled=True
        ).astype(jnp.float32),
        lax.psum_scatter(
            grad_wo.astype(jnp.bfloat16), "cols", scatter_dimension=1, tiled=True
        ).astype(jnp.float32),
        lax.psum_scatter(
            second_gain_gradient.astype(jnp.bfloat16), "cols", scatter_dimension=0, tiled=True
        ).astype(jnp.float32),
        lax.psum_scatter(
            grad_router.astype(jnp.bfloat16), "cols", scatter_dimension=0, tiled=True
        ).astype(jnp.float32),
        lax.psum_scatter(
            grad_sg.astype(jnp.bfloat16), "cols", scatter_dimension=0, tiled=True
        ).astype(jnp.float32),
        lax.psum_scatter(
            grad_su.astype(jnp.bfloat16), "cols", scatter_dimension=0, tiled=True
        ).astype(jnp.float32),
        lax.psum_scatter(
            grad_sd.astype(jnp.bfloat16), "cols", scatter_dimension=1, tiled=True
        ).astype(jnp.float32),
    )
    return (
        layer_out,
        grad_in,
        g_gain_one,
        g_wq,
        g_wk,
        g_wv,
        g_wo,
        g_gain_two,
        g_router,
        g_sg,
        g_su,
        g_sd,
        grad_eg.reshape(expert_gate.shape),
        grad_eu.reshape(expert_up.shape),
        grad_ed.reshape(expert_down.shape),
    )


def scores_of(keys, queries, scale):
    return matmul_nt(keys, queries) * scale


def causal_mask(scores):
    key_pos = lax.broadcasted_iota(jnp.int32, scores.shape, 0)
    query_pos = lax.broadcasted_iota(jnp.int32, scores.shape, 1)
    return query_pos >= key_pos


MESH_ID = pl.DeviceIdType.MESH
MIB = 1024 * 1024


class Links:
    def __init__(self, n_rows, n_cols):
        self.n_rows, self.n_cols, self.ring = n_rows, n_cols, n_cols // 2
        self.r = lax.axis_index("rows")
        self.c = lax.axis_index("cols")
        self.z = lax.div(self.c, 2)
        self.k = lax.rem(self.c, 2)
        self.x = (self.flip(1), self.c)
        self.y = (self.flip(2), self.c)
        self.up = (self.r, lax.rem(self.c + 2, n_cols))
        self.down = (self.r, lax.rem(self.c + n_cols - 2, n_cols))
        self.twin = (self.r, self.c + 1 - 2 * self.k)
        self.started = []

    def flip(self, bits):
        low, high = lax.rem(self.r, 2), lax.div(self.r, 2)
        low = 1 - low if bits & 1 else low
        high = 1 - high if bits & 2 else high
        return low + 2 * high

    def chip(self, hops):
        return lax.rem(self.z + (2 * self.ring - hops), self.ring)

    def place(self, hops):
        other = self.chip(hops)
        low = lax.rem(lax.rem(self.r, 2) + lax.rem(other, 2), 2)
        high = lax.rem(lax.div(self.r, 2) + lax.div(other, 2), 2)
        return low + 2 * high

    def spread_partners(self):
        return [
            (hops, bits, (self.flip(bits), lax.rem(self.c + 2 * hops, self.n_cols)))
            for hops in range(self.ring)
            for bits in range(self.n_rows)
            if hops or bits
        ]

    def greet(self, partners):
        barrier = pltpu.get_barrier_semaphore()
        for partner in partners:
            pl.semaphore_signal(barrier, inc=1, device_id=partner, device_id_type=MESH_ID)
        pl.semaphore_wait(barrier, len(partners))

    def send(self, src, dst, sems, number, partner):
        copy = pltpu.make_async_remote_copy(
            src_ref=src,
            dst_ref=dst,
            send_sem=sems[0].at[number],
            recv_sem=sems[1].at[number],
            device_id=partner,
            device_id_type=MESH_ID,
        )
        copy.start()
        self.started.append(copy)
        return copy

    def finish(self):
        for copy in self.started:
            copy.wait_send()


def run_together(*steps):
    live = list(steps)
    while live:
        live = [step for step in live if next(step, True) is None]


def pair_sems(count):
    return [pltpu.SemaphoreType.DMA((count,)), pltpu.SemaphoreType.DMA((count,))]


def gather_square(net, src, out, sems, local_sem, chunks):
    rows, width = src.shape
    half = rows // 2

    def block(s, j, part=None):
        columns = pl.ds(j * width, width)
        if part is None:
            return out.at[s, :, columns]
        return out.at[s, pl.ds(part * half, half), columns]

    def part_of(s, part):
        return src.at[pl.ds(part * half, half), :] if s == 0 else block(s, 0, part)

    own = pltpu.make_async_copy(src, block(0, 0), local_sem)
    own.start()
    ups, xs, ys, lasts = [], [], [], []

    def send_chunk(s):
        if s < chunks - 1:
            whole = src if s == 0 else block(s, 0)
            ups.append(net.send(whole, block(s + 1, 0), sems, 7 * s, net.up))
        xs.append([net.send(part_of(s, p), block(s, 1, p), sems, 7 * s + 1 + p, net.x) for p in (0, 1)])
        ys.append(
            [net.send(part_of(s, p), block(s, 2, p), sems, 7 * s + 3 + p, net.y) for p in (1, 0)][::-1]
        )

    def forward(s):
        xs[s][0].wait_recv()
        first = net.send(block(s, 1, 0), block(s, 3, 0), sems, 7 * s + 5, net.y)
        ys[s][1].wait_recv()
        second = net.send(block(s, 2, 1), block(s, 3, 1), sems, 7 * s + 6, net.x)
        lasts.append([first, second])

    send_chunk(0)
    yield
    for s in range(1, chunks):
        ups[s - 1].wait_recv()
        send_chunk(s)
        yield
        forward(s - 1)
        yield
    forward(chunks - 1)
    yield
    own.wait()
    for s in range(chunks):
        xs[s][1].wait_recv()
        ys[s][0].wait_recv()
        lasts[s][0].wait_recv()
        lasts[s][1].wait_recv()


def gather_columns(net, src, spot, sems, local_sem):
    own = pltpu.make_async_copy(src, spot(0, net.k), local_sem)
    own.start()
    twins = []
    for hops in range(net.ring):
        if hops:
            up.wait_recv()
        here = src if hops == 0 else spot(hops, net.k)
        if hops < net.ring - 1:
            up = net.send(here, spot(hops, net.k), sems, hops, net.up)
        twins.append(net.send(here, spot(hops, net.k), sems, net.ring + hops, net.twin))
        yield
    own.wait()
    for copy in twins:
        copy.wait_recv()


def add_slabs(target, terms, slab=64):
    rows = target.shape[0]

    @pl.loop(0, rows // slab)
    def _(i):
        at = pl.ds(pl.multiple_of(i * slab, slab), slab)
        total = terms[0](at)
        for term in terms[1:]:
            total = total + term(at)
        target[at, :] = total.astype(target.dtype)


def part_reader(ref, *lead, columns=None):
    def read(at):
        values = ref[(*lead, at, slice(None) if columns is None else columns)]
        return values.astype(jnp.float32)

    return read


def scatter_scratch(chunks, rows, width):
    half = rows // 2
    return [
        pltpu.VMEM((chunks, 2, half, width), jnp.bfloat16),
        pltpu.VMEM((chunks, half, 2 * width), jnp.bfloat16),
        pltpu.VMEM((chunks, 2, half, width), jnp.bfloat16),
        pltpu.VMEM((chunks, half, 2 * width), jnp.bfloat16),
        pltpu.VMEM((chunks, 2, half, width), jnp.bfloat16),
        pltpu.VMEM((chunks, 2, half, width), jnp.bfloat16),
        pltpu.SemaphoreType.DMA((chunks, 3)),
    ] + pair_sems(5 * chunks)


def scatter_square(net, src, scratch, order, finish):
    my_up, my_low, got_x, got_y, got_last, stage, load_sems, *sems = scratch
    half, width = my_up.shape[2:]
    upper, lower = pl.ds(0, half), pl.ds(half, half)
    column = lambda j, count=1: pl.ds(j * width, count * width)
    left, right = pl.ds(0, width), pl.ds(width, width)
    loads, sent = {}, {}

    def first(s):
        loads[s] = [
            pltpu.make_async_copy(src.at[s, upper, column(0)], my_up.at[s, 0], load_sems.at[s, 0]),
            pltpu.make_async_copy(src.at[s, upper, column(2)], my_up.at[s, 1], load_sems.at[s, 1]),
            pltpu.make_async_copy(src.at[s, lower, column(0, 2)], my_low.at[s], load_sems.at[s, 2]),
        ]
        sent[s] = [
            net.send(src.at[s, upper, column(3)], got_x.at[s, 1], sems, 5 * s, net.x),
            net.send(src.at[s, lower, column(2, 2)], got_y.at[s], sems, 5 * s + 1, net.y),
            net.send(src.at[s, upper, column(1)], got_x.at[s, 0], sems, 5 * s + 2, net.x),
        ]
        for load in loads[s]:
            load.start()

    def second(s):
        loads[s][1].wait()
        sent[s][0].wait_recv()
        add_slabs(stage.at[s, 0], [part_reader(my_up, s, 1), part_reader(got_x, s, 1)])
        sent[s].append(net.send(stage.at[s, 0], got_last.at[s, 0], sems, 5 * s + 3, net.y))
        loads[s][2].wait()
        sent[s][1].wait_recv()
        add_slabs(
            stage.at[s, 1],
            [part_reader(my_low, s, columns=right), part_reader(got_y, s, columns=right)],
        )
        sent[s].append(net.send(stage.at[s, 1], got_last.at[s, 1], sems, 5 * s + 4, net.x))

    def third(s):
        loads[s][0].wait()
        for copy in sent[s][2:]:
            copy.wait_recv()
        finish(
            s,
            [part_reader(my_up, s, 0), part_reader(got_x, s, 0), part_reader(got_last, s, 0)],
            [
                part_reader(my_low, s, columns=left),
                part_reader(got_y, s, columns=left),
                part_reader(got_last, s, 1),
            ],
        )

    for i in range(len(order) + 2):
        if i < len(order):
            first(order[i])
            yield
        if 0 <= i - 1 < len(order):
            second(order[i - 1])
            yield
        if 0 <= i - 2:
            third(order[i - 2])
            yield


def ring_scratch(ring, rows, width):
    return [
        pltpu.VMEM((ring - 1, rows, width), jnp.bfloat16),
        pltpu.VMEM((ring - 1, rows, width), jnp.bfloat16),
    ] + pair_sems(ring - 1)


def ring_finish(net, scratch, target):
    landed, leaving, *sems = scratch
    rows = landed.shape[1]
    copies = []

    def finish(s, upper, lower):
        turn = (s - 1) % net.ring
        for part, terms in ((0, upper), (1, lower)):
            at = pl.ds(part * (rows // 2), rows // 2)
            if turn and not part:
                copies[turn - 1].wait_recv()
            if turn:
                terms = terms + [part_reader(landed.at[turn - 1, at, :])]
            goal = target.at[at, :] if s == 0 else leaving.at[turn, at, :]
            add_slabs(goal, terms)
        if s:
            copies.append(net.send(leaving.at[turn], landed.at[turn], sems, turn, net.up))

    return finish


def scatter_columns(net, src, out, scratch):
    mine, got_twin, landed, leaving, load_sems, twin_send, twin_recv, *sems = scratch
    loads, twins, copies = {}, {}, []
    order = list(range(1, net.ring)) + [0]
    for hops in order:
        loads[hops] = pltpu.make_async_copy(
            src.at[net.place(hops), net.k], mine.at[hops], load_sems.at[hops]
        )
        loads[hops].start()
        twins[hops] = net.send(
            src.at[net.place(hops), 1 - net.k],
            got_twin.at[hops],
            (twin_send, twin_recv),
            hops,
            net.twin,
        )
    yield
    for turn, hops in enumerate(order):
        loads[hops].wait()
        twins[hops].wait_recv()
        terms = [part_reader(mine, hops), part_reader(got_twin, hops)]
        if turn:
            copies[turn - 1].wait_recv()
            terms.append(part_reader(landed, turn - 1))
        add_slabs(leaving.at[turn] if hops else out, terms, 32)
        if hops:
            copies.append(net.send(leaving.at[turn], landed.at[turn], sems, turn, net.up))
        yield


def scatter_columns_scratch(ring, rows, width):
    return [
        pltpu.VMEM((ring, rows, width), jnp.bfloat16),
        pltpu.VMEM((ring, rows, width), jnp.bfloat16),
        pltpu.VMEM((ring - 1, rows, width), jnp.bfloat16),
        pltpu.VMEM((ring - 1, rows, width), jnp.bfloat16),
        pltpu.SemaphoreType.DMA((ring,)),
    ] + pair_sems(ring) + pair_sems(ring - 1)


def remote_call(kernel, name, collective_id, out_shape, scratch, operands, in_vmem=(), out_vmem=(), cost=None):
    anywhere = pl.BlockSpec(memory_space=pl.ANY)
    vmem = pl.BlockSpec(memory_space=pltpu.VMEM)
    return pl.pallas_call(
        kernel,
        out_shape=out_shape,
        in_specs=[vmem if i in in_vmem else anywhere for i in range(len(operands))],
        out_specs=[vmem if i in out_vmem else anywhere for i in range(len(out_shape))],
        scratch_shapes=scratch,
        compiler_params=pltpu.CompilerParams(
            collective_id=collective_id, has_side_effects=True, vmem_limit_bytes=60 * MIB
        ),
        cost_estimate=cost,
        name=name,
    )(*operands)


def front_gather(n_rows, n_cols, block, weights, small):
    ring = n_cols // 2
    shape = lambda *dims: jax.ShapeDtypeStruct(dims, jnp.bfloat16)

    def kernel(x, w, s, x_out, w_out, s_out, xs, xr, ws, wr, ss, sr, local):
        net = Links(n_rows, n_cols)
        net.greet([net.x, net.y, net.up, net.down, net.twin])
        spot = lambda out: lambda hops, core: out.at[net.place(hops), core]
        run_together(
            gather_columns(net, s, spot(s_out), (ss, sr), local.at[2]),
            gather_square(net, x, x_out, (xs, xr), local.at[0], 1),
            gather_columns(net, w, spot(w_out), (ws, wr), local.at[1]),
        )
        net.finish()

    return remote_call(
        kernel,
        "front_gather",
        1,
        [
            shape(1, block.shape[0], n_rows * block.shape[1]),
            shape(ring, 2, *weights.shape),
            shape(ring, 2, *small.shape),
        ],
        pair_sems(7) + pair_sems(2 * ring) + pair_sems(2 * ring) + [pltpu.SemaphoreType.DMA((3,))],
        (block, weights, small),
    )


def attention_gather(n_rows, n_cols, queries, kv, grads, weights, slot_map):
    ring = n_cols // 2
    length, width = queries.shape
    heads = width // HEAD_DIM
    scale = 1.0 / math.sqrt(HEAD_DIM)
    shape = jax.ShapeDtypeStruct

    def kernel(
        q, kv_in, g, w, m, out, lse, kv_out, g_out, w_out, m_out,
        kv_all, top, total, acc, gs, gr, ws, wr, ks, kr, ms, mr, local,
    ):
        net = Links(n_rows, n_cols)
        others = net.spread_partners()
        net.greet([device for _, _, device in others] + [net.twin])
        kv_steps = gather_columns(
            net, kv_in, lambda hops, core: kv_all.at[2 * net.chip(hops) + core], (ks, kr), local.at[0]
        )
        next(kv_steps)
        maps = []
        for number, (hops, bits, device) in enumerate(others):
            maps.append(net.send(m, m_out.at[hops, net.r], (ms, mr), number, device))
        own_map = pltpu.make_async_copy(m, m_out.at[0, net.r], local.at[1])
        own_map.start()
        w_steps = gather_columns(
            net, w, lambda hops, core: w_out.at[net.place(hops), core], (ws, wr), local.at[2]
        )
        g_steps = gather_square(net, g, g_out, (gs, gr), local.at[3], ring)
        next(g_steps)
        next(w_steps)
        run_together(kv_steps)
        kv_save = pltpu.make_async_copy(kv_all, kv_out, local.at[4])
        kv_save.start()

        for head in range(heads):
            columns = slice(head * HEAD_DIM, (head + 1) * HEAD_DIM)
            queries = q[:, columns]

            def part(block):
                return scores_of(kv_all[block, :, :HEAD_DIM], queries, scale), kv_all[block, :, HEAD_DIM:]

            scores, values = part(net.c)
            scores = jnp.where(causal_mask(scores), scores, NEG_LARGE)
            high = jnp.max(scores, 0, keepdims=True)
            probs = jnp.exp(scores - high)
            top[...] = high
            total[...] = jnp.sum(probs, 0, keepdims=True)
            acc[...] = matmul_tn(values, probs.astype(jnp.bfloat16))

            @pl.loop(0, net.c)
            def _(block):
                scores, values = part(block)
                high = jnp.maximum(top[...], jnp.max(scores, 0, keepdims=True))
                probs = jnp.exp(scores - high)
                shrink = jnp.exp(top[...] - high)
                top[...] = high
                total[...] = total[...] * shrink + jnp.sum(probs, 0, keepdims=True)
                acc[...] = acc[...] * shrink + matmul_tn(values, probs.astype(jnp.bfloat16))

            out[:, columns] = (acc[...] / total[...]).T
            lse[head] = top[...] + jnp.log(total[...])
            next(g_steps, None)
            next(w_steps, None)

        run_together(g_steps, w_steps)
        own_map.wait()
        for copy in maps:
            copy.wait_recv()
        kv_save.wait()
        net.finish()

    partners = n_rows * ring - 1
    return remote_call(
        kernel,
        "attention_gather",
        2,
        [
            shape((length, width), jnp.float32),
            shape((heads, 1, length), jnp.float32),
            shape((n_cols, *kv.shape), jnp.bfloat16),
            shape((ring, grads.shape[0], n_rows * grads.shape[1]), jnp.bfloat16),
            shape((ring, 2, *weights.shape), jnp.bfloat16),
            shape((ring, n_rows, *slot_map.shape), jnp.float32),
        ],
        [
            pltpu.VMEM((n_cols, *kv.shape), jnp.bfloat16),
            pltpu.VMEM((1, length), jnp.float32),
            pltpu.VMEM((1, length), jnp.float32),
            pltpu.VMEM((HEAD_DIM, length), jnp.float32),
        ]
        + pair_sems(7 * ring)
        + pair_sems(2 * ring)
        + pair_sems(2 * ring)
        + pair_sems(partners)
        + [pltpu.SemaphoreType.DMA((5,))],
        (queries, kv, grads, weights, slot_map),
        in_vmem=(0,),
        out_vmem=(0, 1),
    )


def rows_sum(n_rows, n_cols, parts):
    pieces = 2
    rows, whole = parts.shape
    width = whole // n_rows
    piece = rows // pieces
    shape = jax.ShapeDtypeStruct((pieces, piece, whole), jnp.bfloat16)

    def kernel(src, out, result, *rest):
        scratch, (gs0, gr0, gs1, gr1, local) = rest[:-5], rest[-5:]
        net = Links(n_rows, n_cols)
        net.greet([net.x, net.y])
        gathers = []

        def finish(s, upper, lower):
            add_slabs(result.at[s, pl.ds(0, piece // 2), :], upper)
            add_slabs(result.at[s, pl.ds(piece // 2, piece // 2), :], lower)
            sems = ((gs0, gr0), (gs1, gr1))[s]
            steps = gather_square(net, result.at[s], out.at[pl.ds(s, 1)], sems, local.at[s], 1)
            next(steps)
            gathers.append(steps)

        run_together(scatter_square(net, src, scratch, list(range(pieces)), finish))
        run_together(*gathers)
        net.finish()

    return remote_call(
        kernel,
        "rows_sum",
        3,
        [shape],
        [pltpu.VMEM((pieces, piece, width), jnp.bfloat16)]
        + scatter_scratch(pieces, piece, width)
        + pair_sems(7)
        + pair_sems(7)
        + [pltpu.SemaphoreType.DMA((pieces,))],
        (parts.reshape(shape.shape),),
    )[0].reshape(rows, whole)


def token_gather(n_rows, n_cols, block):
    ring = n_cols // 2

    def kernel(x, out, xs, xr, local):
        net = Links(n_rows, n_cols)
        net.greet([net.x, net.y, net.up, net.down])
        run_together(gather_square(net, x, out, (xs, xr), local.at[0], ring))
        net.finish()

    return remote_call(
        kernel,
        "token_gather",
        4,
        [jax.ShapeDtypeStruct((ring, block.shape[0], n_rows * block.shape[1]), jnp.bfloat16)],
        pair_sems(7 * ring) + [pltpu.SemaphoreType.DMA((1,))],
        (block,),
    )[0]


def token_sum(n_rows, n_cols, parts, gates):
    ring = n_cols // 2
    rows, width = parts.shape[1], parts.shape[2] // n_rows
    experts = n_rows * ring

    def kernel(src, gate, out, gate_out, result, *rest):
        scratch, ring_parts = rest[:9], rest[9:13]
        gs, gr, ms, mr, local = rest[13:]
        net = Links(n_rows, n_cols)
        others = net.spread_partners()
        net.greet([device for _, _, device in others])
        mine = net.r * ring + net.z
        copies = []
        own = pltpu.make_async_copy(gate, gate_out.at[mine], local.at[1])
        own.start()
        for number, (hops, bits, device) in enumerate(others):
            copies.append(net.send(gate, gate_out.at[mine], (ms, mr), number, device))
        order = list(range(1, ring)) + [0]
        run_together(
            scatter_square(net, src, scratch, order, ring_finish(net, ring_parts, result))
        )
        run_together(gather_square(net, result, out, (gs, gr), local.at[0], 1))
        own.wait()
        for copy in copies:
            copy.wait_recv()
        net.finish()

    out, gate_out = remote_call(
        kernel,
        "token_sum",
        5,
        [
            jax.ShapeDtypeStruct((1, rows, n_rows * width), jnp.bfloat16),
            jax.ShapeDtypeStruct((experts, *gates.shape), jnp.float32),
        ],
        [pltpu.VMEM((rows, width), jnp.bfloat16)]
        + scatter_scratch(ring, rows, width)
        + ring_scratch(ring, rows, width)
        + pair_sems(7)
        + pair_sems(experts - 1)
        + [pltpu.SemaphoreType.DMA((2,))],
        (parts, gates),
    )
    return out[0], gate_out


def last_sums(n_rows, n_cols, parts, weights):
    ring = n_cols // 2
    rows, width = parts.shape[1], parts.shape[2] // n_rows

    def kernel(src, w, out, w_out, *rest):
        scratch, ring_parts, column_parts = rest[:9], rest[9:13], rest[13:]
        net = Links(n_rows, n_cols)
        net.greet([net.x, net.y, net.up, net.down, net.twin])
        order = list(range(1, ring)) + [0]
        run_together(
            scatter_columns(net, w, w_out, column_parts),
            scatter_square(net, src, scratch, order, ring_finish(net, ring_parts, out)),
        )
        net.finish()

    return remote_call(
        kernel,
        "last_sums",
        6,
        [
            jax.ShapeDtypeStruct((rows, width), jnp.float32),
            jax.ShapeDtypeStruct(weights.shape[2:], jnp.float32),
        ],
        scatter_scratch(ring, rows, width)
        + ring_scratch(ring, rows, width)
        + scatter_columns_scratch(ring, *weights.shape[2:]),
        (parts, weights),
        out_vmem=(0, 1),
    )


def expert_kernel(
    info, rows, grads, slot_row, chosen, mine_hot, gate_own, gate_twin, up_own, up_twin, down_own,
    down_twin, token_w, shared_down,
    d_rows_out, rows_out, slot_rows, d_part, e_act, d_gate, d_up, s_act, d_shared, probs_out, d_gates,
    w_gate, w_up, w_down, slot_dx, part, sems,
):
    tokens, model = rows.shape[1:]
    n_slots = slot_rows.shape[1]
    half_hidden = gate_own.shape[1]
    hidden = 2 * half_hidden
    pad = shared_down.shape[1]
    row = info[0]
    width = model // 4
    bf16, f32 = jnp.bfloat16, jnp.float32

    @pl.when(pl.program_id(0) == 0)
    def _():
        copies = []
        for j in range(4):
            flipped = row + (1 - 2 * lax.rem(row, 2)) * (j & 1) + (2 - 4 * lax.div(row, 2)) * (j >> 1)
            there = pl.ds(pl.multiple_of(flipped * width, width), width)
            here = pl.ds(j * width, width)
            for h, sources in enumerate(((gate_own, up_own, down_own), (gate_twin, up_twin, down_twin))):
                cols = pl.ds(h * half_hidden, half_hidden)
                number = 6 * j + 3 * h
                copies += [
                    pltpu.make_async_copy(
                        sources[0].at[there, :], w_gate.at[here, cols], sems.at[number]
                    ),
                    pltpu.make_async_copy(
                        sources[1].at[there, :], w_up.at[here, cols], sems.at[number + 1]
                    ),
                    pltpu.make_async_copy(
                        sources[2].at[:, there], w_down.at[cols, here], sems.at[number + 2]
                    ),
                ]
        for copy in copies:
            copy.start()
        for copy in copies:
            copy.wait()

    x = rows[0]
    pick = (
        lax.broadcasted_iota(jnp.int32, (n_slots, tokens), 0).astype(f32) == slot_row[0]
    ).astype(f32)
    pick_b = pick.astype(bf16)
    pick_t = pick.T.astype(bf16)
    exact = lambda a, b, dims: lax.dot_general(
        a, b, (dims, ((), ())), precision=PRECISE, preferred_element_type=f32
    )

    logits = matmul(x, token_w[:, 2 * pad :])
    logits = jnp.where(chosen[0] > 0, logits, NEG_LARGE)
    logits = jnp.exp(logits - jnp.max(logits, -1, keepdims=True))
    probs = logits / jnp.sum(logits, -1, keepdims=True)
    probs_out[0] = probs
    my_gate = jnp.sum(probs * mine_hot[...], -1, keepdims=True)
    slot_gate = exact(pick, jnp.broadcast_to(my_gate, (tokens, 128)), ((1,), (0,)))[:, :1]
    s_gate = matmul(x, token_w[:, :pad])
    s_up = matmul(x, token_w[:, pad : 2 * pad])
    through = matmul(grads[0], shared_down[...])
    s_silu, s_slope = silu_parts(s_gate)
    s_act[0] = (s_silu * s_up).astype(bf16)
    d_shared[0, :, :pad] = (through * s_up * s_slope).astype(bf16)
    d_shared[0, :, pad:] = (through * s_silu).astype(bf16)

    tile = 512
    for t in range(model // tile):
        at = slice(t * tile, (t + 1) * tile)
        slot_rows[0, :, at] = matmul(pick_b, rows[0, :, at]).astype(bf16)
        picked = matmul(pick_b, grads[0, :, at])
        part[:, at] = picked.astype(bf16)
        d_part[0, :, at] = (picked * slot_gate).astype(bf16)

    step = 256

    def hidden_tile(t, total):
        at = pl.ds(pl.multiple_of(t * step, step), step)
        e_gate = matmul(slot_rows[0], w_gate[:, at])
        e_up = matmul(slot_rows[0], w_up[:, at])
        through = matmul_nt(part[...], w_down[at, :])
        e_silu, e_slope = silu_parts(e_gate)
        act = e_silu * e_up
        d_act = through * slot_gate
        e_act[0, :, at] = act.astype(bf16)
        d_gate[0, :, at] = (d_act * e_up * e_slope).astype(bf16)
        d_up[0, :, at] = (d_act * e_silu).astype(bf16)
        return total + jnp.sum(act * through, -1, keepdims=True)

    d_gate_slot = lax.fori_loop(0, hidden // step, hidden_tile, jnp.zeros((n_slots, 1), f32))
    d_gates[0] = exact(jnp.broadcast_to(d_gate_slot, (n_slots, 128)), pick, ((0,), (0,)))[:1]

    @pl.loop(0, model // tile)
    def _(t):
        at = pl.ds(pl.multiple_of(t * tile, tile), tile)
        d_slot = matmul_nt(d_gate[0], w_gate[at, :]) + matmul_nt(d_up[0], w_up[at, :])
        d_rows_out[0, :, at] = (
            matmul(pick_t, d_slot.astype(bf16)) + matmul_nt(d_shared[0], token_w[at, : 2 * pad])
        ).astype(bf16)
        out = (matmul(e_act[0], w_down[:, at]) * slot_gate).astype(bf16)
        rows_out[0, :, at] = (
            matmul(pick_t, out) + matmul_nt(s_act[0], shared_down[at, :])
        ).astype(bf16)


def expert_chunks(
    info, rows, grads, slot_row, chosen, mine_hot, experts_w, token_w, shared_down, slots
):
    chunks, tokens, model = rows.shape
    half_hidden = experts_w[0].shape[1]
    hidden = 2 * half_hidden
    pad = shared_down.shape[1]
    by_chunk = lambda *dims: pl.BlockSpec((1, *dims), lambda i, s: (i, 0, 0))
    once = lambda *dims: pl.BlockSpec(dims, lambda i, s: (0, 0), pipeline_mode=pl.Buffered(1))
    anywhere = pl.BlockSpec(memory_space=pl.ANY)
    single = lambda *dims: pl.BlockSpec(
        (1, *dims), lambda i, s: (i, 0, 0), pipeline_mode=pl.Buffered(1)
    )
    bf16, f32 = jnp.bfloat16, jnp.float32
    shape = lambda dtype, *dims: jax.ShapeDtypeStruct((chunks, *dims), dtype)
    return pl.pallas_call(
        expert_kernel,
        grid_spec=pltpu.PrefetchScalarGridSpec(
            num_scalar_prefetch=1,
            grid=(chunks,),
            in_specs=[
                by_chunk(tokens, model),
                by_chunk(tokens, model),
                by_chunk(1, tokens),
                by_chunk(tokens, 128),
                once(1, 128),
            ]
            + [anywhere] * 6
            + [once(*token_w.shape), once(*shared_down.shape)],
            out_specs=[
                single(tokens, model),
                single(tokens, model),
                single(slots, model),
                single(slots, model),
                single(slots, hidden),
                single(slots, hidden),
                single(slots, hidden),
                single(tokens, pad),
                single(tokens, 2 * pad),
                single(tokens, 128),
                pl.BlockSpec((1, 1, tokens), lambda i, s: (s[1 + i], 0, 0)),
            ],
            scratch_shapes=[
                pltpu.VMEM((model, hidden), bf16),
                pltpu.VMEM((model, hidden), bf16),
                pltpu.VMEM((hidden, model), bf16),
                pltpu.VMEM((8, 128), bf16),
                pltpu.VMEM((slots, model), bf16),
                pltpu.SemaphoreType.DMA((24,)),
            ],
        ),
        out_shape=[
            shape(bf16, tokens, model),
            shape(bf16, tokens, model),
            shape(bf16, slots, model),
            shape(bf16, slots, model),
            shape(bf16, slots, hidden),
            shape(bf16, slots, hidden),
            shape(bf16, slots, hidden),
            shape(bf16, tokens, pad),
            shape(bf16, tokens, 2 * pad),
            shape(f32, tokens, 128),
            shape(f32, 1, tokens),
        ],
        compiler_params=pltpu.CompilerParams(vmem_limit_bytes=63 * MIB),
        cost_estimate=pl.CostEstimate(
            flops=chunks * 2 * tokens * model * (4 * hidden + 6 * pad),
            bytes_accessed=40 * MIB,
            transcendentals=chunks * slots * hidden,
        ),
        name="expert_chunks",
    )(info, rows, grads, slot_row, chosen, mine_hot, *experts_w, token_w, shared_down)


def attention_backward_kernel(
    scale, block_ref, q_ref, k_ref, kt_ref, v_ref, go_ref, lse_ref, delta_ref, dq_ref, dkv_ref, dqt
):
    length, width = q_ref.shape
    heads = width // HEAD_DIM
    step = pl.program_id(0)
    own = block_ref[0]

    @pl.when(step == 0)
    def _():
        dqt[...] = jnp.zeros_like(dqt)

    def one_block(masked):
        keys = k_ref[...]
        keys_t = kt_ref[...]
        values = v_ref[...]
        d_key = jnp.zeros((length, HEAD_DIM), jnp.float32)
        d_value = jnp.zeros((length, HEAD_DIM), jnp.float32)
        for head in range(heads):
            columns = slice(head * HEAD_DIM, (head + 1) * HEAD_DIM)
            queries = q_ref[:, columns]
            grads = go_ref[:, columns]
            probs = jnp.exp(scores_of(keys, queries, scale) - lse_ref[head])
            if masked:
                probs = jnp.where(causal_mask(probs), probs, 0.0)
            d_probs = matmul_nt(values, grads)
            d_scores = (probs * (d_probs - delta_ref[head])).astype(jnp.bfloat16)
            d_value = d_value + matmul(probs.astype(jnp.bfloat16), grads)
            d_key = d_key + matmul(d_scores, queries)
            dqt[head] = dqt[head] + matmul(keys_t, d_scores)
        dkv_ref[:, :HEAD_DIM] = (d_key * scale).astype(dkv_ref.dtype)
        dkv_ref[:, HEAD_DIM:] = d_value.astype(dkv_ref.dtype)

    @pl.when(step < own)
    def _():
        one_block(False)

    @pl.when(step == own)
    def _():
        one_block(True)

    @pl.when(step > own)
    def _():
        dkv_ref[...] = jnp.zeros_like(dkv_ref)

    @pl.when(step == pl.num_programs(0) - 1)
    def _():
        for head in range(heads):
            dq_ref[:, head * HEAD_DIM : (head + 1) * HEAD_DIM] = (dqt[head] * scale).T


def attention_backward(block, queries, keys, keys_t, values, grads, lse, delta):
    length, width = queries.shape
    heads = width // HEAD_DIM
    whole = keys.shape[0]
    fixed = lambda b, s: (0, 0)
    fixed_three = lambda b, s: (0, 0, 0)
    return pl.pallas_call(
        lambda *refs: attention_backward_kernel(1.0 / math.sqrt(HEAD_DIM), *refs),
        grid_spec=pltpu.PrefetchScalarGridSpec(
            num_scalar_prefetch=1,
            grid=(whole // length,),
            in_specs=[
                pl.BlockSpec((length, width), fixed),
                pl.BlockSpec((length, HEAD_DIM), lambda b, s: (jnp.minimum(b, s[0]), 0)),
                pl.BlockSpec((HEAD_DIM, length), lambda b, s: (0, jnp.minimum(b, s[0]))),
                pl.BlockSpec((length, HEAD_DIM), lambda b, s: (jnp.minimum(b, s[0]), 0)),
                pl.BlockSpec((length, width), fixed),
                pl.BlockSpec((heads, 1, length), fixed_three),
                pl.BlockSpec((heads, 1, length), fixed_three),
            ],
            out_specs=[
                pl.BlockSpec((length, width), fixed),
                pl.BlockSpec((length, 2 * HEAD_DIM), lambda b, s: (b, 0)),
            ],
            scratch_shapes=[pltpu.VMEM((heads, HEAD_DIM, length), jnp.float32)],
        ),
        out_shape=[
            jax.ShapeDtypeStruct((length, width), jnp.float32),
            jax.ShapeDtypeStruct((whole, 2 * HEAD_DIM), jnp.bfloat16),
        ],
        compiler_params=pltpu.CompilerParams(vmem_limit_bytes=48 * 1024 * 1024),
        cost_estimate=pl.CostEstimate(
            flops=10 * length * width * whole,
            bytes_accessed=6 * whole * HEAD_DIM * 2 + length * width * 8,
            transcendentals=length * heads * whole,
        ),
        name="attention_backward",
    )(block, queries, keys, keys_t, values, grads, lse, delta)


def add_bf16(left, right):
    return (left.astype(jnp.float32) + right.astype(jnp.float32)).astype(jnp.bfloat16)


class Exchange:
    def __init__(self):
        self.n_rows = lax.axis_size("rows")
        self.n_cols = lax.axis_size("cols")
        self.ring = self.n_cols // 2
        self.r = lax.axis_index("rows")
        self.c = lax.axis_index("cols")
        self.z = self.c // 2
        self.k = self.c % 2

    def move(self, values, target):
        pairs = []
        for r in range(self.n_rows):
            for c in range(self.n_cols):
                to_r, to_c = target(r, c)
                pairs.append((r * self.n_cols + c, to_r * self.n_cols + to_c))
        return lax.ppermute(values, ("rows", "cols"), pairs)

    def along_x(self, values):
        return self.move(values, lambda r, c: (r ^ 1, c))

    def along_y(self, values):
        return self.move(values, lambda r, c: (r ^ 2, c))

    def along_z(self, values, hops=1):
        return self.move(values, lambda r, c: (r, (c + 2 * hops) % self.n_cols))

    def across_z(self, values, bit):
        return self.move(values, lambda r, c: (r, c ^ (2 * bit)))

    def sibling(self, values):
        return self.move(values, lambda r, c: (r, c ^ 1))

    def chip(self, hops):
        return (self.z - hops + self.ring) % self.ring

    def place(self, hops):
        return self.r ^ self.chip(hops)

    def mixed(self, values, axis):
        width = values.shape[axis] // self.n_rows

        def branch(row):
            return lambda whole: jnp.concatenate(
                [
                    lax.slice_in_dim(whole, (row ^ j) * width, ((row ^ j) + 1) * width, axis=axis)
                    for j in range(self.n_rows)
                ],
                axis,
            )

        return lax.switch(self.r, [branch(row) for row in range(self.n_rows)], values)

    def rows_gather(self, block):
        half = block.shape[0] // 2
        from_x = self.along_x(block)
        from_y = self.along_y(block)
        first = self.along_y(from_x[:half])
        second = self.along_x(from_y[half:])
        return [block, from_x, from_y, jnp.concatenate([first, second], 0)]

    def rows_scatter(self, blocks):
        half = blocks[0].shape[0] // 2
        upper = [block[:half] for block in blocks]
        lower = [block[half:] for block in blocks]
        sent = self.along_x(jnp.stack([upper[1], upper[3]]))
        forward = add_bf16(upper[2], sent[1])
        upper_sum = upper[0].astype(jnp.float32) + sent[0].astype(jnp.float32)
        upper_sum = upper_sum + self.along_y(forward).astype(jnp.float32)
        sent = self.along_y(jnp.stack([lower[2], lower[3]]))
        forward = add_bf16(lower[1], sent[1])
        lower_sum = lower[0].astype(jnp.float32) + sent[0].astype(jnp.float32)
        lower_sum = lower_sum + self.along_x(forward).astype(jnp.float32)
        return jnp.concatenate([upper_sum, lower_sum], 0)

    def cols_gather(self, block, place):
        shape = (self.ring, 2) + block.shape
        whole = jnp.zeros(shape, block.dtype)
        rest = (0,) * block.ndim
        for hops in range(self.ring):
            twin = self.sibling(block)
            spot = place(hops)
            whole = lax.dynamic_update_slice(whole, block[None, None], (spot, self.k) + rest)
            whole = lax.dynamic_update_slice(whole, twin[None, None], (spot, 1 - self.k) + rest)
            if hops < self.ring - 1:
                block = self.along_z(block)
        return whole

    def pair_sum(self, parts):
        mine = lax.dynamic_index_in_dim(parts, self.k, 1, False)
        other = lax.dynamic_index_in_dim(parts, 1 - self.k, 1, False)
        return add_bf16(mine, self.sibling(other))

    def cols_scatter(self, parts, place):
        summed = self.pair_sum(parts)
        pick = lambda hops: lax.dynamic_index_in_dim(summed, place(hops), 0, False)
        run = pick(1)
        for hops in range(2, self.ring):
            run = add_bf16(self.along_z(run), pick(hops))
        return self.along_z(run).astype(jnp.float32) + pick(0).astype(jnp.float32)


def split_terms(values):
    high = lax.reduce_precision(values, 8, 7)
    return high.astype(jnp.bfloat16), (values - high).astype(jnp.bfloat16)


def gathered_layer(
    layer_in,
    norm1_gain,
    w_query,
    key_matrix,
    value_matrix,
    w_out,
    norm2_gain,
    w_router,
    shared_gate,
    shared_up,
    shared_down,
    expert_gate,
    expert_up,
    expert_down,
    routes,
    cotangent,
):
    net = Exchange()
    n_rows, ring = net.n_rows, net.ring
    r, c, z, k = net.r, net.c, net.z, net.k
    length, row_width = layer_in.shape[1:]
    rows_dev, top_k = routes.shape[2:]
    experts = w_router.shape[1]
    model_width = row_width * n_rows
    col_width = w_query.shape[0]
    q_width = w_query.shape[1]
    q_heads = q_width // HEAD_DIM
    kv_width = key_matrix.shape[1]
    shared_hidden = shared_gate.shape[1] // ring
    half_hidden = expert_gate.shape[2]
    slots = -(-2 * max(1, 5 * rows_dev * top_k // (8 * experts)) // 16) * 16
    index = lax.dynamic_index_in_dim

    expert_ids = jnp.arange(experts, dtype=jnp.int32)
    hot = jnp.sum(
        (routes.reshape(rows_dev, top_k)[:, :, None] == expert_ids).astype(jnp.float32), 1
    )
    earlier = jnp.tril(jnp.ones((rows_dev, rows_dev), jnp.float32), -1)
    rank = jnp.dot(earlier, hot, precision=PRECISE)
    slot_map = jnp.where(hot > 0, rank, -1.0).T

    small = jnp.concatenate([w_router, norm1_gain[:, None], norm2_gain[:, None]], 1)
    small = jnp.pad(small, ((0, 0), (0, 128 - small.shape[1])))
    token_input, weights_in, small = front_gather(
        n_rows, net.n_cols, layer_in[0],
        jnp.concatenate([w_query, key_matrix, value_matrix], 1), small,
    )
    token_input = token_input[0].astype(jnp.float32)
    weights_in = weights_in.reshape(model_width, -1)
    small = small.reshape(model_width, 128)
    router_full = small[:, :experts]
    gains = small[:, experts : experts + 2].astype(jnp.float32).T
    first_gain, second_gain = gains[0][None], gains[1][None]
    first_inverse = lax.rsqrt(jnp.mean(token_input * token_input, -1, keepdims=True) + NORM_EPS)
    first_unit = token_input * first_inverse
    first_normed = (first_unit * first_gain).astype(jnp.bfloat16)
    projected = matmul(first_normed, weights_in)
    positions = c * length + jnp.arange(length, dtype=jnp.int32)
    cosine_table, sine_table = rope_tables(positions, HEAD_DIM)
    rotated = apply_rotary(
        projected[:, : q_width + kv_width].reshape(length, -1, HEAD_DIM), cosine_table, sine_table
    ).astype(jnp.bfloat16)
    queries = rotated[:, :q_heads].reshape(length, q_width)
    kv_local = jnp.concatenate(
        [rotated[:, q_heads], projected[:, q_width + kv_width :].astype(jnp.bfloat16)], 1
    )
    block_no = c.astype(jnp.int32)[None]
    attn_f32, log_total, kv_all, grad_rows, weights_out_t, slot_maps = attention_gather(
        n_rows, net.n_cols, queries, kv_local, cotangent[0], w_out.T, slot_map
    )
    weights_out_t = weights_out_t.reshape(model_width, -1)
    kv_all = kv_all.reshape(-1, 2 * HEAD_DIM)
    keys_all, values_all = kv_all[:, :HEAD_DIM], kv_all[:, HEAD_DIM:]
    attn_rows = attn_f32.astype(jnp.bfloat16)
    proj = matmul_nt(attn_rows, weights_out_t).astype(jnp.bfloat16)
    blocks_of = lambda whole: [
        whole[:, j * row_width : (j + 1) * row_width] for j in range(n_rows)
    ]
    attn_proj = rows_sum(n_rows, net.n_cols, proj).astype(jnp.float32)
    residual = token_input + attn_proj
    second_inverse = lax.rsqrt(jnp.mean(residual * residual, -1, keepdims=True) + NORM_EPS)
    second_unit = residual * second_inverse
    second_normed = (second_unit * second_gain).astype(jnp.bfloat16)

    pad_to = -(-shared_hidden // 128) * 128
    padded = lambda w: jnp.pad(
        w.reshape(col_width, ring, shared_hidden), ((0, 0), (0, 0), (0, pad_to - shared_hidden))
    )
    packed = jnp.concatenate([padded(shared_gate), padded(shared_up), padded(shared_down.T)], 2)
    packed = jnp.swapaxes(packed, 0, 1)
    shared_w = jnp.zeros((ring, 2) + packed.shape[1:], jnp.bfloat16)
    for hops in range(ring):
        piece = index(packed, net.chip(-hops), 0, False)
        piece = net.along_z(piece, hops) if hops else piece
        twin = net.sibling(piece)
        spot = net.place(hops)
        shared_w = lax.dynamic_update_slice(shared_w, piece[None, None], (spot, k, 0, 0))
        shared_w = lax.dynamic_update_slice(shared_w, twin[None, None], (spot, 1 - k, 0, 0))
    shared_w = shared_w.reshape(model_width, 3 * pad_to)
    shared_down_t = shared_w[:, 2 * pad_to :]
    token_w = jnp.concatenate(
        [shared_w[:, : 2 * pad_to], jnp.pad(router_full, ((0, 0), (0, 128 - experts)))], 1
    )
    experts_w = []
    for own in (expert_gate[0], expert_up[0], expert_down[0]):
        experts_w += [own, net.sibling(own)]

    my_expert = r * ring + z
    mine_hot = (jnp.arange(128, dtype=jnp.int32) == my_expert).astype(jnp.float32)[None]
    my_map = index(slot_maps, my_expert, 2, False)
    first_slot = (jnp.arange(n_rows, dtype=jnp.float32) * slots)[None, :, None]
    slot_row = jnp.where(my_map >= 0, my_map + first_slot, -1.0).reshape(ring, 1, length)
    chosen = jnp.swapaxes(slot_maps >= 0, 2, 3).reshape(ring, length, experts)
    chosen = jnp.pad(chosen.astype(jnp.float32), ((0, 0), (0, 0), (0, 128 - experts)))
    rows_all = token_gather(n_rows, net.n_cols, second_normed[:, :row_width])
    info = jnp.stack([r] + [net.chip(hops) for hops in range(ring)]).astype(jnp.int32)
    (
        d_rows, out_rows, slot_rows, d_part, e_act, d_e_gate, d_e_up, s_act, d_shared, gate_probs,
        d_gate_mine,
    ) = expert_chunks(
        info, rows_all, grad_rows, slot_row, chosen, mine_hot, experts_w, token_w, shared_down_t,
        n_rows * slots,
    )

    d_second, d_gate_all = token_sum(
        n_rows, net.n_cols, d_rows, d_gate_mine.reshape(ring, length)
    )
    grad_router = jnp.zeros((row_width, experts), jnp.float32)
    d_logits_own = None
    for hops in range(ring):
        probs = gate_probs[hops][:, :experts]
        d_gates = index(d_gate_all, net.chip(hops), 1, False).T
        d_logits = probs * (d_gates - jnp.sum(probs * d_gates, -1, keepdims=True))
        if hops == 0:
            d_logits_own = d_logits
        quarter = lax.dynamic_slice(rows_all[hops], (r * rows_dev, 0), (rows_dev, model_width))
        quarter = lax.switch(
            r ^ z,
            [
                lambda rows, j=j: rows[:, j * row_width : (j + 1) * row_width]
                for j in range(n_rows)
            ],
            quarter,
        )
        d_quarter = lax.dynamic_slice_in_dim(d_logits, r * rows_dev, rows_dev, 0)
        high, low = split_terms(d_quarter)
        both = matmul_tn(quarter, jnp.concatenate([high, low], 1))
        grad_router = grad_router + both[:, :experts] + both[:, experts:]
    grad_router = grad_router.reshape(2, col_width, experts)
    g_router = index(grad_router, k, 0, False) + net.sibling(index(grad_router, 1 - k, 0, False))
    g_router = g_router + net.along_x(g_router)
    g_router = g_router + net.along_y(g_router)
    high, low = split_terms(d_logits_own)
    d_router_in = matmul_nt(
        jnp.concatenate([high, low], 1), jnp.concatenate([router_full, router_full], 1)
    )
    d_second = d_second.astype(jnp.float32) + d_router_in
    d_second_unit = d_second * second_gain
    second_gain_grad = jnp.sum((d_second * second_unit)[:, :row_width], 0)
    d_resid = grad_rows[0].astype(jnp.float32) + second_inverse * (
        d_second_unit
        - second_unit * jnp.mean(d_second_unit * second_unit, -1, keepdims=True)
    )
    d_attn = d_resid.astype(jnp.bfloat16)

    d_heads = matmul(d_attn, weights_out_t).astype(jnp.bfloat16)
    delta = jnp.sum(
        (d_heads.astype(jnp.float32) * attn_f32).reshape(length, q_heads, HEAD_DIM), -1
    ).T[:, None, :]
    d_query, d_kv_all = attention_backward(
        block_no, queries, keys_all, keys_all.T, values_all, d_heads, log_total, delta
    )
    d_kv = net.cols_scatter(d_kv_all.reshape(ring, 2, length, 2 * HEAD_DIM), net.chip)
    d_rotated = jnp.concatenate([d_query, d_kv[:, :HEAD_DIM]], 1).reshape(length, -1, HEAD_DIM)
    d_rotated = apply_rotary(d_rotated, cosine_table, -sine_table).reshape(length, -1)
    d_projected = jnp.concatenate([d_rotated, d_kv[:, HEAD_DIM:]], 1).astype(jnp.bfloat16)
    d_first = matmul_nt(d_projected, weights_in).astype(jnp.bfloat16)
    d_first = net.rows_scatter(blocks_of(d_first))
    unit_mine = first_unit[:, :row_width]
    d_first_unit = d_first * first_gain[:, :row_width]
    moment = jnp.sum(d_first_unit * unit_mine, -1).reshape(-1, 128)
    moment = moment + net.along_x(moment)
    moment = moment + net.along_y(moment)
    moment = moment.reshape(length, 1) / model_width
    grad_in = d_resid[:, :row_width] + first_inverse * (d_first_unit - unit_mine * moment)
    first_gain_grad = jnp.sum(d_first * unit_mine, 0)
    gain_grads = jnp.stack([first_gain_grad, second_gain_grad])
    gain_grads = gain_grads + net.sibling(gain_grads)
    bit = 1
    while bit < ring:
        gain_grads = gain_grads + net.across_z(gain_grads, bit)
        bit *= 2
    gain_grads = jnp.stack([gain_grads, net.along_x(gain_grads)])
    gain_grads = jnp.concatenate([gain_grads, net.along_y(gain_grads)])
    gain_grads = index(gain_grads, r ^ z, 0, False).reshape(2, 2, col_width)
    gain_grads = index(gain_grads, k, 1, False)

    column_parts = lambda whole: whole.astype(jnp.bfloat16).reshape(ring, 2, col_width, -1)
    joined = lambda whole: whole.reshape(-1, whole.shape[-1])
    slot_rows, e_act, d_part = joined(slot_rows), joined(e_act), joined(d_part)
    d_e_gate, d_e_up = joined(d_e_gate), joined(d_e_up)

    def halves(left, right, axis):
        own = lambda v: v[:, :half_hidden]
        other = lambda v: v[:, half_hidden:]
        if axis == 0:
            mine = matmul_tn(left, own(right))
            sent = matmul_tn(left, other(right)).astype(jnp.bfloat16)
        else:
            mine = matmul_tn(own(left), right)
            sent = matmul_tn(other(left), right).astype(jnp.bfloat16)
        return net.mixed(mine + net.sibling(sent).astype(jnp.float32), axis)[None]

    g_expert_gate = halves(slot_rows, d_e_gate, 0)
    g_expert_up = halves(slot_rows, d_e_up, 0)
    g_expert_down = halves(e_act, d_part, 1)

    shared_parts = jnp.concatenate(
        [
            matmul_tn(joined(rows_all), joined(d_shared)),
            matmul_tn(joined(grad_rows), joined(s_act)),
        ],
        1,
    )
    shared_parts = net.pair_sum(column_parts(shared_parts))
    g_shared = jnp.zeros(shared_parts.shape, jnp.bfloat16)
    for hops in range(ring):
        piece = index(shared_parts, net.place(-hops), 0, False)
        piece = net.along_z(piece, hops) if hops else piece
        g_shared = lax.dynamic_update_slice(g_shared, piece[None], (net.chip(hops), 0, 0))
    g_shared = g_shared.astype(jnp.float32)
    shared_cols = lambda n: jnp.swapaxes(
        g_shared[:, :, n * pad_to : n * pad_to + shared_hidden], 0, 1
    ).reshape(col_width, -1)

    weight_parts = jnp.concatenate(
        [matmul_tn(first_normed, d_projected), matmul_tn(d_attn, attn_rows)], 1
    )
    out_mine, g_in = last_sums(n_rows, net.n_cols, out_rows, column_parts(weight_parts))
    layer_out = (residual[:, :row_width] + out_mine).astype(jnp.bfloat16)
    width_in = q_width + 2 * kv_width
    return (
        layer_out[None],
        grad_in[None],
        gain_grads[0],
        g_in[:, :q_width],
        g_in[:, q_width : q_width + kv_width],
        g_in[:, q_width + kv_width : width_in],
        g_in[:, width_in:].T,
        gain_grads[1],
        g_router,
        shared_cols(0),
        shared_cols(1),
        shared_cols(2).T,
        g_expert_gate,
        g_expert_up,
        g_expert_down,
    )


def per_device(layer_in, *others):
    routes = others[13]
    w_router = others[6]
    n_rows, n_cols = lax.axis_size("rows"), lax.axis_size("cols")
    experts, top_k = w_router.shape[1], routes.shape[3]
    gathers = (
        experts <= 4 * top_k
        and layer_in.shape[0] == 1
        and n_rows == 4
        and n_cols == 2 * n_rows
        and 2 * experts == n_rows * n_cols
    )
    return (gathered_layer if gathers else routed_layer)(layer_in, *others)


def solution(mesh):
    placed = (
        P(None, "cols", "rows"),
        P("cols"),
        P("cols", "rows"),
        P("cols", "rows"),
        P("cols", "rows"),
        P("rows", "cols"),
        P("cols"),
        P("cols", None),
        P("cols", "rows"),
        P("cols", "rows"),
        P("rows", "cols"),
        P(("rows", "cols"), None, None),
        P(("rows", "cols"), None, None),
        P(("rows", "cols"), None, None),
        P("cols", "rows", None, None),
        P(None, "cols", "rows"),
    )
    return jax.shard_map(
        per_device,
        mesh=mesh,
        in_specs=placed,
        out_specs=(
            P(None, "cols", "rows"),
            P(None, "cols", "rows"),
            P("cols"),
            P("cols", "rows"),
            P("cols", "rows"),
            P("cols", "rows"),
            P("rows", "cols"),
            P("cols"),
            P("cols", None),
            P("cols", "rows"),
            P("cols", "rows"),
            P("rows", "cols"),
            P(("rows", "cols"), None, None),
            P(("rows", "cols"), None, None),
            P(("rows", "cols"), None, None),
        ),
        check_vma=False,
    )
```

```python
import math

import jax
import jax.numpy as jnp
from jax import lax
from jax.experimental import pallas as pl
from jax.experimental.pallas import tpu as pltpu
from jax.sharding import PartitionSpec as P

HEAD_DIM = 128


NORM_EPS = 1e-05
ROPE_BASE = 500000.0
NEG_LARGE = -1e30
PRECISE = lax.Precision.HIGHEST


def rope_tables(positions, head_size):
    half_size = head_size // 2
    inv_freq = ROPE_BASE ** (-(2.0 * jnp.arange(half_size, dtype=jnp.float32)) / head_size)
    angles = positions.astype(jnp.float32)[:, None] * inv_freq[None, :]
    return (jnp.cos(angles), jnp.sin(angles))


def apply_rotary(values, cosine_table, sine_table):
    half_size = values.shape[-1] // 2
    first_half = values[..., :half_size]
    second = values[..., half_size:]
    cos_b = cosine_table[:, None, :]
    sin_b = sine_table[:, None, :]
    return jnp.concatenate(
        [first_half * cos_b - second * sin_b, second * cos_b + first_half * sin_b], -1
    )


def matmul(left_op, right_op):
    return jnp.dot(left_op, right_op, preferred_element_type=jnp.float32)


def matmul_tn(left_op, right_op):
    return lax.dot_general(
        left_op, right_op, (((0,), (0,)), ((), ())), preferred_element_type=jnp.float32
    )


def matmul_nt(left_op, right_op):
    return lax.dot_general(
        left_op, right_op, (((1,), (1,)), ((), ())), preferred_element_type=jnp.float32
    )


def silu_parts(pre_act):
    sigma = jax.nn.sigmoid(pre_act)
    return (pre_act * sigma, sigma * (1.0 + pre_act * (1.0 - sigma)))


def keep_same(carry_in):
    return carry_in


def routed_layer(
    layer_in,
    norm1_gain,
    w_query,
    key_matrix,
    value_matrix,
    w_out,
    norm2_gain,
    w_router,
    shared_gate,
    shared_up,
    shared_down,
    expert_gate,
    expert_up,
    expert_down,
    routes,
    cotangent,
):
    n_rows = lax.axis_size("rows")
    n_cols = lax.axis_size("cols")
    row_idx = lax.axis_index("rows")
    col_idx = lax.axis_index("cols")
    sequence_count, len_dev, row_width = layer_in.shape
    tok_dev = sequence_count * len_dev
    rows_dev = routes.shape[2]
    top_k = routes.shape[3]
    experts = w_router.shape[1]
    devices = n_rows * n_cols
    capacity = 2 * max(1, 5 * rows_dev * top_k // (8 * experts))
    full_in = lax.all_gather(layer_in, "rows", axis=2, tiled=True)
    (
        gain_one,
        wq_full,
        wk_full,
        wv_full,
        wo_full,
        gain_two,
        router_full,
        sg_full,
        su_full,
        sd_full,
    ) = (
        lax.all_gather(norm1_gain, "cols", axis=0, tiled=True),
        lax.all_gather(w_query, "cols", axis=0, tiled=True),
        lax.all_gather(key_matrix, "cols", axis=0, tiled=True),
        lax.all_gather(value_matrix, "cols", axis=0, tiled=True),
        lax.all_gather(w_out, "cols", axis=1, tiled=True),
        lax.all_gather(norm2_gain, "cols", axis=0, tiled=True),
        lax.all_gather(w_router, "cols", axis=0, tiled=True),
        lax.all_gather(shared_gate, "cols", axis=0, tiled=True),
        lax.all_gather(shared_up, "cols", axis=0, tiled=True),
        lax.all_gather(shared_down, "cols", axis=1, tiled=True),
    )
    model_width = full_in.shape[2]
    token_input = full_in.reshape(tok_dev, model_width).astype(jnp.float32)
    first_inverse_deviation = lax.rsqrt(
        jnp.mean(token_input * token_input, -1, keepdims=True) + NORM_EPS
    )
    first_unit_rows = token_input * first_inverse_deviation
    first_gain_float = gain_one.astype(jnp.float32)
    first_normed = (first_unit_rows * first_gain_float).astype(jnp.bfloat16)
    q_pre = matmul(first_normed, wq_full)
    key_unrotated = matmul(first_normed, wk_full)
    value_projected = matmul(first_normed, wv_full).astype(jnp.bfloat16)
    q_heads = q_pre.shape[1] // HEAD_DIM
    positions = col_idx * len_dev + jnp.arange(len_dev, dtype=jnp.int32)
    cosine_table, sine_table = rope_tables(positions, HEAD_DIM)
    rotated_queries = apply_rotary(
        q_pre.reshape(sequence_count, len_dev, q_heads, HEAD_DIM), cosine_table, sine_table
    ).astype(jnp.bfloat16)
    rotated_keys = apply_rotary(
        key_unrotated.reshape(sequence_count, len_dev, 1, HEAD_DIM), cosine_table, sine_table
    ).astype(jnp.bfloat16)
    kv_local = jnp.concatenate(
        [
            rotated_keys.reshape(sequence_count, len_dev, HEAD_DIM),
            value_projected.reshape(sequence_count, len_dev, HEAD_DIM),
        ],
        -1,
    )
    kv_local = jnp.swapaxes(kv_local, 0, 1)
    query_t = jnp.transpose(rotated_queries, (0, 2, 1, 3))
    score_scale = 1.0 / math.sqrt(HEAD_DIM)
    q_last = col_idx * len_dev + len_dev - 1

    def online_update(carry_in, key_part, k_start):
        run_max, run_sum, run_acc = carry_in
        block_len = key_part.shape[0]
        scores = (
            jnp.einsum(
                "shqd,bsd->shqb",
                query_t,
                key_part[:, :, :HEAD_DIM],
                preferred_element_type=jnp.float32,
            )
            * score_scale
        )
        key_pos = k_start + jnp.arange(block_len, dtype=jnp.int32)
        causal = positions[:, None] >= key_pos[None, :]
        scores = jnp.where(causal, scores, NEG_LARGE)
        new_max = jnp.maximum(run_max, jnp.max(scores, -1))
        prob_vals = jnp.where(causal, jnp.exp(scores - new_max[..., None]), 0.0)
        rescale = jnp.exp(run_max - new_max)
        run_sum = run_sum * rescale + jnp.sum(prob_vals, -1)
        run_acc = run_acc * rescale[..., None] + jnp.einsum(
            "shqb,bsd->shqd",
            prob_vals.astype(jnp.bfloat16),
            key_part[:, :, HEAD_DIM:],
            preferred_element_type=jnp.float32,
        )
        return (new_max, run_sum, run_acc)

    fold_start = (
        jnp.full((sequence_count, q_heads, len_dev), NEG_LARGE, jnp.float32),
        jnp.zeros((sequence_count, q_heads, len_dev), jnp.float32),
        jnp.zeros((sequence_count, q_heads, len_dev, HEAD_DIM), jnp.float32),
    )
    carry_in = fold_start
    piece = lax.all_gather(kv_local, "cols", axis=0, tiled=True)
    start = jnp.int32(0)
    piece_len = piece.shape[0]
    step_len = min(512, piece_len)
    for offset in range(0, piece_len, step_len):
        key_part = piece[offset : offset + step_len]
        k_start = start + offset

        def updated(state_in, key_part=key_part, k_start=k_start):
            return online_update(state_in, key_part, k_start)

        carry_in = lax.cond(k_start <= q_last, updated, keep_same, carry_in)
    run_max, run_sum, run_acc = carry_in
    attn_f32 = run_acc / run_sum[..., None]
    log_total = run_max + jnp.log(run_sum)
    attn_bf = attn_f32.astype(jnp.bfloat16)
    attn_rows = jnp.transpose(attn_bf, (0, 2, 1, 3)).reshape(tok_dev, q_heads * HEAD_DIM)
    attn_proj = lax.psum(matmul(attn_rows, wo_full).astype(jnp.bfloat16), "rows").astype(
        jnp.float32
    )
    residual_stream = token_input + attn_proj
    second_inverse_deviation = lax.rsqrt(
        jnp.mean(residual_stream * residual_stream, -1, keepdims=True) + NORM_EPS
    )
    second_unit_rows = residual_stream * second_inverse_deviation
    second_gain_float = gain_two.astype(jnp.float32)
    second_normed = (second_unit_rows * second_gain_float).astype(jnp.bfloat16)
    gate_pre = matmul(second_normed, sg_full)
    up_pre = matmul(second_normed, su_full)
    silu_gate, silu_slope = silu_parts(gate_pre)
    shared_act = (silu_gate * up_pre).astype(jnp.bfloat16)
    ffn_part = matmul(shared_act, sd_full)
    my_rows = row_idx * rows_dev
    normed_mine = lax.dynamic_slice_in_dim(second_normed, my_rows, rows_dev, 0)
    route_mine = routes.reshape(rows_dev, top_k)
    logits = matmul(normed_mine, router_full)
    expert_ids = jnp.arange(experts, dtype=jnp.int32)
    chosen_hot = (route_mine[:, :, None] == expert_ids[None, None, :]).astype(jnp.float32)
    chosen = jnp.sum(chosen_hot * logits[:, None, :], -1)
    gate_probs = jax.nn.softmax(chosen, -1)
    assign_count = rows_dev * top_k
    flat_routes = route_mine.reshape(assign_count)
    assign_hot = (flat_routes[:, None] == expert_ids[None, :]).astype(jnp.int32)
    rank_in = jnp.sum((jnp.cumsum(assign_hot, 0) - assign_hot) * assign_hot, 1)
    slot_of = flat_routes * capacity + rank_in
    assign_of_slot = (
        jnp.zeros((experts * capacity,), jnp.int32)
        .at[slot_of]
        .set(jnp.arange(assign_count, dtype=jnp.int32))
    )
    slot_used = jnp.zeros((experts * capacity,), jnp.int32).at[slot_of].set(1)
    slot_row = assign_of_slot // top_k

    def send_rows(slot_vals):
        slot_vals = slot_vals.reshape(experts, capacity, model_width)
        outgoing = jnp.broadcast_to(
            slot_vals[:, None], (experts, 2, capacity, model_width)
        ).reshape(devices, capacity, model_width)
        received = lax.all_to_all(
            outgoing, ("rows", "cols"), split_axis=0, concat_axis=0, tiled=True
        )
        return received.reshape(devices * capacity, model_width)

    def return_rows(slot_vals):
        returned = lax.all_to_all(
            slot_vals.reshape(devices, capacity, model_width),
            ("rows", "cols"),
            split_axis=0,
            concat_axis=0,
            tiled=True,
        )
        returned = returned.reshape(experts, 2, capacity, model_width).astype(jnp.float32)
        summed = (returned[:, 0] + returned[:, 1]).astype(jnp.bfloat16)
        return summed.reshape(experts * capacity, model_width).astype(jnp.float32)

    slot_inputs = jnp.where(slot_used[:, None] > 0, normed_mine[slot_row], 0)
    expert_rows = send_rows(slot_inputs)
    eg_mat = expert_gate.reshape(model_width, -1)
    eu_mat = expert_up.reshape(model_width, -1)
    ed_mat = expert_down.reshape(-1, model_width)
    e_gate = matmul(expert_rows, eg_mat)
    e_up = matmul(expert_rows, eu_mat)
    e_silu, e_slope = silu_parts(e_gate)
    e_act = (e_silu * e_up).astype(jnp.bfloat16)
    e_out = matmul(e_act, ed_mat).astype(jnp.bfloat16)
    expert_sum = return_rows(e_out)
    picked = expert_sum[slot_of].reshape(rows_dev, top_k, model_width)
    routed = jnp.sum(gate_probs[:, :, None] * picked, 1)
    ffn_full = lax.dynamic_update_slice_in_dim(
        ffn_part, lax.dynamic_slice_in_dim(ffn_part, my_rows, rows_dev, 0) + routed, my_rows, 0
    )
    ffn_mine = lax.psum_scatter(
        ffn_full.reshape(sequence_count, len_dev, model_width).astype(jnp.bfloat16),
        "rows",
        scatter_dimension=2,
        tiled=True,
    ).astype(jnp.float32)
    resid_mine = lax.dynamic_slice_in_dim(
        residual_stream.reshape(sequence_count, len_dev, model_width),
        row_idx * row_width,
        row_width,
        2,
    )
    layer_out = (resid_mine + ffn_mine).astype(jnp.bfloat16)
    grad_full = lax.all_gather(cotangent, "rows", axis=2, tiled=True).reshape(tok_dev, model_width)
    d_shared_act = matmul_nt(grad_full, sd_full)
    grad_sd = matmul_tn(shared_act, grad_full)
    d_gate_pre = (d_shared_act * up_pre * silu_slope).astype(jnp.bfloat16)
    d_up_pre = (d_shared_act * silu_gate).astype(jnp.bfloat16)
    grad_sg = matmul_tn(second_normed, d_gate_pre)
    grad_su = matmul_tn(second_normed, d_up_pre)
    grad_second_normed = matmul_nt(d_gate_pre, sg_full) + matmul_nt(d_up_pre, su_full)
    grad_mine = lax.dynamic_slice_in_dim(grad_full, my_rows, rows_dev, 0).astype(jnp.float32)
    d_gates = jnp.sum(grad_mine[:, None, :] * picked, -1)
    to_experts = (
        (gate_probs[:, :, None] * grad_mine[:, None, :])
        .reshape(assign_count, model_width)
        .astype(jnp.bfloat16)
    )
    slot_grads = jnp.where(slot_used[:, None] > 0, to_experts[assign_of_slot], 0)
    d_expert_out = send_rows(slot_grads)
    grad_ed = matmul_tn(e_act, d_expert_out)
    d_e_act = matmul_nt(d_expert_out, ed_mat)
    d_e_gate = (d_e_act * e_up * e_slope).astype(jnp.bfloat16)
    d_e_up = (d_e_act * e_silu).astype(jnp.bfloat16)
    grad_eg = matmul_tn(expert_rows, d_e_gate)
    grad_eu = matmul_tn(expert_rows, d_e_up)
    d_rows = (matmul_nt(d_e_gate, eg_mat) + matmul_nt(d_e_up, eu_mat)).astype(jnp.bfloat16)
    d_assign = return_rows(d_rows)[slot_of].reshape(rows_dev, top_k, model_width)
    d_routed_in = jnp.sum(d_assign, 1)
    d_chosen = gate_probs * (d_gates - jnp.sum(gate_probs * d_gates, -1, keepdims=True))
    d_logits = jnp.sum(chosen_hot * d_chosen[:, :, None], 1)
    router_f = router_full.astype(jnp.float32)
    grad_router_part = jnp.dot(normed_mine.astype(jnp.float32).T, d_logits, precision=PRECISE)
    d_router_in = jnp.dot(d_logits, router_f.T, precision=PRECISE)
    d_mine = (
        lax.dynamic_slice_in_dim(grad_second_normed, my_rows, rows_dev, 0)
        + d_routed_in
        + d_router_in
    )
    grad_second_normed = lax.dynamic_update_slice_in_dim(grad_second_normed, d_mine, my_rows, 0)
    grad_second_normed, grad_router = (
        lax.psum(grad_second_normed.astype(jnp.bfloat16), "rows").astype(jnp.float32),
        lax.psum(grad_router_part.astype(jnp.bfloat16), "rows").astype(jnp.float32),
    )
    grad_second_unit = grad_second_normed * second_gain_float
    second_gain_gradient = jnp.sum(grad_second_normed * second_unit_rows, 0)
    d_resid = grad_full.astype(jnp.float32) + second_inverse_deviation * (
        grad_second_unit
        - second_unit_rows * jnp.mean(grad_second_unit * second_unit_rows, -1, keepdims=True)
    )
    d_attn = d_resid.astype(jnp.bfloat16)
    grad_wo = matmul_tn(attn_rows, d_attn)
    d_heads = matmul_nt(d_attn, wo_full).astype(jnp.bfloat16)
    d_heads_t = jnp.transpose(
        d_heads.reshape(sequence_count, len_dev, q_heads, HEAD_DIM), (0, 2, 1, 3)
    )
    delta_rows = jnp.sum(d_heads_t.astype(jnp.float32) * attn_f32, -1)
    kv_all = lax.all_gather(kv_local, "cols", axis=0, tiled=True)
    seq_len = kv_all.shape[0]
    key_block = min(512, seq_len)

    def key_step(block_no, carry_in):
        k_start = block_no * key_block
        key_part = lax.dynamic_slice_in_dim(kv_all, k_start, key_block, 0)

        def contribute(state_in):
            d_query_in, d_kv_in = state_in
            keys_bf = key_part[:, :, :HEAD_DIM]
            values_bf = key_part[:, :, HEAD_DIM:]
            scores = (
                jnp.einsum("shqd,bsd->shqb", query_t, keys_bf, preferred_element_type=jnp.float32)
                * score_scale
            )
            key_pos = k_start + jnp.arange(key_block, dtype=jnp.int32)
            causal = positions[:, None] >= key_pos[None, :]
            prob_vals = jnp.where(causal, jnp.exp(scores - log_total[..., None]), 0.0)
            d_prob = jnp.einsum(
                "shqd,bsd->shqb", d_heads_t, values_bf, preferred_element_type=jnp.float32
            )
            d_scores = (prob_vals * (d_prob - delta_rows[..., None])).astype(jnp.bfloat16)
            d_query_in = (
                d_query_in
                + jnp.einsum(
                    "shqb,bsd->shqd", d_scores, keys_bf, preferred_element_type=jnp.float32
                )
                * score_scale
            )
            d_key = (
                jnp.einsum("shqb,shqd->bsd", d_scores, query_t, preferred_element_type=jnp.float32)
                * score_scale
            )
            d_value = jnp.einsum(
                "shqb,shqd->bsd",
                prob_vals.astype(jnp.bfloat16),
                d_heads_t,
                preferred_element_type=jnp.float32,
            )
            d_kv_in = lax.dynamic_update_slice_in_dim(
                d_kv_in, jnp.concatenate([d_key, d_value], -1), k_start, 0
            )
            return (d_query_in, d_kv_in)

        return lax.cond(k_start <= q_last, contribute, keep_same, carry_in)

    grad_start = (
        jnp.zeros((sequence_count, q_heads, len_dev, HEAD_DIM), jnp.float32),
        jnp.zeros((seq_len, sequence_count, 2 * HEAD_DIM), jnp.float32),
    )
    d_query, d_kv_all = lax.fori_loop(0, seq_len // key_block, key_step, grad_start)
    d_kv = lax.psum_scatter(
        d_kv_all.astype(jnp.bfloat16), "cols", scatter_dimension=0, tiled=True
    ).astype(jnp.float32)
    d_query_rows = (
        apply_rotary(jnp.transpose(d_query, (0, 2, 1, 3)), cosine_table, -sine_table)
        .reshape(tok_dev, q_heads * HEAD_DIM)
        .astype(jnp.bfloat16)
    )
    d_kv_t = jnp.swapaxes(d_kv, 0, 1)
    d_key_rows = (
        apply_rotary(
            d_kv_t[:, :, :HEAD_DIM].reshape(sequence_count, len_dev, 1, HEAD_DIM),
            cosine_table,
            -sine_table,
        )
        .reshape(tok_dev, HEAD_DIM)
        .astype(jnp.bfloat16)
    )
    d_value_rows = d_kv_t[:, :, HEAD_DIM:].reshape(tok_dev, HEAD_DIM).astype(jnp.bfloat16)
    grad_wq = matmul_tn(first_normed, d_query_rows)
    grad_wk = matmul_tn(first_normed, d_key_rows)
    grad_wv = matmul_tn(first_normed, d_value_rows)
    grad_first_normed = (
        matmul_nt(d_query_rows, wq_full)
        + matmul_nt(d_key_rows, wk_full)
        + matmul_nt(d_value_rows, wv_full)
    )
    grad_first_normed = lax.psum(grad_first_normed.astype(jnp.bfloat16), "rows").astype(jnp.float32)
    grad_first_unit = grad_first_normed * first_gain_float
    first_gain_gradient = jnp.sum(grad_first_normed * first_unit_rows, 0)
    d_input = d_resid + first_inverse_deviation * (
        grad_first_unit
        - first_unit_rows * jnp.mean(grad_first_unit * first_unit_rows, -1, keepdims=True)
    )
    grad_in = lax.dynamic_slice_in_dim(
        d_input.reshape(sequence_count, len_dev, model_width), row_idx * row_width, row_width, 2
    )
    g_gain_one, g_wq, g_wk, g_wv, g_wo, g_gain_two, g_router, g_sg, g_su, g_sd = (
        lax.psum_scatter(
            first_gain_gradient.astype(jnp.bfloat16), "cols", scatter_dimension=0, tiled=True
        ).astype(jnp.float32),
        lax.psum_scatter(
            grad_wq.astype(jnp.bfloat16), "cols", scatter_dimension=0, tiled=True
        ).astype(jnp.float32),
        lax.psum_scatter(
            grad_wk.astype(jnp.bfloat16), "cols", scatter_dimension=0, tiled=True
        ).astype(jnp.float32),
        lax.psum_scatter(
            grad_wv.astype(jnp.bfloat16), "cols", scatter_dimension=0, tiled=True
        ).astype(jnp.float32),
        lax.psum_scatter(
            grad_wo.astype(jnp.bfloat16), "cols", scatter_dimension=1, tiled=True
        ).astype(jnp.float32),
        lax.psum_scatter(
            second_gain_gradient.astype(jnp.bfloat16), "cols", scatter_dimension=0, tiled=True
        ).astype(jnp.float32),
        lax.psum_scatter(
            grad_router.astype(jnp.bfloat16), "cols", scatter_dimension=0, tiled=True
        ).astype(jnp.float32),
        lax.psum_scatter(
            grad_sg.astype(jnp.bfloat16), "cols", scatter_dimension=0, tiled=True
        ).astype(jnp.float32),
        lax.psum_scatter(
            grad_su.astype(jnp.bfloat16), "cols", scatter_dimension=0, tiled=True
        ).astype(jnp.float32),
        lax.psum_scatter(
            grad_sd.astype(jnp.bfloat16), "cols", scatter_dimension=1, tiled=True
        ).astype(jnp.float32),
    )
    return (
        layer_out,
        grad_in,
        g_gain_one,
        g_wq,
        g_wk,
        g_wv,
        g_wo,
        g_gain_two,
        g_router,
        g_sg,
        g_su,
        g_sd,
        grad_eg.reshape(expert_gate.shape),
        grad_eu.reshape(expert_up.shape),
        grad_ed.reshape(expert_down.shape),
    )


def scores_of(keys, queries, scale):
    return matmul_nt(keys, queries) * scale


def causal_mask(scores):
    key_pos = lax.broadcasted_iota(jnp.int32, scores.shape, 0)
    query_pos = lax.broadcasted_iota(jnp.int32, scores.shape, 1)
    return query_pos >= key_pos


MESH_ID = pl.DeviceIdType.MESH
MIB = 1024 * 1024


class Links:
    def __init__(self, n_rows, n_cols):
        self.n_rows, self.n_cols, self.ring = n_rows, n_cols, n_cols // 2
        self.r = lax.axis_index("rows")
        self.c = lax.axis_index("cols")
        self.z = lax.div(self.c, 2)
        self.k = lax.rem(self.c, 2)
        self.x = (self.flip(1), self.c)
        self.y = (self.flip(2), self.c)
        self.up = (self.r, lax.rem(self.c + 2, n_cols))
        self.down = (self.r, lax.rem(self.c + n_cols - 2, n_cols))
        self.twin = (self.r, self.c + 1 - 2 * self.k)
        self.started = []

    def flip(self, bits):
        low, high = lax.rem(self.r, 2), lax.div(self.r, 2)
        low = 1 - low if bits & 1 else low
        high = 1 - high if bits & 2 else high
        return low + 2 * high

    def chip(self, hops):
        return lax.rem(self.z + (2 * self.ring - hops), self.ring)

    def place(self, hops):
        other = self.chip(hops)
        low = lax.rem(lax.rem(self.r, 2) + lax.rem(other, 2), 2)
        high = lax.rem(lax.div(self.r, 2) + lax.div(other, 2), 2)
        return low + 2 * high

    def spread_partners(self):
        return [
            (hops, bits, (self.flip(bits), lax.rem(self.c + 2 * hops, self.n_cols)))
            for hops in range(self.ring)
            for bits in range(self.n_rows)
            if hops or bits
        ]

    def greet(self, partners):
        barrier = pltpu.get_barrier_semaphore()
        for partner in partners:
            pl.semaphore_signal(barrier, inc=1, device_id=partner, device_id_type=MESH_ID)
        pl.semaphore_wait(barrier, len(partners))

    def send(self, src, dst, sems, number, partner):
        copy = pltpu.make_async_remote_copy(
            src_ref=src,
            dst_ref=dst,
            send_sem=sems[0].at[number],
            recv_sem=sems[1].at[number],
            device_id=partner,
            device_id_type=MESH_ID,
        )
        copy.start()
        self.started.append(copy)
        return copy

    def finish(self):
        for copy in self.started:
            copy.wait_send()


def run_together(*steps):
    live = list(steps)
    while live:
        live = [step for step in live if next(step, True) is None]


def pair_sems(count):
    return [pltpu.SemaphoreType.DMA((count,)), pltpu.SemaphoreType.DMA((count,))]


def gather_square(net, src, out, sems, local_sem, chunks, known=None):
    rows, width = src.shape
    half = rows // 2

    def block(s, j, part=None):
        columns = pl.ds(j * width, width)
        if part is None:
            return out.at[s, :, columns]
        return out.at[s, pl.ds(part * half, half), columns]

    def part_of(s, part):
        return src.at[pl.ds(part * half, half), :] if s == 0 else block(s, 0, part)

    if known is None:
        own = pltpu.make_async_copy(src, block(0, 0), local_sem)
    else:
        own = pltpu.make_async_copy(known, out.at[0], local_sem)
    own.start()
    ups, xs, ys, lasts = {}, {}, {}, {}
    first = 0 if known is None else 1

    def send_up(s):
        if s < chunks - 1:
            whole = src if s == 0 else block(s, 0)
            ups[s + 1] = net.send(whole, block(s + 1, 0), sems, 7 * s, net.up)

    def send_chunk(s):
        xs[s] = {p: net.send(part_of(s, p), block(s, 1, p), sems, 7 * s + 1 + p, net.x) for p in (0, 1)}
        ys[s] = {p: net.send(part_of(s, p), block(s, 2, p), sems, 7 * s + 3 + p, net.y) for p in (1, 0)}

    def forward(s):
        xs[s][0].wait_recv()
        one = net.send(block(s, 1, 0), block(s, 3, 0), sems, 7 * s + 5, net.y)
        ys[s][1].wait_recv()
        two = net.send(block(s, 2, 1), block(s, 3, 1), sems, 7 * s + 6, net.x)
        lasts[s] = [one, two]

    if known is None:
        send_chunk(0)
        yield
    if chunks > 1:
        send_up(0)
        yield
    if known is None:
        forward(0)
        yield
    for s in range(1, chunks):
        ups[s].wait_recv()
        send_up(s)
        send_chunk(s)
        yield
        forward(s)
        yield
    own.wait()
    for s in range(first, chunks):
        xs[s][1].wait_recv()
        ys[s][0].wait_recv()
        lasts[s][0].wait_recv()
        lasts[s][1].wait_recv()


def gather_columns(net, src, spot, sems, local_sem=None):
    if local_sem is not None:
        own = pltpu.make_async_copy(src, spot(0, net.k), local_sem)
        own.start()
    twins = []
    for hops in range(net.ring):
        if hops:
            up.wait_recv()
        here = src if hops == 0 else spot(hops, net.k)
        if hops < net.ring - 1:
            up = net.send(here, spot(hops, net.k), sems, hops, net.up)
        twins.append(net.send(here, spot(hops, net.k), sems, net.ring + hops, net.twin))
        yield
    if local_sem is not None:
        own.wait()
    for copy in twins:
        copy.wait_recv()


def add_slabs(target, terms, slab=64):
    rows = target.shape[0]

    @pl.loop(0, rows // slab)
    def _(i):
        at = pl.ds(pl.multiple_of(i * slab, slab), slab)
        total = terms[0](at)
        for term in terms[1:]:
            total = total + term(at)
        target[at, :] = total.astype(target.dtype)


def part_reader(ref, *lead, columns=None):
    def read(at):
        values = ref[(*lead, at, slice(None) if columns is None else columns)]
        return values.astype(jnp.float32)

    return read


def scatter_scratch(chunks, rows, width, resident=False):
    half = rows // 2
    kept = (1, 2, 16, 128) if resident else (chunks, 2, half, width)
    return [
        pltpu.VMEM(kept, jnp.bfloat16),
        pltpu.VMEM(kept[:1] + kept[2:] if resident else (chunks, half, 2 * width), jnp.bfloat16),
        pltpu.VMEM((chunks, 2, half, width), jnp.bfloat16),
        pltpu.VMEM((chunks, half, 2 * width), jnp.bfloat16),
        pltpu.VMEM((chunks, 2, half, width), jnp.bfloat16),
        pltpu.VMEM((chunks, 2, half, width), jnp.bfloat16),
        pltpu.SemaphoreType.DMA((chunks, 3)),
    ] + pair_sems(5 * chunks)


def scatter_square(net, src, scratch, order, finish, resident=False):
    my_up, my_low, got_x, got_y, got_last, stage, load_sems, *sems = scratch
    half, width = got_x.shape[2:]
    upper, lower = pl.ds(0, half), pl.ds(half, half)
    column = lambda j, count=1: pl.ds(j * width, count * width)
    left, right = pl.ds(0, width), pl.ds(width, width)
    loads, sent = {}, {}

    def mine(i, part, j):
        if resident:
            return part_reader(src.at[order[i], upper if part == 0 else lower, column(j)])
        if part == 0:
            return part_reader(my_up, i, j // 2)
        return part_reader(my_low, i, columns=(left, right)[j])

    def first(i):
        s = order[i]
        loads[i] = [] if resident else [
            pltpu.make_async_copy(src.at[s, upper, column(0)], my_up.at[i, 0], load_sems.at[i, 0]),
            pltpu.make_async_copy(src.at[s, upper, column(2)], my_up.at[i, 1], load_sems.at[i, 1]),
            pltpu.make_async_copy(src.at[s, lower, column(0, 2)], my_low.at[i], load_sems.at[i, 2]),
        ]
        sent[i] = [
            net.send(src.at[s, upper, column(3)], got_x.at[i, 1], sems, 5 * i, net.x),
            net.send(src.at[s, lower, column(2, 2)], got_y.at[i], sems, 5 * i + 1, net.y),
            net.send(src.at[s, upper, column(1)], got_x.at[i, 0], sems, 5 * i + 2, net.x),
        ]
        for load in loads[i]:
            load.start()

    def second(i):
        for load in loads[i]:
            load.wait()
        sent[i][0].wait_recv()
        add_slabs(stage.at[i, 0], [mine(i, 0, 2), part_reader(got_x, i, 1)])
        sent[i].append(net.send(stage.at[i, 0], got_last.at[i, 0], sems, 5 * i + 3, net.y))
        sent[i][1].wait_recv()
        add_slabs(stage.at[i, 1], [mine(i, 1, 1), part_reader(got_y, i, columns=right)])
        sent[i].append(net.send(stage.at[i, 1], got_last.at[i, 1], sems, 5 * i + 4, net.x))

    def third(i):
        for copy in sent[i][2:]:
            copy.wait_recv()
        finish(
            order[i],
            [mine(i, 0, 0), part_reader(got_x, i, 0), part_reader(got_last, i, 0)],
            [
                mine(i, 1, 0),
                part_reader(got_y, i, columns=left),
                part_reader(got_last, i, 1),
            ],
        )

    for i in range(len(order) + 2):
        if i < len(order):
            first(i)
            yield
        if 0 <= i - 1 < len(order):
            second(i - 1)
            yield
        if 0 <= i - 2:
            third(i - 2)
            yield


def ring_scratch(ring, rows, width):
    return [
        pltpu.VMEM((ring - 1, rows, width), jnp.bfloat16),
        pltpu.VMEM((ring - 1, rows, width), jnp.bfloat16),
    ] + pair_sems(ring - 1)


def ring_finish(net, scratch, target, copies):
    landed, leaving, *sems = scratch
    rows = landed.shape[1]

    def finish(s, upper, lower):
        turn = (s - 1) % net.ring
        for part, terms in ((0, upper), (1, lower)):
            at = pl.ds(part * (rows // 2), rows // 2)
            if turn and not part:
                copies[turn - 1].wait_recv()
            if turn:
                terms = terms + [part_reader(landed.at[turn - 1, at, :])]
            goal = target.at[at, :] if s == 0 else leaving.at[turn, at, :]
            add_slabs(goal, terms)
        if s:
            copies.append(net.send(leaving.at[turn], landed.at[turn], sems, turn, net.up))

    return finish


def scatter_columns(net, part, out, scratch):
    got_twin, landed, leaving, twin_send, twin_recv, *sems = scratch
    twins, copies = {}, []
    order = list(range(1, net.ring)) + [0]
    for hops in order:
        twins[hops] = net.send(
            part(hops, 1 - net.k), got_twin.at[hops], (twin_send, twin_recv), hops, net.twin
        )
    yield
    for turn, hops in enumerate(order):
        twins[hops].wait_recv()
        terms = [part_reader(part(hops, net.k)), part_reader(got_twin, hops)]
        if turn:
            copies[turn - 1].wait_recv()
            terms.append(part_reader(landed, turn - 1))
        add_slabs(leaving.at[turn] if hops else out, terms, 32)
        if hops:
            copies.append(net.send(leaving.at[turn], landed.at[turn], sems, turn, net.up))
        yield


def scatter_columns_scratch(ring, rows, width):
    return [
        pltpu.VMEM((ring, rows, width), jnp.bfloat16),
        pltpu.VMEM((ring - 1, rows, width), jnp.bfloat16),
        pltpu.VMEM((ring - 1, rows, width), jnp.bfloat16),
    ] + pair_sems(ring) + pair_sems(ring - 1)


def remote_call(kernel, name, collective_id, out_shape, scratch, operands, in_vmem=(), out_vmem=(), cost=None):
    anywhere = pl.BlockSpec(memory_space=pl.ANY)
    vmem = pl.BlockSpec(memory_space=pltpu.VMEM)
    return pl.pallas_call(
        kernel,
        out_shape=out_shape,
        in_specs=[vmem if i in in_vmem else anywhere for i in range(len(operands))],
        out_specs=[vmem if i in out_vmem else anywhere for i in range(len(out_shape))],
        scratch_shapes=scratch,
        compiler_params=pltpu.CompilerParams(
            collective_id=collective_id, has_side_effects=True, vmem_limit_bytes=63 * MIB
        ),
        cost_estimate=cost,
        name=name,
    )(*operands)


def spread_columns(net, packed, spot, sems, local_sem):
    own = pltpu.make_async_copy(packed.at[net.chip(0)], spot(0, net.k), local_sem)
    own.start()
    pieces = []
    for hops in range(1, net.ring):
        target = (net.r, lax.rem(net.c + 2 * hops, net.n_cols))
        pieces.append(
            net.send(packed.at[net.chip(-hops)], spot_at(spot, net, hops), sems, hops, target)
        )
    yield
    own.wait()
    twins = [net.send(spot(0, net.k), spot(0, net.k), sems, net.ring, net.twin)]
    yield
    for hops in range(1, net.ring):
        pieces[hops - 1].wait_recv()
        here = spot(hops, net.k)
        twins.append(net.send(here, here, sems, net.ring + hops, net.twin))
        yield
    for copy in twins:
        copy.wait_recv()


def spot_at(spot, net, hops):
    return spot(0, net.k)


def first_phase(n_rows, n_cols, block, grads, weights, small, weights_out, packed, slot_map, tables):
    ring = n_cols // 2
    length, row_width = block.shape
    model = n_rows * row_width
    col_width, in_width = weights.shape
    q_width = weights_out.shape[1]
    heads = q_width // HEAD_DIM
    small_width = small.shape[1]
    experts = slot_map.shape[0]
    scale = 1.0 / math.sqrt(HEAD_DIM)
    pieces = 2
    piece = length // pieces
    bf16, f32 = jnp.bfloat16, jnp.float32
    shape = jax.ShapeDtypeStruct

    def kernel(
        x_in, g_in, w_in, small_in, wo_in, packed_in, map_in, cosine, sine,
        x_out, normed_out, w_out, small_out, q, kv_out, out, lse, wo_out, g_out, rows_out, map_out,
        shared_out, sum_out, gains_out,
        x, normed, w, small_all, kv, wo, proj, proj_sum, second, result, projected, top, total, acc,
        *sems,
    ):
        scratch, sems = list(sems[:9]), list(sems[9:])
        pairs = lambda: (sems.pop(0), sems.pop(0))
        x_sems, g_sems, w_sems, small_sems, wo_sems, kv_sems = [pairs() for _ in range(6)]
        map_sems, rows_sems, shared_sems, sum_sems, sum_sems_two = [pairs() for _ in range(5)]
        local = sems.pop(0)
        net = Links(n_rows, n_cols)
        others = net.spread_partners()
        net.greet([device for _, _, device in others] + [net.twin])
        by_place = lambda ref: lambda hops, core: ref.at[
            pl.ds((net.place(hops) * 2 + core) * col_width, col_width), :
        ]

        x_steps = gather_square(net, x_in, x, x_sems, local.at[0], 1)
        small_steps = gather_columns(net, small_in, by_place(small_all), small_sems, local.at[1])
        w_steps = gather_columns(net, w_in, by_place(w), w_sems, local.at[2])
        wo_steps = gather_columns(net, wo_in, by_place(wo), wo_sems, local.at[3])
        g_steps = gather_square(net, g_in, g_out, g_sems, local.at[4], ring)
        saves = []

        def save(src, dst):
            copy = pltpu.make_async_copy(src, dst, local.at[8 + len(saves)])
            copy.start()
            saves.append(copy)

        next(small_steps)
        next(x_steps)
        next(w_steps)
        maps = []
        for number, (hops, bits, device) in enumerate(others):
            maps.append(net.send(map_in, map_out.at[hops, net.r], map_sems, number, device))
        own_map = pltpu.make_async_copy(map_in, map_out.at[0, net.r], local.at[5])
        own_map.start()
        next(small_steps)
        next(w_steps)
        next(x_steps)
        next(g_steps)
        next(small_steps)
        next(small_steps)
        next(w_steps)
        run_together(x_steps, small_steps)
        save(x.at[0], x_out)
        save(small_all, small_out)
        gains = small_all[...].astype(f32).T
        gains_out[...] = gains[experts : experts + 8]
        first_gain = gains[experts : experts + 1]
        second_gain = gains[experts + 1 : experts + 2]

        @pl.loop(0, length // 64)
        def _(i):
            at = pl.ds(pl.multiple_of(i * 64, 64), 64)
            values = x[0, at, :].astype(f32)
            inverse = lax.rsqrt(jnp.mean(values * values, -1, keepdims=True) + NORM_EPS)
            normed[at, :] = (values * inverse * first_gain).astype(bf16)

        save(normed, normed_out)
        next(wo_steps)
        next(w_steps)
        run_together(w_steps)
        save(w, w_out)
        next(g_steps)

        projected[...] = matmul(normed[...], w[...])
        next(wo_steps)

        def rotate(columns):
            values = projected[:, columns]
            turned = pltpu.roll(values, HEAD_DIM // 2, 1)
            return (values * cosine[...] + turned * sine[...]).astype(bf16)

        for head in range(heads + 1):
            columns = slice(head * HEAD_DIM, (head + 1) * HEAD_DIM)
            if head < heads:
                q[:, columns] = rotate(columns)
            else:
                kv[net.c, :, :HEAD_DIM] = rotate(columns)
        kv[net.c, :, HEAD_DIM:] = projected[:, q_width + HEAD_DIM :].astype(bf16)
        kv_steps = gather_columns(
            net, kv.at[net.c], lambda hops, core: kv.at[2 * net.chip(hops) + core], kv_sems
        )
        next(kv_steps)
        next(g_steps)
        next(kv_steps)
        next(wo_steps)
        next(kv_steps)
        next(g_steps)
        next(kv_steps)
        next(wo_steps)
        run_together(kv_steps)
        save(kv, kv_out)

        for head in range(heads):
            columns = slice(head * HEAD_DIM, (head + 1) * HEAD_DIM)
            queries = q[:, columns]

            def part(number):
                return scores_of(kv[number, :, :HEAD_DIM], queries, scale), kv[number, :, HEAD_DIM:]

            scores, values = part(net.c)
            scores = jnp.where(causal_mask(scores), scores, NEG_LARGE)
            high = jnp.max(scores, 0, keepdims=True)
            probs = jnp.exp(scores - high)
            top[...] = high
            total[...] = jnp.sum(probs, 0, keepdims=True)
            acc[...] = matmul_tn(values, probs.astype(bf16))

            @pl.loop(0, net.c)
            def _(number):
                scores, values = part(number)
                high = jnp.maximum(top[...], jnp.max(scores, 0, keepdims=True))
                probs = jnp.exp(scores - high)
                shrink = jnp.exp(top[...] - high)
                top[...] = high
                total[...] = total[...] * shrink + jnp.sum(probs, 0, keepdims=True)
                acc[...] = acc[...] * shrink + matmul_tn(values, probs.astype(bf16))

            out[:, columns] = (acc[...] / total[...]).T
            lse[head] = top[...] + jnp.log(total[...])
            if head in (0, 3):
                next(g_steps)

        run_together(wo_steps)
        save(wo, wo_out)
        heads_out = out[...].astype(bf16)
        for s in range(pieces):
            for j in range(n_rows):
                at = slice(j * row_width, (j + 1) * row_width)
                proj[s, :, at] = matmul_nt(
                    heads_out[s * piece : (s + 1) * piece], wo[at, :]
                ).astype(bf16)
        gathers = []

        def finish(s, upper, lower):
            add_slabs(result.at[s, pl.ds(0, piece // 2), :], upper)
            add_slabs(result.at[s, pl.ds(piece // 2, piece // 2), :], lower)
            steps = gather_square(
                net, result.at[s], proj_sum.at[pl.ds(s, 1)], (sum_sems, sum_sems_two)[s],
                local.at[6 + s], 1,
            )
            next(steps)
            gathers.append(steps)

        shared_steps = spread_columns(
            net, packed_in, by_place(shared_out), shared_sems, local.at[8 + 8]
        )
        sum_steps = scatter_square(net, proj, scratch, list(range(pieces)), finish, resident=True)
        next(sum_steps)
        next(shared_steps)
        next(sum_steps)
        run_together(sum_steps)
        next(shared_steps)

        def second_norm(s):
            @pl.loop(0, piece // 64)
            def _(i):
                at = pl.ds(pl.multiple_of(i * 64, 64), 64)
                there = pl.ds(pl.multiple_of(s * piece + i * 64, 64), 64)
                values = x[0, there, :].astype(f32) + proj_sum[s, at, :].astype(f32)
                inverse = lax.rsqrt(jnp.mean(values * values, -1, keepdims=True) + NORM_EPS)
                second[there, :] = (values * inverse * second_gain).astype(bf16)

        for s in range(pieces):
            run_together(gathers[s])
            second_norm(s)
        save(proj_sum, sum_out)
        rows_steps = gather_square(
            net, second.at[:, pl.ds(0, row_width)], rows_out, rows_sems, local.at[8 + 9], ring,
            known=second,
        )
        next(rows_steps)
        next(g_steps, None)
        next(rows_steps)
        next(shared_steps)
        next(g_steps, None)
        run_together(rows_steps, g_steps, shared_steps)
        own_map.wait()
        for copy in maps:
            copy.wait_recv()
        for copy in saves:
            copy.wait()
        net.finish()

    partners = n_rows * ring - 1
    vmem = pltpu.VMEM
    return remote_call(
        kernel,
        "first_phase",
        1,
        [
            shape((length, model), bf16),
            shape((length, model), bf16),
            shape((model, in_width), bf16),
            shape((model, small_width), bf16),
            shape((length, q_width), bf16),
            shape((n_cols, length, 2 * HEAD_DIM), bf16),
            shape((length, q_width), f32),
            shape((heads, 1, length), f32),
            shape((model, q_width), bf16),
            shape((ring, length, model), bf16),
            shape((ring, length, model), bf16),
            shape((ring, n_rows, *slot_map.shape), f32),
            shape((model, packed.shape[2]), bf16),
            shape((pieces, piece, model), bf16),
            shape((8, model), f32),
        ],
        [
            vmem((1, length, model), bf16),
            vmem((length, model), bf16),
            vmem((model, in_width), bf16),
            vmem((model, small_width), bf16),
            vmem((n_cols, length, 2 * HEAD_DIM), bf16),
            vmem((model, q_width), bf16),
            vmem((pieces, piece, model), bf16),
            vmem((pieces, piece, model), bf16),
            vmem((length, model), bf16),
            vmem((pieces, piece, row_width), bf16),
            vmem((length, in_width), f32),
            vmem((1, length), f32),
            vmem((1, length), f32),
            vmem((HEAD_DIM, length), f32),
        ]
        + scatter_scratch(pieces, piece, row_width, resident=True)
        + pair_sems(7)
        + pair_sems(7 * ring)
        + pair_sems(2 * ring)
        + pair_sems(2 * ring)
        + pair_sems(2 * ring)
        + pair_sems(2 * ring)
        + pair_sems(partners)
        + pair_sems(7 * ring)
        + pair_sems(2 * ring)
        + pair_sems(7)
        + pair_sems(7)
        + [pltpu.SemaphoreType.DMA((18,))],
        (block, grads, weights, small, weights_out, packed, slot_map, *tables),
        in_vmem=(7, 8),
        out_vmem=(4, 6, 7, 14),
    )


def token_sum(n_rows, n_cols, parts, gates, expert_rows, probs, router, token_rows, gains):
    ring = n_cols // 2
    rows, model = parts.shape[1:]
    width = model // n_rows
    experts = n_rows * ring
    slot_rows, d_part, e_act, d_gate, d_up = expert_rows
    n_slots, hidden = e_act.shape
    half = hidden // 2
    bf16, f32 = jnp.bfloat16, jnp.float32
    shape = jax.ShapeDtypeStruct

    def kernel(
        src, gate, xr_in, dp_in, act_in, dg_in, du_in, probs, router, x_in, proj_in, g_in, gains,
        d_attn, d_resid, gain_out, gate_out, out_g, out_u, out_d, land_g, land_u, land_d,
        result, second, xr, dp, act, dg, du, leave_a, leave_b, landed_a, landed_b, full_a, full_b,
        gate_own, high_ref, low_ref, *rest,
    ):
        scratch, ring_parts = rest[:9], rest[9:13]
        gs, gr, ms, mr, es, er, local, sem = rest[13:]
        leaving, landed, full = (leave_a, leave_b), (landed_a, landed_b), (full_a, full_b)
        net = Links(n_rows, n_cols)
        others = net.spread_partners()
        net.greet([device for _, _, device in others] + [net.twin])
        mine = net.r * ring + net.z
        order = list(range(1, ring)) + [0]
        steps = scatter_square(net, src, scratch, order, ring_finish(net, ring_parts, result, []))
        next(steps)
        copies = []
        own = pltpu.make_async_copy(gate, gate_out.at[mine], local.at[1])
        own.start()
        for number, (hops, bits, device) in enumerate(others):
            copies.append(net.send(gate, gate_out.at[mine], (ms, mr), number, device))
        next(steps)

        loads = [
            pltpu.make_async_copy(a, b, sem.at[i])
            for i, (a, b) in enumerate(
                ((xr_in, xr), (dg_in, dg), (du_in, du), (act_in, act), (dp_in, dp))
            )
        ]
        for load in loads:
            load.start()
        ours, theirs = slice(0, half), slice(half, hidden)
        sends, leaves, stores = [], {}, {}

        def slot_of(kind, j):
            return kind // 2, j % 2 if kind < 2 else 0

        def tile(kind, j, part):
            columns = slice(j * width, (j + 1) * width)
            if kind < 2:
                return matmul_tn(xr[:, columns], (dg, du)[kind][:, part])
            return matmul_tn(act[:, part], dp[:, columns])

        def land(kind, j, order=False):
            place = net.flip(j) if order else j
            at = pl.ds(pl.multiple_of(place * width, width), width)
            if kind < 2:
                ref = ((land_g, land_u), (out_g, out_u))[order][kind]
                return ref.at[at, :]
            return (land_d, out_d)[order].at[:, at]

        def give(kind, j):
            group, slot = slot_of(kind, j)
            if (group, slot) in leaves:
                leaves[group, slot].wait_send()
            buffer = leaving[group]
            buffer[slot] = tile(kind, j, theirs).astype(bf16)
            copy = net.send(buffer.at[slot], land(kind, j), (es, er), 4 * kind + j, net.twin)
            net.started.pop()
            leaves[group, slot] = copy
            sends.append(copy)

        def keep(kind, j):
            group, slot = slot_of(kind, j)
            buffer, got = full[group], landed[group]
            sends[4 * kind + j].wait_recv()
            load = pltpu.make_async_copy(land(kind, j), got.at[slot], sem.at[5 + slot])
            load.start()
            if (group, slot) in stores:
                stores[group, slot].wait()
            product = tile(kind, j, ours)
            load.wait()
            buffer[slot] = product + got[slot].astype(f32)
            store = pltpu.make_async_copy(
                buffer.at[slot], land(kind, j, True), sem.at[7 + 2 * group + slot]
            )
            store.start()
            stores[group, slot] = store

        for load in loads[:3]:
            load.wait()
        for kind in (0, 1):
            for j in range(n_rows):
                give(kind, j)
            next(steps)
        for load in loads[3:]:
            load.wait()
        for j in range(n_rows):
            give(2, j)
        next(steps)
        next(steps)
        for kind in (0, 1, 2):
            next(steps)
            for j in range(n_rows):
                keep(kind, j)
            next(steps)
        for copy in leaves.values():
            copy.wait_send()
        for store in stores.values():
            store.wait()

        run_together(steps)

        x, proj, g = xr.at[pl.ds(0, rows)], xr.at[pl.ds(rows, rows)], dp.at[pl.ds(0, rows)]
        loads = [
            pltpu.make_async_copy(a, b, sem.at[i])
            for i, (a, b) in enumerate(((x_in, x), (proj_in, proj), (g_in, g)))
        ]
        for load in loads:
            load.start()
        gather = gather_square(net, result, second, (gs, gr), local.at[0], 1)
        next(gather)
        own.wait()
        for copy in copies:
            copy.wait_recv()
        gate_load = pltpu.make_async_copy(gate_out.at[:, net.z], gate_own, sem.at[3])
        gate_load.start()
        gate_load.wait()
        d_gates = jnp.concatenate([gate_own[...], jnp.zeros((128 - experts, rows), f32)], 0).T
        d_logits = probs[...] * (d_gates - jnp.sum(probs[...] * d_gates, -1, keepdims=True))
        high = d_logits.astype(bf16)
        high_ref[...] = high
        low_ref[...] = (d_logits - high.astype(f32)).astype(bf16)
        for load in loads:
            load.wait()
        run_together(gather)
        gain = gains[1:2]
        gain_out[...] = jnp.zeros_like(gain_out)

        @pl.loop(0, rows // 128)
        def _(i):
            at = pl.ds(pl.multiple_of(i * 128, 128), 128)
            values = x[at, :].astype(f32) + proj[at, :].astype(f32)
            inverse = lax.rsqrt(jnp.mean(values * values, -1, keepdims=True) + NORM_EPS)
            unit = values * inverse
            d_second = second[0, at, :].astype(f32)
            d_second = d_second + matmul_nt(high_ref[at, :], router[...])
            d_second = d_second + matmul_nt(low_ref[at, :], router[...])
            d_unit = d_second * gain
            moment = jnp.mean(d_unit * unit, -1, keepdims=True)
            resid = g[at, :].astype(f32) + inverse * (d_unit - unit * moment)
            d_attn[at, :] = resid.astype(bf16)
            d_resid[at, :] = resid[:, :width]
            along = (d_second[:, :width] * unit[:, :width]).reshape(16, 8, width)
            gain_out[...] += jnp.sum(along, 0)

        net.finish()

    x, proj, g = token_rows
    return remote_call(
        kernel,
        "token_sum",
        5,
        [
            shape((rows, model), bf16),
            shape((rows, width), f32),
            shape((8, width), f32),
            shape((experts, *gates.shape), f32),
            shape((model, half), f32),
            shape((model, half), f32),
            shape((half, model), f32),
            shape((model, half), bf16),
            shape((model, half), bf16),
            shape((half, model), bf16),
        ],
        [
            pltpu.VMEM((rows, width), bf16),
            pltpu.VMEM((1, rows, model), bf16),
            pltpu.VMEM((n_slots, model), bf16),
            pltpu.VMEM((n_slots, model), bf16),
            pltpu.VMEM((n_slots, hidden), bf16),
            pltpu.VMEM((n_slots, hidden), bf16),
            pltpu.VMEM((n_slots, hidden), bf16),
            pltpu.VMEM((2, width, half), bf16),
            pltpu.VMEM((1, half, width), bf16),
            pltpu.VMEM((2, width, half), bf16),
            pltpu.VMEM((1, half, width), bf16),
            pltpu.VMEM((2, width, half), f32),
            pltpu.VMEM((1, half, width), f32),
            pltpu.VMEM((experts, rows), f32),
            pltpu.VMEM((rows, 128), bf16),
            pltpu.VMEM((rows, 128), bf16),
        ]
        + scatter_scratch(ring, rows, width)
        + ring_scratch(ring, rows, width)
        + pair_sems(7)
        + pair_sems(experts - 1)
        + pair_sems(3 * n_rows)
        + [pltpu.SemaphoreType.DMA((2,)), pltpu.SemaphoreType.DMA((10,))],
        (parts, gates, *expert_rows, probs, router, x, proj, g, gains),
        in_vmem=(7, 8, 12),
        out_vmem=(0, 1, 2),
    )


def attention_back(
    n_rows, n_cols, d_attn, weights_out, weights_in, queries, kv, heads_out, lse, tables, parts
):
    ring = n_cols // 2
    length, model = d_attn.shape
    q_width = weights_out.shape[1]
    in_width = weights_in.shape[1]
    col_width = model // n_cols
    width = model // n_rows
    heads = q_width // HEAD_DIM
    scale = 1.0 / math.sqrt(HEAD_DIM)
    bf16, f32 = jnp.bfloat16, jnp.float32
    shape = jax.ShapeDtypeStruct

    def kernel(
        d_attn, wo, w_in, q, kv, out, lse, cosine, sine, y_in,
        d_proj, d_first, y_out, wo_out,
        w, go, delta, dqt, dkv, dkv_own, wo_part, *rest,
    ):
        scratch, ring_parts = rest[:9], rest[9:13]
        kv_parts, wo_parts, local = rest[13:20], rest[20:27], rest[27]
        net = Links(n_rows, n_cols)
        net.greet([net.x, net.y, net.up, net.down, net.twin])
        w_load = pltpu.make_async_copy(w_in, w, local.at[0])
        w_load.start()
        copies = []
        y_steps = scatter_square(
            net, y_in, scratch, list(range(1, ring)), ring_finish(net, ring_parts, None, copies)
        )
        next(y_steps)
        next(y_steps)
        by_place = lambda ref: lambda hops, core: ref.at[
            pl.ds((net.place(hops) * 2 + core) * col_width, col_width), :
        ]

        go[...] = matmul(d_attn[...], wo[...]).astype(bf16)
        wo_part[...] = matmul_tn(d_attn[...], out[...].astype(bf16)).astype(bf16)
        wo_steps = scatter_columns(net, by_place(wo_part), wo_out, wo_parts)
        next(wo_steps)
        for head in range(heads):
            columns = slice(head * HEAD_DIM, (head + 1) * HEAD_DIM)
            product = (go[:, columns].astype(f32) * out[:, columns]).T
            delta[head] = jnp.sum(product, 0, keepdims=True)
        dqt[...] = jnp.zeros_like(dqt)
        dkv[...] = jnp.zeros_like(dkv)
        next(wo_steps)
        next(y_steps)

        def one_block(number, masked):
            keys = kv[number, :, :HEAD_DIM]
            values = kv[number, :, HEAD_DIM:]
            keys_t = keys.T
            d_key = jnp.zeros((length, HEAD_DIM), f32)
            d_value = jnp.zeros((length, HEAD_DIM), f32)
            for head in range(heads):
                columns = slice(head * HEAD_DIM, (head + 1) * HEAD_DIM)
                queries = q[:, columns]
                grads = go[:, columns]
                probs = jnp.exp(scores_of(keys, queries, scale) - lse[head])
                if masked:
                    probs = jnp.where(causal_mask(probs), probs, 0.0)
                d_probs = matmul_nt(values, grads)
                d_scores = (probs * (d_probs - delta[head])).astype(bf16)
                d_value = d_value + matmul(probs.astype(bf16), grads)
                d_key = d_key + matmul(d_scores, queries)
                dqt[head] = dqt[head] + matmul(keys_t, d_scores)
            dkv[number, :, :HEAD_DIM] = (d_key * scale).astype(bf16)
            dkv[number, :, HEAD_DIM:] = d_value.astype(bf16)

        one_block(net.c, True)

        @pl.loop(0, net.c)
        def _(number):
            one_block(number, False)

        kv_steps = scatter_columns(
            net, lambda hops, core: dkv.at[2 * net.chip(hops) + core], dkv_own, kv_parts
        )
        next(kv_steps)
        next(kv_steps)
        next(y_steps)
        next(wo_steps)

        def turned_back(values):
            return (values * cosine[...] - pltpu.roll(values, HEAD_DIM // 2, 1) * sine[...]).astype(bf16)

        for head in range(heads):
            columns = slice(head * HEAD_DIM, (head + 1) * HEAD_DIM)
            d_proj[:, columns] = turned_back((dqt[head] * scale).T)
        next(kv_steps)
        next(y_steps)
        next(kv_steps)
        run_together(kv_steps)
        d_proj[:, q_width : q_width + HEAD_DIM] = turned_back(dkv_own[:, :HEAD_DIM])
        d_proj[:, q_width + HEAD_DIM :] = dkv_own[:, HEAD_DIM:].astype(bf16)
        w_load.wait()
        for j in range(n_rows):
            at = slice(j * width, (j + 1) * width)
            d_first[:, at] = matmul_nt(d_proj[...], w[at, :]).astype(bf16)
        run_together(y_steps, wo_steps)
        copies[-1].wait_recv()
        y_out[...] = ring_parts[0][ring - 2]
        net.finish()

    vmem = pltpu.VMEM
    return remote_call(
        kernel,
        "attention_back",
        6,
        [
            shape((length, in_width), bf16),
            shape((length, model), bf16),
            shape((length, width), bf16),
            shape((col_width, q_width), f32),
        ],
        [
            vmem((model, in_width), bf16),
            vmem((length, q_width), bf16),
            vmem((heads, 1, length), f32),
            vmem((heads, HEAD_DIM, length), f32),
            vmem((n_cols, length, 2 * HEAD_DIM), bf16),
            vmem((length, 2 * HEAD_DIM), f32),
            vmem((model, q_width), bf16),
        ]
        + scatter_scratch(ring - 1, length, width)
        + ring_scratch(ring, length, width)
        + scatter_columns_scratch(ring, length, 2 * HEAD_DIM)
        + scatter_columns_scratch(ring, col_width, q_width)
        + [pltpu.SemaphoreType.DMA((1,))],
        (d_attn, weights_out, weights_in, queries, kv, heads_out, lse, *tables, parts),
        in_vmem=(0, 1, 3, 4, 5, 6, 7, 8),
        out_vmem=(0, 1, 2, 3),
    )


def last_phase(n_rows, n_cols, d_first, d_proj, normed, parts, part_sum, x, proj, d_resid, gains, gain_part):
    ring = n_cols // 2
    length, model = d_first.shape
    width = model // n_rows
    in_width = d_proj.shape[1]
    col_width = model // n_cols
    pieces = 2
    piece = length // pieces
    bf16, f32 = jnp.bfloat16, jnp.float32
    shape = jax.ShapeDtypeStruct
    chips = n_rows * ring

    def kernel(
        d_first, d_proj, normed, y_in, y_sum, x, proj, d_resid, gains, gain_two,
        layer_out, grad_in, gain_out, w_out,
        d_own, w_part, moment, moments, gain_own, gain_twin, gain_sums, *rest,
    ):
        scratch, y_scratch = rest[:9], rest[9:18]
        w_parts = rest[18:25]
        mo_s, mo_r, ga_s, ga_r, gt_s, gt_r = rest[25:]
        net = Links(n_rows, n_cols)
        others = net.spread_partners()
        net.greet([device for _, _, device in others] + [net.twin])

        def finish(s, upper, lower):
            at = lambda p: pl.ds(s * piece + p * (piece // 2), piece // 2)
            add_slabs(d_own.at[at(0), :], upper)
            add_slabs(d_own.at[at(1), :], lower)

        def finish_out(s, upper, lower):
            for part, terms in ((0, upper), (1, lower)):
                at = pl.ds(part * (length // 2), length // 2)
                extra = [
                    part_reader(y_sum.at[at, :]),
                    part_reader(x.at[at, pl.ds(0, width)]),
                    part_reader(proj.at[at, pl.ds(0, width)]),
                ]
                add_slabs(layer_out.at[at, :], terms + extra)

        steps = scatter_square(net, d_first, scratch, list(range(pieces)), finish, resident=True)
        y_steps = scatter_square(net, y_in, y_scratch, [0], finish_out)
        next(steps)
        next(steps)
        w_part[...] = matmul_tn(normed[...], d_proj[...]).astype(bf16)
        by_place = lambda hops, core: w_part.at[
            pl.ds((net.place(hops) * 2 + core) * col_width, col_width), :
        ]
        w_steps = scatter_columns(net, by_place, w_out, w_parts)
        next(w_steps)
        next(y_steps)
        next(w_steps)
        run_together(steps)

        gain = gains[0:1, :width]
        slab = 128
        gain_own[...] = jnp.zeros_like(gain_own)

        def unit_of(at):
            values = x[at, :].astype(f32)
            inverse = lax.rsqrt(jnp.mean(values * values, -1, keepdims=True) + NORM_EPS)
            return values[:, :width] * inverse, inverse

        for i in range(length // slab):
            at = slice(i * slab, (i + 1) * slab)
            unit, _ = unit_of(at)
            d_normed = d_own[at, :]
            share = jnp.sum(d_normed * gain * unit, -1, keepdims=True)
            moment[:, at] = jnp.broadcast_to(share, (slab, 128)).T[:8]
            gain_own[:8] += jnp.sum((d_normed * unit).reshape(slab // 8, 8, width), 0)
        sends = [
            net.send(moment, moments.at[bits - 1], (mo_s, mo_r), bits - 1, (net.flip(bits), net.c))
            for bits in range(1, n_rows)
        ]
        gain_own[8:] = gain_two[...]
        twin = net.send(gain_own, gain_twin, (gt_s, gt_r), 0, net.twin)
        for copy in sends:
            copy.wait_recv()
        whole = moment[...] + moments[0] + moments[1] + moments[2]
        for i in range(length // slab):
            at = slice(i * slab, (i + 1) * slab)
            unit, inverse = unit_of(at)
            mean = jnp.broadcast_to(whole[:1, at], (128, slab)).T[:, :1] / model
            grad_in[at, :] = d_resid[at, :] + inverse * (d_own[at, :] * gain - unit * mean)
        twin.wait_recv()
        mine = net.r * ring + net.z
        gain_sums[mine] = gain_own[...] + gain_twin[...]
        sends = [
            net.send(gain_sums.at[mine], gain_sums.at[mine], (ga_s, ga_r), number, device)
            for number, (hops, bits, device) in enumerate(others)
        ]
        next(w_steps)
        run_together(y_steps)
        for copy in sends:
            copy.wait_recv()
        total = gain_sums[net.z * ring]
        for i in range(1, ring):
            total = total + gain_sums[net.z * ring + i]
        gain_out[0:1] = jnp.sum(total[:8], 0, keepdims=True)
        gain_out[1:2] = jnp.sum(total[8:], 0, keepdims=True)
        gain_out[2:8] = jnp.zeros((6, width), f32)
        run_together(w_steps)
        net.finish()

    vmem = pltpu.VMEM
    return remote_call(
        kernel,
        "last_phase",
        7,
        [
            shape((length, width), bf16),
            shape((length, width), f32),
            shape((8, width), f32),
            shape((col_width, in_width), f32),
        ],
        [
            vmem((length, width), f32),
            vmem((model, in_width), bf16),
            vmem((8, length), f32),
            vmem((n_rows - 1, 8, length), f32),
            vmem((16, width), f32),
            vmem((16, width), f32),
            vmem((chips, 16, width), f32),
        ]
        + scatter_scratch(pieces, piece, width, resident=True)
        + scatter_scratch(1, length, width)
        + scatter_columns_scratch(ring, col_width, in_width)
        + pair_sems(n_rows - 1)
        + pair_sems(chips - 1)
        + pair_sems(1),
        (
            d_first.reshape(pieces, piece, model), d_proj, normed, parts, part_sum, x, proj, d_resid,
            gains, gain_part,
        ),
        in_vmem=(0, 1, 2, 4, 5, 6, 7, 8, 9),
        out_vmem=(0, 1, 2, 3),
    )


def expert_kernel(
    info, rows, grads, maps, gate_own, gate_twin, up_own, up_twin, down_own, down_twin, shared, router,
    d_rows_out, rows_out, slot_rows, d_part, e_act, d_gate, d_up, s_act, d_shared, probs_out, d_gates,
    w_gate, w_up, w_down, part, sems,
):
    tokens, model = rows.shape[1:]
    n_slots = slot_rows.shape[1]
    half_hidden = gate_own.shape[1]
    hidden = 2 * half_hidden
    pad = shared.shape[1] // 3
    gate_up, down = slice(0, 2 * pad), slice(2 * pad, 3 * pad)
    row, own_expert = info[0], info[1]
    width = model // 4
    bf16, f32 = jnp.bfloat16, jnp.float32
    blocks, experts, block_rows = maps.shape[1:]

    @pl.when(pl.program_id(0) == 0)
    def _():
        copies = []
        for j in range(4):
            flipped = row + (1 - 2 * lax.rem(row, 2)) * (j & 1) + (2 - 4 * lax.div(row, 2)) * (j >> 1)
            there = pl.ds(pl.multiple_of(flipped * width, width), width)
            here = pl.ds(j * width, width)
            for h, sources in enumerate(((gate_own, up_own, down_own), (gate_twin, up_twin, down_twin))):
                cols = pl.ds(h * half_hidden, half_hidden)
                number = 6 * j + 3 * h
                copies += [
                    pltpu.make_async_copy(
                        sources[0].at[there, :], w_gate.at[here, cols], sems.at[number]
                    ),
                    pltpu.make_async_copy(
                        sources[1].at[there, :], w_up.at[here, cols], sems.at[number + 1]
                    ),
                    pltpu.make_async_copy(
                        sources[2].at[:, there], w_down.at[cols, here], sems.at[number + 2]
                    ),
                ]
        for copy in copies:
            copy.start()
        for copy in copies:
            copy.wait()

    x = rows[0]
    slot_row, chosen = [], []
    for b in range(blocks):
        own_map = jnp.where(
            lax.broadcasted_iota(jnp.int32, (experts, block_rows), 0) == own_expert, maps[0, b], 0.0
        )
        own_map = jnp.sum(own_map, 0, keepdims=True)
        slot_row.append(jnp.where(own_map >= 0, own_map + b * (n_slots // blocks), -1.0))
        filled = jnp.concatenate([maps[0, b], jnp.full((128 - experts, block_rows), -1.0, f32)], 0)
        chosen.append(filled.T)
    slot_row, chosen = jnp.concatenate(slot_row, 1), jnp.concatenate(chosen, 0)
    mine_hot = (lax.broadcasted_iota(jnp.int32, (1, 128), 1) == own_expert).astype(f32)
    pick = (
        lax.broadcasted_iota(jnp.int32, (n_slots, tokens), 0).astype(f32) == slot_row
    ).astype(f32)
    pick_b = pick.astype(bf16)
    pick_t = pick.T.astype(bf16)
    exact = lambda a, b, dims: lax.dot_general(
        a, b, (dims, ((), ())), precision=PRECISE, preferred_element_type=f32
    )

    logits = matmul(x, router[...])
    logits = jnp.where(chosen >= 0, logits, NEG_LARGE)
    logits = jnp.exp(logits - jnp.max(logits, -1, keepdims=True))
    probs = logits / jnp.sum(logits, -1, keepdims=True)
    probs_out[0] = probs
    my_gate = jnp.sum(probs * mine_hot, -1, keepdims=True)
    slot_gate = exact(pick, jnp.broadcast_to(my_gate, (tokens, 128)), ((1,), (0,)))[:, :1]
    s_gate = matmul(x, shared[:, :pad])
    s_up = matmul(x, shared[:, pad : 2 * pad])
    through = matmul(grads[0], shared[:, down])
    s_silu, s_slope = silu_parts(s_gate)
    s_act[0] = (s_silu * s_up).astype(bf16)
    d_shared[0, :, :pad] = (through * s_up * s_slope).astype(bf16)
    d_shared[0, :, pad:] = (through * s_silu).astype(bf16)

    tile = 512
    for t in range(model // tile):
        at = slice(t * tile, (t + 1) * tile)
        slot_rows[0, :, at] = matmul(pick_b, rows[0, :, at]).astype(bf16)
        picked = matmul(pick_b, grads[0, :, at])
        part[:, at] = picked.astype(bf16)
        d_part[0, :, at] = (picked * slot_gate).astype(bf16)

    step = 256

    def hidden_tile(t, total):
        at = pl.ds(pl.multiple_of(t * step, step), step)
        e_gate = matmul(slot_rows[0], w_gate[:, at])
        e_up = matmul(slot_rows[0], w_up[:, at])
        through = matmul_nt(part[...], w_down[at, :])
        e_silu, e_slope = silu_parts(e_gate)
        act = e_silu * e_up
        d_act = through * slot_gate
        e_act[0, :, at] = act.astype(bf16)
        d_gate[0, :, at] = (d_act * e_up * e_slope).astype(bf16)
        d_up[0, :, at] = (d_act * e_silu).astype(bf16)
        return total + jnp.sum(act * through, -1, keepdims=True)

    d_gate_slot = lax.fori_loop(0, hidden // step, hidden_tile, jnp.zeros((n_slots, 1), f32))
    d_gates[0] = exact(jnp.broadcast_to(d_gate_slot, (n_slots, 128)), pick, ((0,), (0,)))[:1]

    @pl.loop(0, model // tile)
    def _(t):
        at = pl.ds(pl.multiple_of(t * tile, tile), tile)
        d_slot = matmul_nt(d_gate[0], w_gate[at, :]) + matmul_nt(d_up[0], w_up[at, :])
        d_rows_out[0, :, at] = (
            matmul(pick_t, d_slot.astype(bf16)) + matmul_nt(d_shared[0], shared[at, gate_up])
        ).astype(bf16)
        out = (matmul(e_act[0], w_down[:, at]) * slot_gate).astype(bf16)
        rows_out[0, :, at] = (
            matmul(pick_t, out) + matmul_nt(s_act[0], shared[at, down])
        ).astype(bf16)


def expert_chunks(info, rows, grads, maps, experts_w, shared, router, slots):
    chunks, tokens, model = rows.shape
    half_hidden = experts_w[0].shape[1]
    hidden = 2 * half_hidden
    pad = shared.shape[1] // 3
    by_chunk = lambda *dims: pl.BlockSpec((1, *dims), lambda i, s: (i, 0, 0))
    once = lambda *dims: pl.BlockSpec(dims, lambda i, s: (0, 0), pipeline_mode=pl.Buffered(1))
    anywhere = pl.BlockSpec(memory_space=pl.ANY)
    single = lambda *dims: pl.BlockSpec(
        (1, *dims), lambda i, s: (i, 0, 0), pipeline_mode=pl.Buffered(1)
    )
    bf16, f32 = jnp.bfloat16, jnp.float32
    shape = lambda dtype, *dims: jax.ShapeDtypeStruct((chunks, *dims), dtype)
    return pl.pallas_call(
        expert_kernel,
        grid_spec=pltpu.PrefetchScalarGridSpec(
            num_scalar_prefetch=1,
            grid=(chunks,),
            in_specs=[
                by_chunk(tokens, model),
                by_chunk(tokens, model),
                pl.BlockSpec((1, *maps.shape[1:]), lambda i, s: (i, 0, 0, 0)),
            ]
            + [anywhere] * 6
            + [once(*shared.shape), once(*router.shape)],
            out_specs=[
                single(tokens, model),
                single(tokens, model),
                single(slots, model),
                single(slots, model),
                single(slots, hidden),
                single(slots, hidden),
                single(slots, hidden),
                single(tokens, pad),
                single(tokens, 2 * pad),
                single(tokens, 128),
                pl.BlockSpec((1, 1, tokens), lambda i, s: (s[2 + i], 0, 0)),
            ],
            scratch_shapes=[
                pltpu.VMEM((model, hidden), bf16),
                pltpu.VMEM((model, hidden), bf16),
                pltpu.VMEM((hidden, model), bf16),
                pltpu.VMEM((slots, model), bf16),
                pltpu.SemaphoreType.DMA((24,)),
            ],
        ),
        out_shape=[
            shape(bf16, tokens, model),
            shape(bf16, tokens, model),
            shape(bf16, slots, model),
            shape(bf16, slots, model),
            shape(bf16, slots, hidden),
            shape(bf16, slots, hidden),
            shape(bf16, slots, hidden),
            shape(bf16, tokens, pad),
            shape(bf16, tokens, 2 * pad),
            shape(f32, tokens, 128),
            shape(f32, 1, tokens),
        ],
        compiler_params=pltpu.CompilerParams(vmem_limit_bytes=63 * MIB),
        cost_estimate=pl.CostEstimate(
            flops=chunks * 2 * tokens * model * (4 * hidden + 6 * pad),
            bytes_accessed=40 * MIB,
            transcendentals=chunks * slots * hidden,
        ),
        name="expert_chunks",
    )(info, rows, grads, maps, *experts_w, shared, router)


def add_bf16(left, right):
    return (left.astype(jnp.float32) + right.astype(jnp.float32)).astype(jnp.bfloat16)


class Exchange:
    def __init__(self):
        self.n_rows = lax.axis_size("rows")
        self.n_cols = lax.axis_size("cols")
        self.ring = self.n_cols // 2
        self.r = lax.axis_index("rows")
        self.c = lax.axis_index("cols")
        self.z = self.c // 2
        self.k = self.c % 2

    def move(self, values, target):
        pairs = []
        for r in range(self.n_rows):
            for c in range(self.n_cols):
                to_r, to_c = target(r, c)
                pairs.append((r * self.n_cols + c, to_r * self.n_cols + to_c))
        return lax.ppermute(values, ("rows", "cols"), pairs)

    def along_x(self, values):
        return self.move(values, lambda r, c: (r ^ 1, c))

    def along_y(self, values):
        return self.move(values, lambda r, c: (r ^ 2, c))

    def along_z(self, values, hops=1):
        return self.move(values, lambda r, c: (r, (c + 2 * hops) % self.n_cols))

    def across_z(self, values, bit):
        return self.move(values, lambda r, c: (r, c ^ (2 * bit)))

    def sibling(self, values):
        return self.move(values, lambda r, c: (r, c ^ 1))

    def chip(self, hops):
        return (self.z - hops + self.ring) % self.ring

    def place(self, hops):
        return self.r ^ self.chip(hops)

    def mixed(self, values, axis):
        width = values.shape[axis] // self.n_rows

        def branch(row):
            return lambda whole: jnp.concatenate(
                [
                    lax.slice_in_dim(whole, (row ^ j) * width, ((row ^ j) + 1) * width, axis=axis)
                    for j in range(self.n_rows)
                ],
                axis,
            )

        return lax.switch(self.r, [branch(row) for row in range(self.n_rows)], values)

    def rows_gather(self, block):
        half = block.shape[0] // 2
        from_x = self.along_x(block)
        from_y = self.along_y(block)
        first = self.along_y(from_x[:half])
        second = self.along_x(from_y[half:])
        return [block, from_x, from_y, jnp.concatenate([first, second], 0)]

    def rows_scatter(self, blocks):
        half = blocks[0].shape[0] // 2
        upper = [block[:half] for block in blocks]
        lower = [block[half:] for block in blocks]
        sent = self.along_x(jnp.stack([upper[1], upper[3]]))
        forward = add_bf16(upper[2], sent[1])
        upper_sum = upper[0].astype(jnp.float32) + sent[0].astype(jnp.float32)
        upper_sum = upper_sum + self.along_y(forward).astype(jnp.float32)
        sent = self.along_y(jnp.stack([lower[2], lower[3]]))
        forward = add_bf16(lower[1], sent[1])
        lower_sum = lower[0].astype(jnp.float32) + sent[0].astype(jnp.float32)
        lower_sum = lower_sum + self.along_x(forward).astype(jnp.float32)
        return jnp.concatenate([upper_sum, lower_sum], 0)

    def cols_gather(self, block, place):
        shape = (self.ring, 2) + block.shape
        whole = jnp.zeros(shape, block.dtype)
        rest = (0,) * block.ndim
        for hops in range(self.ring):
            twin = self.sibling(block)
            spot = place(hops)
            whole = lax.dynamic_update_slice(whole, block[None, None], (spot, self.k) + rest)
            whole = lax.dynamic_update_slice(whole, twin[None, None], (spot, 1 - self.k) + rest)
            if hops < self.ring - 1:
                block = self.along_z(block)
        return whole

    def pair_sum(self, parts):
        mine = lax.dynamic_index_in_dim(parts, self.k, 1, False)
        other = lax.dynamic_index_in_dim(parts, 1 - self.k, 1, False)
        return add_bf16(mine, self.sibling(other))

    def cols_scatter(self, parts, place):
        summed = self.pair_sum(parts)
        pick = lambda hops: lax.dynamic_index_in_dim(summed, place(hops), 0, False)
        run = pick(1)
        for hops in range(2, self.ring):
            run = add_bf16(self.along_z(run), pick(hops))
        return self.along_z(run).astype(jnp.float32) + pick(0).astype(jnp.float32)


def split_terms(values):
    high = lax.reduce_precision(values, 8, 7)
    return high.astype(jnp.bfloat16), (values - high).astype(jnp.bfloat16)


def gathered_layer(
    layer_in,
    norm1_gain,
    w_query,
    key_matrix,
    value_matrix,
    w_out,
    norm2_gain,
    w_router,
    shared_gate,
    shared_up,
    shared_down,
    expert_gate,
    expert_up,
    expert_down,
    routes,
    cotangent,
):
    net = Exchange()
    n_rows, ring = net.n_rows, net.ring
    r, c, z, k = net.r, net.c, net.z, net.k
    length, row_width = layer_in.shape[1:]
    rows_dev, top_k = routes.shape[2:]
    experts = w_router.shape[1]
    model_width = row_width * n_rows
    col_width = w_query.shape[0]
    q_width = w_query.shape[1]
    q_heads = q_width // HEAD_DIM
    kv_width = key_matrix.shape[1]
    shared_hidden = shared_gate.shape[1] // ring
    half_hidden = expert_gate.shape[2]
    slots = -(-2 * max(1, 5 * rows_dev * top_k // (8 * experts)) // 16) * 16
    index = lax.dynamic_index_in_dim

    expert_ids = jnp.arange(experts, dtype=jnp.int32)
    hot = jnp.sum(
        (routes.reshape(rows_dev, top_k)[:, :, None] == expert_ids).astype(jnp.float32), 1
    )
    earlier = jnp.tril(jnp.ones((rows_dev, rows_dev), jnp.float32), -1)
    rank = jnp.dot(earlier, hot, precision=PRECISE)
    slot_map = jnp.where(hot > 0, rank, -1.0).T

    small = jnp.concatenate([w_router, norm1_gain[:, None], norm2_gain[:, None]], 1)
    small = jnp.pad(small, ((0, 0), (0, 128 - small.shape[1])))
    pad_to = -(-shared_hidden // 128) * 128
    padded = lambda w: jnp.pad(
        w.reshape(col_width, ring, shared_hidden), ((0, 0), (0, 0), (0, pad_to - shared_hidden))
    )
    packed = jnp.concatenate([padded(shared_gate), padded(shared_up), padded(shared_down.T)], 2)
    packed = jnp.swapaxes(packed, 0, 1)
    experts_w = []
    for own in (expert_gate[0], expert_up[0], expert_down[0]):
        experts_w += [own, net.sibling(own)]
    positions = c * length + jnp.arange(length, dtype=jnp.int32)
    cosine_table, sine_table = rope_tables(positions, HEAD_DIM)
    tables = (
        jnp.concatenate([cosine_table, cosine_table], 1),
        jnp.concatenate([-sine_table, sine_table], 1),
    )

    (
        token_input, first_normed, weights_in, small, queries, kv_all, attn_f32, log_total,
        weights_out_t, grad_rows, rows_all, slot_maps, shared_w, attn_proj, gains,
    ) = first_phase(
        n_rows, net.n_cols, layer_in[0], cotangent[0],
        jnp.concatenate([w_query, key_matrix, value_matrix], 1), small, w_out.T, packed, slot_map,
        tables,
    )
    info = jnp.stack([r, r * ring + z] + [net.chip(hops) for hops in range(ring)]).astype(jnp.int32)
    (
        d_rows, out_rows, slot_rows, d_part, e_act, d_e_gate, d_e_up, s_act, d_shared, gate_probs,
        d_gate_mine,
    ) = expert_chunks(
        info, rows_all, grad_rows, slot_maps, experts_w, shared_w, small, n_rows * slots
    )

    joined = lambda whole: whole.reshape(-1, whole.shape[-1])
    attn_proj = joined(attn_proj)
    d_attn, d_resid, gain_part, d_gate_all, g_expert_gate, g_expert_up, g_expert_down = token_sum(
        n_rows, net.n_cols, d_rows, d_gate_mine.reshape(ring, length),
        [joined(part) for part in (slot_rows, d_part, e_act, d_e_gate, d_e_up)],
        gate_probs[0], small, (token_input, attn_proj, grad_rows[0]), gains,
    )[:7]

    grad_router = jnp.zeros((row_width, experts), jnp.float32)
    for hops in range(ring):
        probs = gate_probs[hops][:, :experts]
        d_gates = index(d_gate_all, net.chip(hops), 1, False).T
        d_logits = probs * (d_gates - jnp.sum(probs * d_gates, -1, keepdims=True))
        quarter = lax.dynamic_slice(rows_all[hops], (r * rows_dev, 0), (rows_dev, model_width))
        quarter = lax.switch(
            r ^ z,
            [
                lambda rows, j=j: rows[:, j * row_width : (j + 1) * row_width]
                for j in range(n_rows)
            ],
            quarter,
        )
        d_quarter = lax.dynamic_slice_in_dim(d_logits, r * rows_dev, rows_dev, 0)
        high, low = split_terms(d_quarter)
        both = matmul_tn(quarter, jnp.concatenate([high, low], 1))
        grad_router = grad_router + both[:, :experts] + both[:, experts:]
    grad_router = grad_router.reshape(2, col_width, experts)
    g_router = index(grad_router, k, 0, False) + net.sibling(index(grad_router, 1 - k, 0, False))
    g_router = g_router + net.along_x(g_router)
    g_router = g_router + net.along_y(g_router)

    d_projected, d_first, part_sum, g_out = attention_back(
        n_rows, net.n_cols, d_attn, weights_out_t, weights_in, queries, kv_all, attn_f32, log_total,
        tables, out_rows,
    )
    layer_out, grad_in, gain_grads, g_in = last_phase(
        n_rows, net.n_cols, d_first, d_projected, first_normed, out_rows, part_sum, token_input,
        attn_proj, d_resid, gains, gain_part,
    )
    gain_grads = index(gain_grads[:2].reshape(2, 2, col_width), k, 1, False)

    column_parts = lambda whole: whole.astype(jnp.bfloat16).reshape(ring, 2, col_width, -1)
    shared_parts = jnp.concatenate(
        [
            matmul_tn(joined(rows_all), joined(d_shared)),
            matmul_tn(joined(grad_rows), joined(s_act)),
        ],
        1,
    )
    shared_parts = net.pair_sum(column_parts(shared_parts))
    g_shared = jnp.zeros(shared_parts.shape, jnp.bfloat16)
    for hops in range(ring):
        piece = index(shared_parts, net.place(-hops), 0, False)
        piece = net.along_z(piece, hops) if hops else piece
        g_shared = lax.dynamic_update_slice(g_shared, piece[None], (net.chip(hops), 0, 0))
    g_shared = g_shared.astype(jnp.float32)
    shared_cols = lambda n: jnp.swapaxes(
        g_shared[:, :, n * pad_to : n * pad_to + shared_hidden], 0, 1
    ).reshape(col_width, -1)

    return (
        layer_out[None],
        grad_in[None],
        gain_grads[0],
        g_in[:, :q_width],
        g_in[:, q_width : q_width + kv_width],
        g_in[:, q_width + kv_width :],
        g_out.T,
        gain_grads[1],
        g_router,
        shared_cols(0),
        shared_cols(1),
        shared_cols(2).T,
        g_expert_gate[None],
        g_expert_up[None],
        g_expert_down[None],
    )


def per_device(layer_in, *others):
    routes = others[13]
    w_router = others[6]
    n_rows, n_cols = lax.axis_size("rows"), lax.axis_size("cols")
    experts, top_k = w_router.shape[1], routes.shape[3]
    gathers = (
        experts <= 4 * top_k
        and layer_in.shape[0] == 1
        and n_rows == 4
        and n_cols == 2 * n_rows
        and 2 * experts == n_rows * n_cols
    )
    return (gathered_layer if gathers else routed_layer)(layer_in, *others)


def solution(mesh):
    placed = (
        P(None, "cols", "rows"),
        P("cols"),
        P("cols", "rows"),
        P("cols", "rows"),
        P("cols", "rows"),
        P("rows", "cols"),
        P("cols"),
        P("cols", None),
        P("cols", "rows"),
        P("cols", "rows"),
        P("rows", "cols"),
        P(("rows", "cols"), None, None),
        P(("rows", "cols"), None, None),
        P(("rows", "cols"), None, None),
        P("cols", "rows", None, None),
        P(None, "cols", "rows"),
    )
    return jax.shard_map(
        per_device,
        mesh=mesh,
        in_specs=placed,
        out_specs=(
            P(None, "cols", "rows"),
            P(None, "cols", "rows"),
            P("cols"),
            P("cols", "rows"),
            P("cols", "rows"),
            P("cols", "rows"),
            P("rows", "cols"),
            P("cols"),
            P("cols", None),
            P("cols", "rows"),
            P("cols", "rows"),
            P("rows", "cols"),
            P(("rows", "cols"), None, None),
            P(("rows", "cols"), None, None),
            P(("rows", "cols"), None, None),
        ),
        check_vma=False,
    )
```

```python
import math

import jax
import jax.numpy as jnp
from jax import lax
from jax.experimental import pallas as pl
from jax.experimental.pallas import tpu as pltpu
from jax.sharding import PartitionSpec as P

HEAD_DIM = 128


NORM_EPS = 1e-05
ROPE_BASE = 500000.0
NEG_LARGE = -1e30
PRECISE = lax.Precision.HIGHEST


def rope_tables(positions, head_size):
    half_size = head_size // 2
    inv_freq = ROPE_BASE ** (-(2.0 * jnp.arange(half_size, dtype=jnp.float32)) / head_size)
    angles = positions.astype(jnp.float32)[:, None] * inv_freq[None, :]
    return (jnp.cos(angles), jnp.sin(angles))


def apply_rotary(values, cosine_table, sine_table):
    half_size = values.shape[-1] // 2
    first_half = values[..., :half_size]
    second = values[..., half_size:]
    cos_b = cosine_table[:, None, :]
    sin_b = sine_table[:, None, :]
    return jnp.concatenate(
        [first_half * cos_b - second * sin_b, second * cos_b + first_half * sin_b], -1
    )


def matmul(left_op, right_op):
    return jnp.dot(left_op, right_op, preferred_element_type=jnp.float32)


def matmul_tn(left_op, right_op):
    return lax.dot_general(
        left_op, right_op, (((0,), (0,)), ((), ())), preferred_element_type=jnp.float32
    )


def matmul_nt(left_op, right_op):
    return lax.dot_general(
        left_op, right_op, (((1,), (1,)), ((), ())), preferred_element_type=jnp.float32
    )


def silu_parts(pre_act):
    sigma = jax.nn.sigmoid(pre_act)
    return (pre_act * sigma, sigma * (1.0 + pre_act * (1.0 - sigma)))


def keep_same(carry_in):
    return carry_in


def routed_layer(
    layer_in,
    norm1_gain,
    w_query,
    key_matrix,
    value_matrix,
    w_out,
    norm2_gain,
    w_router,
    shared_gate,
    shared_up,
    shared_down,
    expert_gate,
    expert_up,
    expert_down,
    routes,
    cotangent,
):
    n_rows = lax.axis_size("rows")
    n_cols = lax.axis_size("cols")
    row_idx = lax.axis_index("rows")
    col_idx = lax.axis_index("cols")
    sequence_count, len_dev, row_width = layer_in.shape
    tok_dev = sequence_count * len_dev
    rows_dev = routes.shape[2]
    top_k = routes.shape[3]
    experts = w_router.shape[1]
    devices = n_rows * n_cols
    capacity = 2 * max(1, 5 * rows_dev * top_k // (8 * experts))
    full_in = lax.all_gather(layer_in, "rows", axis=2, tiled=True)
    (
        gain_one,
        wq_full,
        wk_full,
        wv_full,
        wo_full,
        gain_two,
        router_full,
        sg_full,
        su_full,
        sd_full,
    ) = (
        lax.all_gather(norm1_gain, "cols", axis=0, tiled=True),
        lax.all_gather(w_query, "cols", axis=0, tiled=True),
        lax.all_gather(key_matrix, "cols", axis=0, tiled=True),
        lax.all_gather(value_matrix, "cols", axis=0, tiled=True),
        lax.all_gather(w_out, "cols", axis=1, tiled=True),
        lax.all_gather(norm2_gain, "cols", axis=0, tiled=True),
        lax.all_gather(w_router, "cols", axis=0, tiled=True),
        lax.all_gather(shared_gate, "cols", axis=0, tiled=True),
        lax.all_gather(shared_up, "cols", axis=0, tiled=True),
        lax.all_gather(shared_down, "cols", axis=1, tiled=True),
    )
    model_width = full_in.shape[2]
    token_input = full_in.reshape(tok_dev, model_width).astype(jnp.float32)
    first_inverse_deviation = lax.rsqrt(
        jnp.mean(token_input * token_input, -1, keepdims=True) + NORM_EPS
    )
    first_unit_rows = token_input * first_inverse_deviation
    first_gain_float = gain_one.astype(jnp.float32)
    first_normed = (first_unit_rows * first_gain_float).astype(jnp.bfloat16)
    q_pre = matmul(first_normed, wq_full)
    key_unrotated = matmul(first_normed, wk_full)
    value_projected = matmul(first_normed, wv_full).astype(jnp.bfloat16)
    q_heads = q_pre.shape[1] // HEAD_DIM
    positions = col_idx * len_dev + jnp.arange(len_dev, dtype=jnp.int32)
    cosine_table, sine_table = rope_tables(positions, HEAD_DIM)
    rotated_queries = apply_rotary(
        q_pre.reshape(sequence_count, len_dev, q_heads, HEAD_DIM), cosine_table, sine_table
    ).astype(jnp.bfloat16)
    rotated_keys = apply_rotary(
        key_unrotated.reshape(sequence_count, len_dev, 1, HEAD_DIM), cosine_table, sine_table
    ).astype(jnp.bfloat16)
    kv_local = jnp.concatenate(
        [
            rotated_keys.reshape(sequence_count, len_dev, HEAD_DIM),
            value_projected.reshape(sequence_count, len_dev, HEAD_DIM),
        ],
        -1,
    )
    kv_local = jnp.swapaxes(kv_local, 0, 1)
    query_t = jnp.transpose(rotated_queries, (0, 2, 1, 3))
    score_scale = 1.0 / math.sqrt(HEAD_DIM)
    q_last = col_idx * len_dev + len_dev - 1

    def online_update(carry_in, key_part, k_start):
        run_max, run_sum, run_acc = carry_in
        block_len = key_part.shape[0]
        scores = (
            jnp.einsum(
                "shqd,bsd->shqb",
                query_t,
                key_part[:, :, :HEAD_DIM],
                preferred_element_type=jnp.float32,
            )
            * score_scale
        )
        key_pos = k_start + jnp.arange(block_len, dtype=jnp.int32)
        causal = positions[:, None] >= key_pos[None, :]
        scores = jnp.where(causal, scores, NEG_LARGE)
        new_max = jnp.maximum(run_max, jnp.max(scores, -1))
        prob_vals = jnp.where(causal, jnp.exp(scores - new_max[..., None]), 0.0)
        rescale = jnp.exp(run_max - new_max)
        run_sum = run_sum * rescale + jnp.sum(prob_vals, -1)
        run_acc = run_acc * rescale[..., None] + jnp.einsum(
            "shqb,bsd->shqd",
            prob_vals.astype(jnp.bfloat16),
            key_part[:, :, HEAD_DIM:],
            preferred_element_type=jnp.float32,
        )
        return (new_max, run_sum, run_acc)

    fold_start = (
        jnp.full((sequence_count, q_heads, len_dev), NEG_LARGE, jnp.float32),
        jnp.zeros((sequence_count, q_heads, len_dev), jnp.float32),
        jnp.zeros((sequence_count, q_heads, len_dev, HEAD_DIM), jnp.float32),
    )
    carry_in = fold_start
    piece = lax.all_gather(kv_local, "cols", axis=0, tiled=True)
    start = jnp.int32(0)
    piece_len = piece.shape[0]
    step_len = min(512, piece_len)
    for offset in range(0, piece_len, step_len):
        key_part = piece[offset : offset + step_len]
        k_start = start + offset

        def updated(state_in, key_part=key_part, k_start=k_start):
            return online_update(state_in, key_part, k_start)

        carry_in = lax.cond(k_start <= q_last, updated, keep_same, carry_in)
    run_max, run_sum, run_acc = carry_in
    attn_f32 = run_acc / run_sum[..., None]
    log_total = run_max + jnp.log(run_sum)
    attn_bf = attn_f32.astype(jnp.bfloat16)
    attn_rows = jnp.transpose(attn_bf, (0, 2, 1, 3)).reshape(tok_dev, q_heads * HEAD_DIM)
    attn_proj = lax.psum(matmul(attn_rows, wo_full).astype(jnp.bfloat16), "rows").astype(
        jnp.float32
    )
    residual_stream = token_input + attn_proj
    second_inverse_deviation = lax.rsqrt(
        jnp.mean(residual_stream * residual_stream, -1, keepdims=True) + NORM_EPS
    )
    second_unit_rows = residual_stream * second_inverse_deviation
    second_gain_float = gain_two.astype(jnp.float32)
    second_normed = (second_unit_rows * second_gain_float).astype(jnp.bfloat16)
    gate_pre = matmul(second_normed, sg_full)
    up_pre = matmul(second_normed, su_full)
    silu_gate, silu_slope = silu_parts(gate_pre)
    shared_act = (silu_gate * up_pre).astype(jnp.bfloat16)
    ffn_part = matmul(shared_act, sd_full)
    my_rows = row_idx * rows_dev
    normed_mine = lax.dynamic_slice_in_dim(second_normed, my_rows, rows_dev, 0)
    route_mine = routes.reshape(rows_dev, top_k)
    logits = matmul(normed_mine, router_full)
    expert_ids = jnp.arange(experts, dtype=jnp.int32)
    chosen_hot = (route_mine[:, :, None] == expert_ids[None, None, :]).astype(jnp.float32)
    chosen = jnp.sum(chosen_hot * logits[:, None, :], -1)
    gate_probs = jax.nn.softmax(chosen, -1)
    assign_count = rows_dev * top_k
    flat_routes = route_mine.reshape(assign_count)
    assign_hot = (flat_routes[:, None] == expert_ids[None, :]).astype(jnp.int32)
    rank_in = jnp.sum((jnp.cumsum(assign_hot, 0) - assign_hot) * assign_hot, 1)
    slot_of = flat_routes * capacity + rank_in
    assign_of_slot = (
        jnp.zeros((experts * capacity,), jnp.int32)
        .at[slot_of]
        .set(jnp.arange(assign_count, dtype=jnp.int32))
    )
    slot_used = jnp.zeros((experts * capacity,), jnp.int32).at[slot_of].set(1)
    slot_row = assign_of_slot // top_k

    def send_rows(slot_vals):
        slot_vals = slot_vals.reshape(experts, capacity, model_width)
        outgoing = jnp.broadcast_to(
            slot_vals[:, None], (experts, 2, capacity, model_width)
        ).reshape(devices, capacity, model_width)
        received = lax.all_to_all(
            outgoing, ("rows", "cols"), split_axis=0, concat_axis=0, tiled=True
        )
        return received.reshape(devices * capacity, model_width)

    def return_rows(slot_vals):
        returned = lax.all_to_all(
            slot_vals.reshape(devices, capacity, model_width),
            ("rows", "cols"),
            split_axis=0,
            concat_axis=0,
            tiled=True,
        )
        returned = returned.reshape(experts, 2, capacity, model_width).astype(jnp.float32)
        summed = (returned[:, 0] + returned[:, 1]).astype(jnp.bfloat16)
        return summed.reshape(experts * capacity, model_width).astype(jnp.float32)

    slot_inputs = jnp.where(slot_used[:, None] > 0, normed_mine[slot_row], 0)
    expert_rows = send_rows(slot_inputs)
    eg_mat = expert_gate.reshape(model_width, -1)
    eu_mat = expert_up.reshape(model_width, -1)
    ed_mat = expert_down.reshape(-1, model_width)
    e_gate = matmul(expert_rows, eg_mat)
    e_up = matmul(expert_rows, eu_mat)
    e_silu, e_slope = silu_parts(e_gate)
    e_act = (e_silu * e_up).astype(jnp.bfloat16)
    e_out = matmul(e_act, ed_mat).astype(jnp.bfloat16)
    expert_sum = return_rows(e_out)
    picked = expert_sum[slot_of].reshape(rows_dev, top_k, model_width)
    routed = jnp.sum(gate_probs[:, :, None] * picked, 1)
    ffn_full = lax.dynamic_update_slice_in_dim(
        ffn_part, lax.dynamic_slice_in_dim(ffn_part, my_rows, rows_dev, 0) + routed, my_rows, 0
    )
    ffn_mine = lax.psum_scatter(
        ffn_full.reshape(sequence_count, len_dev, model_width).astype(jnp.bfloat16),
        "rows",
        scatter_dimension=2,
        tiled=True,
    ).astype(jnp.float32)
    resid_mine = lax.dynamic_slice_in_dim(
        residual_stream.reshape(sequence_count, len_dev, model_width),
        row_idx * row_width,
        row_width,
        2,
    )
    layer_out = (resid_mine + ffn_mine).astype(jnp.bfloat16)
    grad_full = lax.all_gather(cotangent, "rows", axis=2, tiled=True).reshape(tok_dev, model_width)
    d_shared_act = matmul_nt(grad_full, sd_full)
    grad_sd = matmul_tn(shared_act, grad_full)
    d_gate_pre = (d_shared_act * up_pre * silu_slope).astype(jnp.bfloat16)
    d_up_pre = (d_shared_act * silu_gate).astype(jnp.bfloat16)
    grad_sg = matmul_tn(second_normed, d_gate_pre)
    grad_su = matmul_tn(second_normed, d_up_pre)
    grad_second_normed = matmul_nt(d_gate_pre, sg_full) + matmul_nt(d_up_pre, su_full)
    grad_mine = lax.dynamic_slice_in_dim(grad_full, my_rows, rows_dev, 0).astype(jnp.float32)
    d_gates = jnp.sum(grad_mine[:, None, :] * picked, -1)
    to_experts = (
        (gate_probs[:, :, None] * grad_mine[:, None, :])
        .reshape(assign_count, model_width)
        .astype(jnp.bfloat16)
    )
    slot_grads = jnp.where(slot_used[:, None] > 0, to_experts[assign_of_slot], 0)
    d_expert_out = send_rows(slot_grads)
    grad_ed = matmul_tn(e_act, d_expert_out)
    d_e_act = matmul_nt(d_expert_out, ed_mat)
    d_e_gate = (d_e_act * e_up * e_slope).astype(jnp.bfloat16)
    d_e_up = (d_e_act * e_silu).astype(jnp.bfloat16)
    grad_eg = matmul_tn(expert_rows, d_e_gate)
    grad_eu = matmul_tn(expert_rows, d_e_up)
    d_rows = (matmul_nt(d_e_gate, eg_mat) + matmul_nt(d_e_up, eu_mat)).astype(jnp.bfloat16)
    d_assign = return_rows(d_rows)[slot_of].reshape(rows_dev, top_k, model_width)
    d_routed_in = jnp.sum(d_assign, 1)
    d_chosen = gate_probs * (d_gates - jnp.sum(gate_probs * d_gates, -1, keepdims=True))
    d_logits = jnp.sum(chosen_hot * d_chosen[:, :, None], 1)
    router_f = router_full.astype(jnp.float32)
    grad_router_part = jnp.dot(normed_mine.astype(jnp.float32).T, d_logits, precision=PRECISE)
    d_router_in = jnp.dot(d_logits, router_f.T, precision=PRECISE)
    d_mine = (
        lax.dynamic_slice_in_dim(grad_second_normed, my_rows, rows_dev, 0)
        + d_routed_in
        + d_router_in
    )
    grad_second_normed = lax.dynamic_update_slice_in_dim(grad_second_normed, d_mine, my_rows, 0)
    grad_second_normed, grad_router = (
        lax.psum(grad_second_normed.astype(jnp.bfloat16), "rows").astype(jnp.float32),
        lax.psum(grad_router_part.astype(jnp.bfloat16), "rows").astype(jnp.float32),
    )
    grad_second_unit = grad_second_normed * second_gain_float
    second_gain_gradient = jnp.sum(grad_second_normed * second_unit_rows, 0)
    d_resid = grad_full.astype(jnp.float32) + second_inverse_deviation * (
        grad_second_unit
        - second_unit_rows * jnp.mean(grad_second_unit * second_unit_rows, -1, keepdims=True)
    )
    d_attn = d_resid.astype(jnp.bfloat16)
    grad_wo = matmul_tn(attn_rows, d_attn)
    d_heads = matmul_nt(d_attn, wo_full).astype(jnp.bfloat16)
    d_heads_t = jnp.transpose(
        d_heads.reshape(sequence_count, len_dev, q_heads, HEAD_DIM), (0, 2, 1, 3)
    )
    delta_rows = jnp.sum(d_heads_t.astype(jnp.float32) * attn_f32, -1)
    kv_all = lax.all_gather(kv_local, "cols", axis=0, tiled=True)
    seq_len = kv_all.shape[0]
    key_block = min(512, seq_len)

    def key_step(block_no, carry_in):
        k_start = block_no * key_block
        key_part = lax.dynamic_slice_in_dim(kv_all, k_start, key_block, 0)

        def contribute(state_in):
            d_query_in, d_kv_in = state_in
            keys_bf = key_part[:, :, :HEAD_DIM]
            values_bf = key_part[:, :, HEAD_DIM:]
            scores = (
                jnp.einsum("shqd,bsd->shqb", query_t, keys_bf, preferred_element_type=jnp.float32)
                * score_scale
            )
            key_pos = k_start + jnp.arange(key_block, dtype=jnp.int32)
            causal = positions[:, None] >= key_pos[None, :]
            prob_vals = jnp.where(causal, jnp.exp(scores - log_total[..., None]), 0.0)
            d_prob = jnp.einsum(
                "shqd,bsd->shqb", d_heads_t, values_bf, preferred_element_type=jnp.float32
            )
            d_scores = (prob_vals * (d_prob - delta_rows[..., None])).astype(jnp.bfloat16)
            d_query_in = (
                d_query_in
                + jnp.einsum(
                    "shqb,bsd->shqd", d_scores, keys_bf, preferred_element_type=jnp.float32
                )
                * score_scale
            )
            d_key = (
                jnp.einsum("shqb,shqd->bsd", d_scores, query_t, preferred_element_type=jnp.float32)
                * score_scale
            )
            d_value = jnp.einsum(
                "shqb,shqd->bsd",
                prob_vals.astype(jnp.bfloat16),
                d_heads_t,
                preferred_element_type=jnp.float32,
            )
            d_kv_in = lax.dynamic_update_slice_in_dim(
                d_kv_in, jnp.concatenate([d_key, d_value], -1), k_start, 0
            )
            return (d_query_in, d_kv_in)

        return lax.cond(k_start <= q_last, contribute, keep_same, carry_in)

    grad_start = (
        jnp.zeros((sequence_count, q_heads, len_dev, HEAD_DIM), jnp.float32),
        jnp.zeros((seq_len, sequence_count, 2 * HEAD_DIM), jnp.float32),
    )
    d_query, d_kv_all = lax.fori_loop(0, seq_len // key_block, key_step, grad_start)
    d_kv = lax.psum_scatter(
        d_kv_all.astype(jnp.bfloat16), "cols", scatter_dimension=0, tiled=True
    ).astype(jnp.float32)
    d_query_rows = (
        apply_rotary(jnp.transpose(d_query, (0, 2, 1, 3)), cosine_table, -sine_table)
        .reshape(tok_dev, q_heads * HEAD_DIM)
        .astype(jnp.bfloat16)
    )
    d_kv_t = jnp.swapaxes(d_kv, 0, 1)
    d_key_rows = (
        apply_rotary(
            d_kv_t[:, :, :HEAD_DIM].reshape(sequence_count, len_dev, 1, HEAD_DIM),
            cosine_table,
            -sine_table,
        )
        .reshape(tok_dev, HEAD_DIM)
        .astype(jnp.bfloat16)
    )
    d_value_rows = d_kv_t[:, :, HEAD_DIM:].reshape(tok_dev, HEAD_DIM).astype(jnp.bfloat16)
    grad_wq = matmul_tn(first_normed, d_query_rows)
    grad_wk = matmul_tn(first_normed, d_key_rows)
    grad_wv = matmul_tn(first_normed, d_value_rows)
    grad_first_normed = (
        matmul_nt(d_query_rows, wq_full)
        + matmul_nt(d_key_rows, wk_full)
        + matmul_nt(d_value_rows, wv_full)
    )
    grad_first_normed = lax.psum(grad_first_normed.astype(jnp.bfloat16), "rows").astype(jnp.float32)
    grad_first_unit = grad_first_normed * first_gain_float
    first_gain_gradient = jnp.sum(grad_first_normed * first_unit_rows, 0)
    d_input = d_resid + first_inverse_deviation * (
        grad_first_unit
        - first_unit_rows * jnp.mean(grad_first_unit * first_unit_rows, -1, keepdims=True)
    )
    grad_in = lax.dynamic_slice_in_dim(
        d_input.reshape(sequence_count, len_dev, model_width), row_idx * row_width, row_width, 2
    )
    g_gain_one, g_wq, g_wk, g_wv, g_wo, g_gain_two, g_router, g_sg, g_su, g_sd = (
        lax.psum_scatter(
            first_gain_gradient.astype(jnp.bfloat16), "cols", scatter_dimension=0, tiled=True
        ).astype(jnp.float32),
        lax.psum_scatter(
            grad_wq.astype(jnp.bfloat16), "cols", scatter_dimension=0, tiled=True
        ).astype(jnp.float32),
        lax.psum_scatter(
            grad_wk.astype(jnp.bfloat16), "cols", scatter_dimension=0, tiled=True
        ).astype(jnp.float32),
        lax.psum_scatter(
            grad_wv.astype(jnp.bfloat16), "cols", scatter_dimension=0, tiled=True
        ).astype(jnp.float32),
        lax.psum_scatter(
            grad_wo.astype(jnp.bfloat16), "cols", scatter_dimension=1, tiled=True
        ).astype(jnp.float32),
        lax.psum_scatter(
            second_gain_gradient.astype(jnp.bfloat16), "cols", scatter_dimension=0, tiled=True
        ).astype(jnp.float32),
        lax.psum_scatter(
            grad_router.astype(jnp.bfloat16), "cols", scatter_dimension=0, tiled=True
        ).astype(jnp.float32),
        lax.psum_scatter(
            grad_sg.astype(jnp.bfloat16), "cols", scatter_dimension=0, tiled=True
        ).astype(jnp.float32),
        lax.psum_scatter(
            grad_su.astype(jnp.bfloat16), "cols", scatter_dimension=0, tiled=True
        ).astype(jnp.float32),
        lax.psum_scatter(
            grad_sd.astype(jnp.bfloat16), "cols", scatter_dimension=1, tiled=True
        ).astype(jnp.float32),
    )
    return (
        layer_out,
        grad_in,
        g_gain_one,
        g_wq,
        g_wk,
        g_wv,
        g_wo,
        g_gain_two,
        g_router,
        g_sg,
        g_su,
        g_sd,
        grad_eg.reshape(expert_gate.shape),
        grad_eu.reshape(expert_up.shape),
        grad_ed.reshape(expert_down.shape),
    )


def scores_of(keys, queries, scale):
    return matmul_nt(keys, queries) * scale


def causal_mask(scores):
    key_pos = lax.broadcasted_iota(jnp.int32, scores.shape, 0)
    query_pos = lax.broadcasted_iota(jnp.int32, scores.shape, 1)
    return query_pos >= key_pos


MESH_ID = pl.DeviceIdType.MESH
MIB = 1024 * 1024


class Links:
    def __init__(self, n_rows, n_cols):
        self.n_rows, self.n_cols, self.ring = n_rows, n_cols, n_cols // 2
        self.r = lax.axis_index("rows")
        self.c = lax.axis_index("cols")
        self.z = lax.div(self.c, 2)
        self.k = lax.rem(self.c, 2)
        self.x = (self.flip(1), self.c)
        self.y = (self.flip(2), self.c)
        self.up = (self.r, lax.rem(self.c + 2, n_cols))
        self.down = (self.r, lax.rem(self.c + n_cols - 2, n_cols))
        self.twin = (self.r, self.c + 1 - 2 * self.k)
        self.started = []

    def flip(self, bits):
        low, high = lax.rem(self.r, 2), lax.div(self.r, 2)
        low = 1 - low if bits & 1 else low
        high = 1 - high if bits & 2 else high
        return low + 2 * high

    def chip(self, hops):
        return lax.rem(self.z + (2 * self.ring - hops), self.ring)

    def place(self, hops):
        other = self.chip(hops)
        low = lax.rem(lax.rem(self.r, 2) + lax.rem(other, 2), 2)
        high = lax.rem(lax.div(self.r, 2) + lax.div(other, 2), 2)
        return low + 2 * high

    def spread_partners(self):
        return [
            (hops, bits, (self.flip(bits), lax.rem(self.c + 2 * hops, self.n_cols)))
            for hops in range(self.ring)
            for bits in range(self.n_rows)
            if hops or bits
        ]

    def greet(self, partners):
        barrier = pltpu.get_barrier_semaphore()
        for partner in partners:
            pl.semaphore_signal(barrier, inc=1, device_id=partner, device_id_type=MESH_ID)
        pl.semaphore_wait(barrier, len(partners))

    def send(self, src, dst, sems, number, partner):
        copy = pltpu.make_async_remote_copy(
            src_ref=src,
            dst_ref=dst,
            send_sem=sems[0].at[number],
            recv_sem=sems[1].at[number],
            device_id=partner,
            device_id_type=MESH_ID,
        )
        copy.start()
        self.started.append(copy)
        return copy

    def settle(self, copies):
        for copy in copies:
            copy.wait_send()
            self.started = [other for other in self.started if other is not copy]

    def finish(self):
        for copy in self.started:
            copy.wait_send()


def run_together(*steps):
    live = list(steps)
    while live:
        live = [step for step in live if next(step, True) is None]


def pair_sems(count):
    return [pltpu.SemaphoreType.DMA((count,)), pltpu.SemaphoreType.DMA((count,))]


class SquareGather:
    def __init__(self, net, src, out, sems, local_sem, chunks, known=None):
        self.net, self.src, self.out, self.sems, self.chunks = net, src, out, sems, chunks
        self.rows, self.width = src.shape
        if known is None:
            self.own = pltpu.make_async_copy(src, self.block(0, 0), local_sem)
        else:
            self.own = pltpu.make_async_copy(known, out.at[0], local_sem)
        self.own.start()
        self.ups, self.xs, self.ys, self.lasts = {}, {}, {}, {}

    def block(self, s, j, part=None):
        columns = pl.ds(j * self.width, self.width)
        if part is None:
            return self.out.at[s, :, columns]
        half = self.rows // 2
        return self.out.at[s, pl.ds(part * half, half), columns]

    def up(self, s):
        if s:
            self.ups[s].wait_recv()
        if s < self.chunks - 1:
            whole = self.src if s == 0 else self.block(s, 0)
            self.ups[s + 1] = self.net.send(
                whole, self.block(s + 1, 0), self.sems, 7 * s, self.net.up
            )

    def across(self, s):
        half = self.rows // 2
        part_of = lambda p: (
            self.src.at[pl.ds(p * half, half), :] if s == 0 else self.block(s, 0, p)
        )
        send = self.net.send
        self.xs[s] = {
            p: send(part_of(p), self.block(s, 1, p), self.sems, 7 * s + 1 + p, self.net.x)
            for p in (0, 1)
        }
        self.ys[s] = {
            p: send(part_of(p), self.block(s, 2, p), self.sems, 7 * s + 3 + p, self.net.y)
            for p in (1, 0)
        }

    def forward(self, s):
        block, send = self.block, self.net.send
        self.xs[s][0].wait_recv()
        one = send(block(s, 1, 0), block(s, 3, 0), self.sems, 7 * s + 5, self.net.y)
        self.ys[s][1].wait_recv()
        two = send(block(s, 2, 1), block(s, 3, 1), self.sems, 7 * s + 6, self.net.x)
        self.lasts[s] = [one, two]

    def complete(self, s):
        self.xs[s][1].wait_recv()
        self.ys[s][0].wait_recv()
        for copy in self.lasts[s]:
            copy.wait_recv()


def gather_square(net, src, out, sems, local_sem, chunks):
    gather = SquareGather(net, src, out, sems, local_sem, chunks)
    gather.across(0)
    yield
    if chunks > 1:
        gather.up(0)
        yield
    gather.forward(0)
    yield
    for s in range(1, chunks):
        gather.up(s)
        gather.across(s)
        yield
        gather.forward(s)
        yield
    gather.own.wait()
    for s in range(chunks):
        gather.complete(s)


def gather_columns(net, src, spot, sems, local_sem=None):
    if local_sem is not None:
        own = pltpu.make_async_copy(src, spot(0, net.k), local_sem)
        own.start()
    twins = []
    for hops in range(net.ring):
        if hops:
            up.wait_recv()
        here = src if hops == 0 else spot(hops, net.k)
        if hops < net.ring - 1:
            up = net.send(here, spot(hops, net.k), sems, hops, net.up)
        twins.append(net.send(here, spot(hops, net.k), sems, net.ring + hops, net.twin))
        yield
    if local_sem is not None:
        own.wait()
    for copy in twins:
        copy.wait_recv()


def add_slabs(target, terms, slab=64):
    rows = target.shape[0]

    @pl.loop(0, rows // slab)
    def _(i):
        at = pl.ds(pl.multiple_of(i * slab, slab), slab)
        total = terms[0](at)
        for term in terms[1:]:
            total = total + term(at)
        target[at, :] = total.astype(target.dtype)


def part_reader(ref, *lead, columns=None):
    def read(at):
        values = ref[(*lead, at, slice(None) if columns is None else columns)]
        return values.astype(jnp.float32)

    return read


def scatter_scratch(chunks, rows, width, resident=False):
    half = rows // 2
    kept = (1, 2, 16, 128) if resident else (chunks, 2, half, width)
    return [
        pltpu.VMEM(kept, jnp.bfloat16),
        pltpu.VMEM(kept[:1] + kept[2:] if resident else (chunks, half, 2 * width), jnp.bfloat16),
        pltpu.VMEM((chunks, 2, half, width), jnp.bfloat16),
        pltpu.VMEM((chunks, half, 2 * width), jnp.bfloat16),
        pltpu.VMEM((chunks, 2, half, width), jnp.bfloat16),
        pltpu.VMEM((chunks, 2, half, width), jnp.bfloat16),
        pltpu.SemaphoreType.DMA((chunks, 3)),
    ] + pair_sems(6 * chunks)


class SquareScatter:
    def __init__(self, net, scratch, resident=False):
        self.net, self.resident = net, resident
        self.my_up, self.my_low, self.got_x, self.got_y, self.got_last = scratch[:5]
        self.stage, self.load_sems, *self.sems = scratch[5:]
        self.half, self.width = self.got_x.shape[2:]
        self.src, self.loads, self.sent = {}, {}, {}
        self.left, self.right = pl.ds(0, self.width), pl.ds(self.width, self.width)

    def part(self, i, part, j, count=1):
        rows = pl.ds(part * self.half, self.half)
        return self.src[i].at[rows, pl.ds(j * self.width, count * self.width)]

    def mine(self, i, part, j):
        if self.resident:
            return part_reader(self.part(i, part, j))
        if part == 0:
            return part_reader(self.my_up, i, j // 2)
        return part_reader(self.my_low, i, columns=(self.left, self.right)[j])

    def give(self, i, src, j):
        self.src[i] = src
        net, sems = self.net, self.sems
        sent = self.sent.setdefault(i, {})
        if j & 1:
            sent["x", j] = net.send(
                self.part(i, 0, j), self.got_x.at[i, j // 2], sems, 6 * i + j // 2, net.x
            )
        if j & 2:
            columns = pl.ds((j - 2) * self.width, self.width)
            sent["y", j] = net.send(
                self.part(i, 1, j), self.got_y.at[i, :, columns], sems, 6 * i + j, net.y
            )

    def first(self, i, src):
        for j in (3, 1, 2):
            self.give(i, src, j)
        if not self.resident:
            load = pltpu.make_async_copy
            self.loads[i] = [
                load(self.part(i, 0, 0), self.my_up.at[i, 0], self.load_sems.at[i, 0]),
                load(self.part(i, 0, 2), self.my_up.at[i, 1], self.load_sems.at[i, 1]),
                load(self.part(i, 1, 0, 2), self.my_low.at[i], self.load_sems.at[i, 2]),
            ]
            for copy in self.loads[i]:
                copy.start()

    def second(self, i):
        net, sent, sems = self.net, self.sent[i], self.sems
        for copy in self.loads.get(i, []):
            copy.wait()
        sent["x", 3].wait_recv()
        add_slabs(self.stage.at[i, 0], [self.mine(i, 0, 2), part_reader(self.got_x, i, 1)])
        sent["up"] = net.send(self.stage.at[i, 0], self.got_last.at[i, 0], sems, 6 * i + 4, net.y)
        sent["y", 3].wait_recv()
        add_slabs(
            self.stage.at[i, 1],
            [self.mine(i, 1, 1), part_reader(self.got_y, i, columns=self.right)],
        )
        sent["low"] = net.send(self.stage.at[i, 1], self.got_last.at[i, 1], sems, 6 * i + 5, net.x)

    def third(self, i):
        for key in (("x", 1), ("y", 2), "up", "low"):
            self.sent[i][key].wait_recv()
        upper = [
            self.mine(i, 0, 0), part_reader(self.got_x, i, 0), part_reader(self.got_last, i, 0)
        ]
        lower = [
            self.mine(i, 1, 0),
            part_reader(self.got_y, i, columns=self.left),
            part_reader(self.got_last, i, 1),
        ]
        return upper, lower

    def release(self, i):
        self.net.settle([self.sent[i][key] for key in (("x", 3), ("y", 3), ("x", 1), ("y", 2))])


def scatter_square(net, src, scratch, order, finish, resident=False):
    scatter = SquareScatter(net, scratch, resident)
    for i in range(len(order) + 2):
        if i < len(order):
            scatter.first(i, src.at[order[i]])
            yield
        if 0 <= i - 1 < len(order):
            scatter.second(i - 1)
            yield
        if 0 <= i - 2:
            finish(order[i - 2], *scatter.third(i - 2))
            yield


def ring_scratch(ring, rows, width):
    return [
        pltpu.VMEM((ring - 1, rows, width), jnp.bfloat16),
        pltpu.VMEM((ring - 1, rows, width), jnp.bfloat16),
    ] + pair_sems(ring - 1)


def ring_finish(net, scratch, target, copies):
    landed, leaving, *sems = scratch
    rows = landed.shape[1]

    def finish(s, upper, lower):
        turn = (s - 1) % net.ring
        for part, terms in ((0, upper), (1, lower)):
            at = pl.ds(part * (rows // 2), rows // 2)
            if turn and not part:
                copies[turn - 1].wait_recv()
            if turn:
                terms = terms + [part_reader(landed.at[turn - 1, at, :])]
            goal = target.at[at, :] if s == 0 else leaving.at[turn, at, :]
            add_slabs(goal, terms)
        if s:
            copies.append(net.send(leaving.at[turn], landed.at[turn], sems, turn, net.up))

    return finish


def scatter_columns(net, part, out, scratch):
    got_twin, landed, leaving, twin_send, twin_recv, *sems = scratch
    twins, copies = {}, []
    order = list(range(1, net.ring)) + [0]
    for hops in order:
        twins[hops] = net.send(
            part(hops, 1 - net.k), got_twin.at[hops], (twin_send, twin_recv), hops, net.twin
        )
    yield
    for turn, hops in enumerate(order):
        twins[hops].wait_recv()
        terms = [part_reader(part(hops, net.k)), part_reader(got_twin, hops)]
        if turn:
            copies[turn - 1].wait_recv()
            terms.append(part_reader(landed, turn - 1))
        add_slabs(leaving.at[turn] if hops else out, terms, 32)
        if hops:
            copies.append(net.send(leaving.at[turn], landed.at[turn], sems, turn, net.up))
        yield


def scatter_columns_scratch(ring, rows, width):
    return [
        pltpu.VMEM((ring, rows, width), jnp.bfloat16),
        pltpu.VMEM((ring - 1, rows, width), jnp.bfloat16),
        pltpu.VMEM((ring - 1, rows, width), jnp.bfloat16),
    ] + pair_sems(ring) + pair_sems(ring - 1)


def remote_call(kernel, name, collective_id, out_shape, scratch, operands, in_vmem=(), out_vmem=(), cost=None):
    anywhere = pl.BlockSpec(memory_space=pl.ANY)
    vmem = pl.BlockSpec(memory_space=pltpu.VMEM)
    return pl.pallas_call(
        kernel,
        out_shape=out_shape,
        in_specs=[vmem if i in in_vmem else anywhere for i in range(len(operands))],
        out_specs=[vmem if i in out_vmem else anywhere for i in range(len(out_shape))],
        scratch_shapes=scratch,
        compiler_params=pltpu.CompilerParams(
            collective_id=collective_id, has_side_effects=True, vmem_limit_bytes=63 * MIB
        ),
        cost_estimate=cost,
        name=name,
    )(*operands)


def spread_columns(net, packed, spot, sems, local_sem):
    own = pltpu.make_async_copy(packed.at[net.chip(0)], spot(0, net.k), local_sem)
    own.start()
    pieces = []
    for hops in range(1, net.ring):
        target = (net.r, lax.rem(net.c + 2 * hops, net.n_cols))
        pieces.append(
            net.send(packed.at[net.chip(-hops)], spot_at(spot, net, hops), sems, hops, target)
        )
    yield
    own.wait()
    twins = [net.send(spot(0, net.k), spot(0, net.k), sems, net.ring, net.twin)]
    yield
    for hops in range(1, net.ring):
        pieces[hops - 1].wait_recv()
        here = spot(hops, net.k)
        twins.append(net.send(here, here, sems, net.ring + hops, net.twin))
        yield
    for copy in twins:
        copy.wait_recv()


def spot_at(spot, net, hops):
    return spot(0, net.k)


def first_phase(n_rows, n_cols, block, grads, weights, small, weights_out, packed, slot_map, tables):
    ring = n_cols // 2
    length, row_width = block.shape
    model = n_rows * row_width
    col_width, in_width = weights.shape
    q_width = weights_out.shape[1]
    heads = q_width // HEAD_DIM
    small_width = small.shape[1]
    experts = slot_map.shape[0]
    scale = 1.0 / math.sqrt(HEAD_DIM)
    pieces = 2
    piece = length // pieces
    bf16, f32 = jnp.bfloat16, jnp.float32
    shape = jax.ShapeDtypeStruct

    def kernel(
        x_in, g_in, w_in, small_in, wo_in, packed_in, map_in, cosine, sine,
        x_out, normed_out, w_out, small_out, q, kv_out, out, lse, wo_out, g_out, second, map_out,
        shared_out, sum_out, gains_out,
        x, normed, w, small_all, kv, wo, proj, proj_sum, result, projected, top, total, acc,
        *sems,
    ):
        scratch, sems = list(sems[:9]), list(sems[9:])
        pairs = lambda: (sems.pop(0), sems.pop(0))
        x_sems, g_sems, w_sems, small_sems, wo_sems, kv_sems = [pairs() for _ in range(6)]
        map_sems, shared_sems, sum_sems, sum_sems_two = [pairs() for _ in range(4)]
        local = sems.pop(0)
        net = Links(n_rows, n_cols)
        others = net.spread_partners()
        net.greet([device for _, _, device in others] + [net.twin])
        by_place = lambda ref: lambda hops, core: ref.at[
            pl.ds((net.place(hops) * 2 + core) * col_width, col_width), :
        ]

        x_steps = gather_square(net, x_in, x, x_sems, local.at[0], 1)
        small_steps = gather_columns(net, small_in, by_place(small_all), small_sems, local.at[1])
        w_steps = gather_columns(net, w_in, by_place(w), w_sems, local.at[2])
        wo_steps = gather_columns(net, wo_in, by_place(wo), wo_sems, local.at[3])
        g_steps = gather_square(net, g_in, g_out, g_sems, local.at[4], ring)
        saves = []

        def save(src, dst):
            copy = pltpu.make_async_copy(src, dst, local.at[8 + len(saves)])
            copy.start()
            saves.append(copy)

        next(small_steps)
        next(x_steps)
        next(w_steps)
        maps = []
        for number, (hops, bits, device) in enumerate(others):
            maps.append(net.send(map_in, map_out.at[hops, net.r], map_sems, number, device))
        own_map = pltpu.make_async_copy(map_in, map_out.at[0, net.r], local.at[5])
        own_map.start()
        next(small_steps)
        next(w_steps)
        next(x_steps)
        next(g_steps)
        next(small_steps)
        next(small_steps)
        next(w_steps)
        run_together(x_steps, small_steps)
        save(x.at[0], x_out)
        save(small_all, small_out)
        gains = small_all[...].astype(f32).T
        gains_out[...] = gains[experts : experts + 8]
        first_gain = gains[experts : experts + 1]
        second_gain = gains[experts + 1 : experts + 2]

        @pl.loop(0, length // 64)
        def _(i):
            at = pl.ds(pl.multiple_of(i * 64, 64), 64)
            values = x[0, at, :].astype(f32)
            inverse = lax.rsqrt(jnp.mean(values * values, -1, keepdims=True) + NORM_EPS)
            normed[at, :] = (values * inverse * first_gain).astype(bf16)

        save(normed, normed_out)
        next(wo_steps)
        next(w_steps)
        run_together(w_steps)
        save(w, w_out)
        next(g_steps)

        projected[...] = matmul(normed[...], w[...])
        next(wo_steps)

        def rotate(columns):
            values = projected[:, columns]
            turned = pltpu.roll(values, HEAD_DIM // 2, 1)
            return (values * cosine[...] + turned * sine[...]).astype(bf16)

        for head in range(heads + 1):
            columns = slice(head * HEAD_DIM, (head + 1) * HEAD_DIM)
            if head < heads:
                q[:, columns] = rotate(columns)
            else:
                kv[net.c, :, :HEAD_DIM] = rotate(columns)
        kv[net.c, :, HEAD_DIM:] = projected[:, q_width + HEAD_DIM :].astype(bf16)
        kv_steps = gather_columns(
            net, kv.at[net.c], lambda hops, core: kv.at[2 * net.chip(hops) + core], kv_sems
        )
        next(kv_steps)
        next(g_steps)
        next(kv_steps)
        next(wo_steps)
        next(kv_steps)
        next(g_steps)
        next(kv_steps)
        next(wo_steps)
        run_together(kv_steps)
        save(kv, kv_out)

        for head in range(heads):
            columns = slice(head * HEAD_DIM, (head + 1) * HEAD_DIM)
            queries = q[:, columns]

            def part(number):
                return scores_of(kv[number, :, :HEAD_DIM], queries, scale), kv[number, :, HEAD_DIM:]

            scores, values = part(net.c)
            scores = jnp.where(causal_mask(scores), scores, NEG_LARGE)
            high = jnp.max(scores, 0, keepdims=True)
            probs = jnp.exp(scores - high)
            top[...] = high
            total[...] = jnp.sum(probs, 0, keepdims=True)
            acc[...] = matmul_tn(values, probs.astype(bf16))

            @pl.loop(0, net.c)
            def _(number):
                scores, values = part(number)
                high = jnp.maximum(top[...], jnp.max(scores, 0, keepdims=True))
                probs = jnp.exp(scores - high)
                shrink = jnp.exp(top[...] - high)
                top[...] = high
                total[...] = total[...] * shrink + jnp.sum(probs, 0, keepdims=True)
                acc[...] = acc[...] * shrink + matmul_tn(values, probs.astype(bf16))

            out[:, columns] = (acc[...] / total[...]).T
            lse[head] = top[...] + jnp.log(total[...])
            if head in (0, 3):
                next(g_steps)

        run_together(wo_steps)
        save(wo, wo_out)
        heads_out = out[...].astype(bf16)
        for s in range(pieces):
            for j in range(n_rows):
                at = slice(j * row_width, (j + 1) * row_width)
                proj[s, :, at] = matmul_nt(
                    heads_out[s * piece : (s + 1) * piece], wo[at, :]
                ).astype(bf16)
        gathers = []

        def finish(s, upper, lower):
            add_slabs(result.at[s, pl.ds(0, piece // 2), :], upper)
            add_slabs(result.at[s, pl.ds(piece // 2, piece // 2), :], lower)
            steps = gather_square(
                net, result.at[s], proj_sum.at[pl.ds(s, 1)], (sum_sems, sum_sems_two)[s],
                local.at[6 + s], 1,
            )
            next(steps)
            gathers.append(steps)

        shared_steps = spread_columns(
            net, packed_in, by_place(shared_out), shared_sems, local.at[8 + 8]
        )
        sum_steps = scatter_square(net, proj, scratch, list(range(pieces)), finish, resident=True)
        next(sum_steps)
        next(shared_steps)
        next(sum_steps)
        run_together(sum_steps)
        next(shared_steps)

        def second_norm(s):
            @pl.loop(0, piece // 64)
            def _(i):
                at = pl.ds(pl.multiple_of(i * 64, 64), 64)
                there = pl.ds(pl.multiple_of(s * piece + i * 64, 64), 64)
                values = x[0, there, :].astype(f32) + proj_sum[s, at, :].astype(f32)
                inverse = lax.rsqrt(jnp.mean(values * values, -1, keepdims=True) + NORM_EPS)
                second[there, :] = (values * inverse * second_gain).astype(bf16)

        for s in range(pieces):
            run_together(gathers[s])
            second_norm(s)
        save(proj_sum, sum_out)
        run_together(g_steps, shared_steps)
        own_map.wait()
        for copy in maps:
            copy.wait_recv()
        for copy in saves:
            copy.wait()
        net.finish()

    partners = n_rows * ring - 1
    vmem = pltpu.VMEM
    return remote_call(
        kernel,
        "first_phase",
        1,
        [
            shape((length, model), bf16),
            shape((length, model), bf16),
            shape((model, in_width), bf16),
            shape((model, small_width), bf16),
            shape((length, q_width), bf16),
            shape((n_cols, length, 2 * HEAD_DIM), bf16),
            shape((length, q_width), f32),
            shape((heads, 1, length), f32),
            shape((model, q_width), bf16),
            shape((ring, length, model), bf16),
            shape((length, model), bf16),
            shape((ring, n_rows, *slot_map.shape), f32),
            shape((model, packed.shape[2]), bf16),
            shape((pieces, piece, model), bf16),
            shape((8, model), f32),
        ],
        [
            vmem((1, length, model), bf16),
            vmem((length, model), bf16),
            vmem((model, in_width), bf16),
            vmem((model, small_width), bf16),
            vmem((n_cols, length, 2 * HEAD_DIM), bf16),
            vmem((model, q_width), bf16),
            vmem((pieces, piece, model), bf16),
            vmem((pieces, piece, model), bf16),
            vmem((pieces, piece, row_width), bf16),
            vmem((length, in_width), f32),
            vmem((1, length), f32),
            vmem((1, length), f32),
            vmem((HEAD_DIM, length), f32),
        ]
        + scatter_scratch(pieces, piece, row_width, resident=True)
        + pair_sems(7)
        + pair_sems(7 * ring)
        + pair_sems(2 * ring)
        + pair_sems(2 * ring)
        + pair_sems(2 * ring)
        + pair_sems(2 * ring)
        + pair_sems(partners)
        + pair_sems(2 * ring)
        + pair_sems(7)
        + pair_sems(7)
        + [pltpu.SemaphoreType.DMA((18,))],
        (block, grads, weights, small, weights_out, packed, slot_map, *tables),
        in_vmem=(7, 8),
        out_vmem=(4, 6, 7, 10, 14),
    )


def experts_phase(n_rows, n_cols, second, grads, maps, experts_w, shared, router, slots):
    ring = n_cols // 2
    tokens, model = second.shape
    width = model // n_rows
    experts = n_rows * ring
    half_hidden = experts_w[0].shape[1]
    hidden = 2 * half_hidden
    pad = shared.shape[1] // 3
    blocks, _, block_rows = maps.shape[1:]
    n_slots = blocks * slots
    bf16, f32 = jnp.bfloat16, jnp.float32
    shape = jax.ShapeDtypeStruct

    def kernel(
        known, g_in, maps, gate_own, gate_twin, up_own, up_twin, down_own, down_twin, shared_in,
        router_in,
        result, rows_out, y_out, slot_out, d_part_out, act_out, d_gate_out, d_up_out, s_act_out,
        d_shared_out, probs_out, gate_out,
        w_gate, w_up, w_down, shared, router, x, g, slot_rows, part, e_act, d_gate, d_up, s_act,
        d_shared, probs, d_x, d_gates, *rest,
    ):
        scratch, (landed, leaving, ring_s, ring_r) = rest[:9], rest[9:13]
        xs, xr, ms, mr, local, w_sems, out_sems = rest[13:]
        net = Links(n_rows, n_cols)
        others = net.spread_partners()
        net.greet([device for _, _, device in others])
        mine = net.r * ring + net.z
        gather = SquareGather(
            net, known.at[:, pl.ds(0, width)], rows_out, (xs, xr), local.at[0], ring, known=known
        )
        gather.up(0)
        x_load = lambda s: pltpu.make_async_copy(
            known if s == 0 else rows_out.at[s], x, local.at[1]
        )
        g_load = lambda s: pltpu.make_async_copy(g_in.at[s], g, local.at[2])
        x_load(0).start()
        g_load(0).start()
        shared_load = pltpu.make_async_copy(shared_in, shared, local.at[3])
        shared_load.start()
        router_load = pltpu.make_async_copy(router_in, router, local.at[4])
        router_load.start()
        weights = []
        for j in range(n_rows):
            there = pl.ds(pl.multiple_of(net.flip(j) * width, width), width)
            here = pl.ds(j * width, width)
            for h, sources in enumerate(((gate_own, up_own, down_own), (gate_twin, up_twin, down_twin))):
                cols = pl.ds(h * half_hidden, half_hidden)
                number = 6 * j + 3 * h
                weights += [
                    pltpu.make_async_copy(
                        sources[0].at[there, :], w_gate.at[here, cols], w_sems.at[number]
                    ),
                    pltpu.make_async_copy(
                        sources[1].at[there, :], w_up.at[here, cols], w_sems.at[number + 1]
                    ),
                    pltpu.make_async_copy(
                        sources[2].at[:, there], w_down.at[cols, here], w_sems.at[number + 2]
                    ),
                ]
        for copy in weights:
            copy.start()

        scatter = SquareScatter(net, scratch, resident=True)
        ring_copies, stores = [], {}
        kept = {
            "slot": (slot_rows, slot_out), "part": (part, d_part_out), "act": (e_act, act_out),
            "d_gate": (d_gate, d_gate_out), "d_up": (d_up, d_up_out), "s_act": (s_act, s_act_out),
            "d_shared": (d_shared, d_shared_out), "probs": (probs, probs_out), "y": (g, y_out),
        }

        def store(s, *names):
            for name in names:
                source, target = kept[name]
                number = list(kept).index(name)
                stores[name] = pltpu.make_async_copy(source, target.at[s], out_sems.at[number])
                stores[name].start()

        def stored(*names):
            for name in names:
                if name in stores:
                    stores.pop(name).wait()

        def pass_on(s):
            turn = s - 1
            for p, terms in enumerate(scatter.third(s)):
                at = pl.ds(p * (tokens // 2), tokens // 2)
                if s == 0:
                    add_slabs(result.at[at, :], terms)
                    continue
                if turn and not p:
                    ring_copies[turn - 1].wait_recv()
                if turn > 1 and not p:
                    net.settle([ring_copies[turn - 2]])
                if turn:
                    terms = terms + [part_reader(landed.at[turn - 1, at, :])]
                add_slabs(leaving.at[turn % 2, at, :], terms)
            if s:
                ring_copies.append(
                    net.send(leaving.at[turn % 2], landed.at[turn], (ring_s, ring_r), turn, net.up)
                )

        def in_lanes(column):
            high = column.astype(bf16)
            rest = column - high.astype(f32)
            middle = rest.astype(bf16)
            low = (rest - middle.astype(f32)).astype(bf16)
            lane = lax.broadcasted_iota(jnp.int32, (column.shape[0], 128), 1)
            terms = jnp.where(lane == 0, high.astype(f32), 0.0)
            terms = jnp.where(lane == 1, middle.astype(f32), terms)
            return jnp.where(lane == 2, low.astype(f32), terms).astype(bf16)

        tile = 512

        def compute(s, ticks):
            def tick(name):
                for step in ticks.get(name, []):
                    step()

            lanes = lax.broadcasted_iota(jnp.int32, (1, 128), 1)
            mine_hot = (lanes == mine).astype(f32)
            slot_row, slot_column, chosen = [], [], []
            for b in range(blocks):
                own_map = jnp.where(
                    lax.broadcasted_iota(jnp.int32, (experts, block_rows), 0) == mine, maps[s, b], 0.0
                )
                own_map = jnp.sum(own_map, 0, keepdims=True)
                slot_row.append(jnp.where(own_map >= 0, own_map + b * slots, -1.0))
                filled = jnp.concatenate(
                    [maps[s, b], jnp.full((128 - experts, block_rows), -1.0, f32)], 0
                ).T
                chosen.append(filled)
                own_map = jnp.sum(filled * mine_hot, -1, keepdims=True)
                slot_column.append(jnp.where(own_map >= 0, own_map + b * slots, -1.0))
            slot_row, chosen = jnp.concatenate(slot_row, 1), jnp.concatenate(chosen, 0)
            slot_column = jnp.concatenate(slot_column, 0)
            numbers = lambda dims, axis: lax.broadcasted_iota(jnp.int32, dims, axis).astype(f32)
            pick = (numbers((n_slots, tokens), 0) == slot_row).astype(f32).astype(bf16)
            pick_t = (numbers((tokens, n_slots), 1) == slot_column).astype(f32).astype(bf16)

            stored("probs", "s_act", "d_shared", "y")
            if s:
                g_load(s).start()
            x_load(s).wait()
            if s == 0:
                router_load.wait()
                shared_load.wait()
            logits = matmul(x[...], router[...])
            logits = jnp.where(chosen >= 0, logits, NEG_LARGE)
            logits = jnp.exp(logits - jnp.max(logits, -1, keepdims=True))
            gate_probs = logits / jnp.sum(logits, -1, keepdims=True)
            probs[...] = gate_probs
            my_gate = jnp.sum(gate_probs * mine_hot, -1, keepdims=True)
            slot_gate = jnp.sum(matmul(pick, in_lanes(my_gate)), -1, keepdims=True)
            s_gate = matmul(x[...], shared[:, :pad])
            s_up = matmul(x[...], shared[:, pad : 2 * pad])
            g_load(s).wait()
            through = matmul(g[...], shared[:, 2 * pad :])
            s_silu, s_slope = silu_parts(s_gate)
            s_act[...] = (s_silu * s_up).astype(bf16)
            d_shared[:, :pad] = (through * s_up * s_slope).astype(bf16)
            d_shared[:, pad:] = (through * s_silu).astype(bf16)
            store(s, "probs", "s_act", "d_shared")
            tick("shared")

            stored("slot", "part", "act", "d_gate", "d_up")
            for t in range(model // tile):
                at = slice(t * tile, (t + 1) * tile)
                slot_rows[:, at] = matmul(pick, x[:, at]).astype(bf16)
                part[:, at] = matmul(pick, g[:, at]).astype(bf16)
            if s == 0:
                for copy in weights:
                    copy.wait()
            tick("picked")

            step = half_hidden // 3

            def hidden_tile(t, total):
                at = pl.ds(pl.multiple_of(t * step, step), step)
                e_gate = matmul(slot_rows[...], w_gate[:, at])
                e_up = matmul(slot_rows[...], w_up[:, at])
                through = matmul_nt(part[...], w_down[at, :])
                e_silu, e_slope = silu_parts(e_gate)
                act = e_silu * e_up
                d_act = through * slot_gate
                e_act[:, at] = act.astype(bf16)
                d_gate[:, at] = (d_act * e_up * e_slope).astype(bf16)
                d_up[:, at] = (d_act * e_silu).astype(bf16)
                return total + jnp.sum(act * through, -1, keepdims=True)

            d_slot_gate = lax.fori_loop(0, 3, hidden_tile, jnp.zeros((n_slots, 1), f32))
            tick("half")
            d_slot_gate = lax.fori_loop(3, 6, hidden_tile, d_slot_gate)
            d_gates[net.chip(s)] = jnp.sum(
                matmul_tn(in_lanes(d_slot_gate), pick), 0, keepdims=True
            )
            part[...] = (part[...].astype(f32) * slot_gate).astype(bf16)
            store(s, "slot", "part", "act", "d_gate", "d_up")
            tick("hidden")

            d_chunk = d_x.at[s % 2]
            if s >= 2:
                scatter.release(s - 2)
            def out_tile(t):
                at = pl.ds(pl.multiple_of(t * tile, tile), tile)
                d_slot = matmul_nt(d_gate[...], w_gate[at, :]) + matmul_nt(d_up[...], w_up[at, :])
                d_chunk[:, at] = (
                    matmul(pick_t, d_slot.astype(bf16))
                    + matmul_nt(d_shared[...], shared[at, : 2 * pad])
                ).astype(bf16)
                out = (matmul(e_act[...], w_down[:, at]) * slot_gate).astype(bf16)
                g[:, at] = (
                    matmul(pick_t, out) + matmul_nt(s_act[...], shared[at, 2 * pad :])
                ).astype(bf16)

            pl.loop(2, 5)(out_tile)
            scatter.give(s, d_chunk, 3)
            scatter.give(s, d_chunk, 2)
            tick("right")
            pl.loop(0, 2)(out_tile)
            scatter.give(s, d_chunk, 1)
            store(s, "y")
            tick("left")

        def arrive(s):
            def step():
                gather.up(s)
                gather.across(s)

            return step

        def take(s):
            def step():
                gather.complete(s)
                x_load(s).start()

            return step

        pass_x = lambda s: lambda: gather.forward(s)
        second_of = lambda s: lambda: scatter.second(s)
        third_of = lambda s: lambda: pass_on(s)
        compute(0, {"hidden": [arrive(1)], "left": [pass_x(1), arrive(2), take(1)]})
        compute(
            1,
            {
                "half": [pass_x(2), arrive(3)],
                "hidden": [second_of(0)],
                "left": [third_of(0), take(2)],
            },
        )
        compute(2, {"picked": [pass_x(3)], "hidden": [second_of(1)], "left": [third_of(1), take(3)]})
        compute(3, {"hidden": [second_of(2)], "left": [third_of(2)]})
        copies = []
        own = pltpu.make_async_copy(d_gates, gate_out.at[mine], local.at[5])
        own.start()
        for number, (hops, bits, device) in enumerate(others):
            copies.append(net.send(d_gates, gate_out.at[mine], (ms, mr), number, device))
        scatter.second(3)
        pass_on(3)
        ring_copies[-1].wait_recv()
        add_slabs(result, [part_reader(result), part_reader(landed.at[ring - 2])])
        stored(*kept)
        own.wait()
        gather.own.wait()
        for copy in copies:
            copy.wait_recv()
        net.finish()

    vmem = pltpu.VMEM
    by_chunk = lambda dtype, *dims: shape((ring, *dims), dtype)
    return remote_call(
        kernel,
        "experts_phase",
        5,
        [
            shape((tokens, width), bf16),
            by_chunk(bf16, tokens, model),
            by_chunk(bf16, tokens, model),
            by_chunk(bf16, n_slots, model),
            by_chunk(bf16, n_slots, model),
            by_chunk(bf16, n_slots, hidden),
            by_chunk(bf16, n_slots, hidden),
            by_chunk(bf16, n_slots, hidden),
            by_chunk(bf16, tokens, pad),
            by_chunk(bf16, tokens, 2 * pad),
            by_chunk(f32, tokens, 128),
            shape((experts, ring, 1, tokens), f32),
        ],
        [
            vmem((model, hidden), bf16),
            vmem((model, hidden), bf16),
            vmem((hidden, model), bf16),
            vmem(shared.shape, bf16),
            vmem(router.shape, bf16),
            vmem((tokens, model), bf16),
            vmem((tokens, model), bf16),
            vmem((n_slots, model), bf16),
            vmem((n_slots, model), bf16),
            vmem((n_slots, hidden), bf16),
            vmem((n_slots, hidden), bf16),
            vmem((n_slots, hidden), bf16),
            vmem((tokens, pad), bf16),
            vmem((tokens, 2 * pad), bf16),
            vmem((tokens, 128), f32),
            vmem((2, tokens, model), bf16),
            vmem((ring, 1, tokens), f32),
        ]
        + scatter_scratch(ring, tokens, width, resident=True)
        + [vmem((ring - 1, tokens, width), bf16), vmem((2, tokens, width), bf16)]
        + pair_sems(ring - 1)
        + pair_sems(7 * ring)
        + pair_sems(experts - 1)
        + [
            pltpu.SemaphoreType.DMA((6,)),
            pltpu.SemaphoreType.DMA((24,)),
            pltpu.SemaphoreType.DMA((9,)),
        ],
        (second, grads, maps, *experts_w, shared, router),
        in_vmem=(2,),
        out_vmem=(0,),
    )


def attention_back(
    n_rows, n_cols, d_block, d_gates, probs, router, token_rows, gains, weights_out, weights_in,
    queries, kv, heads_out, lse, tables, parts,
):
    ring = n_cols // 2
    length, model = token_rows[0].shape
    experts = n_rows * ring
    q_width = weights_out.shape[1]
    in_width = weights_in.shape[1]
    col_width = model // n_cols
    width = model // n_rows
    heads = q_width // HEAD_DIM
    scale = 1.0 / math.sqrt(HEAD_DIM)
    bf16, f32 = jnp.bfloat16, jnp.float32
    shape = jax.ShapeDtypeStruct

    def kernel(
        block, gates, probs, router, x_in, proj_in, g_in, gains, wo_in, w_in, q, kv, out, lse, cosine,
        sine, y_in,
        d_proj, d_first, y_out, wo_out, d_resid, gain_out,
        second, proj, g, high_ref, low_ref,
        wo, w, go, delta, dqt, dkv, dkv_own, wo_part, *rest,
    ):
        scratch, ring_parts = rest[:9], rest[9:13]
        kv_parts, wo_parts, gs, gr, local = rest[13:20], rest[20:27], rest[27], rest[28], rest[29]
        net = Links(n_rows, n_cols)
        net.greet([net.x, net.y, net.up, net.down, net.twin])
        gather = gather_square(net, block, second, (gs, gr), local.at[1], 1)
        next(gather)
        x, d_attn = d_first, proj
        loads = [
            pltpu.make_async_copy(a, b, local.at[2 + i])
            for i, (a, b) in enumerate(((x_in, x), (proj_in, proj), (g_in.at[0], g)))
        ]
        for load in loads:
            load.start()
        wo_load = pltpu.make_async_copy(wo_in, wo, local.at[5])
        wo_load.start()
        w_load = pltpu.make_async_copy(w_in, w, local.at[0])
        w_load.start()
        d_gates = jnp.concatenate(
            [gates[...].reshape(experts, length), jnp.zeros((128 - experts, length), f32)], 0
        ).T
        d_logits = probs[...] * (d_gates - jnp.sum(probs[...] * d_gates, -1, keepdims=True))
        high = d_logits.astype(bf16)
        high_ref[...] = high
        low_ref[...] = (d_logits - high.astype(f32)).astype(bf16)
        for load in loads:
            load.wait()
        copies = []
        y_steps = scatter_square(
            net, y_in, scratch, list(range(1, ring)), ring_finish(net, ring_parts, None, copies)
        )
        by_place = lambda ref: lambda hops, core: ref.at[
            pl.ds((net.place(hops) * 2 + core) * col_width, col_width), :
        ]

        run_together(gather)
        next(y_steps)
        next(y_steps)
        gain = gains[1:2]
        gain_out[...] = jnp.zeros_like(gain_out)

        @pl.loop(0, length // 128)
        def _(i):
            at = pl.ds(pl.multiple_of(i * 128, 128), 128)
            values = x[at, :].astype(f32) + proj[at, :].astype(f32)
            inverse = lax.rsqrt(jnp.mean(values * values, -1, keepdims=True) + NORM_EPS)
            unit = values * inverse
            d_second = second[0, at, :].astype(f32)
            d_second = d_second + matmul_nt(high_ref[at, :], router[...])
            d_second = d_second + matmul_nt(low_ref[at, :], router[...])
            d_unit = d_second * gain
            moment = jnp.mean(d_unit * unit, -1, keepdims=True)
            resid = g[at, :].astype(f32) + inverse * (d_unit - unit * moment)
            d_attn[at, :] = resid.astype(bf16)
            d_resid[at, :] = resid[:, :width]
            along = (d_second[:, :width] * unit[:, :width]).reshape(16, 8, width)
            gain_out[...] += jnp.sum(along, 0)

        wo_load.wait()
        go[...] = matmul(d_attn[...], wo[...]).astype(bf16)
        wo_part[...] = matmul_tn(d_attn[...], out[...].astype(bf16)).astype(bf16)
        wo_steps = scatter_columns(net, by_place(wo_part), wo_out, wo_parts)
        next(wo_steps)
        for head in range(heads):
            columns = slice(head * HEAD_DIM, (head + 1) * HEAD_DIM)
            product = (go[:, columns].astype(f32) * out[:, columns]).T
            delta[head] = jnp.sum(product, 0, keepdims=True)
        dqt[...] = jnp.zeros_like(dqt)
        dkv[...] = jnp.zeros_like(dkv)
        next(wo_steps)
        next(y_steps)
        next(y_steps)

        def one_block(number, masked):
            keys = kv[number, :, :HEAD_DIM]
            values = kv[number, :, HEAD_DIM:]
            keys_t = keys.T
            d_key = jnp.zeros((length, HEAD_DIM), f32)
            d_value = jnp.zeros((length, HEAD_DIM), f32)
            for head in range(heads):
                columns = slice(head * HEAD_DIM, (head + 1) * HEAD_DIM)
                queries = q[:, columns]
                grads = go[:, columns]
                probs = jnp.exp(scores_of(keys, queries, scale) - lse[head])
                if masked:
                    probs = jnp.where(causal_mask(probs), probs, 0.0)
                d_probs = matmul_nt(values, grads)
                d_scores = (probs * (d_probs - delta[head])).astype(bf16)
                d_value = d_value + matmul(probs.astype(bf16), grads)
                d_key = d_key + matmul(d_scores, queries)
                dqt[head] = dqt[head] + matmul(keys_t, d_scores)
            dkv[number, :, :HEAD_DIM] = (d_key * scale).astype(bf16)
            dkv[number, :, HEAD_DIM:] = d_value.astype(bf16)

        one_block(net.c, True)

        @pl.loop(0, net.c)
        def _(number):
            one_block(number, False)

        kv_steps = scatter_columns(
            net, lambda hops, core: dkv.at[2 * net.chip(hops) + core], dkv_own, kv_parts
        )
        next(kv_steps)
        next(kv_steps)
        next(wo_steps)
        next(y_steps)

        def turned_back(values):
            return (values * cosine[...] - pltpu.roll(values, HEAD_DIM // 2, 1) * sine[...]).astype(bf16)

        for head in range(heads):
            columns = slice(head * HEAD_DIM, (head + 1) * HEAD_DIM)
            d_proj[:, columns] = turned_back((dqt[head] * scale).T)
        next(kv_steps)
        next(wo_steps)
        next(y_steps)
        next(kv_steps)
        next(y_steps)
        run_together(kv_steps)
        d_proj[:, q_width : q_width + HEAD_DIM] = turned_back(dkv_own[:, :HEAD_DIM])
        d_proj[:, q_width + HEAD_DIM :] = dkv_own[:, HEAD_DIM:].astype(bf16)
        w_load.wait()
        for j in range(n_rows):
            at = slice(j * width, (j + 1) * width)
            d_first[:, at] = matmul_nt(d_proj[...], w[at, :]).astype(bf16)
        run_together(y_steps, wo_steps)
        copies[-1].wait_recv()
        y_out[...] = ring_parts[0][ring - 2]
        net.finish()

    vmem = pltpu.VMEM
    return remote_call(
        kernel,
        "attention_back",
        6,
        [
            shape((length, in_width), bf16),
            shape((length, model), bf16),
            shape((length, width), bf16),
            shape((col_width, q_width), f32),
            shape((length, width), f32),
            shape((8, width), f32),
        ],
        [
            vmem((1, length, model), bf16),
            vmem((length, model), bf16),
            vmem((length, model), bf16),
            vmem((length, 128), bf16),
            vmem((length, 128), bf16),
            vmem((model, q_width), bf16),
            vmem((model, in_width), bf16),
            vmem((length, q_width), bf16),
            vmem((heads, 1, length), f32),
            vmem((heads, HEAD_DIM, length), f32),
            vmem((n_cols, length, 2 * HEAD_DIM), bf16),
            vmem((length, 2 * HEAD_DIM), f32),
            vmem((model, q_width), bf16),
        ]
        + scatter_scratch(ring - 1, length, width)
        + ring_scratch(ring, length, width)
        + scatter_columns_scratch(ring, length, 2 * HEAD_DIM)
        + scatter_columns_scratch(ring, col_width, q_width)
        + pair_sems(7)
        + [pltpu.SemaphoreType.DMA((6,))],
        (
            d_block, d_gates, probs, router, *token_rows, gains, weights_out, weights_in, queries, kv,
            heads_out, lse, *tables, parts,
        ),
        in_vmem=(1, 2, 3, 7, 10, 11, 12, 13, 14, 15),
        out_vmem=(0, 1, 2, 3, 4, 5),
    )


def last_phase(
    n_rows, n_cols, d_first, d_proj, normed, parts, part_sum, x, proj, d_resid, gains, gain_part,
    expert_rows, router_rows,
):
    ring = n_cols // 2
    length, model = d_first.shape
    width = model // n_rows
    in_width = d_proj.shape[1]
    col_width = model // n_cols
    pieces = 2
    piece = length // pieces
    bf16, f32 = jnp.bfloat16, jnp.float32
    shape = jax.ShapeDtypeStruct
    chips = n_rows * ring
    slot_rows, d_part, e_act, d_gate, d_up = expert_rows
    n_slots, hidden = e_act.shape
    half = hidden // 2
    experts = router_rows[2].shape[0]
    rows_dev = length // n_rows

    def kernel(
        d_first, d_proj, normed, y_in, y_sum, x, proj_in, d_resid, gains, gain_two,
        xr_in, dp_in, act_in, dg_in, du_in, rows_in, probs_in, gates_in,
        layer_out, grad_in, gain_out, w_out, router_out, out_g, out_u, out_d, land_g, land_u, land_d,
        d_own, w_part, moment, moments, gain_own, gain_twin, gain_sums, proj,
        xr, dg, du, leave_a, leave_b, landed_a, landed_b, full_a, full_b,
        x_q, probs_q, gates_q, router_part, router_got, router_sum, *rest,
    ):
        scratch, y_scratch = rest[:9], rest[9:18]
        w_parts = rest[18:25]
        mo_s, mo_r, ga_s, ga_r, gt_s, gt_r, es, er, sem, ro_s, ro_r, router_sems = rest[25:]
        leaving, landed, full = (leave_a, leave_b), (landed_a, landed_b), (full_a, full_b)
        net = Links(n_rows, n_cols)
        others = net.spread_partners()
        net.greet([device for _, _, device in others] + [net.twin])

        def finish(s, upper, lower):
            at = lambda p: pl.ds(s * piece + p * (piece // 2), piece // 2)
            add_slabs(d_own.at[at(0), :], upper)
            add_slabs(d_own.at[at(1), :], lower)

        def finish_out(s, upper, lower):
            for part, terms in ((0, upper), (1, lower)):
                at = pl.ds(part * (length // 2), length // 2)
                extra = [
                    part_reader(y_sum.at[at, :]),
                    part_reader(x.at[at, pl.ds(0, width)]),
                    part_reader(proj.at[at, :]),
                ]
                add_slabs(layer_out.at[at, :], terms + extra)

        steps = scatter_square(net, d_first, scratch, list(range(pieces)), finish, resident=True)
        y_steps = scatter_square(net, y_in, y_scratch, [0], finish_out)
        next(steps)
        next(steps)
        loads = [
            pltpu.make_async_copy(a, b, sem.at[i])
            for i, (a, b) in enumerate(
                ((xr_in, xr), (dg_in, dg), (du_in, du), (act_in, dg), (dp_in, xr))
            )
        ]
        for load in loads[:3]:
            load.start()
        ours, theirs = slice(0, half), slice(half, hidden)
        given, leaves, stores = [], {}, {}

        def slot_of(kind, j):
            return kind // 2, j % 2 if kind < 2 else 0

        def tile(kind, j, part):
            columns = slice(j * width, (j + 1) * width)
            if kind < 2:
                return matmul_tn(xr[:, columns], (dg, du)[kind][:, part])
            return matmul_tn(dg[:, part], xr[:, columns])

        def land(kind, j, order=False):
            place = net.flip(j) if order else j
            at = pl.ds(pl.multiple_of(place * width, width), width)
            if kind < 2:
                ref = ((land_g, land_u), (out_g, out_u))[order][kind]
                return ref.at[at, :]
            return (land_d, out_d)[order].at[:, at]

        def give(kind, j):
            group, slot = slot_of(kind, j)
            if (group, slot) in leaves:
                leaves[group, slot].wait_send()
            buffer = leaving[group]
            buffer[slot] = tile(kind, j, theirs).astype(bf16)
            copy = net.send(buffer.at[slot], land(kind, j), (es, er), 4 * kind + j, net.twin)
            net.started.pop()
            leaves[group, slot] = copy
            given.append(copy)

        def keep(kind, j):
            group, slot = slot_of(kind, j)
            buffer, got = full[group], landed[group]
            given[4 * kind + j].wait_recv()
            load = pltpu.make_async_copy(land(kind, j), got.at[slot], sem.at[5 + slot])
            load.start()
            if (group, slot) in stores:
                stores[group, slot].wait()
            product = tile(kind, j, ours)
            load.wait()
            buffer[slot] = product + got[slot].astype(f32)
            store = pltpu.make_async_copy(
                buffer.at[slot], land(kind, j, True), sem.at[7 + 2 * group + slot]
            )
            store.start()
            stores[group, slot] = store

        proj_load = pltpu.make_async_copy(proj_in.at[:, pl.ds(0, width)], proj, sem.at[10])
        proj_load.start()
        quarter = pl.ds(pl.multiple_of(net.r * rows_dev, rows_dev), rows_dev)
        column = pl.ds(pl.multiple_of(net.place(0) * width, width), width)
        router_loads = []
        for s in range(ring):
            router_loads += [
                pltpu.make_async_copy(
                    rows_in.at[s, quarter, column], x_q.at[s], router_sems.at[s, 0]
                ),
                pltpu.make_async_copy(probs_in.at[s, quarter, :], probs_q.at[s], router_sems.at[s, 1]),
                pltpu.make_async_copy(
                    gates_in.at[:, net.chip(s), 0, quarter], gates_q.at[s], router_sems.at[s, 2]
                ),
            ]
        for load in router_loads:
            load.start()
        w_part[...] = matmul_tn(normed[...], d_proj[...]).astype(bf16)
        by_place = lambda hops, core: w_part.at[
            pl.ds((net.place(hops) * 2 + core) * col_width, col_width), :
        ]
        w_steps = scatter_columns(net, by_place, w_out, w_parts)
        next(w_steps)
        next(steps)
        next(w_steps)
        next(steps)
        next(y_steps)
        for load in loads[:3]:
            load.wait()
        for j in range(2):
            give(0, j)
        run_together(steps)

        gain = gains[0:1, :width]
        slab = 128
        gain_own[...] = jnp.zeros_like(gain_own)

        def unit_of(at):
            values = x[at, :].astype(f32)
            inverse = lax.rsqrt(jnp.mean(values * values, -1, keepdims=True) + NORM_EPS)
            return values[:, :width] * inverse, inverse

        for i in range(length // slab):
            at = slice(i * slab, (i + 1) * slab)
            unit, _ = unit_of(at)
            d_normed = d_own[at, :]
            share = jnp.sum(d_normed * gain * unit, -1, keepdims=True)
            moment[:, at] = jnp.broadcast_to(share, (slab, 128)).T[:8]
            gain_own[:8] += jnp.sum((d_normed * unit).reshape(slab // 8, 8, width), 0)
        sends = [
            net.send(moment, moments.at[bits - 1], (mo_s, mo_r), bits - 1, (net.flip(bits), net.c))
            for bits in range(1, n_rows)
        ]
        gain_own[8:] = gain_two[...]
        twin = net.send(gain_own, gain_twin, (gt_s, gt_r), 0, net.twin)
        for j in range(2, n_rows):
            give(0, j)
        next(w_steps)
        for copy in sends:
            copy.wait_recv()
        whole = moment[...] + moments[0] + moments[1] + moments[2]
        for i in range(length // slab):
            at = slice(i * slab, (i + 1) * slab)
            unit, inverse = unit_of(at)
            mean = jnp.broadcast_to(whole[:1, at], (128, slab)).T[:, :1] / model
            grad_in[at, :] = d_resid[at, :] + inverse * (d_own[at, :] * gain - unit * mean)
        twin.wait_recv()
        mine = net.r * ring + net.z
        gain_sums[mine] = gain_own[...] + gain_twin[...]
        sends = [
            net.send(gain_sums.at[mine], gain_sums.at[mine], (ga_s, ga_r), number, device)
            for number, (hops, bits, device) in enumerate(others)
        ]
        proj_load.wait()
        next(y_steps)
        for j in range(n_rows):
            give(1, j)
        next(w_steps)
        next(y_steps)
        for load in router_loads:
            load.wait()
        for s in range(ring):
            d_gates = jnp.concatenate([gates_q[s], jnp.zeros((128 - experts, rows_dev), f32)], 0).T
            d_logits = probs_q[s] * (d_gates - jnp.sum(probs_q[s] * d_gates, -1, keepdims=True))
            high = d_logits.astype(bf16)
            low = (d_logits - high.astype(f32)).astype(bf16)
            part = matmul_tn(x_q[s], high) + matmul_tn(x_q[s], low)
            for core in range(2):
                rows = part[core * col_width : (core + 1) * col_width]
                router_part[core] = rows if s == 0 else router_part[core] + rows
        router_twin = net.send(router_part.at[1 - net.k], router_got.at[0], (ro_s, ro_r), 0, net.twin)
        for kind in (0, 1):
            for j in range(n_rows):
                keep(kind, j)
            if kind == 0:
                router_twin.wait_recv()
                router_sum[0] = router_part[net.k] + router_got[0]
                router_x = net.send(router_sum.at[0], router_got.at[1], (ro_s, ro_r), 1, net.x)
            next(w_steps, None)
        router_x.wait_recv()
        router_sum[1] = router_sum[0] + router_got[1]
        router_y = net.send(router_sum.at[1], router_got.at[2], (ro_s, ro_r), 2, net.y)
        for load in loads[3:]:
            load.start()
        next(y_steps, None)
        for load in loads[3:]:
            load.wait()
        for j in range(n_rows):
            give(2, j)
        run_together(y_steps, w_steps)
        for j in range(n_rows):
            keep(2, j)
        for copy in leaves.values():
            copy.wait_send()
        for store in stores.values():
            store.wait()
        for copy in sends:
            copy.wait_recv()
        router_y.wait_recv()
        router_out[...] = router_sum[1] + router_got[2]
        total = gain_sums[net.z * ring]
        for i in range(1, ring):
            total = total + gain_sums[net.z * ring + i]
        gain_out[0:1] = jnp.sum(total[:8], 0, keepdims=True)
        gain_out[1:2] = jnp.sum(total[8:], 0, keepdims=True)
        gain_out[2:8] = jnp.zeros((6, width), f32)
        run_together(w_steps)
        net.finish()

    vmem = pltpu.VMEM
    return remote_call(
        kernel,
        "last_phase",
        7,
        [
            shape((length, width), bf16),
            shape((length, width), f32),
            shape((8, width), f32),
            shape((col_width, in_width), f32),
            shape((col_width, 128), f32),
            shape((model, half), f32),
            shape((model, half), f32),
            shape((half, model), f32),
            shape((model, half), bf16),
            shape((model, half), bf16),
            shape((half, model), bf16),
        ],
        [
            vmem((length, width), f32),
            vmem((model, in_width), bf16),
            vmem((8, length), f32),
            vmem((n_rows - 1, 8, length), f32),
            vmem((16, width), f32),
            vmem((16, width), f32),
            vmem((chips, 16, width), f32),
            vmem((length, width), bf16),
            vmem((n_slots, model), bf16),
            vmem((n_slots, hidden), bf16),
            vmem((n_slots, hidden), bf16),
            vmem((2, width, half), bf16),
            vmem((1, half, width), bf16),
            vmem((2, width, half), bf16),
            vmem((1, half, width), bf16),
            vmem((2, width, half), f32),
            vmem((1, half, width), f32),
            vmem((ring, rows_dev, width), bf16),
            vmem((ring, rows_dev, 128), f32),
            vmem((ring, experts, rows_dev), f32),
            vmem((2, col_width, 128), f32),
            vmem((3, col_width, 128), f32),
            vmem((2, col_width, 128), f32),
        ]
        + scatter_scratch(pieces, piece, width, resident=True)
        + scatter_scratch(1, length, width)
        + scatter_columns_scratch(ring, col_width, in_width)
        + pair_sems(n_rows - 1)
        + pair_sems(chips - 1)
        + pair_sems(1)
        + pair_sems(3 * n_rows)
        + [pltpu.SemaphoreType.DMA((11,))]
        + pair_sems(3)
        + [pltpu.SemaphoreType.DMA((ring, 3))],
        (
            d_first.reshape(pieces, piece, model), d_proj, normed, parts, part_sum, x, proj, d_resid,
            gains, gain_part, *expert_rows, *router_rows,
        ),
        in_vmem=(0, 1, 2, 4, 5, 7, 8, 9),
        out_vmem=(0, 1, 2, 3, 4),
    )


def add_bf16(left, right):
    return (left.astype(jnp.float32) + right.astype(jnp.float32)).astype(jnp.bfloat16)


class Exchange:
    def __init__(self):
        self.n_rows = lax.axis_size("rows")
        self.n_cols = lax.axis_size("cols")
        self.ring = self.n_cols // 2
        self.r = lax.axis_index("rows")
        self.c = lax.axis_index("cols")
        self.z = self.c // 2
        self.k = self.c % 2

    def move(self, values, target):
        pairs = []
        for r in range(self.n_rows):
            for c in range(self.n_cols):
                to_r, to_c = target(r, c)
                pairs.append((r * self.n_cols + c, to_r * self.n_cols + to_c))
        return lax.ppermute(values, ("rows", "cols"), pairs)

    def along_x(self, values):
        return self.move(values, lambda r, c: (r ^ 1, c))

    def along_y(self, values):
        return self.move(values, lambda r, c: (r ^ 2, c))

    def along_z(self, values, hops=1):
        return self.move(values, lambda r, c: (r, (c + 2 * hops) % self.n_cols))

    def across_z(self, values, bit):
        return self.move(values, lambda r, c: (r, c ^ (2 * bit)))

    def sibling(self, values):
        return self.move(values, lambda r, c: (r, c ^ 1))

    def chip(self, hops):
        return (self.z - hops + self.ring) % self.ring

    def place(self, hops):
        return self.r ^ self.chip(hops)

    def mixed(self, values, axis):
        width = values.shape[axis] // self.n_rows

        def branch(row):
            return lambda whole: jnp.concatenate(
                [
                    lax.slice_in_dim(whole, (row ^ j) * width, ((row ^ j) + 1) * width, axis=axis)
                    for j in range(self.n_rows)
                ],
                axis,
            )

        return lax.switch(self.r, [branch(row) for row in range(self.n_rows)], values)

    def rows_gather(self, block):
        half = block.shape[0] // 2
        from_x = self.along_x(block)
        from_y = self.along_y(block)
        first = self.along_y(from_x[:half])
        second = self.along_x(from_y[half:])
        return [block, from_x, from_y, jnp.concatenate([first, second], 0)]

    def rows_scatter(self, blocks):
        half = blocks[0].shape[0] // 2
        upper = [block[:half] for block in blocks]
        lower = [block[half:] for block in blocks]
        sent = self.along_x(jnp.stack([upper[1], upper[3]]))
        forward = add_bf16(upper[2], sent[1])
        upper_sum = upper[0].astype(jnp.float32) + sent[0].astype(jnp.float32)
        upper_sum = upper_sum + self.along_y(forward).astype(jnp.float32)
        sent = self.along_y(jnp.stack([lower[2], lower[3]]))
        forward = add_bf16(lower[1], sent[1])
        lower_sum = lower[0].astype(jnp.float32) + sent[0].astype(jnp.float32)
        lower_sum = lower_sum + self.along_x(forward).astype(jnp.float32)
        return jnp.concatenate([upper_sum, lower_sum], 0)

    def cols_gather(self, block, place):
        shape = (self.ring, 2) + block.shape
        whole = jnp.zeros(shape, block.dtype)
        rest = (0,) * block.ndim
        for hops in range(self.ring):
            twin = self.sibling(block)
            spot = place(hops)
            whole = lax.dynamic_update_slice(whole, block[None, None], (spot, self.k) + rest)
            whole = lax.dynamic_update_slice(whole, twin[None, None], (spot, 1 - self.k) + rest)
            if hops < self.ring - 1:
                block = self.along_z(block)
        return whole

    def pair_sum(self, parts):
        mine = lax.dynamic_index_in_dim(parts, self.k, 1, False)
        other = lax.dynamic_index_in_dim(parts, 1 - self.k, 1, False)
        return add_bf16(mine, self.sibling(other))

    def cols_scatter(self, parts, place):
        summed = self.pair_sum(parts)
        pick = lambda hops: lax.dynamic_index_in_dim(summed, place(hops), 0, False)
        run = pick(1)
        for hops in range(2, self.ring):
            run = add_bf16(self.along_z(run), pick(hops))
        return self.along_z(run).astype(jnp.float32) + pick(0).astype(jnp.float32)


def split_terms(values):
    high = lax.reduce_precision(values, 8, 7)
    return high.astype(jnp.bfloat16), (values - high).astype(jnp.bfloat16)


def gathered_layer(
    layer_in,
    norm1_gain,
    w_query,
    key_matrix,
    value_matrix,
    w_out,
    norm2_gain,
    w_router,
    shared_gate,
    shared_up,
    shared_down,
    expert_gate,
    expert_up,
    expert_down,
    routes,
    cotangent,
):
    net = Exchange()
    n_rows, ring = net.n_rows, net.ring
    r, c, z, k = net.r, net.c, net.z, net.k
    length, row_width = layer_in.shape[1:]
    rows_dev, top_k = routes.shape[2:]
    experts = w_router.shape[1]
    model_width = row_width * n_rows
    col_width = w_query.shape[0]
    q_width = w_query.shape[1]
    q_heads = q_width // HEAD_DIM
    kv_width = key_matrix.shape[1]
    shared_hidden = shared_gate.shape[1] // ring
    half_hidden = expert_gate.shape[2]
    slots = -(-2 * max(1, 5 * rows_dev * top_k // (8 * experts)) // 16) * 16
    index = lax.dynamic_index_in_dim

    expert_ids = jnp.arange(experts, dtype=jnp.int32)
    hot = jnp.sum(
        (routes.reshape(rows_dev, top_k)[:, :, None] == expert_ids).astype(jnp.float32), 1
    )
    earlier = jnp.tril(jnp.ones((rows_dev, rows_dev), jnp.float32), -1)
    rank = jnp.dot(earlier, hot, precision=PRECISE)
    slot_map = jnp.where(hot > 0, rank, -1.0).T

    small = jnp.concatenate([w_router, norm1_gain[:, None], norm2_gain[:, None]], 1)
    small = jnp.pad(small, ((0, 0), (0, 128 - small.shape[1])))
    pad_to = -(-shared_hidden // 128) * 128
    padded = lambda w: jnp.pad(
        w.reshape(col_width, ring, shared_hidden), ((0, 0), (0, 0), (0, pad_to - shared_hidden))
    )
    packed = jnp.concatenate([padded(shared_gate), padded(shared_up), padded(shared_down.T)], 2)
    packed = jnp.swapaxes(packed, 0, 1)
    experts_w = []
    for own in (expert_gate[0], expert_up[0], expert_down[0]):
        experts_w += [own, net.sibling(own)]
    positions = c * length + jnp.arange(length, dtype=jnp.int32)
    cosine_table, sine_table = rope_tables(positions, HEAD_DIM)
    tables = (
        jnp.concatenate([cosine_table, cosine_table], 1),
        jnp.concatenate([-sine_table, sine_table], 1),
    )

    (
        token_input, first_normed, weights_in, small, queries, kv_all, attn_f32, log_total,
        weights_out_t, grad_rows, second_normed, slot_maps, shared_w, attn_proj, gains,
    ) = first_phase(
        n_rows, net.n_cols, layer_in[0], cotangent[0],
        jnp.concatenate([w_query, key_matrix, value_matrix], 1), small, w_out.T, packed, slot_map,
        tables,
    )
    joined = lambda whole: whole.reshape(-1, whole.shape[-1])
    attn_proj = joined(attn_proj)
    (
        d_block, rows_all, out_rows, slot_rows, d_part, e_act, d_e_gate, d_e_up, s_act, d_shared,
        gate_probs, d_gate_all,
    ) = experts_phase(
        n_rows, net.n_cols, second_normed, grad_rows, slot_maps, experts_w, shared_w, small, slots
    )
    d_projected, d_first, part_sum, g_out, d_resid, gain_part = attention_back(
        n_rows, net.n_cols, d_block, index(d_gate_all, z, 1, False)[:, 0], gate_probs[0], small,
        (token_input, attn_proj, grad_rows), gains, weights_out_t, weights_in, queries, kv_all,
        attn_f32, log_total, tables, out_rows,
    )
    layer_out, grad_in, gain_grads, g_in, g_router, *g_experts = last_phase(
        n_rows, net.n_cols, d_first, d_projected, first_normed, out_rows, part_sum, token_input,
        attn_proj, d_resid, gains, gain_part,
        [joined(part) for part in (slot_rows, d_part, e_act, d_e_gate, d_e_up)],
        (rows_all, gate_probs, d_gate_all),
    )[:8]
    gain_grads = index(gain_grads[:2].reshape(2, 2, col_width), k, 1, False)

    column_parts = lambda whole: whole.astype(jnp.bfloat16).reshape(ring, 2, col_width, -1)
    shared_parts = jnp.concatenate(
        [
            matmul_tn(joined(rows_all), joined(d_shared)),
            matmul_tn(joined(grad_rows), joined(s_act)),
        ],
        1,
    )
    shared_parts = net.pair_sum(column_parts(shared_parts))
    g_shared = jnp.zeros(shared_parts.shape, jnp.bfloat16)
    for hops in range(ring):
        piece = index(shared_parts, net.place(-hops), 0, False)
        piece = net.along_z(piece, hops) if hops else piece
        g_shared = lax.dynamic_update_slice(g_shared, piece[None], (net.chip(hops), 0, 0))
    g_shared = g_shared.astype(jnp.float32)
    shared_cols = lambda n: jnp.swapaxes(
        g_shared[:, :, n * pad_to : n * pad_to + shared_hidden], 0, 1
    ).reshape(col_width, -1)

    return (
        layer_out[None],
        grad_in[None],
        gain_grads[0],
        g_in[:, :q_width],
        g_in[:, q_width : q_width + kv_width],
        g_in[:, q_width + kv_width :],
        g_out.T,
        gain_grads[1],
        g_router[:, :experts],
        shared_cols(0),
        shared_cols(1),
        shared_cols(2).T,
        g_experts[0][None],
        g_experts[1][None],
        g_experts[2][None],
    )


def per_device(layer_in, *others):
    routes = others[13]
    w_router = others[6]
    n_rows, n_cols = lax.axis_size("rows"), lax.axis_size("cols")
    experts, top_k = w_router.shape[1], routes.shape[3]
    gathers = (
        experts <= 4 * top_k
        and layer_in.shape[0] == 1
        and n_rows == 4
        and n_cols == 2 * n_rows
        and 2 * experts == n_rows * n_cols
    )
    return (gathered_layer if gathers else routed_layer)(layer_in, *others)


def solution(mesh):
    placed = (
        P(None, "cols", "rows"),
        P("cols"),
        P("cols", "rows"),
        P("cols", "rows"),
        P("cols", "rows"),
        P("rows", "cols"),
        P("cols"),
        P("cols", None),
        P("cols", "rows"),
        P("cols", "rows"),
        P("rows", "cols"),
        P(("rows", "cols"), None, None),
        P(("rows", "cols"), None, None),
        P(("rows", "cols"), None, None),
        P("cols", "rows", None, None),
        P(None, "cols", "rows"),
    )
    return jax.shard_map(
        per_device,
        mesh=mesh,
        in_specs=placed,
        out_specs=(
            P(None, "cols", "rows"),
            P(None, "cols", "rows"),
            P("cols"),
            P("cols", "rows"),
            P("cols", "rows"),
            P("cols", "rows"),
            P("rows", "cols"),
            P("cols"),
            P("cols", None),
            P("cols", "rows"),
            P("cols", "rows"),
            P("rows", "cols"),
            P(("rows", "cols"), None, None),
            P(("rows", "cols"), None, None),
            P(("rows", "cols"), None, None),
        ),
        check_vma=False,
    )
```

```python
import math

import jax
import jax.numpy as jnp
from jax import lax
from jax.experimental import pallas as pl
from jax.experimental.pallas import tpu as pltpu
from jax.sharding import PartitionSpec as P

HEAD_DIM = 128


NORM_EPS = 1e-05
ROPE_BASE = 500000.0
NEG_LARGE = -1e30
PRECISE = lax.Precision.HIGHEST


def rope_tables(positions, head_size):
    half_size = head_size // 2
    inv_freq = ROPE_BASE ** (-(2.0 * jnp.arange(half_size, dtype=jnp.float32)) / head_size)
    angles = positions.astype(jnp.float32)[:, None] * inv_freq[None, :]
    return (jnp.cos(angles), jnp.sin(angles))


def apply_rotary(values, cosine_table, sine_table):
    half_size = values.shape[-1] // 2
    first_half = values[..., :half_size]
    second = values[..., half_size:]
    cos_b = cosine_table[:, None, :]
    sin_b = sine_table[:, None, :]
    return jnp.concatenate(
        [first_half * cos_b - second * sin_b, second * cos_b + first_half * sin_b], -1
    )


def matmul(left_op, right_op):
    return jnp.dot(left_op, right_op, preferred_element_type=jnp.float32)


def matmul_tn(left_op, right_op):
    return lax.dot_general(
        left_op, right_op, (((0,), (0,)), ((), ())), preferred_element_type=jnp.float32
    )


def matmul_nt(left_op, right_op):
    return lax.dot_general(
        left_op, right_op, (((1,), (1,)), ((), ())), preferred_element_type=jnp.float32
    )


def silu_parts(pre_act):
    sigma = jax.nn.sigmoid(pre_act)
    return (pre_act * sigma, sigma * (1.0 + pre_act * (1.0 - sigma)))


def keep_same(carry_in):
    return carry_in


def routed_layer(
    layer_in,
    norm1_gain,
    w_query,
    key_matrix,
    value_matrix,
    w_out,
    norm2_gain,
    w_router,
    shared_gate,
    shared_up,
    shared_down,
    expert_gate,
    expert_up,
    expert_down,
    routes,
    cotangent,
):
    n_rows = lax.axis_size("rows")
    n_cols = lax.axis_size("cols")
    row_idx = lax.axis_index("rows")
    col_idx = lax.axis_index("cols")
    sequence_count, len_dev, row_width = layer_in.shape
    tok_dev = sequence_count * len_dev
    rows_dev = routes.shape[2]
    top_k = routes.shape[3]
    experts = w_router.shape[1]
    devices = n_rows * n_cols
    capacity = 2 * max(1, 5 * rows_dev * top_k // (8 * experts))
    full_in = lax.all_gather(layer_in, "rows", axis=2, tiled=True)
    (
        gain_one,
        wq_full,
        wk_full,
        wv_full,
        wo_full,
        gain_two,
        router_full,
        sg_full,
        su_full,
        sd_full,
    ) = (
        lax.all_gather(norm1_gain, "cols", axis=0, tiled=True),
        lax.all_gather(w_query, "cols", axis=0, tiled=True),
        lax.all_gather(key_matrix, "cols", axis=0, tiled=True),
        lax.all_gather(value_matrix, "cols", axis=0, tiled=True),
        lax.all_gather(w_out, "cols", axis=1, tiled=True),
        lax.all_gather(norm2_gain, "cols", axis=0, tiled=True),
        lax.all_gather(w_router, "cols", axis=0, tiled=True),
        lax.all_gather(shared_gate, "cols", axis=0, tiled=True),
        lax.all_gather(shared_up, "cols", axis=0, tiled=True),
        lax.all_gather(shared_down, "cols", axis=1, tiled=True),
    )
    model_width = full_in.shape[2]
    token_input = full_in.reshape(tok_dev, model_width).astype(jnp.float32)
    first_inverse_deviation = lax.rsqrt(
        jnp.mean(token_input * token_input, -1, keepdims=True) + NORM_EPS
    )
    first_unit_rows = token_input * first_inverse_deviation
    first_gain_float = gain_one.astype(jnp.float32)
    first_normed = (first_unit_rows * first_gain_float).astype(jnp.bfloat16)
    q_pre = matmul(first_normed, wq_full)
    key_unrotated = matmul(first_normed, wk_full)
    value_projected = matmul(first_normed, wv_full).astype(jnp.bfloat16)
    q_heads = q_pre.shape[1] // HEAD_DIM
    positions = col_idx * len_dev + jnp.arange(len_dev, dtype=jnp.int32)
    cosine_table, sine_table = rope_tables(positions, HEAD_DIM)
    rotated_queries = apply_rotary(
        q_pre.reshape(sequence_count, len_dev, q_heads, HEAD_DIM), cosine_table, sine_table
    ).astype(jnp.bfloat16)
    rotated_keys = apply_rotary(
        key_unrotated.reshape(sequence_count, len_dev, 1, HEAD_DIM), cosine_table, sine_table
    ).astype(jnp.bfloat16)
    kv_local = jnp.concatenate(
        [
            rotated_keys.reshape(sequence_count, len_dev, HEAD_DIM),
            value_projected.reshape(sequence_count, len_dev, HEAD_DIM),
        ],
        -1,
    )
    kv_local = jnp.swapaxes(kv_local, 0, 1)
    query_t = jnp.transpose(rotated_queries, (0, 2, 1, 3))
    score_scale = 1.0 / math.sqrt(HEAD_DIM)
    q_last = col_idx * len_dev + len_dev - 1

    def online_update(carry_in, key_part, k_start):
        run_max, run_sum, run_acc = carry_in
        block_len = key_part.shape[0]
        scores = (
            jnp.einsum(
                "shqd,bsd->shqb",
                query_t,
                key_part[:, :, :HEAD_DIM],
                preferred_element_type=jnp.float32,
            )
            * score_scale
        )
        key_pos = k_start + jnp.arange(block_len, dtype=jnp.int32)
        causal = positions[:, None] >= key_pos[None, :]
        scores = jnp.where(causal, scores, NEG_LARGE)
        new_max = jnp.maximum(run_max, jnp.max(scores, -1))
        prob_vals = jnp.where(causal, jnp.exp(scores - new_max[..., None]), 0.0)
        rescale = jnp.exp(run_max - new_max)
        run_sum = run_sum * rescale + jnp.sum(prob_vals, -1)
        run_acc = run_acc * rescale[..., None] + jnp.einsum(
            "shqb,bsd->shqd",
            prob_vals.astype(jnp.bfloat16),
            key_part[:, :, HEAD_DIM:],
            preferred_element_type=jnp.float32,
        )
        return (new_max, run_sum, run_acc)

    fold_start = (
        jnp.full((sequence_count, q_heads, len_dev), NEG_LARGE, jnp.float32),
        jnp.zeros((sequence_count, q_heads, len_dev), jnp.float32),
        jnp.zeros((sequence_count, q_heads, len_dev, HEAD_DIM), jnp.float32),
    )
    carry_in = fold_start
    piece = lax.all_gather(kv_local, "cols", axis=0, tiled=True)
    start = jnp.int32(0)
    piece_len = piece.shape[0]
    step_len = min(512, piece_len)
    for offset in range(0, piece_len, step_len):
        key_part = piece[offset : offset + step_len]
        k_start = start + offset

        def updated(state_in, key_part=key_part, k_start=k_start):
            return online_update(state_in, key_part, k_start)

        carry_in = lax.cond(k_start <= q_last, updated, keep_same, carry_in)
    run_max, run_sum, run_acc = carry_in
    attn_f32 = run_acc / run_sum[..., None]
    log_total = run_max + jnp.log(run_sum)
    attn_bf = attn_f32.astype(jnp.bfloat16)
    attn_rows = jnp.transpose(attn_bf, (0, 2, 1, 3)).reshape(tok_dev, q_heads * HEAD_DIM)
    attn_proj = lax.psum(matmul(attn_rows, wo_full).astype(jnp.bfloat16), "rows").astype(
        jnp.float32
    )
    residual_stream = token_input + attn_proj
    second_inverse_deviation = lax.rsqrt(
        jnp.mean(residual_stream * residual_stream, -1, keepdims=True) + NORM_EPS
    )
    second_unit_rows = residual_stream * second_inverse_deviation
    second_gain_float = gain_two.astype(jnp.float32)
    second_normed = (second_unit_rows * second_gain_float).astype(jnp.bfloat16)
    gate_pre = matmul(second_normed, sg_full)
    up_pre = matmul(second_normed, su_full)
    silu_gate, silu_slope = silu_parts(gate_pre)
    shared_act = (silu_gate * up_pre).astype(jnp.bfloat16)
    ffn_part = matmul(shared_act, sd_full)
    my_rows = row_idx * rows_dev
    normed_mine = lax.dynamic_slice_in_dim(second_normed, my_rows, rows_dev, 0)
    route_mine = routes.reshape(rows_dev, top_k)
    logits = matmul(normed_mine, router_full)
    expert_ids = jnp.arange(experts, dtype=jnp.int32)
    chosen_hot = (route_mine[:, :, None] == expert_ids[None, None, :]).astype(jnp.float32)
    chosen = jnp.sum(chosen_hot * logits[:, None, :], -1)
    gate_probs = jax.nn.softmax(chosen, -1)
    assign_count = rows_dev * top_k
    flat_routes = route_mine.reshape(assign_count)
    assign_hot = (flat_routes[:, None] == expert_ids[None, :]).astype(jnp.int32)
    rank_in = jnp.sum((jnp.cumsum(assign_hot, 0) - assign_hot) * assign_hot, 1)
    slot_of = flat_routes * capacity + rank_in
    assign_of_slot = (
        jnp.zeros((experts * capacity,), jnp.int32)
        .at[slot_of]
        .set(jnp.arange(assign_count, dtype=jnp.int32))
    )
    slot_used = jnp.zeros((experts * capacity,), jnp.int32).at[slot_of].set(1)
    slot_row = assign_of_slot // top_k

    def send_rows(slot_vals):
        slot_vals = slot_vals.reshape(experts, capacity, model_width)
        outgoing = jnp.broadcast_to(
            slot_vals[:, None], (experts, 2, capacity, model_width)
        ).reshape(devices, capacity, model_width)
        received = lax.all_to_all(
            outgoing, ("rows", "cols"), split_axis=0, concat_axis=0, tiled=True
        )
        return received.reshape(devices * capacity, model_width)

    def return_rows(slot_vals):
        returned = lax.all_to_all(
            slot_vals.reshape(devices, capacity, model_width),
            ("rows", "cols"),
            split_axis=0,
            concat_axis=0,
            tiled=True,
        )
        returned = returned.reshape(experts, 2, capacity, model_width).astype(jnp.float32)
        summed = (returned[:, 0] + returned[:, 1]).astype(jnp.bfloat16)
        return summed.reshape(experts * capacity, model_width).astype(jnp.float32)

    slot_inputs = jnp.where(slot_used[:, None] > 0, normed_mine[slot_row], 0)
    expert_rows = send_rows(slot_inputs)
    eg_mat = expert_gate.reshape(model_width, -1)
    eu_mat = expert_up.reshape(model_width, -1)
    ed_mat = expert_down.reshape(-1, model_width)
    e_gate = matmul(expert_rows, eg_mat)
    e_up = matmul(expert_rows, eu_mat)
    e_silu, e_slope = silu_parts(e_gate)
    e_act = (e_silu * e_up).astype(jnp.bfloat16)
    e_out = matmul(e_act, ed_mat).astype(jnp.bfloat16)
    expert_sum = return_rows(e_out)
    picked = expert_sum[slot_of].reshape(rows_dev, top_k, model_width)
    routed = jnp.sum(gate_probs[:, :, None] * picked, 1)
    ffn_full = lax.dynamic_update_slice_in_dim(
        ffn_part, lax.dynamic_slice_in_dim(ffn_part, my_rows, rows_dev, 0) + routed, my_rows, 0
    )
    ffn_mine = lax.psum_scatter(
        ffn_full.reshape(sequence_count, len_dev, model_width).astype(jnp.bfloat16),
        "rows",
        scatter_dimension=2,
        tiled=True,
    ).astype(jnp.float32)
    resid_mine = lax.dynamic_slice_in_dim(
        residual_stream.reshape(sequence_count, len_dev, model_width),
        row_idx * row_width,
        row_width,
        2,
    )
    layer_out = (resid_mine + ffn_mine).astype(jnp.bfloat16)
    grad_full = lax.all_gather(cotangent, "rows", axis=2, tiled=True).reshape(tok_dev, model_width)
    d_shared_act = matmul_nt(grad_full, sd_full)
    grad_sd = matmul_tn(shared_act, grad_full)
    d_gate_pre = (d_shared_act * up_pre * silu_slope).astype(jnp.bfloat16)
    d_up_pre = (d_shared_act * silu_gate).astype(jnp.bfloat16)
    grad_sg = matmul_tn(second_normed, d_gate_pre)
    grad_su = matmul_tn(second_normed, d_up_pre)
    grad_second_normed = matmul_nt(d_gate_pre, sg_full) + matmul_nt(d_up_pre, su_full)
    grad_mine = lax.dynamic_slice_in_dim(grad_full, my_rows, rows_dev, 0).astype(jnp.float32)
    d_gates = jnp.sum(grad_mine[:, None, :] * picked, -1)
    to_experts = (
        (gate_probs[:, :, None] * grad_mine[:, None, :])
        .reshape(assign_count, model_width)
        .astype(jnp.bfloat16)
    )
    slot_grads = jnp.where(slot_used[:, None] > 0, to_experts[assign_of_slot], 0)
    d_expert_out = send_rows(slot_grads)
    grad_ed = matmul_tn(e_act, d_expert_out)
    d_e_act = matmul_nt(d_expert_out, ed_mat)
    d_e_gate = (d_e_act * e_up * e_slope).astype(jnp.bfloat16)
    d_e_up = (d_e_act * e_silu).astype(jnp.bfloat16)
    grad_eg = matmul_tn(expert_rows, d_e_gate)
    grad_eu = matmul_tn(expert_rows, d_e_up)
    d_rows = (matmul_nt(d_e_gate, eg_mat) + matmul_nt(d_e_up, eu_mat)).astype(jnp.bfloat16)
    d_assign = return_rows(d_rows)[slot_of].reshape(rows_dev, top_k, model_width)
    d_routed_in = jnp.sum(d_assign, 1)
    d_chosen = gate_probs * (d_gates - jnp.sum(gate_probs * d_gates, -1, keepdims=True))
    d_logits = jnp.sum(chosen_hot * d_chosen[:, :, None], 1)
    router_f = router_full.astype(jnp.float32)
    grad_router_part = jnp.dot(normed_mine.astype(jnp.float32).T, d_logits, precision=PRECISE)
    d_router_in = jnp.dot(d_logits, router_f.T, precision=PRECISE)
    d_mine = (
        lax.dynamic_slice_in_dim(grad_second_normed, my_rows, rows_dev, 0)
        + d_routed_in
        + d_router_in
    )
    grad_second_normed = lax.dynamic_update_slice_in_dim(grad_second_normed, d_mine, my_rows, 0)
    grad_second_normed, grad_router = (
        lax.psum(grad_second_normed.astype(jnp.bfloat16), "rows").astype(jnp.float32),
        lax.psum(grad_router_part.astype(jnp.bfloat16), "rows").astype(jnp.float32),
    )
    grad_second_unit = grad_second_normed * second_gain_float
    second_gain_gradient = jnp.sum(grad_second_normed * second_unit_rows, 0)
    d_resid = grad_full.astype(jnp.float32) + second_inverse_deviation * (
        grad_second_unit
        - second_unit_rows * jnp.mean(grad_second_unit * second_unit_rows, -1, keepdims=True)
    )
    d_attn = d_resid.astype(jnp.bfloat16)
    grad_wo = matmul_tn(attn_rows, d_attn)
    d_heads = matmul_nt(d_attn, wo_full).astype(jnp.bfloat16)
    d_heads_t = jnp.transpose(
        d_heads.reshape(sequence_count, len_dev, q_heads, HEAD_DIM), (0, 2, 1, 3)
    )
    delta_rows = jnp.sum(d_heads_t.astype(jnp.float32) * attn_f32, -1)
    kv_all = lax.all_gather(kv_local, "cols", axis=0, tiled=True)
    seq_len = kv_all.shape[0]
    key_block = min(512, seq_len)

    def key_step(block_no, carry_in):
        k_start = block_no * key_block
        key_part = lax.dynamic_slice_in_dim(kv_all, k_start, key_block, 0)

        def contribute(state_in):
            d_query_in, d_kv_in = state_in
            keys_bf = key_part[:, :, :HEAD_DIM]
            values_bf = key_part[:, :, HEAD_DIM:]
            scores = (
                jnp.einsum("shqd,bsd->shqb", query_t, keys_bf, preferred_element_type=jnp.float32)
                * score_scale
            )
            key_pos = k_start + jnp.arange(key_block, dtype=jnp.int32)
            causal = positions[:, None] >= key_pos[None, :]
            prob_vals = jnp.where(causal, jnp.exp(scores - log_total[..., None]), 0.0)
            d_prob = jnp.einsum(
                "shqd,bsd->shqb", d_heads_t, values_bf, preferred_element_type=jnp.float32
            )
            d_scores = (prob_vals * (d_prob - delta_rows[..., None])).astype(jnp.bfloat16)
            d_query_in = (
                d_query_in
                + jnp.einsum(
                    "shqb,bsd->shqd", d_scores, keys_bf, preferred_element_type=jnp.float32
                )
                * score_scale
            )
            d_key = (
                jnp.einsum("shqb,shqd->bsd", d_scores, query_t, preferred_element_type=jnp.float32)
                * score_scale
            )
            d_value = jnp.einsum(
                "shqb,shqd->bsd",
                prob_vals.astype(jnp.bfloat16),
                d_heads_t,
                preferred_element_type=jnp.float32,
            )
            d_kv_in = lax.dynamic_update_slice_in_dim(
                d_kv_in, jnp.concatenate([d_key, d_value], -1), k_start, 0
            )
            return (d_query_in, d_kv_in)

        return lax.cond(k_start <= q_last, contribute, keep_same, carry_in)

    grad_start = (
        jnp.zeros((sequence_count, q_heads, len_dev, HEAD_DIM), jnp.float32),
        jnp.zeros((seq_len, sequence_count, 2 * HEAD_DIM), jnp.float32),
    )
    d_query, d_kv_all = lax.fori_loop(0, seq_len // key_block, key_step, grad_start)
    d_kv = lax.psum_scatter(
        d_kv_all.astype(jnp.bfloat16), "cols", scatter_dimension=0, tiled=True
    ).astype(jnp.float32)
    d_query_rows = (
        apply_rotary(jnp.transpose(d_query, (0, 2, 1, 3)), cosine_table, -sine_table)
        .reshape(tok_dev, q_heads * HEAD_DIM)
        .astype(jnp.bfloat16)
    )
    d_kv_t = jnp.swapaxes(d_kv, 0, 1)
    d_key_rows = (
        apply_rotary(
            d_kv_t[:, :, :HEAD_DIM].reshape(sequence_count, len_dev, 1, HEAD_DIM),
            cosine_table,
            -sine_table,
        )
        .reshape(tok_dev, HEAD_DIM)
        .astype(jnp.bfloat16)
    )
    d_value_rows = d_kv_t[:, :, HEAD_DIM:].reshape(tok_dev, HEAD_DIM).astype(jnp.bfloat16)
    grad_wq = matmul_tn(first_normed, d_query_rows)
    grad_wk = matmul_tn(first_normed, d_key_rows)
    grad_wv = matmul_tn(first_normed, d_value_rows)
    grad_first_normed = (
        matmul_nt(d_query_rows, wq_full)
        + matmul_nt(d_key_rows, wk_full)
        + matmul_nt(d_value_rows, wv_full)
    )
    grad_first_normed = lax.psum(grad_first_normed.astype(jnp.bfloat16), "rows").astype(jnp.float32)
    grad_first_unit = grad_first_normed * first_gain_float
    first_gain_gradient = jnp.sum(grad_first_normed * first_unit_rows, 0)
    d_input = d_resid + first_inverse_deviation * (
        grad_first_unit
        - first_unit_rows * jnp.mean(grad_first_unit * first_unit_rows, -1, keepdims=True)
    )
    grad_in = lax.dynamic_slice_in_dim(
        d_input.reshape(sequence_count, len_dev, model_width), row_idx * row_width, row_width, 2
    )
    g_gain_one, g_wq, g_wk, g_wv, g_wo, g_gain_two, g_router, g_sg, g_su, g_sd = (
        lax.psum_scatter(
            first_gain_gradient.astype(jnp.bfloat16), "cols", scatter_dimension=0, tiled=True
        ).astype(jnp.float32),
        lax.psum_scatter(
            grad_wq.astype(jnp.bfloat16), "cols", scatter_dimension=0, tiled=True
        ).astype(jnp.float32),
        lax.psum_scatter(
            grad_wk.astype(jnp.bfloat16), "cols", scatter_dimension=0, tiled=True
        ).astype(jnp.float32),
        lax.psum_scatter(
            grad_wv.astype(jnp.bfloat16), "cols", scatter_dimension=0, tiled=True
        ).astype(jnp.float32),
        lax.psum_scatter(
            grad_wo.astype(jnp.bfloat16), "cols", scatter_dimension=1, tiled=True
        ).astype(jnp.float32),
        lax.psum_scatter(
            second_gain_gradient.astype(jnp.bfloat16), "cols", scatter_dimension=0, tiled=True
        ).astype(jnp.float32),
        lax.psum_scatter(
            grad_router.astype(jnp.bfloat16), "cols", scatter_dimension=0, tiled=True
        ).astype(jnp.float32),
        lax.psum_scatter(
            grad_sg.astype(jnp.bfloat16), "cols", scatter_dimension=0, tiled=True
        ).astype(jnp.float32),
        lax.psum_scatter(
            grad_su.astype(jnp.bfloat16), "cols", scatter_dimension=0, tiled=True
        ).astype(jnp.float32),
        lax.psum_scatter(
            grad_sd.astype(jnp.bfloat16), "cols", scatter_dimension=1, tiled=True
        ).astype(jnp.float32),
    )
    return (
        layer_out,
        grad_in,
        g_gain_one,
        g_wq,
        g_wk,
        g_wv,
        g_wo,
        g_gain_two,
        g_router,
        g_sg,
        g_su,
        g_sd,
        grad_eg.reshape(expert_gate.shape),
        grad_eu.reshape(expert_up.shape),
        grad_ed.reshape(expert_down.shape),
    )


def scores_of(keys, queries, scale):
    return matmul_nt(keys, queries) * scale


def causal_mask(scores):
    key_pos = lax.broadcasted_iota(jnp.int32, scores.shape, 0)
    query_pos = lax.broadcasted_iota(jnp.int32, scores.shape, 1)
    return query_pos >= key_pos


MESH_ID = pl.DeviceIdType.MESH
MIB = 1024 * 1024


class Links:
    def __init__(self, n_rows, n_cols):
        self.n_rows, self.n_cols, self.ring = n_rows, n_cols, n_cols // 2
        self.r = lax.axis_index("rows")
        self.c = lax.axis_index("cols")
        self.z = lax.div(self.c, 2)
        self.k = lax.rem(self.c, 2)
        self.x = (self.flip(1), self.c)
        self.y = (self.flip(2), self.c)
        self.up = (self.r, lax.rem(self.c + 2, n_cols))
        self.down = (self.r, lax.rem(self.c + n_cols - 2, n_cols))
        self.twin = (self.r, self.c + 1 - 2 * self.k)
        self.started = []

    def flip(self, bits):
        low, high = lax.rem(self.r, 2), lax.div(self.r, 2)
        low = 1 - low if bits & 1 else low
        high = 1 - high if bits & 2 else high
        return low + 2 * high

    def chip(self, hops):
        return lax.rem(self.z + (2 * self.ring - hops), self.ring)

    def place(self, hops):
        other = self.chip(hops)
        low = lax.rem(lax.rem(self.r, 2) + lax.rem(other, 2), 2)
        high = lax.rem(lax.div(self.r, 2) + lax.div(other, 2), 2)
        return low + 2 * high

    def spread_partners(self):
        return [
            (hops, bits, (self.flip(bits), lax.rem(self.c + 2 * hops, self.n_cols)))
            for hops in range(self.ring)
            for bits in range(self.n_rows)
            if hops or bits
        ]

    def greet(self, partners):
        barrier = pltpu.get_barrier_semaphore()
        for partner in partners:
            pl.semaphore_signal(barrier, inc=1, device_id=partner, device_id_type=MESH_ID)
        pl.semaphore_wait(barrier, len(partners))

    def send(self, src, dst, sems, number, partner):
        copy = pltpu.make_async_remote_copy(
            src_ref=src,
            dst_ref=dst,
            send_sem=sems[0].at[number],
            recv_sem=sems[1].at[number],
            device_id=partner,
            device_id_type=MESH_ID,
        )
        copy.start()
        self.started.append(copy)
        return copy

    def settle(self, copies):
        for copy in copies:
            copy.wait_send()
            self.started = [other for other in self.started if other is not copy]

    def finish(self):
        for copy in self.started:
            copy.wait_send()


def run_together(*steps):
    live = list(steps)
    while live:
        live = [step for step in live if next(step, True) is None]


def pair_sems(count):
    return [pltpu.SemaphoreType.DMA((count,)), pltpu.SemaphoreType.DMA((count,))]


class SquareGather:
    def __init__(self, net, src, out, sems, local_sem, chunks, known=None):
        self.net, self.src, self.out, self.sems, self.chunks = net, src, out, sems, chunks
        self.rows, self.width = src.shape
        if known is None:
            self.own = pltpu.make_async_copy(src, self.block(0, 0), local_sem)
        else:
            self.own = pltpu.make_async_copy(known, out.at[0], local_sem)
        self.own.start()
        self.ups, self.xs, self.ys, self.lasts = {}, {}, {}, {}

    def block(self, s, j, part=None):
        columns = pl.ds(j * self.width, self.width)
        if part is None:
            return self.out.at[s, :, columns]
        half = self.rows // 2
        return self.out.at[s, pl.ds(part * half, half), columns]

    def up(self, s):
        if s:
            self.ups[s].wait_recv()
        if s < self.chunks - 1:
            whole = self.src if s == 0 else self.block(s, 0)
            self.ups[s + 1] = self.net.send(
                whole, self.block(s + 1, 0), self.sems, 7 * s, self.net.up
            )

    def across(self, s):
        half = self.rows // 2
        part_of = lambda p: (
            self.src.at[pl.ds(p * half, half), :] if s == 0 else self.block(s, 0, p)
        )
        send = self.net.send
        self.xs[s] = {
            p: send(part_of(p), self.block(s, 1, p), self.sems, 7 * s + 1 + p, self.net.x)
            for p in (0, 1)
        }
        self.ys[s] = {
            p: send(part_of(p), self.block(s, 2, p), self.sems, 7 * s + 3 + p, self.net.y)
            for p in (1, 0)
        }

    def forward(self, s):
        block, send = self.block, self.net.send
        self.xs[s][0].wait_recv()
        one = send(block(s, 1, 0), block(s, 3, 0), self.sems, 7 * s + 5, self.net.y)
        self.ys[s][1].wait_recv()
        two = send(block(s, 2, 1), block(s, 3, 1), self.sems, 7 * s + 6, self.net.x)
        self.lasts[s] = [one, two]

    def complete(self, s):
        self.xs[s][1].wait_recv()
        self.ys[s][0].wait_recv()
        for copy in self.lasts[s]:
            copy.wait_recv()


def gather_square(net, src, out, sems, local_sem, chunks):
    gather = SquareGather(net, src, out, sems, local_sem, chunks)
    gather.across(0)
    yield
    if chunks > 1:
        gather.up(0)
        yield
    gather.forward(0)
    yield
    for s in range(1, chunks):
        gather.up(s)
        gather.across(s)
        yield
        gather.forward(s)
        yield
    gather.own.wait()
    for s in range(chunks):
        gather.complete(s)


def gather_columns(net, src, spot, sems, local_sem=None):
    if local_sem is not None:
        own = pltpu.make_async_copy(src, spot(0, net.k), local_sem)
        own.start()
    twins = []
    for hops in range(net.ring):
        if hops:
            up.wait_recv()
        here = src if hops == 0 else spot(hops, net.k)
        if hops < net.ring - 1:
            up = net.send(here, spot(hops, net.k), sems, hops, net.up)
        twins.append(net.send(here, spot(hops, net.k), sems, net.ring + hops, net.twin))
        yield
    if local_sem is not None:
        own.wait()
    for copy in twins:
        copy.wait_recv()


def add_slabs(target, terms, slab=64):
    rows = target.shape[0]

    @pl.loop(0, rows // slab)
    def _(i):
        at = pl.ds(pl.multiple_of(i * slab, slab), slab)
        total = terms[0](at)
        for term in terms[1:]:
            total = total + term(at)
        target[at, :] = total.astype(target.dtype)


def part_reader(ref, *lead, columns=None):
    def read(at):
        values = ref[(*lead, at, slice(None) if columns is None else columns)]
        return values.astype(jnp.float32)

    return read


def scatter_scratch(chunks, rows, width, resident=False):
    half = rows // 2
    kept = (1, 2, 16, 128) if resident else (chunks, 2, half, width)
    return [
        pltpu.VMEM(kept, jnp.bfloat16),
        pltpu.VMEM(kept[:1] + kept[2:] if resident else (chunks, half, 2 * width), jnp.bfloat16),
        pltpu.VMEM((chunks, 2, half, width), jnp.bfloat16),
        pltpu.VMEM((chunks, half, 2 * width), jnp.bfloat16),
        pltpu.VMEM((chunks, 2, half, width), jnp.bfloat16),
        pltpu.VMEM((chunks, 2, half, width), jnp.bfloat16),
        pltpu.SemaphoreType.DMA((chunks, 3)),
    ] + pair_sems(6 * chunks)


class SquareScatter:
    def __init__(self, net, scratch, resident=False):
        self.net, self.resident = net, resident
        self.my_up, self.my_low, self.got_x, self.got_y, self.got_last = scratch[:5]
        self.stage, self.load_sems, *self.sems = scratch[5:]
        self.half, self.width = self.got_x.shape[2:]
        self.src, self.loads, self.sent = {}, {}, {}
        self.left, self.right = pl.ds(0, self.width), pl.ds(self.width, self.width)

    def part(self, i, part, j, count=1):
        rows = pl.ds(part * self.half, self.half)
        return self.src[i].at[rows, pl.ds(j * self.width, count * self.width)]

    def mine(self, i, part, j):
        if self.resident:
            return part_reader(self.part(i, part, j))
        if part == 0:
            return part_reader(self.my_up, i, j // 2)
        return part_reader(self.my_low, i, columns=(self.left, self.right)[j])

    def give(self, i, src, j):
        self.src[i] = src
        net, sems = self.net, self.sems
        sent = self.sent.setdefault(i, {})
        if j & 1:
            sent["x", j] = net.send(
                self.part(i, 0, j), self.got_x.at[i, j // 2], sems, 6 * i + j // 2, net.x
            )
        if j & 2:
            columns = pl.ds((j - 2) * self.width, self.width)
            sent["y", j] = net.send(
                self.part(i, 1, j), self.got_y.at[i, :, columns], sems, 6 * i + j, net.y
            )

    def first(self, i, src):
        for j in (3, 1, 2):
            self.give(i, src, j)
        if not self.resident:
            load = pltpu.make_async_copy
            self.loads[i] = [
                load(self.part(i, 0, 0), self.my_up.at[i, 0], self.load_sems.at[i, 0]),
                load(self.part(i, 0, 2), self.my_up.at[i, 1], self.load_sems.at[i, 1]),
                load(self.part(i, 1, 0, 2), self.my_low.at[i], self.load_sems.at[i, 2]),
            ]
            for copy in self.loads[i]:
                copy.start()

    def second(self, i):
        net, sent, sems = self.net, self.sent[i], self.sems
        for copy in self.loads.get(i, []):
            copy.wait()
        sent["x", 3].wait_recv()
        add_slabs(self.stage.at[i, 0], [self.mine(i, 0, 2), part_reader(self.got_x, i, 1)])
        sent["up"] = net.send(self.stage.at[i, 0], self.got_last.at[i, 0], sems, 6 * i + 4, net.y)
        sent["y", 3].wait_recv()
        add_slabs(
            self.stage.at[i, 1],
            [self.mine(i, 1, 1), part_reader(self.got_y, i, columns=self.right)],
        )
        sent["low"] = net.send(self.stage.at[i, 1], self.got_last.at[i, 1], sems, 6 * i + 5, net.x)

    def third(self, i):
        for key in (("x", 1), ("y", 2), "up", "low"):
            self.sent[i][key].wait_recv()
        upper = [
            self.mine(i, 0, 0), part_reader(self.got_x, i, 0), part_reader(self.got_last, i, 0)
        ]
        lower = [
            self.mine(i, 1, 0),
            part_reader(self.got_y, i, columns=self.left),
            part_reader(self.got_last, i, 1),
        ]
        return upper, lower

    def release(self, i):
        self.net.settle([self.sent[i][key] for key in (("x", 3), ("y", 3), ("x", 1), ("y", 2))])


def scatter_square(net, src, scratch, order, finish, resident=False):
    scatter = SquareScatter(net, scratch, resident)
    for i in range(len(order) + 2):
        if i < len(order):
            scatter.first(i, src.at[order[i]])
            yield
        if 0 <= i - 1 < len(order):
            scatter.second(i - 1)
            yield
        if 0 <= i - 2:
            finish(order[i - 2], *scatter.third(i - 2))
            yield


def ring_scratch(ring, rows, width):
    return [
        pltpu.VMEM((ring - 1, rows, width), jnp.bfloat16),
        pltpu.VMEM((ring - 1, rows, width), jnp.bfloat16),
    ] + pair_sems(ring - 1)


def ring_finish(net, scratch, target, copies):
    landed, leaving, *sems = scratch
    rows = landed.shape[1]

    def finish(s, upper, lower):
        turn = (s - 1) % net.ring
        for part, terms in ((0, upper), (1, lower)):
            at = pl.ds(part * (rows // 2), rows // 2)
            if turn and not part:
                copies[turn - 1].wait_recv()
            if turn:
                terms = terms + [part_reader(landed.at[turn - 1, at, :])]
            goal = target.at[at, :] if s == 0 else leaving.at[turn, at, :]
            add_slabs(goal, terms)
        if s:
            copies.append(net.send(leaving.at[turn], landed.at[turn], sems, turn, net.up))

    return finish


def scatter_columns(net, part, out, scratch):
    got_twin, landed, leaving, twin_send, twin_recv, *sems = scratch
    twins, copies = {}, []
    order = list(range(1, net.ring)) + [0]
    for hops in order:
        twins[hops] = net.send(
            part(hops, 1 - net.k), got_twin.at[hops], (twin_send, twin_recv), hops, net.twin
        )
    yield
    for turn, hops in enumerate(order):
        twins[hops].wait_recv()
        terms = [part_reader(part(hops, net.k)), part_reader(got_twin, hops)]
        if turn:
            copies[turn - 1].wait_recv()
            terms.append(part_reader(landed, turn - 1))
        add_slabs(leaving.at[turn] if hops else out, terms, 32)
        if hops:
            copies.append(net.send(leaving.at[turn], landed.at[turn], sems, turn, net.up))
        yield


def scatter_columns_scratch(ring, rows, width):
    return [
        pltpu.VMEM((ring, rows, width), jnp.bfloat16),
        pltpu.VMEM((ring - 1, rows, width), jnp.bfloat16),
        pltpu.VMEM((ring - 1, rows, width), jnp.bfloat16),
    ] + pair_sems(ring) + pair_sems(ring - 1)


def remote_call(kernel, name, collective_id, out_shape, scratch, operands, in_vmem=(), out_vmem=(), cost=None):
    anywhere = pl.BlockSpec(memory_space=pl.ANY)
    vmem = pl.BlockSpec(memory_space=pltpu.VMEM)
    return pl.pallas_call(
        kernel,
        out_shape=out_shape,
        in_specs=[vmem if i in in_vmem else anywhere for i in range(len(operands))],
        out_specs=[vmem if i in out_vmem else anywhere for i in range(len(out_shape))],
        scratch_shapes=scratch,
        compiler_params=pltpu.CompilerParams(
            collective_id=collective_id, has_side_effects=True, vmem_limit_bytes=63 * MIB
        ),
        cost_estimate=cost,
        name=name,
    )(*operands)


def spread_columns(net, packed, spot, sems, local_sem):
    own = pltpu.make_async_copy(packed.at[net.chip(0)], spot(0, net.k), local_sem)
    own.start()
    pieces = []
    for hops in range(1, net.ring):
        target = (net.r, lax.rem(net.c + 2 * hops, net.n_cols))
        pieces.append(
            net.send(packed.at[net.chip(-hops)], spot_at(spot, net, hops), sems, hops, target)
        )
    yield
    own.wait()
    twins = [net.send(spot(0, net.k), spot(0, net.k), sems, net.ring, net.twin)]
    yield
    for hops in range(1, net.ring):
        pieces[hops - 1].wait_recv()
        here = spot(hops, net.k)
        twins.append(net.send(here, here, sems, net.ring + hops, net.twin))
        yield
    for copy in twins:
        copy.wait_recv()


def spot_at(spot, net, hops):
    return spot(0, net.k)


def first_phase(n_rows, n_cols, block, grads, weights, small, weights_out, packed, slot_map, tables):
    ring = n_cols // 2
    length, row_width = block.shape
    model = n_rows * row_width
    col_width, in_width = weights.shape
    q_width = weights_out.shape[1]
    heads = q_width // HEAD_DIM
    small_width = small.shape[1]
    experts = slot_map.shape[0]
    scale = 1.0 / math.sqrt(HEAD_DIM)
    pieces = 2
    piece = length // pieces
    bf16, f32 = jnp.bfloat16, jnp.float32
    shape = jax.ShapeDtypeStruct

    def kernel(
        x_in, g_in, w_in, small_in, wo_in, packed_in, map_in, cosine, sine,
        x_out, normed_out, w_out, small_out, q, kv_out, out, lse, wo_out, g_out, second, map_out,
        shared_out, sum_out, gains_out, scale_out,
        x, normed, w, small_all, kv, wo, proj, proj_sum, result, projected, top, total, acc,
        *sems,
    ):
        scratch, sems = list(sems[:9]), list(sems[9:])
        pairs = lambda: (sems.pop(0), sems.pop(0))
        x_sems, g_sems, w_sems, small_sems, wo_sems, kv_sems = [pairs() for _ in range(6)]
        map_sems, shared_sems, sum_sems, sum_sems_two = [pairs() for _ in range(4)]
        local = sems.pop(0)
        net = Links(n_rows, n_cols)
        others = net.spread_partners()
        net.greet([device for _, _, device in others] + [net.twin])
        by_place = lambda ref: lambda hops, core: ref.at[
            pl.ds((net.place(hops) * 2 + core) * col_width, col_width), :
        ]

        x_steps = gather_square(net, x_in, x, x_sems, local.at[0], 1)
        small_steps = gather_columns(net, small_in, by_place(small_all), small_sems, local.at[1])
        w_steps = gather_columns(net, w_in, by_place(w), w_sems, local.at[2])
        wo_steps = gather_columns(net, wo_in, by_place(wo), wo_sems, local.at[3])
        g_steps = gather_square(net, g_in, g_out, g_sems, local.at[4], ring)
        saves = []

        def save(src, dst):
            copy = pltpu.make_async_copy(src, dst, local.at[8 + len(saves)])
            copy.start()
            saves.append(copy)

        next(small_steps)
        next(x_steps)
        next(w_steps)
        maps = []
        for number, (hops, bits, device) in enumerate(others):
            maps.append(net.send(map_in, map_out.at[hops, net.r], map_sems, number, device))
        own_map = pltpu.make_async_copy(map_in, map_out.at[0, net.r], local.at[5])
        own_map.start()
        next(small_steps)
        next(w_steps)
        next(x_steps)
        next(g_steps)
        next(small_steps)
        next(small_steps)
        next(w_steps)
        run_together(x_steps, small_steps)
        save(x.at[0], x_out)
        save(small_all, small_out)
        gains = small_all[...].astype(f32).T
        gains_out[...] = gains[experts : experts + 8]
        first_gain = gains[experts : experts + 1]
        second_gain = gains[experts + 1 : experts + 2]

        @pl.loop(0, length // 64)
        def _(i):
            at = pl.ds(pl.multiple_of(i * 64, 64), 64)
            values = x[0, at, :].astype(f32)
            inverse = lax.rsqrt(jnp.mean(values * values, -1, keepdims=True) + NORM_EPS)
            normed[at, :] = (values * inverse * first_gain).astype(bf16)
            scale_out[at, :] = jnp.broadcast_to(inverse, (64, 128))

        save(normed, normed_out)
        next(wo_steps)
        next(w_steps)
        run_together(w_steps)
        save(w, w_out)
        next(g_steps)

        projected[...] = matmul(normed[...], w[...])
        next(wo_steps)

        def rotate(columns):
            values = projected[:, columns]
            turned = pltpu.roll(values, HEAD_DIM // 2, 1)
            return (values * cosine[...] + turned * sine[...]).astype(bf16)

        for head in range(heads + 1):
            columns = slice(head * HEAD_DIM, (head + 1) * HEAD_DIM)
            if head < heads:
                q[:, columns] = rotate(columns)
            else:
                kv[net.c, :, :HEAD_DIM] = rotate(columns)
        kv[net.c, :, HEAD_DIM:] = projected[:, q_width + HEAD_DIM :].astype(bf16)
        kv_steps = gather_columns(
            net, kv.at[net.c], lambda hops, core: kv.at[2 * net.chip(hops) + core], kv_sems
        )
        next(kv_steps)
        next(g_steps)
        next(kv_steps)
        next(wo_steps)
        next(kv_steps)
        next(g_steps)
        next(kv_steps)
        next(wo_steps)
        run_together(kv_steps)
        save(kv, kv_out)

        for head in range(heads):
            columns = slice(head * HEAD_DIM, (head + 1) * HEAD_DIM)
            queries = q[:, columns]

            def part(number):
                return scores_of(kv[number, :, :HEAD_DIM], queries, scale), kv[number, :, HEAD_DIM:]

            scores, values = part(net.c)
            scores = jnp.where(causal_mask(scores), scores, NEG_LARGE)
            high = jnp.max(scores, 0, keepdims=True)
            probs = jnp.exp(scores - high)
            top[...] = high
            total[...] = jnp.sum(probs, 0, keepdims=True)
            acc[...] = matmul_tn(values, probs.astype(bf16))

            @pl.loop(0, net.c)
            def _(number):
                scores, values = part(number)
                high = jnp.maximum(top[...], jnp.max(scores, 0, keepdims=True))
                probs = jnp.exp(scores - high)
                shrink = jnp.exp(top[...] - high)
                top[...] = high
                total[...] = total[...] * shrink + jnp.sum(probs, 0, keepdims=True)
                acc[...] = acc[...] * shrink + matmul_tn(values, probs.astype(bf16))

            out[:, columns] = (acc[...] / total[...]).T
            lse[head] = top[...] + jnp.log(total[...])
            if head in (0, 3):
                next(g_steps)

        run_together(wo_steps)
        save(wo, wo_out)
        heads_out = out[...].astype(bf16)
        for s in range(pieces):
            for j in range(n_rows):
                at = slice(j * row_width, (j + 1) * row_width)
                proj[s, :, at] = matmul_nt(
                    heads_out[s * piece : (s + 1) * piece], wo[at, :]
                ).astype(bf16)
        gathers = []

        def finish(s, upper, lower):
            add_slabs(result.at[s, pl.ds(0, piece // 2), :], upper)
            add_slabs(result.at[s, pl.ds(piece // 2, piece // 2), :], lower)
            steps = gather_square(
                net, result.at[s], proj_sum.at[pl.ds(s, 1)], (sum_sems, sum_sems_two)[s],
                local.at[6 + s], 1,
            )
            next(steps)
            gathers.append(steps)

        shared_steps = spread_columns(
            net, packed_in, by_place(shared_out), shared_sems, local.at[8 + 8]
        )
        sum_steps = scatter_square(net, proj, scratch, list(range(pieces)), finish, resident=True)
        next(sum_steps)
        next(shared_steps)
        next(sum_steps)
        run_together(sum_steps)
        next(shared_steps)

        def second_norm(s):
            @pl.loop(0, piece // 64)
            def _(i):
                at = pl.ds(pl.multiple_of(i * 64, 64), 64)
                there = pl.ds(pl.multiple_of(s * piece + i * 64, 64), 64)
                values = x[0, there, :].astype(f32) + proj_sum[s, at, :].astype(f32)
                inverse = lax.rsqrt(jnp.mean(values * values, -1, keepdims=True) + NORM_EPS)
                second[there, :] = (values * inverse * second_gain).astype(bf16)

        for s in range(pieces):
            run_together(gathers[s])
            second_norm(s)
        save(proj_sum, sum_out)
        run_together(g_steps, shared_steps)
        own_map.wait()
        for copy in maps:
            copy.wait_recv()
        for copy in saves:
            copy.wait()
        net.finish()

    partners = n_rows * ring - 1
    vmem = pltpu.VMEM
    return remote_call(
        kernel,
        "first_phase",
        1,
        [
            shape((length, model), bf16),
            shape((length, model), bf16),
            shape((model, in_width), bf16),
            shape((model, small_width), bf16),
            shape((length, q_width), bf16),
            shape((n_cols, length, 2 * HEAD_DIM), bf16),
            shape((length, q_width), f32),
            shape((heads, 1, length), f32),
            shape((model, q_width), bf16),
            shape((ring, length, model), bf16),
            shape((length, model), bf16),
            shape((ring, n_rows, *slot_map.shape), f32),
            shape((model, packed.shape[2]), bf16),
            shape((pieces, piece, model), bf16),
            shape((8, model), f32),
            shape((length, 128), f32),
        ],
        [
            vmem((1, length, model), bf16),
            vmem((length, model), bf16),
            vmem((model, in_width), bf16),
            vmem((model, small_width), bf16),
            vmem((n_cols, length, 2 * HEAD_DIM), bf16),
            vmem((model, q_width), bf16),
            vmem((pieces, piece, model), bf16),
            vmem((pieces, piece, model), bf16),
            vmem((pieces, piece, row_width), bf16),
            vmem((length, in_width), f32),
            vmem((1, length), f32),
            vmem((1, length), f32),
            vmem((HEAD_DIM, length), f32),
        ]
        + scatter_scratch(pieces, piece, row_width, resident=True)
        + pair_sems(7)
        + pair_sems(7 * ring)
        + pair_sems(2 * ring)
        + pair_sems(2 * ring)
        + pair_sems(2 * ring)
        + pair_sems(2 * ring)
        + pair_sems(partners)
        + pair_sems(2 * ring)
        + pair_sems(7)
        + pair_sems(7)
        + [pltpu.SemaphoreType.DMA((18,))],
        (block, grads, weights, small, weights_out, packed, slot_map, *tables),
        in_vmem=(7, 8),
        out_vmem=(4, 6, 7, 10, 14, 15),
    )


def experts_phase(n_rows, n_cols, second, grads, maps, experts_w, shared, router, slots):
    ring = n_cols // 2
    tokens, model = second.shape
    width = model // n_rows
    experts = n_rows * ring
    half_hidden = experts_w[0].shape[1]
    hidden = 2 * half_hidden
    pad = shared.shape[1] // 3
    blocks, _, block_rows = maps.shape[1:]
    n_slots = blocks * slots
    bf16, f32 = jnp.bfloat16, jnp.float32
    shape = jax.ShapeDtypeStruct

    def kernel(
        known, g_in, maps, gate_own, gate_twin, up_own, up_twin, down_own, down_twin, shared_in,
        router_in,
        result, rows_out, y_out, slot_out, d_part_out, act_out, d_gate_out, d_up_out, s_act_out,
        d_shared_out, probs_out, gate_out,
        w_gate, w_up, w_down, shared, router, x, g, slot_rows, part, e_act, d_gate, d_up, s_act,
        d_shared, probs, d_x, d_gates, *rest,
    ):
        scratch, (landed, leaving, ring_s, ring_r) = rest[:9], rest[9:13]
        xs, xr, ms, mr, local, w_sems, out_sems = rest[13:]
        net = Links(n_rows, n_cols)
        others = net.spread_partners()
        net.greet([device for _, _, device in others])
        mine = net.r * ring + net.z
        gather = SquareGather(
            net, known.at[:, pl.ds(0, width)], rows_out, (xs, xr), local.at[0], ring, known=known
        )
        gather.up(0)
        x_load = lambda s: pltpu.make_async_copy(
            known if s == 0 else rows_out.at[s], x, local.at[1]
        )
        g_load = lambda s: pltpu.make_async_copy(g_in.at[s], g, local.at[2])
        x_load(0).start()
        g_load(0).start()
        shared_load = pltpu.make_async_copy(shared_in, shared, local.at[3])
        shared_load.start()
        router_load = pltpu.make_async_copy(router_in, router, local.at[4])
        router_load.start()
        weights = []
        for j in range(n_rows):
            there = pl.ds(pl.multiple_of(net.flip(j) * width, width), width)
            here = pl.ds(j * width, width)
            for h, sources in enumerate(((gate_own, up_own, down_own), (gate_twin, up_twin, down_twin))):
                cols = pl.ds(h * half_hidden, half_hidden)
                number = 6 * j + 3 * h
                weights += [
                    pltpu.make_async_copy(
                        sources[0].at[there, :], w_gate.at[here, cols], w_sems.at[number]
                    ),
                    pltpu.make_async_copy(
                        sources[1].at[there, :], w_up.at[here, cols], w_sems.at[number + 1]
                    ),
                    pltpu.make_async_copy(
                        sources[2].at[:, there], w_down.at[cols, here], w_sems.at[number + 2]
                    ),
                ]
        for copy in weights:
            copy.start()

        scatter = SquareScatter(net, scratch, resident=True)
        ring_copies, stores = [], {}
        kept = {
            "slot": (slot_rows, slot_out), "part": (part, d_part_out), "act": (e_act, act_out),
            "d_gate": (d_gate, d_gate_out), "d_up": (d_up, d_up_out), "s_act": (s_act, s_act_out),
            "d_shared": (d_shared, d_shared_out), "probs": (probs, probs_out), "y": (g, y_out),
        }

        def store(s, *names):
            for name in names:
                source, target = kept[name]
                number = list(kept).index(name)
                stores[name] = pltpu.make_async_copy(source, target.at[s], out_sems.at[number])
                stores[name].start()

        def stored(*names):
            for name in names:
                if name in stores:
                    stores.pop(name).wait()

        def pass_on(s):
            turn = s - 1
            for p, terms in enumerate(scatter.third(s)):
                at = pl.ds(p * (tokens // 2), tokens // 2)
                if s == 0:
                    add_slabs(result.at[at, :], terms)
                    continue
                if turn and not p:
                    ring_copies[turn - 1].wait_recv()
                if turn > 1 and not p:
                    net.settle([ring_copies[turn - 2]])
                if turn:
                    terms = terms + [part_reader(landed.at[turn - 1, at, :])]
                add_slabs(leaving.at[turn % 2, at, :], terms)
            if s:
                ring_copies.append(
                    net.send(leaving.at[turn % 2], landed.at[turn], (ring_s, ring_r), turn, net.up)
                )

        def in_lanes(column):
            high = column.astype(bf16)
            rest = column - high.astype(f32)
            middle = rest.astype(bf16)
            low = (rest - middle.astype(f32)).astype(bf16)
            lane = lax.broadcasted_iota(jnp.int32, (column.shape[0], 128), 1)
            terms = jnp.where(lane == 0, high.astype(f32), 0.0)
            terms = jnp.where(lane == 1, middle.astype(f32), terms)
            return jnp.where(lane == 2, low.astype(f32), terms).astype(bf16)

        tile = 512

        def compute(s, ticks):
            def tick(name):
                for step in ticks.get(name, []):
                    step()

            lanes = lax.broadcasted_iota(jnp.int32, (1, 128), 1)
            mine_hot = (lanes == mine).astype(f32)
            slot_row, slot_column, chosen = [], [], []
            for b in range(blocks):
                own_map = jnp.where(
                    lax.broadcasted_iota(jnp.int32, (experts, block_rows), 0) == mine, maps[s, b], 0.0
                )
                own_map = jnp.sum(own_map, 0, keepdims=True)
                slot_row.append(jnp.where(own_map >= 0, own_map + b * slots, -1.0))
                filled = jnp.concatenate(
                    [maps[s, b], jnp.full((128 - experts, block_rows), -1.0, f32)], 0
                ).T
                chosen.append(filled)
                own_map = jnp.sum(filled * mine_hot, -1, keepdims=True)
                slot_column.append(jnp.where(own_map >= 0, own_map + b * slots, -1.0))
            slot_row, chosen = jnp.concatenate(slot_row, 1), jnp.concatenate(chosen, 0)
            slot_column = jnp.concatenate(slot_column, 0)
            numbers = lambda dims, axis: lax.broadcasted_iota(jnp.int32, dims, axis).astype(f32)
            pick = (numbers((n_slots, tokens), 0) == slot_row).astype(f32).astype(bf16)
            pick_t = (numbers((tokens, n_slots), 1) == slot_column).astype(f32).astype(bf16)

            stored("probs", "s_act", "d_shared", "y")
            if s:
                g_load(s).start()
            x_load(s).wait()
            if s == 0:
                router_load.wait()
                shared_load.wait()
            logits = matmul(x[...], router[...])
            logits = jnp.where(chosen >= 0, logits, NEG_LARGE)
            logits = jnp.exp(logits - jnp.max(logits, -1, keepdims=True))
            gate_probs = logits / jnp.sum(logits, -1, keepdims=True)
            probs[...] = gate_probs
            my_gate = jnp.sum(gate_probs * mine_hot, -1, keepdims=True)
            slot_gate = jnp.sum(matmul(pick, in_lanes(my_gate)), -1, keepdims=True)
            s_gate = matmul(x[...], shared[:, :pad])
            s_up = matmul(x[...], shared[:, pad : 2 * pad])
            g_load(s).wait()
            through = matmul(g[...], shared[:, 2 * pad :])
            s_silu, s_slope = silu_parts(s_gate)
            s_act[...] = (s_silu * s_up).astype(bf16)
            d_shared[:, :pad] = (through * s_up * s_slope).astype(bf16)
            d_shared[:, pad:] = (through * s_silu).astype(bf16)
            store(s, "probs", "s_act", "d_shared")
            tick("shared")

            stored("slot", "part", "act", "d_gate", "d_up")
            for t in range(model // tile):
                at = slice(t * tile, (t + 1) * tile)
                slot_rows[:, at] = matmul(pick, x[:, at]).astype(bf16)
                part[:, at] = matmul(pick, g[:, at]).astype(bf16)
            if s == 0:
                for copy in weights:
                    copy.wait()
            tick("picked")

            step = half_hidden // 3

            def hidden_tile(t, total):
                at = pl.ds(pl.multiple_of(t * step, step), step)
                e_gate = matmul(slot_rows[...], w_gate[:, at])
                e_up = matmul(slot_rows[...], w_up[:, at])
                through = matmul_nt(part[...], w_down[at, :])
                e_silu, e_slope = silu_parts(e_gate)
                act = e_silu * e_up
                d_act = through * slot_gate
                e_act[:, at] = act.astype(bf16)
                d_gate[:, at] = (d_act * e_up * e_slope).astype(bf16)
                d_up[:, at] = (d_act * e_silu).astype(bf16)
                return total + jnp.sum(act * through, -1, keepdims=True)

            d_slot_gate = lax.fori_loop(0, 3, hidden_tile, jnp.zeros((n_slots, 1), f32))
            tick("half")
            d_slot_gate = lax.fori_loop(3, 6, hidden_tile, d_slot_gate)
            d_gates[net.chip(s)] = jnp.sum(
                matmul_tn(in_lanes(d_slot_gate), pick), 0, keepdims=True
            )
            part[...] = (part[...].astype(f32) * slot_gate).astype(bf16)
            store(s, "slot", "part", "act", "d_gate", "d_up")
            tick("hidden")

            d_chunk = d_x.at[s % 2]
            if s >= 2:
                scatter.release(s - 2)
            def out_tile(t):
                at = pl.ds(pl.multiple_of(t * tile, tile), tile)
                d_slot = matmul_nt(d_gate[...], w_gate[at, :]) + matmul_nt(d_up[...], w_up[at, :])
                d_chunk[:, at] = (
                    matmul(pick_t, d_slot.astype(bf16))
                    + matmul_nt(d_shared[...], shared[at, : 2 * pad])
                ).astype(bf16)
                out = (matmul(e_act[...], w_down[:, at]) * slot_gate).astype(bf16)
                g[:, at] = (
                    matmul(pick_t, out) + matmul_nt(s_act[...], shared[at, 2 * pad :])
                ).astype(bf16)

            pl.loop(2, 5)(out_tile)
            scatter.give(s, d_chunk, 3)
            scatter.give(s, d_chunk, 2)
            tick("right")
            pl.loop(0, 2)(out_tile)
            scatter.give(s, d_chunk, 1)
            store(s, "y")
            tick("left")

        def arrive(s):
            def step():
                gather.up(s)
                gather.across(s)

            return step

        def take(s):
            def step():
                gather.complete(s)
                x_load(s).start()

            return step

        pass_x = lambda s: lambda: gather.forward(s)
        second_of = lambda s: lambda: scatter.second(s)
        third_of = lambda s: lambda: pass_on(s)
        compute(0, {"hidden": [arrive(1)], "left": [pass_x(1), arrive(2), take(1)]})
        compute(
            1,
            {
                "half": [pass_x(2), arrive(3)],
                "hidden": [second_of(0)],
                "left": [third_of(0), take(2)],
            },
        )
        compute(2, {"picked": [pass_x(3)], "hidden": [second_of(1)], "left": [third_of(1), take(3)]})
        compute(3, {"hidden": [second_of(2)], "left": [third_of(2)]})
        copies = []
        own = pltpu.make_async_copy(d_gates, gate_out.at[mine], local.at[5])
        own.start()
        for number, (hops, bits, device) in enumerate(others):
            copies.append(net.send(d_gates, gate_out.at[mine], (ms, mr), number, device))
        scatter.second(3)
        pass_on(3)
        ring_copies[-1].wait_recv()
        add_slabs(result, [part_reader(result), part_reader(landed.at[ring - 2])])
        stored(*kept)
        own.wait()
        gather.own.wait()
        for copy in copies:
            copy.wait_recv()
        net.finish()

    vmem = pltpu.VMEM
    by_chunk = lambda dtype, *dims: shape((ring, *dims), dtype)
    return remote_call(
        kernel,
        "experts_phase",
        5,
        [
            shape((tokens, width), bf16),
            by_chunk(bf16, tokens, model),
            by_chunk(bf16, tokens, model),
            by_chunk(bf16, n_slots, model),
            by_chunk(bf16, n_slots, model),
            by_chunk(bf16, n_slots, hidden),
            by_chunk(bf16, n_slots, hidden),
            by_chunk(bf16, n_slots, hidden),
            by_chunk(bf16, tokens, pad),
            by_chunk(bf16, tokens, 2 * pad),
            by_chunk(f32, tokens, 128),
            shape((experts, ring, 1, tokens), f32),
        ],
        [
            vmem((model, hidden), bf16),
            vmem((model, hidden), bf16),
            vmem((hidden, model), bf16),
            vmem(shared.shape, bf16),
            vmem(router.shape, bf16),
            vmem((tokens, model), bf16),
            vmem((tokens, model), bf16),
            vmem((n_slots, model), bf16),
            vmem((n_slots, model), bf16),
            vmem((n_slots, hidden), bf16),
            vmem((n_slots, hidden), bf16),
            vmem((n_slots, hidden), bf16),
            vmem((tokens, pad), bf16),
            vmem((tokens, 2 * pad), bf16),
            vmem((tokens, 128), f32),
            vmem((2, tokens, model), bf16),
            vmem((ring, 1, tokens), f32),
        ]
        + scatter_scratch(ring, tokens, width, resident=True)
        + [vmem((ring - 1, tokens, width), bf16), vmem((2, tokens, width), bf16)]
        + pair_sems(ring - 1)
        + pair_sems(7 * ring)
        + pair_sems(experts - 1)
        + [
            pltpu.SemaphoreType.DMA((6,)),
            pltpu.SemaphoreType.DMA((24,)),
            pltpu.SemaphoreType.DMA((9,)),
        ],
        (second, grads, maps, *experts_w, shared, router),
        in_vmem=(2,),
        out_vmem=(0,),
    )


def attention_back(
    n_rows, n_cols, d_block, d_gates, probs, router, token_rows, gains, weights_out, weights_in,
    queries, kv, heads_out, lse, tables, parts, expert_rows,
):
    ring = n_cols // 2
    length, model = token_rows[0].shape
    experts = n_rows * ring
    q_width = weights_out.shape[1]
    in_width = weights_in.shape[1]
    col_width = model // n_cols
    width = model // n_rows
    heads = q_width // HEAD_DIM
    scale = 1.0 / math.sqrt(HEAD_DIM)
    half = expert_rows[2].shape[1] // 2
    n_slots = expert_rows[2].shape[0]
    bf16, f32 = jnp.bfloat16, jnp.float32
    shape = jax.ShapeDtypeStruct

    def kernel(
        block, gates, probs, router, x_in, proj_in, g_in, gains, wo_in, w_in, q, kv, out, lse, cosine,
        sine, y_in, xr_in, dp_in, act_in, dg_in, du_in,
        d_proj, d_first, y_out, wo_out, d_resid, gain_out, xr_out, dp_out, act_out, dg_out, du_out,
        second, proj, g, high_ref, low_ref,
        wo, w, go, delta, dqt, dkv, dkv_own, wo_part, y_hold, y_landed, *rest,
    ):
        scratch, kv_parts, wo_parts = rest[:9], rest[9:16], rest[16:23]
        gs, gr, yr_s, yr_r, es, er, local = rest[23:]
        net = Links(n_rows, n_cols)
        net.greet([net.x, net.y, net.up, net.down, net.twin])
        gather = gather_square(net, block, second, (gs, gr), local.at[1], 1)
        next(gather)
        others = pl.ds(half, half)
        twins = [
            net.send(source, target, (es, er), number, net.twin)
            for number, (source, target) in enumerate(
                (
                    (xr_in, xr_out), (dg_in.at[:, others], dg_out), (du_in.at[:, others], du_out),
                    (act_in.at[:, others], act_out), (dp_in, dp_out),
                )
            )
        ]
        x, d_attn = d_first, proj
        loads = [
            pltpu.make_async_copy(a, b, local.at[2 + i])
            for i, (a, b) in enumerate(((x_in, x), (proj_in, proj), (g_in.at[0], g)))
        ]
        for load in loads:
            load.start()
        wo_load = pltpu.make_async_copy(wo_in, wo, local.at[5])
        wo_load.start()
        w_load = pltpu.make_async_copy(w_in, w, local.at[0])
        w_load.start()
        d_gates = jnp.concatenate(
            [gates[...].reshape(experts, length), jnp.zeros((128 - experts, length), f32)], 0
        ).T
        d_logits = probs[...] * (d_gates - jnp.sum(probs[...] * d_gates, -1, keepdims=True))
        high = d_logits.astype(bf16)
        high_ref[...] = high
        low_ref[...] = (d_logits - high.astype(f32)).astype(bf16)
        for load in loads:
            load.wait()

        hop = []

        def keep_sum(s, upper, lower):
            half = length // 2
            target = y_hold if s == 1 else y_out.at[s - 1]
            add_slabs(target.at[pl.ds(0, half), :], upper)
            add_slabs(target.at[pl.ds(half, half), :], lower)
            if s == 1:
                hop.append(net.send(y_hold, y_landed, (yr_s, yr_r), 0, net.up))

        y_steps = scatter_square(net, y_in, scratch, list(range(1, ring)), keep_sum)
        by_place = lambda ref: lambda hops, core: ref.at[
            pl.ds((net.place(hops) * 2 + core) * col_width, col_width), :
        ]

        run_together(gather)
        next(y_steps)
        next(y_steps)
        gain = gains[1:2]
        gain_out[...] = jnp.zeros_like(gain_out)

        @pl.loop(0, length // 128)
        def _(i):
            at = pl.ds(pl.multiple_of(i * 128, 128), 128)
            values = x[at, :].astype(f32) + proj[at, :].astype(f32)
            inverse = lax.rsqrt(jnp.mean(values * values, -1, keepdims=True) + NORM_EPS)
            unit = values * inverse
            d_second = second[0, at, :].astype(f32)
            d_second = d_second + matmul_nt(high_ref[at, :], router[...])
            d_second = d_second + matmul_nt(low_ref[at, :], router[...])
            d_unit = d_second * gain
            moment = jnp.mean(d_unit * unit, -1, keepdims=True)
            resid = g[at, :].astype(f32) + inverse * (d_unit - unit * moment)
            d_attn[at, :] = resid.astype(bf16)
            d_resid[at, :] = resid[:, :width]
            along = (d_second[:, :width] * unit[:, :width]).reshape(16, 8, width)
            gain_out[...] += jnp.sum(along, 0)

        wo_load.wait()
        go[...] = matmul(d_attn[...], wo[...]).astype(bf16)
        wo_part[...] = matmul_tn(d_attn[...], out[...].astype(bf16)).astype(bf16)
        wo_steps = scatter_columns(net, by_place(wo_part), wo_out, wo_parts)
        next(wo_steps)
        for head in range(heads):
            columns = slice(head * HEAD_DIM, (head + 1) * HEAD_DIM)
            product = (go[:, columns].astype(f32) * out[:, columns]).T
            delta[head] = jnp.sum(product, 0, keepdims=True)
        dqt[...] = jnp.zeros_like(dqt)
        dkv[...] = jnp.zeros_like(dkv)
        next(wo_steps)
        next(y_steps)
        next(y_steps)

        def one_block(number, masked):
            keys = kv[number, :, :HEAD_DIM]
            values = kv[number, :, HEAD_DIM:]
            keys_t = keys.T
            d_key = jnp.zeros((length, HEAD_DIM), f32)
            d_value = jnp.zeros((length, HEAD_DIM), f32)
            for head in range(heads):
                columns = slice(head * HEAD_DIM, (head + 1) * HEAD_DIM)
                queries = q[:, columns]
                grads = go[:, columns]
                probs = jnp.exp(scores_of(keys, queries, scale) - lse[head])
                if masked:
                    probs = jnp.where(causal_mask(probs), probs, 0.0)
                d_probs = matmul_nt(values, grads)
                d_scores = (probs * (d_probs - delta[head])).astype(bf16)
                d_value = d_value + matmul(probs.astype(bf16), grads)
                d_key = d_key + matmul(d_scores, queries)
                dqt[head] = dqt[head] + matmul(keys_t, d_scores)
            dkv[number, :, :HEAD_DIM] = (d_key * scale).astype(bf16)
            dkv[number, :, HEAD_DIM:] = d_value.astype(bf16)

        one_block(net.c, True)
        middle = lax.div(net.c, 2)

        @pl.loop(0, middle)
        def _(number):
            one_block(number, False)

        next(y_steps)
        next(y_steps)
        next(wo_steps)

        @pl.loop(middle, net.c)
        def _(number):
            one_block(number, False)

        next(wo_steps)
        kv_steps = scatter_columns(
            net, lambda hops, core: dkv.at[2 * net.chip(hops) + core], dkv_own, kv_parts
        )
        next(kv_steps)
        next(kv_steps)
        next(y_steps)

        def turned_back(values):
            return (values * cosine[...] - pltpu.roll(values, HEAD_DIM // 2, 1) * sine[...]).astype(bf16)

        for head in range(heads):
            columns = slice(head * HEAD_DIM, (head + 1) * HEAD_DIM)
            d_proj[:, columns] = turned_back((dqt[head] * scale).T)
        next(kv_steps)
        next(y_steps)
        next(kv_steps)
        next(wo_steps)
        run_together(kv_steps)
        next(y_steps, None)
        d_proj[:, q_width : q_width + HEAD_DIM] = turned_back(dkv_own[:, :HEAD_DIM])
        d_proj[:, q_width + HEAD_DIM :] = dkv_own[:, HEAD_DIM:].astype(bf16)
        w_load.wait()
        for j in range(n_rows):
            at = slice(j * width, (j + 1) * width)
            d_first[:, at] = matmul_nt(d_proj[...], w[at, :]).astype(bf16)
        run_together(y_steps, wo_steps)
        hop[0].wait_recv()
        y_out[0] = y_landed[...]
        for copy in twins:
            copy.wait_recv()
        net.finish()

    vmem = pltpu.VMEM
    return remote_call(
        kernel,
        "attention_back",
        6,
        [
            shape((length, in_width), bf16),
            shape((length, model), bf16),
            shape((ring - 1, length, width), bf16),
            shape((col_width, q_width), f32),
            shape((length, width), f32),
            shape((8, width), f32),
            shape((n_slots, model), bf16),
            shape((n_slots, model), bf16),
            shape((n_slots, half), bf16),
            shape((n_slots, half), bf16),
            shape((n_slots, half), bf16),
        ],
        [
            vmem((1, length, model), bf16),
            vmem((length, model), bf16),
            vmem((length, model), bf16),
            vmem((length, 128), bf16),
            vmem((length, 128), bf16),
            vmem((model, q_width), bf16),
            vmem((model, in_width), bf16),
            vmem((length, q_width), bf16),
            vmem((heads, 1, length), f32),
            vmem((heads, HEAD_DIM, length), f32),
            vmem((n_cols, length, 2 * HEAD_DIM), bf16),
            vmem((length, 2 * HEAD_DIM), f32),
            vmem((model, q_width), bf16),
            vmem((length, width), bf16),
            vmem((length, width), bf16),
        ]
        + scatter_scratch(ring - 1, length, width)
        + scatter_columns_scratch(ring, length, 2 * HEAD_DIM)
        + scatter_columns_scratch(ring, col_width, q_width)
        + pair_sems(7)
        + pair_sems(1)
        + pair_sems(5)
        + [pltpu.SemaphoreType.DMA((6,))],
        (
            d_block, d_gates, probs, router, *token_rows, gains, weights_out, weights_in, queries, kv,
            heads_out, lse, *tables, parts, *expert_rows,
        ),
        in_vmem=(1, 2, 3, 7, 10, 11, 12, 13, 14, 15),
        out_vmem=(0, 1, 2, 3, 4, 5),
    )


def last_phase(
    n_rows, n_cols, d_first, d_proj, normed, parts, part_sum, x, proj, d_resid, gains, gain_part,
    x_scale, expert_rows, twin_rows, router_rows,
):
    ring = n_cols // 2
    length, model = d_first.shape
    width = model // n_rows
    in_width = d_proj.shape[1]
    col_width = model // n_cols
    pieces = 2
    piece = length // pieces
    bf16, f32 = jnp.bfloat16, jnp.float32
    shape = jax.ShapeDtypeStruct
    chips = n_rows * ring
    slot_rows, d_part, e_act, d_gate, d_up = expert_rows
    n_slots, hidden = e_act.shape
    half = hidden // 2
    experts = router_rows[2].shape[0]
    rows_dev = length // n_rows

    def kernel(
        d_first, d_proj, normed, y_in, y_sum, x_in, proj_in, d_resid, gains, gain_two, x_scale,
        xr_in, dp_in, act_in, dg_in, du_in, xr_twin, dp_twin, act_twin, dg_twin, du_twin,
        rows_in, probs_in, gates_in,
        layer_out, grad_in, gain_out, w_out, router_out, out_g, out_u, out_d,
        d_own, w_part, moment, moments, gain_own, gain_twin, gain_sums, proj, x,
        xr, dg, du, full_a, full_b,
        x_q, probs_q, gates_q, router_part, router_got, router_sum, y_landed, y_leaving, *rest,
    ):
        scratch, y_scratch = rest[:9], rest[9:18]
        w_parts = rest[18:25]
        mo_s, mo_r, ga_s, ga_r, gt_s, gt_r, sem, ro_s, ro_r, router_sems, yr_s, yr_r = rest[25:]
        full = (full_a, full_b)
        net = Links(n_rows, n_cols)
        others = net.spread_partners()
        net.greet([device for _, _, device in others] + [net.twin])

        def finish(s, upper, lower):
            at = lambda p: pl.ds(s * piece + p * (piece // 2), piece // 2)
            add_slabs(d_own.at[at(0), :], upper)
            add_slabs(d_own.at[at(1), :], lower)

        ring_copies = []

        def pass_on(turn):
            if turn == 1:
                before = part_reader(y_sum, 0)
            else:
                ring_copies[turn - 2].wait_recv()
                before = part_reader(y_landed, turn - 2)
            add_slabs(y_leaving.at[turn - 1], [part_reader(y_sum, turn), before])
            ring_copies.append(
                net.send(
                    y_leaving.at[turn - 1], y_landed.at[turn - 1], (yr_s, yr_r), turn - 1, net.up
                )
            )

        pass_on(1)

        def finish_out(s, upper, lower):
            ring_copies[-1].wait_recv()
            for part, terms in ((0, upper), (1, lower)):
                at = pl.ds(part * (length // 2), length // 2)
                extra = [
                    part_reader(y_landed.at[ring - 3, at, :]),
                    part_reader(x.at[at, :]),
                    part_reader(proj.at[at, :]),
                ]
                add_slabs(layer_out.at[at, :], terms + extra)

        steps = scatter_square(net, d_first, scratch, list(range(pieces)), finish, resident=True)
        y_steps = scatter_square(net, y_in, y_scratch, [0], finish_out)
        next(steps)
        next(steps)
        ours, mine, twins = pl.ds(0, half), pl.ds(0, n_slots), pl.ds(n_slots, n_slots)
        loads = [
            pltpu.make_async_copy(a, b, sem.at[i])
            for i, (a, b) in enumerate(
                (
                    (xr_in, xr.at[mine]), (xr_twin, xr.at[twins]),
                    (dg_in.at[:, ours], dg.at[mine]), (dg_twin, dg.at[twins]),
                    (du_in.at[:, ours], du.at[mine]), (du_twin, du.at[twins]),
                    (act_in.at[:, ours], dg.at[mine]), (act_twin, dg.at[twins]),
                    (dp_in, xr.at[mine]), (dp_twin, xr.at[twins]),
                )
            )
        ]
        early, late = loads[:6], loads[6:]
        for load in early:
            load.start()
        stores = {}

        def make(kind, j):
            group, slot = kind // 2, j % 2 if kind < 2 else 0
            columns = slice(j * width, (j + 1) * width)
            at = pl.ds(pl.multiple_of(net.flip(j) * width, width), width)
            if (group, slot) in stores:
                stores[group, slot].wait()
            if kind < 2:
                full[group][slot] = matmul_tn(xr[:, columns], (dg, du)[kind][...])
                target = (out_g, out_u)[kind].at[at, :]
            else:
                full[group][slot] = matmul_tn(dg[...], xr[:, columns])
                target = out_d.at[:, at]
            store = pltpu.make_async_copy(full[group].at[slot], target, sem.at[12 + 2 * group + slot])
            store.start()
            stores[group, slot] = store

        proj_load = pltpu.make_async_copy(proj_in.at[:, pl.ds(0, width)], proj, sem.at[10])
        proj_load.start()
        x_load = pltpu.make_async_copy(x_in.at[:, pl.ds(0, width)], x, sem.at[11])
        x_load.start()
        quarter = pl.ds(pl.multiple_of(net.r * rows_dev, rows_dev), rows_dev)
        column = pl.ds(pl.multiple_of(net.place(0) * width, width), width)
        router_loads = []
        for s in range(ring):
            router_loads += [
                pltpu.make_async_copy(
                    rows_in.at[s, quarter, column], x_q.at[s], router_sems.at[s, 0]
                ),
                pltpu.make_async_copy(probs_in.at[s, quarter, :], probs_q.at[s], router_sems.at[s, 1]),
                pltpu.make_async_copy(
                    gates_in.at[:, net.chip(s), 0, quarter], gates_q.at[s], router_sems.at[s, 2]
                ),
            ]
        for load in router_loads:
            load.start()
        w_part[...] = matmul_tn(normed[...], d_proj[...]).astype(bf16)
        by_place = lambda hops, core: w_part.at[
            pl.ds((net.place(hops) * 2 + core) * col_width, col_width), :
        ]
        w_steps = scatter_columns(net, by_place, w_out, w_parts)
        next(w_steps)
        next(steps)
        for load in early:
            load.wait()
        make(0, 0)
        next(w_steps)
        next(steps)
        next(y_steps)
        make(0, 1)
        pass_on(2)
        run_together(steps)

        x_load.wait()
        gain = gains[0:1, :width]
        slab = 128
        gain_own[...] = jnp.zeros_like(gain_own)

        def unit_of(at):
            inverse = x_scale[at, :1]
            return x[at, :].astype(f32) * inverse, inverse

        for i in range(length // slab):
            at = slice(i * slab, (i + 1) * slab)
            unit, _ = unit_of(at)
            d_normed = d_own[at, :]
            share = jnp.sum(d_normed * gain * unit, -1, keepdims=True)
            moment[:, at] = jnp.broadcast_to(share, (slab, 128)).T[:8]
            gain_own[:8] += jnp.sum((d_normed * unit).reshape(slab // 8, 8, width), 0)
        sends = [
            net.send(moment, moments.at[bits - 1], (mo_s, mo_r), bits - 1, (net.flip(bits), net.c))
            for bits in range(1, n_rows)
        ]
        gain_own[8:] = gain_two[...]
        twin = net.send(gain_own, gain_twin, (gt_s, gt_r), 0, net.twin)
        next(w_steps)
        make(0, 2)
        for copy in sends:
            copy.wait_recv()
        whole = moment[...] + moments[0] + moments[1] + moments[2]
        for i in range(length // slab):
            at = slice(i * slab, (i + 1) * slab)
            unit, inverse = unit_of(at)
            mean = jnp.broadcast_to(whole[:1, at], (128, slab)).T[:, :1] / model
            grad_in[at, :] = d_resid[at, :] + inverse * (d_own[at, :] * gain - unit * mean)
        twin.wait_recv()
        mine = net.r * ring + net.z
        gain_sums[mine] = gain_own[...] + gain_twin[...]
        sends = [
            net.send(gain_sums.at[mine], gain_sums.at[mine], (ga_s, ga_r), number, device)
            for number, (hops, bits, device) in enumerate(others)
        ]
        make(0, 3)
        next(w_steps)
        make(1, 0)
        next(y_steps)
        make(1, 1)
        for load in router_loads:
            load.wait()
        for s in range(ring):
            d_gates = jnp.concatenate([gates_q[s], jnp.zeros((128 - experts, rows_dev), f32)], 0).T
            d_logits = probs_q[s] * (d_gates - jnp.sum(probs_q[s] * d_gates, -1, keepdims=True))
            high = d_logits.astype(bf16)
            low = (d_logits - high.astype(f32)).astype(bf16)
            part = matmul_tn(x_q[s], high) + matmul_tn(x_q[s], low)
            for core in range(2):
                rows = part[core * col_width : (core + 1) * col_width]
                router_part[core] = rows if s == 0 else router_part[core] + rows
        router_twin = net.send(router_part.at[1 - net.k], router_got.at[0], (ro_s, ro_r), 0, net.twin)
        make(1, 2)
        router_twin.wait_recv()
        router_sum[0] = router_part[net.k] + router_got[0]
        router_x = net.send(router_sum.at[0], router_got.at[1], (ro_s, ro_r), 1, net.x)
        proj_load.wait()
        next(y_steps)
        make(1, 3)
        for load in late:
            load.start()
        router_x.wait_recv()
        router_sum[1] = router_sum[0] + router_got[1]
        router_y = net.send(router_sum.at[1], router_got.at[2], (ro_s, ro_r), 2, net.y)
        run_together(y_steps, w_steps)
        for load in late:
            load.wait()
        for j in range(n_rows):
            make(2, j)
        for store in stores.values():
            store.wait()
        for copy in sends:
            copy.wait_recv()
        router_y.wait_recv()
        router_out[...] = router_sum[1] + router_got[2]
        total = gain_sums[net.z * ring]
        for i in range(1, ring):
            total = total + gain_sums[net.z * ring + i]
        gain_out[0:1] = jnp.sum(total[:8], 0, keepdims=True)
        gain_out[1:2] = jnp.sum(total[8:], 0, keepdims=True)
        gain_out[2:8] = jnp.zeros((6, width), f32)
        run_together(w_steps)
        net.finish()

    vmem = pltpu.VMEM
    return remote_call(
        kernel,
        "last_phase",
        7,
        [
            shape((length, width), bf16),
            shape((length, width), f32),
            shape((8, width), f32),
            shape((col_width, in_width), f32),
            shape((col_width, 128), f32),
            shape((model, half), f32),
            shape((model, half), f32),
            shape((half, model), f32),
        ],
        [
            vmem((length, width), f32),
            vmem((model, in_width), bf16),
            vmem((8, length), f32),
            vmem((n_rows - 1, 8, length), f32),
            vmem((16, width), f32),
            vmem((16, width), f32),
            vmem((chips, 16, width), f32),
            vmem((length, width), bf16),
            vmem((length, width), bf16),
            vmem((2 * n_slots, model), bf16),
            vmem((2 * n_slots, half), bf16),
            vmem((2 * n_slots, half), bf16),
            vmem((2, width, half), f32),
            vmem((1, half, width), f32),
            vmem((ring, rows_dev, width), bf16),
            vmem((ring, rows_dev, 128), f32),
            vmem((ring, experts, rows_dev), f32),
            vmem((2, col_width, 128), f32),
            vmem((3, col_width, 128), f32),
            vmem((2, col_width, 128), f32),
            vmem((ring - 2, length, width), bf16),
            vmem((ring - 2, length, width), bf16),
        ]
        + scatter_scratch(pieces, piece, width, resident=True)
        + scatter_scratch(1, length, width)
        + scatter_columns_scratch(ring, col_width, in_width)
        + pair_sems(n_rows - 1)
        + pair_sems(chips - 1)
        + pair_sems(1)
        + [pltpu.SemaphoreType.DMA((16,))]
        + pair_sems(3)
        + [pltpu.SemaphoreType.DMA((ring, 3))]
        + pair_sems(ring - 2),
        (
            d_first.reshape(pieces, piece, model), d_proj, normed, parts, part_sum, x, proj, d_resid,
            gains, gain_part, x_scale, *expert_rows, *twin_rows, *router_rows,
        ),
        in_vmem=(0, 1, 2, 4, 7, 8, 9, 10),
        out_vmem=(0, 1, 2, 3, 4),
    )


def add_bf16(left, right):
    return (left.astype(jnp.float32) + right.astype(jnp.float32)).astype(jnp.bfloat16)


class Exchange:
    def __init__(self):
        self.n_rows = lax.axis_size("rows")
        self.n_cols = lax.axis_size("cols")
        self.ring = self.n_cols // 2
        self.r = lax.axis_index("rows")
        self.c = lax.axis_index("cols")
        self.z = self.c // 2
        self.k = self.c % 2

    def move(self, values, target):
        pairs = []
        for r in range(self.n_rows):
            for c in range(self.n_cols):
                to_r, to_c = target(r, c)
                pairs.append((r * self.n_cols + c, to_r * self.n_cols + to_c))
        return lax.ppermute(values, ("rows", "cols"), pairs)

    def along_x(self, values):
        return self.move(values, lambda r, c: (r ^ 1, c))

    def along_y(self, values):
        return self.move(values, lambda r, c: (r ^ 2, c))

    def along_z(self, values, hops=1):
        return self.move(values, lambda r, c: (r, (c + 2 * hops) % self.n_cols))

    def across_z(self, values, bit):
        return self.move(values, lambda r, c: (r, c ^ (2 * bit)))

    def sibling(self, values):
        return self.move(values, lambda r, c: (r, c ^ 1))

    def chip(self, hops):
        return (self.z - hops + self.ring) % self.ring

    def place(self, hops):
        return self.r ^ self.chip(hops)

    def mixed(self, values, axis):
        width = values.shape[axis] // self.n_rows

        def branch(row):
            return lambda whole: jnp.concatenate(
                [
                    lax.slice_in_dim(whole, (row ^ j) * width, ((row ^ j) + 1) * width, axis=axis)
                    for j in range(self.n_rows)
                ],
                axis,
            )

        return lax.switch(self.r, [branch(row) for row in range(self.n_rows)], values)

    def rows_gather(self, block):
        half = block.shape[0] // 2
        from_x = self.along_x(block)
        from_y = self.along_y(block)
        first = self.along_y(from_x[:half])
        second = self.along_x(from_y[half:])
        return [block, from_x, from_y, jnp.concatenate([first, second], 0)]

    def rows_scatter(self, blocks):
        half = blocks[0].shape[0] // 2
        upper = [block[:half] for block in blocks]
        lower = [block[half:] for block in blocks]
        sent = self.along_x(jnp.stack([upper[1], upper[3]]))
        forward = add_bf16(upper[2], sent[1])
        upper_sum = upper[0].astype(jnp.float32) + sent[0].astype(jnp.float32)
        upper_sum = upper_sum + self.along_y(forward).astype(jnp.float32)
        sent = self.along_y(jnp.stack([lower[2], lower[3]]))
        forward = add_bf16(lower[1], sent[1])
        lower_sum = lower[0].astype(jnp.float32) + sent[0].astype(jnp.float32)
        lower_sum = lower_sum + self.along_x(forward).astype(jnp.float32)
        return jnp.concatenate([upper_sum, lower_sum], 0)

    def cols_gather(self, block, place):
        shape = (self.ring, 2) + block.shape
        whole = jnp.zeros(shape, block.dtype)
        rest = (0,) * block.ndim
        for hops in range(self.ring):
            twin = self.sibling(block)
            spot = place(hops)
            whole = lax.dynamic_update_slice(whole, block[None, None], (spot, self.k) + rest)
            whole = lax.dynamic_update_slice(whole, twin[None, None], (spot, 1 - self.k) + rest)
            if hops < self.ring - 1:
                block = self.along_z(block)
        return whole

    def pair_sum(self, parts):
        mine = lax.dynamic_index_in_dim(parts, self.k, 1, False)
        other = lax.dynamic_index_in_dim(parts, 1 - self.k, 1, False)
        return add_bf16(mine, self.sibling(other))

    def cols_scatter(self, parts, place):
        summed = self.pair_sum(parts)
        pick = lambda hops: lax.dynamic_index_in_dim(summed, place(hops), 0, False)
        run = pick(1)
        for hops in range(2, self.ring):
            run = add_bf16(self.along_z(run), pick(hops))
        return self.along_z(run).astype(jnp.float32) + pick(0).astype(jnp.float32)


def split_terms(values):
    high = lax.reduce_precision(values, 8, 7)
    return high.astype(jnp.bfloat16), (values - high).astype(jnp.bfloat16)


def gathered_layer(
    layer_in,
    norm1_gain,
    w_query,
    key_matrix,
    value_matrix,
    w_out,
    norm2_gain,
    w_router,
    shared_gate,
    shared_up,
    shared_down,
    expert_gate,
    expert_up,
    expert_down,
    routes,
    cotangent,
):
    net = Exchange()
    n_rows, ring = net.n_rows, net.ring
    r, c, z, k = net.r, net.c, net.z, net.k
    length, row_width = layer_in.shape[1:]
    rows_dev, top_k = routes.shape[2:]
    experts = w_router.shape[1]
    model_width = row_width * n_rows
    col_width = w_query.shape[0]
    q_width = w_query.shape[1]
    q_heads = q_width // HEAD_DIM
    kv_width = key_matrix.shape[1]
    shared_hidden = shared_gate.shape[1] // ring
    half_hidden = expert_gate.shape[2]
    slots = -(-2 * max(1, 5 * rows_dev * top_k // (8 * experts)) // 16) * 16
    index = lax.dynamic_index_in_dim

    expert_ids = jnp.arange(experts, dtype=jnp.int32)
    hot = jnp.sum(
        (routes.reshape(rows_dev, top_k)[:, :, None] == expert_ids).astype(jnp.float32), 1
    )
    earlier = jnp.tril(jnp.ones((rows_dev, rows_dev), jnp.float32), -1)
    rank = jnp.dot(earlier, hot, precision=PRECISE)
    slot_map = jnp.where(hot > 0, rank, -1.0).T

    small = jnp.concatenate([w_router, norm1_gain[:, None], norm2_gain[:, None]], 1)
    small = jnp.pad(small, ((0, 0), (0, 128 - small.shape[1])))
    pad_to = -(-shared_hidden // 128) * 128
    padded = lambda w: jnp.pad(
        w.reshape(col_width, ring, shared_hidden), ((0, 0), (0, 0), (0, pad_to - shared_hidden))
    )
    packed = jnp.concatenate([padded(shared_gate), padded(shared_up), padded(shared_down.T)], 2)
    packed = jnp.swapaxes(packed, 0, 1)
    experts_w = []
    for own in (expert_gate[0], expert_up[0], expert_down[0]):
        experts_w += [own, net.sibling(own)]
    positions = c * length + jnp.arange(length, dtype=jnp.int32)
    cosine_table, sine_table = rope_tables(positions, HEAD_DIM)
    tables = (
        jnp.concatenate([cosine_table, cosine_table], 1),
        jnp.concatenate([-sine_table, sine_table], 1),
    )

    (
        token_input, first_normed, weights_in, small, queries, kv_all, attn_f32, log_total,
        weights_out_t, grad_rows, second_normed, slot_maps, shared_w, attn_proj, gains,
        first_scale,
    ) = first_phase(
        n_rows, net.n_cols, layer_in[0], cotangent[0],
        jnp.concatenate([w_query, key_matrix, value_matrix], 1), small, w_out.T, packed, slot_map,
        tables,
    )
    joined = lambda whole: whole.reshape(-1, whole.shape[-1])
    attn_proj = joined(attn_proj)
    (
        d_block, rows_all, out_rows, slot_rows, d_part, e_act, d_e_gate, d_e_up, s_act, d_shared,
        gate_probs, d_gate_all,
    ) = experts_phase(
        n_rows, net.n_cols, second_normed, grad_rows, slot_maps, experts_w, shared_w, small, slots
    )
    expert_rows = [joined(part) for part in (slot_rows, d_part, e_act, d_e_gate, d_e_up)]
    d_projected, d_first, part_sum, g_out, d_resid, gain_part, *twin_rows = attention_back(
        n_rows, net.n_cols, d_block, index(d_gate_all, z, 1, False)[:, 0], gate_probs[0], small,
        (token_input, attn_proj, grad_rows), gains, weights_out_t, weights_in, queries, kv_all,
        attn_f32, log_total, tables, out_rows, expert_rows,
    )
    layer_out, grad_in, gain_grads, g_in, g_router, *g_experts = last_phase(
        n_rows, net.n_cols, d_first, d_projected, first_normed, out_rows, part_sum, token_input,
        attn_proj, d_resid, gains, gain_part, first_scale,
        expert_rows, twin_rows, (rows_all, gate_probs, d_gate_all),
    )
    gain_grads = index(gain_grads[:2].reshape(2, 2, col_width), k, 1, False)

    column_parts = lambda whole: whole.astype(jnp.bfloat16).reshape(ring, 2, col_width, -1)
    shared_parts = jnp.concatenate(
        [
            matmul_tn(joined(rows_all), joined(d_shared)),
            matmul_tn(joined(grad_rows), joined(s_act)),
        ],
        1,
    )
    shared_parts = net.pair_sum(column_parts(shared_parts))
    g_shared = jnp.zeros(shared_parts.shape, jnp.bfloat16)
    for hops in range(ring):
        piece = index(shared_parts, net.place(-hops), 0, False)
        piece = net.along_z(piece, hops) if hops else piece
        g_shared = lax.dynamic_update_slice(g_shared, piece[None], (net.chip(hops), 0, 0))
    g_shared = g_shared.astype(jnp.float32)
    shared_cols = lambda n: jnp.swapaxes(
        g_shared[:, :, n * pad_to : n * pad_to + shared_hidden], 0, 1
    ).reshape(col_width, -1)

    return (
        layer_out[None],
        grad_in[None],
        gain_grads[0],
        g_in[:, :q_width],
        g_in[:, q_width : q_width + kv_width],
        g_in[:, q_width + kv_width :],
        g_out.T,
        gain_grads[1],
        g_router[:, :experts],
        shared_cols(0),
        shared_cols(1),
        shared_cols(2).T,
        g_experts[0][None],
        g_experts[1][None],
        g_experts[2][None],
    )


def per_device(layer_in, *others):
    routes = others[13]
    w_router = others[6]
    n_rows, n_cols = lax.axis_size("rows"), lax.axis_size("cols")
    experts, top_k = w_router.shape[1], routes.shape[3]
    gathers = (
        experts <= 4 * top_k
        and layer_in.shape[0] == 1
        and n_rows == 4
        and n_cols == 2 * n_rows
        and 2 * experts == n_rows * n_cols
    )
    return (gathered_layer if gathers else routed_layer)(layer_in, *others)


def solution(mesh):
    placed = (
        P(None, "cols", "rows"),
        P("cols"),
        P("cols", "rows"),
        P("cols", "rows"),
        P("cols", "rows"),
        P("rows", "cols"),
        P("cols"),
        P("cols", None),
        P("cols", "rows"),
        P("cols", "rows"),
        P("rows", "cols"),
        P(("rows", "cols"), None, None),
        P(("rows", "cols"), None, None),
        P(("rows", "cols"), None, None),
        P("cols", "rows", None, None),
        P(None, "cols", "rows"),
    )
    return jax.shard_map(
        per_device,
        mesh=mesh,
        in_specs=placed,
        out_specs=(
            P(None, "cols", "rows"),
            P(None, "cols", "rows"),
            P("cols"),
            P("cols", "rows"),
            P("cols", "rows"),
            P("cols", "rows"),
            P("rows", "cols"),
            P("cols"),
            P("cols", None),
            P("cols", "rows"),
            P("cols", "rows"),
            P("rows", "cols"),
            P(("rows", "cols"), None, None),
            P(("rows", "cols"), None, None),
            P(("rows", "cols"), None, None),
        ),
        check_vma=False,
    )
```

```python
import math

import jax
import jax.numpy as jnp
from jax import lax
from jax.experimental import pallas as pl
from jax.experimental.pallas import tpu as pltpu
from jax.sharding import PartitionSpec as P

HEAD_DIM = 128


NORM_EPS = 1e-05
ROPE_BASE = 500000.0
NEG_LARGE = -1e30
PRECISE = lax.Precision.HIGHEST


def rope_tables(positions, head_size):
    half_size = head_size // 2
    inv_freq = ROPE_BASE ** (-(2.0 * jnp.arange(half_size, dtype=jnp.float32)) / head_size)
    angles = positions.astype(jnp.float32)[:, None] * inv_freq[None, :]
    return (jnp.cos(angles), jnp.sin(angles))


def apply_rotary(values, cosine_table, sine_table):
    half_size = values.shape[-1] // 2
    first_half = values[..., :half_size]
    second = values[..., half_size:]
    cos_b = cosine_table[:, None, :]
    sin_b = sine_table[:, None, :]
    return jnp.concatenate(
        [first_half * cos_b - second * sin_b, second * cos_b + first_half * sin_b], -1
    )


def matmul(left_op, right_op):
    return jnp.dot(left_op, right_op, preferred_element_type=jnp.float32)


def matmul_tn(left_op, right_op):
    return lax.dot_general(
        left_op, right_op, (((0,), (0,)), ((), ())), preferred_element_type=jnp.float32
    )


def matmul_nt(left_op, right_op):
    return lax.dot_general(
        left_op, right_op, (((1,), (1,)), ((), ())), preferred_element_type=jnp.float32
    )


def silu_parts(pre_act):
    sigma = jax.nn.sigmoid(pre_act)
    return (pre_act * sigma, sigma * (1.0 + pre_act * (1.0 - sigma)))


def keep_same(carry_in):
    return carry_in


def routed_layer(
    layer_in,
    norm1_gain,
    w_query,
    key_matrix,
    value_matrix,
    w_out,
    norm2_gain,
    w_router,
    shared_gate,
    shared_up,
    shared_down,
    expert_gate,
    expert_up,
    expert_down,
    routes,
    cotangent,
):
    n_rows = lax.axis_size("rows")
    n_cols = lax.axis_size("cols")
    row_idx = lax.axis_index("rows")
    col_idx = lax.axis_index("cols")
    sequence_count, len_dev, row_width = layer_in.shape
    tok_dev = sequence_count * len_dev
    rows_dev = routes.shape[2]
    top_k = routes.shape[3]
    experts = w_router.shape[1]
    devices = n_rows * n_cols
    capacity = 2 * max(1, 5 * rows_dev * top_k // (8 * experts))
    full_in = lax.all_gather(layer_in, "rows", axis=2, tiled=True)
    (
        gain_one,
        wq_full,
        wk_full,
        wv_full,
        wo_full,
        gain_two,
        router_full,
        sg_full,
        su_full,
        sd_full,
    ) = (
        lax.all_gather(norm1_gain, "cols", axis=0, tiled=True),
        lax.all_gather(w_query, "cols", axis=0, tiled=True),
        lax.all_gather(key_matrix, "cols", axis=0, tiled=True),
        lax.all_gather(value_matrix, "cols", axis=0, tiled=True),
        lax.all_gather(w_out, "cols", axis=1, tiled=True),
        lax.all_gather(norm2_gain, "cols", axis=0, tiled=True),
        lax.all_gather(w_router, "cols", axis=0, tiled=True),
        lax.all_gather(shared_gate, "cols", axis=0, tiled=True),
        lax.all_gather(shared_up, "cols", axis=0, tiled=True),
        lax.all_gather(shared_down, "cols", axis=1, tiled=True),
    )
    model_width = full_in.shape[2]
    token_input = full_in.reshape(tok_dev, model_width).astype(jnp.float32)
    first_inverse_deviation = lax.rsqrt(
        jnp.mean(token_input * token_input, -1, keepdims=True) + NORM_EPS
    )
    first_unit_rows = token_input * first_inverse_deviation
    first_gain_float = gain_one.astype(jnp.float32)
    first_normed = (first_unit_rows * first_gain_float).astype(jnp.bfloat16)
    q_pre = matmul(first_normed, wq_full)
    key_unrotated = matmul(first_normed, wk_full)
    value_projected = matmul(first_normed, wv_full).astype(jnp.bfloat16)
    q_heads = q_pre.shape[1] // HEAD_DIM
    positions = col_idx * len_dev + jnp.arange(len_dev, dtype=jnp.int32)
    cosine_table, sine_table = rope_tables(positions, HEAD_DIM)
    rotated_queries = apply_rotary(
        q_pre.reshape(sequence_count, len_dev, q_heads, HEAD_DIM), cosine_table, sine_table
    ).astype(jnp.bfloat16)
    rotated_keys = apply_rotary(
        key_unrotated.reshape(sequence_count, len_dev, 1, HEAD_DIM), cosine_table, sine_table
    ).astype(jnp.bfloat16)
    kv_local = jnp.concatenate(
        [
            rotated_keys.reshape(sequence_count, len_dev, HEAD_DIM),
            value_projected.reshape(sequence_count, len_dev, HEAD_DIM),
        ],
        -1,
    )
    kv_local = jnp.swapaxes(kv_local, 0, 1)
    query_t = jnp.transpose(rotated_queries, (0, 2, 1, 3))
    score_scale = 1.0 / math.sqrt(HEAD_DIM)
    q_last = col_idx * len_dev + len_dev - 1

    def online_update(carry_in, key_part, k_start):
        run_max, run_sum, run_acc = carry_in
        block_len = key_part.shape[0]
        scores = (
            jnp.einsum(
                "shqd,bsd->shqb",
                query_t,
                key_part[:, :, :HEAD_DIM],
                preferred_element_type=jnp.float32,
            )
            * score_scale
        )
        key_pos = k_start + jnp.arange(block_len, dtype=jnp.int32)
        causal = positions[:, None] >= key_pos[None, :]
        scores = jnp.where(causal, scores, NEG_LARGE)
        new_max = jnp.maximum(run_max, jnp.max(scores, -1))
        prob_vals = jnp.where(causal, jnp.exp(scores - new_max[..., None]), 0.0)
        rescale = jnp.exp(run_max - new_max)
        run_sum = run_sum * rescale + jnp.sum(prob_vals, -1)
        run_acc = run_acc * rescale[..., None] + jnp.einsum(
            "shqb,bsd->shqd",
            prob_vals.astype(jnp.bfloat16),
            key_part[:, :, HEAD_DIM:],
            preferred_element_type=jnp.float32,
        )
        return (new_max, run_sum, run_acc)

    fold_start = (
        jnp.full((sequence_count, q_heads, len_dev), NEG_LARGE, jnp.float32),
        jnp.zeros((sequence_count, q_heads, len_dev), jnp.float32),
        jnp.zeros((sequence_count, q_heads, len_dev, HEAD_DIM), jnp.float32),
    )
    carry_in = fold_start
    piece = lax.all_gather(kv_local, "cols", axis=0, tiled=True)
    start = jnp.int32(0)
    piece_len = piece.shape[0]
    step_len = min(512, piece_len)
    for offset in range(0, piece_len, step_len):
        key_part = piece[offset : offset + step_len]
        k_start = start + offset

        def updated(state_in, key_part=key_part, k_start=k_start):
            return online_update(state_in, key_part, k_start)

        carry_in = lax.cond(k_start <= q_last, updated, keep_same, carry_in)
    run_max, run_sum, run_acc = carry_in
    attn_f32 = run_acc / run_sum[..., None]
    log_total = run_max + jnp.log(run_sum)
    attn_bf = attn_f32.astype(jnp.bfloat16)
    attn_rows = jnp.transpose(attn_bf, (0, 2, 1, 3)).reshape(tok_dev, q_heads * HEAD_DIM)
    attn_proj = lax.psum(matmul(attn_rows, wo_full).astype(jnp.bfloat16), "rows").astype(
        jnp.float32
    )
    residual_stream = token_input + attn_proj
    second_inverse_deviation = lax.rsqrt(
        jnp.mean(residual_stream * residual_stream, -1, keepdims=True) + NORM_EPS
    )
    second_unit_rows = residual_stream * second_inverse_deviation
    second_gain_float = gain_two.astype(jnp.float32)
    second_normed = (second_unit_rows * second_gain_float).astype(jnp.bfloat16)
    gate_pre = matmul(second_normed, sg_full)
    up_pre = matmul(second_normed, su_full)
    silu_gate, silu_slope = silu_parts(gate_pre)
    shared_act = (silu_gate * up_pre).astype(jnp.bfloat16)
    ffn_part = matmul(shared_act, sd_full)
    my_rows = row_idx * rows_dev
    normed_mine = lax.dynamic_slice_in_dim(second_normed, my_rows, rows_dev, 0)
    route_mine = routes.reshape(rows_dev, top_k)
    logits = matmul(normed_mine, router_full)
    expert_ids = jnp.arange(experts, dtype=jnp.int32)
    chosen_hot = (route_mine[:, :, None] == expert_ids[None, None, :]).astype(jnp.float32)
    chosen = jnp.sum(chosen_hot * logits[:, None, :], -1)
    gate_probs = jax.nn.softmax(chosen, -1)
    assign_count = rows_dev * top_k
    flat_routes = route_mine.reshape(assign_count)
    assign_hot = (flat_routes[:, None] == expert_ids[None, :]).astype(jnp.int32)
    rank_in = jnp.sum((jnp.cumsum(assign_hot, 0) - assign_hot) * assign_hot, 1)
    slot_of = flat_routes * capacity + rank_in
    assign_of_slot = (
        jnp.zeros((experts * capacity,), jnp.int32)
        .at[slot_of]
        .set(jnp.arange(assign_count, dtype=jnp.int32))
    )
    slot_used = jnp.zeros((experts * capacity,), jnp.int32).at[slot_of].set(1)
    slot_row = assign_of_slot // top_k

    def send_rows(slot_vals):
        slot_vals = slot_vals.reshape(experts, capacity, model_width)
        outgoing = jnp.broadcast_to(
            slot_vals[:, None], (experts, 2, capacity, model_width)
        ).reshape(devices, capacity, model_width)
        received = lax.all_to_all(
            outgoing, ("rows", "cols"), split_axis=0, concat_axis=0, tiled=True
        )
        return received.reshape(devices * capacity, model_width)

    def return_rows(slot_vals):
        returned = lax.all_to_all(
            slot_vals.reshape(devices, capacity, model_width),
            ("rows", "cols"),
            split_axis=0,
            concat_axis=0,
            tiled=True,
        )
        returned = returned.reshape(experts, 2, capacity, model_width).astype(jnp.float32)
        summed = (returned[:, 0] + returned[:, 1]).astype(jnp.bfloat16)
        return summed.reshape(experts * capacity, model_width).astype(jnp.float32)

    slot_inputs = jnp.where(slot_used[:, None] > 0, normed_mine[slot_row], 0)
    expert_rows = send_rows(slot_inputs)
    eg_mat = expert_gate.reshape(model_width, -1)
    eu_mat = expert_up.reshape(model_width, -1)
    ed_mat = expert_down.reshape(-1, model_width)
    e_gate = matmul(expert_rows, eg_mat)
    e_up = matmul(expert_rows, eu_mat)
    e_silu, e_slope = silu_parts(e_gate)
    e_act = (e_silu * e_up).astype(jnp.bfloat16)
    e_out = matmul(e_act, ed_mat).astype(jnp.bfloat16)
    expert_sum = return_rows(e_out)
    picked = expert_sum[slot_of].reshape(rows_dev, top_k, model_width)
    routed = jnp.sum(gate_probs[:, :, None] * picked, 1)
    ffn_full = lax.dynamic_update_slice_in_dim(
        ffn_part, lax.dynamic_slice_in_dim(ffn_part, my_rows, rows_dev, 0) + routed, my_rows, 0
    )
    ffn_mine = lax.psum_scatter(
        ffn_full.reshape(sequence_count, len_dev, model_width).astype(jnp.bfloat16),
        "rows",
        scatter_dimension=2,
        tiled=True,
    ).astype(jnp.float32)
    resid_mine = lax.dynamic_slice_in_dim(
        residual_stream.reshape(sequence_count, len_dev, model_width),
        row_idx * row_width,
        row_width,
        2,
    )
    layer_out = (resid_mine + ffn_mine).astype(jnp.bfloat16)
    grad_full = lax.all_gather(cotangent, "rows", axis=2, tiled=True).reshape(tok_dev, model_width)
    d_shared_act = matmul_nt(grad_full, sd_full)
    grad_sd = matmul_tn(shared_act, grad_full)
    d_gate_pre = (d_shared_act * up_pre * silu_slope).astype(jnp.bfloat16)
    d_up_pre = (d_shared_act * silu_gate).astype(jnp.bfloat16)
    grad_sg = matmul_tn(second_normed, d_gate_pre)
    grad_su = matmul_tn(second_normed, d_up_pre)
    grad_second_normed = matmul_nt(d_gate_pre, sg_full) + matmul_nt(d_up_pre, su_full)
    grad_mine = lax.dynamic_slice_in_dim(grad_full, my_rows, rows_dev, 0).astype(jnp.float32)
    d_gates = jnp.sum(grad_mine[:, None, :] * picked, -1)
    to_experts = (
        (gate_probs[:, :, None] * grad_mine[:, None, :])
        .reshape(assign_count, model_width)
        .astype(jnp.bfloat16)
    )
    slot_grads = jnp.where(slot_used[:, None] > 0, to_experts[assign_of_slot], 0)
    d_expert_out = send_rows(slot_grads)
    grad_ed = matmul_tn(e_act, d_expert_out)
    d_e_act = matmul_nt(d_expert_out, ed_mat)
    d_e_gate = (d_e_act * e_up * e_slope).astype(jnp.bfloat16)
    d_e_up = (d_e_act * e_silu).astype(jnp.bfloat16)
    grad_eg = matmul_tn(expert_rows, d_e_gate)
    grad_eu = matmul_tn(expert_rows, d_e_up)
    d_rows = (matmul_nt(d_e_gate, eg_mat) + matmul_nt(d_e_up, eu_mat)).astype(jnp.bfloat16)
    d_assign = return_rows(d_rows)[slot_of].reshape(rows_dev, top_k, model_width)
    d_routed_in = jnp.sum(d_assign, 1)
    d_chosen = gate_probs * (d_gates - jnp.sum(gate_probs * d_gates, -1, keepdims=True))
    d_logits = jnp.sum(chosen_hot * d_chosen[:, :, None], 1)
    router_f = router_full.astype(jnp.float32)
    grad_router_part = jnp.dot(normed_mine.astype(jnp.float32).T, d_logits, precision=PRECISE)
    d_router_in = jnp.dot(d_logits, router_f.T, precision=PRECISE)
    d_mine = (
        lax.dynamic_slice_in_dim(grad_second_normed, my_rows, rows_dev, 0)
        + d_routed_in
        + d_router_in
    )
    grad_second_normed = lax.dynamic_update_slice_in_dim(grad_second_normed, d_mine, my_rows, 0)
    grad_second_normed, grad_router = (
        lax.psum(grad_second_normed.astype(jnp.bfloat16), "rows").astype(jnp.float32),
        lax.psum(grad_router_part.astype(jnp.bfloat16), "rows").astype(jnp.float32),
    )
    grad_second_unit = grad_second_normed * second_gain_float
    second_gain_gradient = jnp.sum(grad_second_normed * second_unit_rows, 0)
    d_resid = grad_full.astype(jnp.float32) + second_inverse_deviation * (
        grad_second_unit
        - second_unit_rows * jnp.mean(grad_second_unit * second_unit_rows, -1, keepdims=True)
    )
    d_attn = d_resid.astype(jnp.bfloat16)
    grad_wo = matmul_tn(attn_rows, d_attn)
    d_heads = matmul_nt(d_attn, wo_full).astype(jnp.bfloat16)
    d_heads_t = jnp.transpose(
        d_heads.reshape(sequence_count, len_dev, q_heads, HEAD_DIM), (0, 2, 1, 3)
    )
    delta_rows = jnp.sum(d_heads_t.astype(jnp.float32) * attn_f32, -1)
    kv_all = lax.all_gather(kv_local, "cols", axis=0, tiled=True)
    seq_len = kv_all.shape[0]
    key_block = min(512, seq_len)

    def key_step(block_no, carry_in):
        k_start = block_no * key_block
        key_part = lax.dynamic_slice_in_dim(kv_all, k_start, key_block, 0)

        def contribute(state_in):
            d_query_in, d_kv_in = state_in
            keys_bf = key_part[:, :, :HEAD_DIM]
            values_bf = key_part[:, :, HEAD_DIM:]
            scores = (
                jnp.einsum("shqd,bsd->shqb", query_t, keys_bf, preferred_element_type=jnp.float32)
                * score_scale
            )
            key_pos = k_start + jnp.arange(key_block, dtype=jnp.int32)
            causal = positions[:, None] >= key_pos[None, :]
            prob_vals = jnp.where(causal, jnp.exp(scores - log_total[..., None]), 0.0)
            d_prob = jnp.einsum(
                "shqd,bsd->shqb", d_heads_t, values_bf, preferred_element_type=jnp.float32
            )
            d_scores = (prob_vals * (d_prob - delta_rows[..., None])).astype(jnp.bfloat16)
            d_query_in = (
                d_query_in
                + jnp.einsum(
                    "shqb,bsd->shqd", d_scores, keys_bf, preferred_element_type=jnp.float32
                )
                * score_scale
            )
            d_key = (
                jnp.einsum("shqb,shqd->bsd", d_scores, query_t, preferred_element_type=jnp.float32)
                * score_scale
            )
            d_value = jnp.einsum(
                "shqb,shqd->bsd",
                prob_vals.astype(jnp.bfloat16),
                d_heads_t,
                preferred_element_type=jnp.float32,
            )
            d_kv_in = lax.dynamic_update_slice_in_dim(
                d_kv_in, jnp.concatenate([d_key, d_value], -1), k_start, 0
            )
            return (d_query_in, d_kv_in)

        return lax.cond(k_start <= q_last, contribute, keep_same, carry_in)

    grad_start = (
        jnp.zeros((sequence_count, q_heads, len_dev, HEAD_DIM), jnp.float32),
        jnp.zeros((seq_len, sequence_count, 2 * HEAD_DIM), jnp.float32),
    )
    d_query, d_kv_all = lax.fori_loop(0, seq_len // key_block, key_step, grad_start)
    d_kv = lax.psum_scatter(
        d_kv_all.astype(jnp.bfloat16), "cols", scatter_dimension=0, tiled=True
    ).astype(jnp.float32)
    d_query_rows = (
        apply_rotary(jnp.transpose(d_query, (0, 2, 1, 3)), cosine_table, -sine_table)
        .reshape(tok_dev, q_heads * HEAD_DIM)
        .astype(jnp.bfloat16)
    )
    d_kv_t = jnp.swapaxes(d_kv, 0, 1)
    d_key_rows = (
        apply_rotary(
            d_kv_t[:, :, :HEAD_DIM].reshape(sequence_count, len_dev, 1, HEAD_DIM),
            cosine_table,
            -sine_table,
        )
        .reshape(tok_dev, HEAD_DIM)
        .astype(jnp.bfloat16)
    )
    d_value_rows = d_kv_t[:, :, HEAD_DIM:].reshape(tok_dev, HEAD_DIM).astype(jnp.bfloat16)
    grad_wq = matmul_tn(first_normed, d_query_rows)
    grad_wk = matmul_tn(first_normed, d_key_rows)
    grad_wv = matmul_tn(first_normed, d_value_rows)
    grad_first_normed = (
        matmul_nt(d_query_rows, wq_full)
        + matmul_nt(d_key_rows, wk_full)
        + matmul_nt(d_value_rows, wv_full)
    )
    grad_first_normed = lax.psum(grad_first_normed.astype(jnp.bfloat16), "rows").astype(jnp.float32)
    grad_first_unit = grad_first_normed * first_gain_float
    first_gain_gradient = jnp.sum(grad_first_normed * first_unit_rows, 0)
    d_input = d_resid + first_inverse_deviation * (
        grad_first_unit
        - first_unit_rows * jnp.mean(grad_first_unit * first_unit_rows, -1, keepdims=True)
    )
    grad_in = lax.dynamic_slice_in_dim(
        d_input.reshape(sequence_count, len_dev, model_width), row_idx * row_width, row_width, 2
    )
    g_gain_one, g_wq, g_wk, g_wv, g_wo, g_gain_two, g_router, g_sg, g_su, g_sd = (
        lax.psum_scatter(
            first_gain_gradient.astype(jnp.bfloat16), "cols", scatter_dimension=0, tiled=True
        ).astype(jnp.float32),
        lax.psum_scatter(
            grad_wq.astype(jnp.bfloat16), "cols", scatter_dimension=0, tiled=True
        ).astype(jnp.float32),
        lax.psum_scatter(
            grad_wk.astype(jnp.bfloat16), "cols", scatter_dimension=0, tiled=True
        ).astype(jnp.float32),
        lax.psum_scatter(
            grad_wv.astype(jnp.bfloat16), "cols", scatter_dimension=0, tiled=True
        ).astype(jnp.float32),
        lax.psum_scatter(
            grad_wo.astype(jnp.bfloat16), "cols", scatter_dimension=1, tiled=True
        ).astype(jnp.float32),
        lax.psum_scatter(
            second_gain_gradient.astype(jnp.bfloat16), "cols", scatter_dimension=0, tiled=True
        ).astype(jnp.float32),
        lax.psum_scatter(
            grad_router.astype(jnp.bfloat16), "cols", scatter_dimension=0, tiled=True
        ).astype(jnp.float32),
        lax.psum_scatter(
            grad_sg.astype(jnp.bfloat16), "cols", scatter_dimension=0, tiled=True
        ).astype(jnp.float32),
        lax.psum_scatter(
            grad_su.astype(jnp.bfloat16), "cols", scatter_dimension=0, tiled=True
        ).astype(jnp.float32),
        lax.psum_scatter(
            grad_sd.astype(jnp.bfloat16), "cols", scatter_dimension=1, tiled=True
        ).astype(jnp.float32),
    )
    return (
        layer_out,
        grad_in,
        g_gain_one,
        g_wq,
        g_wk,
        g_wv,
        g_wo,
        g_gain_two,
        g_router,
        g_sg,
        g_su,
        g_sd,
        grad_eg.reshape(expert_gate.shape),
        grad_eu.reshape(expert_up.shape),
        grad_ed.reshape(expert_down.shape),
    )


def scores_of(keys, queries, scale):
    return matmul_nt(keys, queries) * scale


def causal_mask(scores):
    key_pos = lax.broadcasted_iota(jnp.int32, scores.shape, 0)
    query_pos = lax.broadcasted_iota(jnp.int32, scores.shape, 1)
    return query_pos >= key_pos


MESH_ID = pl.DeviceIdType.MESH
MIB = 1024 * 1024


class Links:
    def __init__(self, n_rows, n_cols):
        self.n_rows, self.n_cols, self.ring = n_rows, n_cols, n_cols // 2
        self.r = lax.axis_index("rows")
        self.c = lax.axis_index("cols")
        self.z = lax.div(self.c, 2)
        self.k = lax.rem(self.c, 2)
        self.x = (self.flip(1), self.c)
        self.y = (self.flip(2), self.c)
        self.up = (self.r, lax.rem(self.c + 2, n_cols))
        self.down = (self.r, lax.rem(self.c + n_cols - 2, n_cols))
        self.twin = (self.r, self.c + 1 - 2 * self.k)
        self.started = []

    def flip(self, bits):
        low, high = lax.rem(self.r, 2), lax.div(self.r, 2)
        low = 1 - low if bits & 1 else low
        high = 1 - high if bits & 2 else high
        return low + 2 * high

    def chip(self, hops):
        return lax.rem(self.z + (2 * self.ring - hops), self.ring)

    def place(self, hops):
        other = self.chip(hops)
        low = lax.rem(lax.rem(self.r, 2) + lax.rem(other, 2), 2)
        high = lax.rem(lax.div(self.r, 2) + lax.div(other, 2), 2)
        return low + 2 * high

    def spread_partners(self):
        return [
            (hops, bits, (self.flip(bits), lax.rem(self.c + 2 * hops, self.n_cols)))
            for hops in range(self.ring)
            for bits in range(self.n_rows)
            if hops or bits
        ]

    def greet(self, partners):
        barrier = pltpu.get_barrier_semaphore()
        for partner in partners:
            pl.semaphore_signal(barrier, inc=1, device_id=partner, device_id_type=MESH_ID)
        pl.semaphore_wait(barrier, len(partners))

    def send(self, src, dst, sems, number, partner):
        copy = pltpu.make_async_remote_copy(
            src_ref=src,
            dst_ref=dst,
            send_sem=sems[0].at[number],
            recv_sem=sems[1].at[number],
            device_id=partner,
            device_id_type=MESH_ID,
        )
        copy.start()
        self.started.append(copy)
        return copy

    def settle(self, copies):
        for copy in copies:
            copy.wait_send()
            self.started = [other for other in self.started if other is not copy]

    def finish(self):
        for copy in self.started:
            copy.wait_send()


def run_together(*steps):
    live = list(steps)
    while live:
        live = [step for step in live if next(step, True) is None]


def pair_sems(count):
    return [pltpu.SemaphoreType.DMA((count,)), pltpu.SemaphoreType.DMA((count,))]


class SquareGather:
    def __init__(self, net, src, out, sems, local_sem, chunks, known=None):
        self.net, self.src, self.out, self.sems, self.chunks = net, src, out, sems, chunks
        self.rows, self.width = src.shape
        if known is None:
            self.own = pltpu.make_async_copy(src, self.block(0, 0), local_sem)
        else:
            self.own = pltpu.make_async_copy(known, out.at[0], local_sem)
        self.own.start()
        self.ups, self.xs, self.ys, self.lasts = {}, {}, {}, {}

    def block(self, s, j, part=None):
        columns = pl.ds(j * self.width, self.width)
        if part is None:
            return self.out.at[s, :, columns]
        half = self.rows // 2
        return self.out.at[s, pl.ds(part * half, half), columns]

    def up(self, s):
        if s:
            self.ups[s].wait_recv()
        if s < self.chunks - 1:
            whole = self.src if s == 0 else self.block(s, 0)
            self.ups[s + 1] = self.net.send(
                whole, self.block(s + 1, 0), self.sems, 7 * s, self.net.up
            )

    def across(self, s):
        half = self.rows // 2
        part_of = lambda p: (
            self.src.at[pl.ds(p * half, half), :] if s == 0 else self.block(s, 0, p)
        )
        send = self.net.send
        self.xs[s] = {
            p: send(part_of(p), self.block(s, 1, p), self.sems, 7 * s + 1 + p, self.net.x)
            for p in (0, 1)
        }
        self.ys[s] = {
            p: send(part_of(p), self.block(s, 2, p), self.sems, 7 * s + 3 + p, self.net.y)
            for p in (1, 0)
        }

    def forward(self, s):
        block, send = self.block, self.net.send
        self.xs[s][0].wait_recv()
        one = send(block(s, 1, 0), block(s, 3, 0), self.sems, 7 * s + 5, self.net.y)
        self.ys[s][1].wait_recv()
        two = send(block(s, 2, 1), block(s, 3, 1), self.sems, 7 * s + 6, self.net.x)
        self.lasts[s] = [one, two]

    def complete(self, s):
        self.xs[s][1].wait_recv()
        self.ys[s][0].wait_recv()
        for copy in self.lasts[s]:
            copy.wait_recv()


def gather_square(net, src, out, sems, local_sem, chunks):
    gather = SquareGather(net, src, out, sems, local_sem, chunks)
    gather.across(0)
    yield
    if chunks > 1:
        gather.up(0)
        yield
    gather.forward(0)
    yield
    for s in range(1, chunks):
        gather.up(s)
        gather.across(s)
        yield
        gather.forward(s)
        yield
    gather.own.wait()
    for s in range(chunks):
        gather.complete(s)


def gather_columns(net, src, spot, sems, local_sem=None):
    if local_sem is not None:
        own = pltpu.make_async_copy(src, spot(0, net.k), local_sem)
        own.start()
    twins = []
    for hops in range(net.ring):
        if hops:
            up.wait_recv()
        here = src if hops == 0 else spot(hops, net.k)
        if hops < net.ring - 1:
            up = net.send(here, spot(hops, net.k), sems, hops, net.up)
        twins.append(net.send(here, spot(hops, net.k), sems, net.ring + hops, net.twin))
        yield
    if local_sem is not None:
        own.wait()
    for copy in twins:
        copy.wait_recv()


def add_slabs(target, terms, slab=64):
    rows = target.shape[0]

    @pl.loop(0, rows // slab)
    def _(i):
        at = pl.ds(pl.multiple_of(i * slab, slab), slab)
        total = terms[0](at)
        for term in terms[1:]:
            total = total + term(at)
        target[at, :] = total.astype(target.dtype)


def part_reader(ref, *lead, columns=None):
    def read(at):
        values = ref[(*lead, at, slice(None) if columns is None else columns)]
        return values.astype(jnp.float32)

    return read


def scatter_scratch(chunks, rows, width, resident=False):
    half = rows // 2
    kept = (1, 2, 16, 128) if resident else (chunks, 2, half, width)
    return [
        pltpu.VMEM(kept, jnp.bfloat16),
        pltpu.VMEM(kept[:1] + kept[2:] if resident else (chunks, half, 2 * width), jnp.bfloat16),
        pltpu.VMEM((chunks, 2, half, width), jnp.bfloat16),
        pltpu.VMEM((chunks, half, 2 * width), jnp.bfloat16),
        pltpu.VMEM((chunks, 2, half, width), jnp.bfloat16),
        pltpu.VMEM((chunks, 2, half, width), jnp.bfloat16),
        pltpu.SemaphoreType.DMA((chunks, 3)),
    ] + pair_sems(6 * chunks)


class SquareScatter:
    def __init__(self, net, scratch, resident=False):
        self.net, self.resident = net, resident
        self.my_up, self.my_low, self.got_x, self.got_y, self.got_last = scratch[:5]
        self.stage, self.load_sems, *self.sems = scratch[5:]
        self.half, self.width = self.got_x.shape[2:]
        self.src, self.loads, self.sent = {}, {}, {}
        self.left, self.right = pl.ds(0, self.width), pl.ds(self.width, self.width)

    def part(self, i, part, j, count=1):
        rows = pl.ds(part * self.half, self.half)
        return self.src[i].at[rows, pl.ds(j * self.width, count * self.width)]

    def mine(self, i, part, j):
        if self.resident:
            return part_reader(self.part(i, part, j))
        if part == 0:
            return part_reader(self.my_up, i, j // 2)
        return part_reader(self.my_low, i, columns=(self.left, self.right)[j])

    def give(self, i, src, j):
        self.src[i] = src
        net, sems = self.net, self.sems
        sent = self.sent.setdefault(i, {})
        if j & 1:
            sent["x", j] = net.send(
                self.part(i, 0, j), self.got_x.at[i, j // 2], sems, 6 * i + j // 2, net.x
            )
        if j & 2:
            columns = pl.ds((j - 2) * self.width, self.width)
            sent["y", j] = net.send(
                self.part(i, 1, j), self.got_y.at[i, :, columns], sems, 6 * i + j, net.y
            )

    def first(self, i, src):
        for j in (3, 1, 2):
            self.give(i, src, j)
        if not self.resident:
            load = pltpu.make_async_copy
            self.loads[i] = [
                load(self.part(i, 0, 0), self.my_up.at[i, 0], self.load_sems.at[i, 0]),
                load(self.part(i, 0, 2), self.my_up.at[i, 1], self.load_sems.at[i, 1]),
                load(self.part(i, 1, 0, 2), self.my_low.at[i], self.load_sems.at[i, 2]),
            ]
            for copy in self.loads[i]:
                copy.start()

    def second(self, i):
        net, sent, sems = self.net, self.sent[i], self.sems
        for copy in self.loads.get(i, []):
            copy.wait()
        sent["x", 3].wait_recv()
        add_slabs(self.stage.at[i, 0], [self.mine(i, 0, 2), part_reader(self.got_x, i, 1)])
        sent["up"] = net.send(self.stage.at[i, 0], self.got_last.at[i, 0], sems, 6 * i + 4, net.y)
        sent["y", 3].wait_recv()
        add_slabs(
            self.stage.at[i, 1],
            [self.mine(i, 1, 1), part_reader(self.got_y, i, columns=self.right)],
        )
        sent["low"] = net.send(self.stage.at[i, 1], self.got_last.at[i, 1], sems, 6 * i + 5, net.x)

    def third(self, i):
        for key in (("x", 1), ("y", 2), "up", "low"):
            self.sent[i][key].wait_recv()
        upper = [
            self.mine(i, 0, 0), part_reader(self.got_x, i, 0), part_reader(self.got_last, i, 0)
        ]
        lower = [
            self.mine(i, 1, 0),
            part_reader(self.got_y, i, columns=self.left),
            part_reader(self.got_last, i, 1),
        ]
        return upper, lower

    def release(self, i):
        self.net.settle([self.sent[i][key] for key in (("x", 3), ("y", 3), ("x", 1), ("y", 2))])


def scatter_square(net, src, scratch, order, finish, resident=False):
    scatter = SquareScatter(net, scratch, resident)
    for i in range(len(order) + 2):
        if i < len(order):
            scatter.first(i, src.at[order[i]])
            yield
        if 0 <= i - 1 < len(order):
            scatter.second(i - 1)
            yield
        if 0 <= i - 2:
            finish(order[i - 2], *scatter.third(i - 2))
            yield


def ring_scratch(ring, rows, width):
    return [
        pltpu.VMEM((ring - 1, rows, width), jnp.bfloat16),
        pltpu.VMEM((ring - 1, rows, width), jnp.bfloat16),
    ] + pair_sems(ring - 1)


def ring_finish(net, scratch, target, copies):
    landed, leaving, *sems = scratch
    rows = landed.shape[1]

    def finish(s, upper, lower):
        turn = (s - 1) % net.ring
        for part, terms in ((0, upper), (1, lower)):
            at = pl.ds(part * (rows // 2), rows // 2)
            if turn and not part:
                copies[turn - 1].wait_recv()
            if turn:
                terms = terms + [part_reader(landed.at[turn - 1, at, :])]
            goal = target.at[at, :] if s == 0 else leaving.at[turn, at, :]
            add_slabs(goal, terms)
        if s:
            copies.append(net.send(leaving.at[turn], landed.at[turn], sems, turn, net.up))

    return finish


def scatter_columns(net, part, out, scratch):
    got_twin, landed, leaving, twin_send, twin_recv, *sems = scratch
    twins, copies = {}, []
    order = list(range(1, net.ring)) + [0]
    for hops in order:
        twins[hops] = net.send(
            part(hops, 1 - net.k), got_twin.at[hops], (twin_send, twin_recv), hops, net.twin
        )
    yield
    for turn, hops in enumerate(order):
        twins[hops].wait_recv()
        terms = [part_reader(part(hops, net.k)), part_reader(got_twin, hops)]
        if turn:
            copies[turn - 1].wait_recv()
            terms.append(part_reader(landed, turn - 1))
        add_slabs(leaving.at[turn] if hops else out, terms, 32)
        if hops:
            copies.append(net.send(leaving.at[turn], landed.at[turn], sems, turn, net.up))
        yield


def scatter_columns_scratch(ring, rows, width):
    return [
        pltpu.VMEM((ring, rows, width), jnp.bfloat16),
        pltpu.VMEM((ring - 1, rows, width), jnp.bfloat16),
        pltpu.VMEM((ring - 1, rows, width), jnp.bfloat16),
    ] + pair_sems(ring) + pair_sems(ring - 1)


def remote_call(kernel, name, collective_id, out_shape, scratch, operands, in_vmem=(), out_vmem=(), cost=None):
    anywhere = pl.BlockSpec(memory_space=pl.ANY)
    vmem = pl.BlockSpec(memory_space=pltpu.VMEM)
    return pl.pallas_call(
        kernel,
        out_shape=out_shape,
        in_specs=[vmem if i in in_vmem else anywhere for i in range(len(operands))],
        out_specs=[vmem if i in out_vmem else anywhere for i in range(len(out_shape))],
        scratch_shapes=scratch,
        compiler_params=pltpu.CompilerParams(
            collective_id=collective_id, has_side_effects=True, vmem_limit_bytes=63 * MIB
        ),
        cost_estimate=cost,
        name=name,
    )(*operands)


def spread_columns(net, packed, spot, sems, local_sem):
    own = pltpu.make_async_copy(packed.at[net.chip(0)], spot(0, net.k), local_sem)
    own.start()
    pieces = []
    for hops in range(1, net.ring):
        target = (net.r, lax.rem(net.c + 2 * hops, net.n_cols))
        pieces.append(
            net.send(packed.at[net.chip(-hops)], spot_at(spot, net, hops), sems, hops, target)
        )
    yield
    own.wait()
    twins = [net.send(spot(0, net.k), spot(0, net.k), sems, net.ring, net.twin)]
    yield
    for hops in range(1, net.ring):
        pieces[hops - 1].wait_recv()
        here = spot(hops, net.k)
        twins.append(net.send(here, here, sems, net.ring + hops, net.twin))
        yield
    for copy in twins:
        copy.wait_recv()


def spot_at(spot, net, hops):
    return spot(0, net.k)


def first_phase(n_rows, n_cols, block, grads, weights, small, weights_out, packed, slot_map, tables):
    ring = n_cols // 2
    length, row_width = block.shape
    model = n_rows * row_width
    col_width, in_width = weights.shape
    q_width = weights_out.shape[1]
    heads = q_width // HEAD_DIM
    small_width = small.shape[1]
    experts = slot_map.shape[0]
    scale = 1.0 / math.sqrt(HEAD_DIM)
    pieces = 2
    piece = length // pieces
    bf16, f32 = jnp.bfloat16, jnp.float32
    shape = jax.ShapeDtypeStruct

    def kernel(
        x_in, g_in, w_in, small_in, wo_in, packed_in, map_in, cosine, sine,
        x_out, normed_out, w_out, small_out, q, kv_out, out, lse, wo_out, g_out, second, map_out,
        shared_out, sum_out, gains_out, scale_out,
        x, normed, w, small_all, kv, wo, proj, proj_sum, result, projected, top, total, acc,
        *sems,
    ):
        scratch, sems = list(sems[:9]), list(sems[9:])
        pairs = lambda: (sems.pop(0), sems.pop(0))
        x_sems, g_sems, w_sems, small_sems, wo_sems, kv_sems = [pairs() for _ in range(6)]
        map_sems, shared_sems, sum_sems, sum_sems_two, u_sems = [pairs() for _ in range(5)]
        local = sems.pop(0)
        net = Links(n_rows, n_cols)
        others = net.spread_partners()
        net.greet([device for _, _, device in others] + [net.twin])
        by_place = lambda ref, columns=slice(None): lambda hops, core: ref.at[
            pl.ds((net.place(hops) * 2 + core) * col_width, col_width), columns
        ]
        for_q, for_kv = pl.ds(0, q_width), pl.ds(q_width, 2 * HEAD_DIM)

        x_steps = gather_square(net, x_in, x, x_sems, local.at[0], 1)
        small_steps = gather_columns(net, small_in, by_place(small_all), small_sems, local.at[1])
        w_steps = gather_columns(net, w_in.at[:, for_q], by_place(w, for_q), w_sems, local.at[2])
        u_steps = gather_columns(net, w_in.at[:, for_kv], by_place(w, for_kv), u_sems, local.at[18])
        wo_steps = gather_columns(net, wo_in, by_place(wo), wo_sems, local.at[3])
        g_steps = gather_square(net, g_in, g_out, g_sems, local.at[4], ring)
        saves = []

        def save(src, dst):
            copy = pltpu.make_async_copy(src, dst, local.at[8 + len(saves)])
            copy.start()
            saves.append(copy)

        next(small_steps)
        next(u_steps)
        next(x_steps)
        next(w_steps)
        maps = []
        for number, (hops, bits, device) in enumerate(others):
            maps.append(net.send(map_in, map_out.at[hops, net.r], map_sems, number, device))
        own_map = pltpu.make_async_copy(map_in, map_out.at[0, net.r], local.at[5])
        own_map.start()
        next(small_steps)
        next(u_steps)
        next(w_steps)
        next(x_steps)
        next(g_steps)
        next(small_steps)
        next(u_steps)
        next(small_steps)
        next(u_steps)
        next(w_steps)
        run_together(x_steps, small_steps)
        save(x.at[0], x_out)
        save(small_all, small_out)
        gains = small_all[...].astype(f32).T
        gains_out[...] = gains[experts : experts + 8]
        first_gain = gains[experts : experts + 1]
        second_gain = gains[experts + 1 : experts + 2]

        @pl.loop(0, length // 64)
        def _(i):
            at = pl.ds(pl.multiple_of(i * 64, 64), 64)
            values = x[0, at, :].astype(f32)
            inverse = lax.rsqrt(jnp.mean(values * values, -1, keepdims=True) + NORM_EPS)
            normed[at, :] = (values * inverse * first_gain).astype(bf16)
            scale_out[at, :] = jnp.broadcast_to(inverse, (64, 128))

        save(normed, normed_out)
        def rotate(columns):
            values = projected[:, columns]
            turned = pltpu.roll(values, HEAD_DIM // 2, 1)
            return (values * cosine[...] + turned * sine[...]).astype(bf16)

        run_together(u_steps)
        projected[:, for_kv] = matmul(normed[...], w[:, for_kv])
        kv[net.c, :, :HEAD_DIM] = rotate(slice(q_width, q_width + HEAD_DIM))
        kv[net.c, :, HEAD_DIM:] = projected[:, q_width + HEAD_DIM :].astype(bf16)
        kv_steps = gather_columns(
            net, kv.at[net.c], lambda hops, core: kv.at[2 * net.chip(hops) + core], kv_sems
        )
        next(kv_steps)
        next(w_steps)
        next(kv_steps)
        run_together(w_steps)
        save(w, w_out)
        next(wo_steps)
        next(g_steps)
        projected[:, for_q] = matmul(normed[...], w[:, for_q])
        for head in range(heads):
            columns = slice(head * HEAD_DIM, (head + 1) * HEAD_DIM)
            q[:, columns] = rotate(columns)
        next(kv_steps)
        next(g_steps)
        next(kv_steps)
        next(wo_steps)
        run_together(kv_steps)
        save(kv, kv_out)
        next(wo_steps)
        next(g_steps)

        for head in range(heads):
            columns = slice(head * HEAD_DIM, (head + 1) * HEAD_DIM)
            queries = q[:, columns]

            def part(number):
                return scores_of(kv[number, :, :HEAD_DIM], queries, scale), kv[number, :, HEAD_DIM:]

            scores, values = part(net.c)
            scores = jnp.where(causal_mask(scores), scores, NEG_LARGE)
            high = jnp.max(scores, 0, keepdims=True)
            probs = jnp.exp(scores - high)
            top[...] = high
            total[...] = jnp.sum(probs, 0, keepdims=True)
            acc[...] = matmul_tn(values, probs.astype(bf16))

            @pl.loop(0, net.c)
            def _(number):
                scores, values = part(number)
                high = jnp.maximum(top[...], jnp.max(scores, 0, keepdims=True))
                probs = jnp.exp(scores - high)
                shrink = jnp.exp(top[...] - high)
                top[...] = high
                total[...] = total[...] * shrink + jnp.sum(probs, 0, keepdims=True)
                acc[...] = acc[...] * shrink + matmul_tn(values, probs.astype(bf16))

            out[:, columns] = (acc[...] / total[...]).T
            lse[head] = top[...] + jnp.log(total[...])
            if head == 0:
                next(g_steps)
            if head == 2:
                next(wo_steps)
            if head == 3:
                next(g_steps)

        run_together(wo_steps)
        save(wo, wo_out)
        heads_out = out[...].astype(bf16)
        for s in range(pieces):
            for j in range(n_rows):
                at = slice(j * row_width, (j + 1) * row_width)
                proj[s, :, at] = matmul_nt(
                    heads_out[s * piece : (s + 1) * piece], wo[at, :]
                ).astype(bf16)
        gathers = []

        def finish(s, upper, lower):
            add_slabs(result.at[s, pl.ds(0, piece // 2), :], upper)
            add_slabs(result.at[s, pl.ds(piece // 2, piece // 2), :], lower)
            steps = gather_square(
                net, result.at[s], proj_sum.at[pl.ds(s, 1)], (sum_sems, sum_sems_two)[s],
                local.at[6 + s], 1,
            )
            next(steps)
            gathers.append(steps)

        shared_steps = spread_columns(
            net, packed_in, by_place(shared_out), shared_sems, local.at[8 + 8]
        )
        sum_steps = scatter_square(net, proj, scratch, list(range(pieces)), finish, resident=True)
        next(sum_steps)
        next(shared_steps)
        next(sum_steps)
        run_together(sum_steps)
        next(shared_steps)

        def second_norm(s):
            @pl.loop(0, piece // 64)
            def _(i):
                at = pl.ds(pl.multiple_of(i * 64, 64), 64)
                there = pl.ds(pl.multiple_of(s * piece + i * 64, 64), 64)
                values = x[0, there, :].astype(f32) + proj_sum[s, at, :].astype(f32)
                inverse = lax.rsqrt(jnp.mean(values * values, -1, keepdims=True) + NORM_EPS)
                second[there, :] = (values * inverse * second_gain).astype(bf16)

        for s in range(pieces):
            run_together(gathers[s])
            second_norm(s)
        save(proj_sum, sum_out)
        run_together(g_steps, shared_steps)
        own_map.wait()
        for copy in maps:
            copy.wait_recv()
        for copy in saves:
            copy.wait()
        net.finish()

    partners = n_rows * ring - 1
    vmem = pltpu.VMEM
    return remote_call(
        kernel,
        "first_phase",
        1,
        [
            shape((length, model), bf16),
            shape((length, model), bf16),
            shape((model, in_width), bf16),
            shape((model, small_width), bf16),
            shape((length, q_width), bf16),
            shape((n_cols, length, 2 * HEAD_DIM), bf16),
            shape((length, q_width), f32),
            shape((heads, 1, length), f32),
            shape((model, q_width), bf16),
            shape((ring, length, model), bf16),
            shape((length, model), bf16),
            shape((ring, n_rows, *slot_map.shape), f32),
            shape((model, packed.shape[2]), bf16),
            shape((pieces, piece, model), bf16),
            shape((8, model), f32),
            shape((length, 128), f32),
        ],
        [
            vmem((1, length, model), bf16),
            vmem((length, model), bf16),
            vmem((model, in_width), bf16),
            vmem((model, small_width), bf16),
            vmem((n_cols, length, 2 * HEAD_DIM), bf16),
            vmem((model, q_width), bf16),
            vmem((pieces, piece, model), bf16),
            vmem((pieces, piece, model), bf16),
            vmem((pieces, piece, row_width), bf16),
            vmem((length, in_width), f32),
            vmem((1, length), f32),
            vmem((1, length), f32),
            vmem((HEAD_DIM, length), f32),
        ]
        + scatter_scratch(pieces, piece, row_width, resident=True)
        + pair_sems(7)
        + pair_sems(7 * ring)
        + pair_sems(2 * ring)
        + pair_sems(2 * ring)
        + pair_sems(2 * ring)
        + pair_sems(2 * ring)
        + pair_sems(partners)
        + pair_sems(2 * ring)
        + pair_sems(7)
        + pair_sems(7)
        + pair_sems(2 * ring)
        + [pltpu.SemaphoreType.DMA((19,))],
        (block, grads, weights, small, weights_out, packed, slot_map, *tables),
        in_vmem=(7, 8),
        out_vmem=(4, 6, 7, 10, 14, 15),
    )


def experts_phase(n_rows, n_cols, second, grads, maps, experts_w, shared, router, slots):
    ring = n_cols // 2
    tokens, model = second.shape
    width = model // n_rows
    experts = n_rows * ring
    half_hidden = experts_w[0].shape[1]
    hidden = 2 * half_hidden
    pad = shared.shape[1] // 3
    blocks, _, block_rows = maps.shape[1:]
    n_slots = blocks * slots
    bf16, f32 = jnp.bfloat16, jnp.float32
    shape = jax.ShapeDtypeStruct

    def kernel(
        known, g_in, maps, gate_own, gate_twin, up_own, up_twin, down_own, down_twin, shared_in,
        router_in,
        result, rows_out, y_out, slot_out, d_part_out, act_out, d_gate_out, d_up_out, s_act_out,
        d_shared_out, probs_out, gate_out,
        w_gate, w_up, w_down, shared, router, x, g, slot_rows, part, e_act, d_gate, d_up, s_act,
        d_shared, probs, d_x, d_gates, *rest,
    ):
        scratch, (landed, leaving, ring_s, ring_r) = rest[:9], rest[9:13]
        xs, xr, ms, mr, local, w_sems, out_sems = rest[13:]
        net = Links(n_rows, n_cols)
        others = net.spread_partners()
        net.greet([device for _, _, device in others])
        mine = net.r * ring + net.z
        gather = SquareGather(
            net, known.at[:, pl.ds(0, width)], rows_out, (xs, xr), local.at[0], ring, known=known
        )
        gather.up(0)
        x_load = lambda s: pltpu.make_async_copy(
            known if s == 0 else rows_out.at[s], x, local.at[1]
        )
        g_load = lambda s: pltpu.make_async_copy(g_in.at[s], g, local.at[2])
        x_load(0).start()
        g_load(0).start()
        shared_load = pltpu.make_async_copy(shared_in, shared, local.at[3])
        shared_load.start()
        router_load = pltpu.make_async_copy(router_in, router, local.at[4])
        router_load.start()
        weights = []
        for j in range(n_rows):
            there = pl.ds(pl.multiple_of(net.flip(j) * width, width), width)
            here = pl.ds(j * width, width)
            for h, sources in enumerate(((gate_own, up_own, down_own), (gate_twin, up_twin, down_twin))):
                cols = pl.ds(h * half_hidden, half_hidden)
                number = 6 * j + 3 * h
                weights += [
                    pltpu.make_async_copy(
                        sources[0].at[there, :], w_gate.at[here, cols], w_sems.at[number]
                    ),
                    pltpu.make_async_copy(
                        sources[1].at[there, :], w_up.at[here, cols], w_sems.at[number + 1]
                    ),
                    pltpu.make_async_copy(
                        sources[2].at[:, there], w_down.at[cols, here], w_sems.at[number + 2]
                    ),
                ]
        scatter = SquareScatter(net, scratch, resident=True)
        ring_copies, stores = {}, {}
        kept = {
            "slot": (slot_rows, slot_out), "part": (part, d_part_out), "act": (e_act, act_out),
            "d_gate": (d_gate, d_gate_out), "d_up": (d_up, d_up_out), "s_act": (s_act, s_act_out),
            "d_shared": (d_shared, d_shared_out), "probs": (probs, probs_out), "y": (g, y_out),
        }

        def store(s, *names):
            for name in names:
                source, target = kept[name]
                number = list(kept).index(name)
                stores[name] = pltpu.make_async_copy(source, target.at[s], out_sems.at[number])
                stores[name].start()

        def stored(*names):
            for name in names:
                if name in stores:
                    stores.pop(name).wait()

        def pass_on(s):
            turn = s - 1
            for p, terms in enumerate(scatter.third(s)):
                at = pl.ds(p * (tokens // 2), tokens // 2)
                if s == 0:
                    add_slabs(result.at[at, :], terms)
                    continue
                if turn:
                    ring_copies[turn - 1, p].wait_recv()
                    terms = terms + [part_reader(landed.at[turn - 1, at, :])]
                if turn > 1:
                    net.settle([ring_copies[turn - 2, p]])
                add_slabs(leaving.at[turn % 2, at, :], terms)
                ring_copies[turn, p] = net.send(
                    leaving.at[turn % 2, at, :], landed.at[turn, at, :], (ring_s, ring_r),
                    2 * turn + p, net.up,
                )

        def in_lanes(column):
            high = column.astype(bf16)
            rest = column - high.astype(f32)
            middle = rest.astype(bf16)
            low = (rest - middle.astype(f32)).astype(bf16)
            lane = lax.broadcasted_iota(jnp.int32, (column.shape[0], 128), 1)
            terms = jnp.where(lane == 0, high.astype(f32), 0.0)
            terms = jnp.where(lane == 1, middle.astype(f32), terms)
            return jnp.where(lane == 2, low.astype(f32), terms).astype(bf16)

        tile = 512

        def compute(s, ticks):
            def tick(name):
                for step in ticks.get(name, []):
                    step()

            lanes = lax.broadcasted_iota(jnp.int32, (1, 128), 1)
            mine_hot = (lanes == mine).astype(f32)
            slot_row, slot_column, chosen = [], [], []
            for b in range(blocks):
                own_map = jnp.where(
                    lax.broadcasted_iota(jnp.int32, (experts, block_rows), 0) == mine, maps[s, b], 0.0
                )
                own_map = jnp.sum(own_map, 0, keepdims=True)
                slot_row.append(jnp.where(own_map >= 0, own_map + b * slots, -1.0))
                filled = jnp.concatenate(
                    [maps[s, b], jnp.full((128 - experts, block_rows), -1.0, f32)], 0
                ).T
                chosen.append(filled)
                own_map = jnp.sum(filled * mine_hot, -1, keepdims=True)
                slot_column.append(jnp.where(own_map >= 0, own_map + b * slots, -1.0))
            slot_row, chosen = jnp.concatenate(slot_row, 1), jnp.concatenate(chosen, 0)
            slot_column = jnp.concatenate(slot_column, 0)
            numbers = lambda dims, axis: lax.broadcasted_iota(jnp.int32, dims, axis).astype(f32)
            pick = (numbers((n_slots, tokens), 0) == slot_row).astype(f32).astype(bf16)
            pick_t = (numbers((tokens, n_slots), 1) == slot_column).astype(f32).astype(bf16)

            stored("probs", "s_act", "d_shared", "y")
            if s:
                g_load(s).start()
            x_load(s).wait()
            if s == 0:
                router_load.wait()
                shared_load.wait()
                g_load(0).wait()
                for copy in weights:
                    copy.start()
            logits = matmul(x[...], router[...])
            logits = jnp.where(chosen >= 0, logits, NEG_LARGE)
            logits = jnp.exp(logits - jnp.max(logits, -1, keepdims=True))
            gate_probs = logits / jnp.sum(logits, -1, keepdims=True)
            probs[...] = gate_probs
            my_gate = jnp.sum(gate_probs * mine_hot, -1, keepdims=True)
            slot_gate = jnp.sum(matmul(pick, in_lanes(my_gate)), -1, keepdims=True)
            s_gate = matmul(x[...], shared[:, :pad])
            s_up = matmul(x[...], shared[:, pad : 2 * pad])
            if s:
                g_load(s).wait()
            through = matmul(g[...], shared[:, 2 * pad :])
            s_silu, s_slope = silu_parts(s_gate)
            s_act[...] = (s_silu * s_up).astype(bf16)
            d_shared[:, :pad] = (through * s_up * s_slope).astype(bf16)
            d_shared[:, pad:] = (through * s_silu).astype(bf16)
            store(s, "probs", "s_act", "d_shared")
            tick("shared")

            stored("slot", "part", "act", "d_gate", "d_up")
            for t in range(model // tile):
                at = slice(t * tile, (t + 1) * tile)
                slot_rows[:, at] = matmul(pick, x[:, at]).astype(bf16)
                part[:, at] = matmul(pick, g[:, at]).astype(bf16)
            if s == 0:
                for copy in weights:
                    copy.wait()
            tick("picked")

            step = half_hidden // 3

            def hidden_tile(t, total):
                at = pl.ds(pl.multiple_of(t * step, step), step)
                e_gate = matmul(slot_rows[...], w_gate[:, at])
                e_up = matmul(slot_rows[...], w_up[:, at])
                through = matmul_nt(part[...], w_down[at, :])
                e_silu, e_slope = silu_parts(e_gate)
                act = e_silu * e_up
                d_act = through * slot_gate
                e_act[:, at] = act.astype(bf16)
                d_gate[:, at] = (d_act * e_up * e_slope).astype(bf16)
                d_up[:, at] = (d_act * e_silu).astype(bf16)
                return total + jnp.sum(act * through, -1, keepdims=True)

            d_slot_gate = lax.fori_loop(0, 3, hidden_tile, jnp.zeros((n_slots, 1), f32))
            tick("half")
            d_slot_gate = lax.fori_loop(3, 6, hidden_tile, d_slot_gate)
            d_gates[net.chip(s)] = jnp.sum(
                matmul_tn(in_lanes(d_slot_gate), pick), 0, keepdims=True
            )
            part[...] = (part[...].astype(f32) * slot_gate).astype(bf16)
            store(s, "slot", "part", "act", "d_gate", "d_up")
            tick("hidden")

            d_chunk = d_x.at[s % 2]
            if s >= 2:
                scatter.release(s - 2)
            def out_tile(t):
                at = pl.ds(pl.multiple_of(t * tile, tile), tile)
                d_slot = matmul_nt(d_gate[...], w_gate[at, :]) + matmul_nt(d_up[...], w_up[at, :])
                d_chunk[:, at] = (
                    matmul(pick_t, d_slot.astype(bf16))
                    + matmul_nt(d_shared[...], shared[at, : 2 * pad])
                ).astype(bf16)
                out = (matmul(e_act[...], w_down[:, at]) * slot_gate).astype(bf16)
                g[:, at] = (
                    matmul(pick_t, out) + matmul_nt(s_act[...], shared[at, 2 * pad :])
                ).astype(bf16)

            pl.loop(2, 5)(out_tile)
            scatter.give(s, d_chunk, 3)
            scatter.give(s, d_chunk, 2)
            tick("right")
            pl.loop(0, 2)(out_tile)
            scatter.give(s, d_chunk, 1)
            store(s, "y")
            tick("left")

        def arrive(s):
            def step():
                gather.up(s)
                gather.across(s)

            return step

        def take(s):
            def step():
                gather.complete(s)
                x_load(s).start()

            return step

        pass_x = lambda s: lambda: gather.forward(s)
        second_of = lambda s: lambda: scatter.second(s)
        third_of = lambda s: lambda: pass_on(s)
        compute(0, {"hidden": [arrive(1)], "left": [pass_x(1), arrive(2), take(1)]})
        compute(
            1,
            {
                "half": [pass_x(2), arrive(3)],
                "hidden": [second_of(0)],
                "left": [third_of(0), take(2)],
            },
        )
        compute(2, {"picked": [pass_x(3)], "hidden": [second_of(1)], "left": [third_of(1), take(3)]})
        compute(3, {"hidden": [second_of(2)], "left": [third_of(2)]})
        copies = []
        own = pltpu.make_async_copy(d_gates, gate_out.at[mine], local.at[5])
        own.start()
        for number, (hops, bits, device) in enumerate(others):
            copies.append(net.send(d_gates, gate_out.at[mine], (ms, mr), number, device))
        scatter.second(3)
        pass_on(3)
        for p in range(2):
            at = pl.ds(p * (tokens // 2), tokens // 2)
            ring_copies[ring - 2, p].wait_recv()
            add_slabs(
                result.at[at, :], [part_reader(result.at[at, :]), part_reader(landed.at[ring - 2, at, :])]
            )
        stored(*kept)
        own.wait()
        gather.own.wait()
        for copy in copies:
            copy.wait_recv()
        net.finish()

    vmem = pltpu.VMEM
    by_chunk = lambda dtype, *dims: shape((ring, *dims), dtype)
    return remote_call(
        kernel,
        "experts_phase",
        5,
        [
            shape((tokens, width), bf16),
            by_chunk(bf16, tokens, model),
            by_chunk(bf16, tokens, model),
            by_chunk(bf16, n_slots, model),
            by_chunk(bf16, n_slots, model),
            by_chunk(bf16, n_slots, hidden),
            by_chunk(bf16, n_slots, hidden),
            by_chunk(bf16, n_slots, hidden),
            by_chunk(bf16, tokens, pad),
            by_chunk(bf16, tokens, 2 * pad),
            by_chunk(f32, tokens, 128),
            shape((experts, ring, 1, tokens), f32),
        ],
        [
            vmem((model, hidden), bf16),
            vmem((model, hidden), bf16),
            vmem((hidden, model), bf16),
            vmem(shared.shape, bf16),
            vmem(router.shape, bf16),
            vmem((tokens, model), bf16),
            vmem((tokens, model), bf16),
            vmem((n_slots, model), bf16),
            vmem((n_slots, model), bf16),
            vmem((n_slots, hidden), bf16),
            vmem((n_slots, hidden), bf16),
            vmem((n_slots, hidden), bf16),
            vmem((tokens, pad), bf16),
            vmem((tokens, 2 * pad), bf16),
            vmem((tokens, 128), f32),
            vmem((2, tokens, model), bf16),
            vmem((ring, 1, tokens), f32),
        ]
        + scatter_scratch(ring, tokens, width, resident=True)
        + [vmem((ring - 1, tokens, width), bf16), vmem((2, tokens, width), bf16)]
        + pair_sems(2 * (ring - 1))
        + pair_sems(7 * ring)
        + pair_sems(experts - 1)
        + [
            pltpu.SemaphoreType.DMA((6,)),
            pltpu.SemaphoreType.DMA((24,)),
            pltpu.SemaphoreType.DMA((9,)),
        ],
        (second, grads, maps, *experts_w, shared, router),
        in_vmem=(2,),
        out_vmem=(0,),
    )


def attention_back(
    n_rows, n_cols, d_block, d_gates, probs, router, token_rows, gains, weights_out, weights_in,
    queries, kv, heads_out, lse, tables, parts, expert_rows,
):
    ring = n_cols // 2
    length, model = token_rows[0].shape
    experts = n_rows * ring
    q_width = weights_out.shape[1]
    in_width = weights_in.shape[1]
    col_width = model // n_cols
    width = model // n_rows
    heads = q_width // HEAD_DIM
    scale = 1.0 / math.sqrt(HEAD_DIM)
    half = expert_rows[2].shape[1] // 2
    n_slots = expert_rows[2].shape[0]
    bf16, f32 = jnp.bfloat16, jnp.float32
    shape = jax.ShapeDtypeStruct

    def kernel(
        block, gates, probs_in, router, x_in, proj_in, g_in, gains, wo_in, w_in, q, kv, out, lse, cosine,
        sine, y_in, xr_in, dp_in, act_in, dg_in, du_in,
        d_proj, d_first, y_out, wo_out, d_resid, gain_out, xr_out, dp_out, act_out, dg_out, du_out,
        second, proj, g, probs, high_ref, low_ref,
        wo, w, go, delta, dqt, dkv, dkv_own, wo_part, y_hold, y_landed, *rest,
    ):
        scratch, kv_parts, wo_parts = rest[:9], rest[9:16], rest[16:23]
        gs, gr, yr_s, yr_r, es, er, local = rest[23:]
        net = Links(n_rows, n_cols)
        net.greet([net.x, net.y, net.up, net.down, net.twin])
        gather = gather_square(net, block, second, (gs, gr), local.at[1], 1)
        next(gather)
        others = pl.ds(half, half)
        twins = [
            net.send(source, target, (es, er), number, net.twin)
            for number, (source, target) in enumerate(
                (
                    (xr_in, xr_out), (dg_in.at[:, others], dg_out), (du_in.at[:, others], du_out),
                    (act_in.at[:, others], act_out), (dp_in, dp_out),
                )
            )
        ]
        x, d_attn = d_first, proj
        loads = [
            pltpu.make_async_copy(a, b, local.at[2 + i])
            for i, (a, b) in enumerate(((x_in, x), (proj_in, proj), (g_in.at[0], g)))
        ]
        probs_load = pltpu.make_async_copy(probs_in.at[0], probs, local.at[6])
        probs_load.start()
        for load in loads:
            load.start()
        wo_load = pltpu.make_async_copy(wo_in, wo, local.at[5])
        wo_load.start()
        w_load = pltpu.make_async_copy(w_in, w, local.at[0])
        w_load.start()
        d_gates = jnp.concatenate(
            [gates[...].reshape(experts, length), jnp.zeros((128 - experts, length), f32)], 0
        ).T
        probs_load.wait()
        d_logits = probs[...] * (d_gates - jnp.sum(probs[...] * d_gates, -1, keepdims=True))
        high = d_logits.astype(bf16)
        high_ref[...] = high
        low_ref[...] = (d_logits - high.astype(f32)).astype(bf16)
        for load in loads:
            load.wait()

        hop = []

        def keep_sum(s, upper, lower):
            half = length // 2
            target = y_hold if s == 1 else y_out.at[s - 1]
            add_slabs(target.at[pl.ds(0, half), :], upper)
            add_slabs(target.at[pl.ds(half, half), :], lower)
            if s == 1:
                hop.append(net.send(y_hold, y_landed, (yr_s, yr_r), 0, net.up))

        y_steps = scatter_square(net, y_in, scratch, list(range(1, ring)), keep_sum)
        by_place = lambda ref: lambda hops, core: ref.at[
            pl.ds((net.place(hops) * 2 + core) * col_width, col_width), :
        ]

        run_together(gather)
        next(y_steps)
        next(y_steps)
        gain = gains[1:2]
        gain_out[...] = jnp.zeros_like(gain_out)

        @pl.loop(0, length // 128)
        def _(i):
            at = pl.ds(pl.multiple_of(i * 128, 128), 128)
            values = x[at, :].astype(f32) + proj[at, :].astype(f32)
            inverse = lax.rsqrt(jnp.mean(values * values, -1, keepdims=True) + NORM_EPS)
            unit = values * inverse
            d_second = second[0, at, :].astype(f32)
            d_second = d_second + matmul_nt(high_ref[at, :], router[...])
            d_second = d_second + matmul_nt(low_ref[at, :], router[...])
            d_unit = d_second * gain
            moment = jnp.mean(d_unit * unit, -1, keepdims=True)
            resid = g[at, :].astype(f32) + inverse * (d_unit - unit * moment)
            d_attn[at, :] = resid.astype(bf16)
            d_resid[at, :] = resid[:, :width]
            along = (d_second[:, :width] * unit[:, :width]).reshape(16, 8, width)
            gain_out[...] += jnp.sum(along, 0)

        wo_load.wait()
        go[...] = matmul(d_attn[...], wo[...]).astype(bf16)
        wo_part[...] = matmul_tn(d_attn[...], out[...].astype(bf16)).astype(bf16)
        wo_steps = scatter_columns(net, by_place(wo_part), wo_out, wo_parts)
        next(wo_steps)
        for head in range(heads):
            columns = slice(head * HEAD_DIM, (head + 1) * HEAD_DIM)
            product = (go[:, columns].astype(f32) * out[:, columns]).T
            delta[head] = jnp.sum(product, 0, keepdims=True)
        dqt[...] = jnp.zeros_like(dqt)
        dkv[...] = jnp.zeros_like(dkv)
        next(wo_steps)
        next(y_steps)
        next(y_steps)

        def one_block(number, masked):
            keys = kv[number, :, :HEAD_DIM]
            values = kv[number, :, HEAD_DIM:]
            keys_t = keys.T
            d_key = jnp.zeros((length, HEAD_DIM), f32)
            d_value = jnp.zeros((length, HEAD_DIM), f32)
            for head in range(heads):
                columns = slice(head * HEAD_DIM, (head + 1) * HEAD_DIM)
                queries = q[:, columns]
                grads = go[:, columns]
                probs = jnp.exp(scores_of(keys, queries, scale) - lse[head])
                if masked:
                    probs = jnp.where(causal_mask(probs), probs, 0.0)
                d_probs = matmul_nt(values, grads)
                d_scores = (probs * (d_probs - delta[head])).astype(bf16)
                d_value = d_value + matmul(probs.astype(bf16), grads)
                d_key = d_key + matmul(d_scores, queries)
                dqt[head] = dqt[head] + matmul(keys_t, d_scores)
            dkv[number, :, :HEAD_DIM] = (d_key * scale).astype(bf16)
            dkv[number, :, HEAD_DIM:] = d_value.astype(bf16)

        one_block(net.c, True)
        middle = lax.div(net.c, 2)

        @pl.loop(0, middle)
        def _(number):
            one_block(number, False)

        next(y_steps)
        next(y_steps)
        next(wo_steps)

        @pl.loop(middle, net.c)
        def _(number):
            one_block(number, False)

        next(wo_steps)
        kv_steps = scatter_columns(
            net, lambda hops, core: dkv.at[2 * net.chip(hops) + core], dkv_own, kv_parts
        )
        next(kv_steps)
        next(kv_steps)
        next(y_steps)

        def turned_back(values):
            return (values * cosine[...] - pltpu.roll(values, HEAD_DIM // 2, 1) * sine[...]).astype(bf16)

        for head in range(heads):
            columns = slice(head * HEAD_DIM, (head + 1) * HEAD_DIM)
            d_proj[:, columns] = turned_back((dqt[head] * scale).T)
        next(kv_steps)
        next(y_steps)
        next(kv_steps)
        next(wo_steps)
        run_together(kv_steps)
        next(y_steps, None)
        d_proj[:, q_width : q_width + HEAD_DIM] = turned_back(dkv_own[:, :HEAD_DIM])
        d_proj[:, q_width + HEAD_DIM :] = dkv_own[:, HEAD_DIM:].astype(bf16)
        w_load.wait()
        for j in range(n_rows):
            at = slice(j * width, (j + 1) * width)
            d_first[:, at] = matmul_nt(d_proj[...], w[at, :]).astype(bf16)
        run_together(y_steps, wo_steps)
        hop[0].wait_recv()
        y_out[0] = y_landed[...]
        for copy in twins:
            copy.wait_recv()
        net.finish()

    vmem = pltpu.VMEM
    return remote_call(
        kernel,
        "attention_back",
        6,
        [
            shape((length, in_width), bf16),
            shape((length, model), bf16),
            shape((ring - 1, length, width), bf16),
            shape((col_width, q_width), f32),
            shape((length, width), f32),
            shape((8, width), f32),
            shape((n_slots, model), bf16),
            shape((n_slots, model), bf16),
            shape((n_slots, half), bf16),
            shape((n_slots, half), bf16),
            shape((n_slots, half), bf16),
        ],
        [
            vmem((1, length, model), bf16),
            vmem((length, model), bf16),
            vmem((length, model), bf16),
            vmem((length, 128), f32),
            vmem((length, 128), bf16),
            vmem((length, 128), bf16),
            vmem((model, q_width), bf16),
            vmem((model, in_width), bf16),
            vmem((length, q_width), bf16),
            vmem((heads, 1, length), f32),
            vmem((heads, HEAD_DIM, length), f32),
            vmem((n_cols, length, 2 * HEAD_DIM), bf16),
            vmem((length, 2 * HEAD_DIM), f32),
            vmem((model, q_width), bf16),
            vmem((length, width), bf16),
            vmem((length, width), bf16),
        ]
        + scatter_scratch(ring - 1, length, width)
        + scatter_columns_scratch(ring, length, 2 * HEAD_DIM)
        + scatter_columns_scratch(ring, col_width, q_width)
        + pair_sems(7)
        + pair_sems(1)
        + pair_sems(5)
        + [pltpu.SemaphoreType.DMA((7,))],
        (
            d_block, d_gates, probs, router, *token_rows, gains, weights_out, weights_in, queries, kv,
            heads_out, lse, *tables, parts, *expert_rows,
        ),
        in_vmem=(1, 3, 7, 10, 11, 12, 13, 14, 15),
        out_vmem=(0, 1, 2, 3, 4, 5),
    )


def last_phase(
    n_rows, n_cols, d_first, d_proj, normed, parts, part_sum, x, proj, d_resid, gains, gain_part,
    x_scale, expert_rows, twin_rows, router_rows,
):
    ring = n_cols // 2
    length, model = d_first.shape
    width = model // n_rows
    in_width = d_proj.shape[1]
    col_width = model // n_cols
    pieces = 2
    piece = length // pieces
    bf16, f32 = jnp.bfloat16, jnp.float32
    shape = jax.ShapeDtypeStruct
    chips = n_rows * ring
    slot_rows, d_part, e_act, d_gate, d_up = expert_rows
    n_slots, hidden = e_act.shape
    half = hidden // 2
    experts = router_rows[2].shape[0]
    rows_dev = length // n_rows

    def kernel(
        d_first, d_proj, normed, y_in, y_sum, x_in, proj_in, d_resid, gains, gain_two, x_scale,
        xr_in, dp_in, act_in, dg_in, du_in, xr_twin, dp_twin, act_twin, dg_twin, du_twin,
        rows_in, probs_in, gates_in,
        layer_out, grad_in, gain_out, w_out, router_out, out_g, out_u, out_d,
        d_own, w_part, moment, moments, gain_own, gain_twin, gain_sums, proj, x,
        xr, dg, du, full_a, full_b,
        x_q, probs_q, gates_q, router_part, router_got, router_sum, y_landed, y_leaving, *rest,
    ):
        scratch, y_scratch = rest[:9], rest[9:18]
        w_parts = rest[18:25]
        mo_s, mo_r, ga_s, ga_r, gt_s, gt_r, sem, ro_s, ro_r, router_sems, yr_s, yr_r = rest[25:]
        full = (full_a, full_b)
        net = Links(n_rows, n_cols)
        others = net.spread_partners()
        net.greet([device for _, _, device in others] + [net.twin])

        def finish(s, upper, lower):
            at = lambda p: pl.ds(s * piece + p * (piece // 2), piece // 2)
            add_slabs(d_own.at[at(0), :], upper)
            add_slabs(d_own.at[at(1), :], lower)

        ring_copies = []

        def pass_on(turn):
            if turn == 1:
                before = part_reader(y_sum, 0)
            else:
                ring_copies[turn - 2].wait_recv()
                before = part_reader(y_landed, turn - 2)
            add_slabs(y_leaving.at[turn - 1], [part_reader(y_sum, turn), before])
            ring_copies.append(
                net.send(
                    y_leaving.at[turn - 1], y_landed.at[turn - 1], (yr_s, yr_r), turn - 1, net.up
                )
            )

        pass_on(1)

        def finish_out(s, upper, lower):
            ring_copies[-1].wait_recv()
            for part, terms in ((0, upper), (1, lower)):
                at = pl.ds(part * (length // 2), length // 2)
                extra = [
                    part_reader(y_landed.at[ring - 3, at, :]),
                    part_reader(x.at[at, :]),
                    part_reader(proj.at[at, :]),
                ]
                add_slabs(layer_out.at[at, :], terms + extra)

        steps = scatter_square(net, d_first, scratch, list(range(pieces)), finish, resident=True)
        y_steps = scatter_square(net, y_in, y_scratch, [0], finish_out)
        next(steps)
        next(steps)
        ours, mine, twins = pl.ds(0, half), pl.ds(0, n_slots), pl.ds(n_slots, n_slots)
        loads = [
            pltpu.make_async_copy(a, b, sem.at[i])
            for i, (a, b) in enumerate(
                (
                    (xr_in, xr.at[mine]), (xr_twin, xr.at[twins]),
                    (dg_in.at[:, ours], dg.at[mine]), (dg_twin, dg.at[twins]),
                    (du_in.at[:, ours], du.at[mine]), (du_twin, du.at[twins]),
                    (act_in.at[:, ours], dg.at[mine]), (act_twin, dg.at[twins]),
                    (dp_in, xr.at[mine]), (dp_twin, xr.at[twins]),
                )
            )
        ]
        early, late = loads[:6], loads[6:]
        for load in early:
            load.start()
        stores = {}

        def make(kind, j):
            group, slot = kind // 2, j % 2 if kind < 2 else 0
            columns = slice(j * width, (j + 1) * width)
            at = pl.ds(pl.multiple_of(net.flip(j) * width, width), width)
            if (group, slot) in stores:
                stores[group, slot].wait()
            if kind < 2:
                full[group][slot] = matmul_tn(xr[:, columns], (dg, du)[kind][...])
                target = (out_g, out_u)[kind].at[at, :]
            else:
                full[group][slot] = matmul_tn(dg[...], xr[:, columns])
                target = out_d.at[:, at]
            store = pltpu.make_async_copy(full[group].at[slot], target, sem.at[12 + 2 * group + slot])
            store.start()
            stores[group, slot] = store

        proj_load = pltpu.make_async_copy(proj_in.at[:, pl.ds(0, width)], proj, sem.at[10])
        proj_load.start()
        x_load = pltpu.make_async_copy(x_in.at[:, pl.ds(0, width)], x, sem.at[11])
        x_load.start()
        quarter = pl.ds(pl.multiple_of(net.r * rows_dev, rows_dev), rows_dev)
        column = pl.ds(pl.multiple_of(net.place(0) * width, width), width)
        router_loads = []
        for s in range(ring):
            router_loads += [
                pltpu.make_async_copy(
                    rows_in.at[s, quarter, column], x_q.at[s], router_sems.at[s, 0]
                ),
                pltpu.make_async_copy(probs_in.at[s, quarter, :], probs_q.at[s], router_sems.at[s, 1]),
                pltpu.make_async_copy(
                    gates_in.at[:, net.chip(s), 0, quarter], gates_q.at[s], router_sems.at[s, 2]
                ),
            ]
        for load in router_loads:
            load.start()
        w_part[...] = matmul_tn(normed[...], d_proj[...]).astype(bf16)
        by_place = lambda hops, core: w_part.at[
            pl.ds((net.place(hops) * 2 + core) * col_width, col_width), :
        ]
        w_steps = scatter_columns(net, by_place, w_out, w_parts)
        next(w_steps)
        next(steps)
        for load in early:
            load.wait()
        make(0, 0)
        next(w_steps)
        next(steps)
        next(y_steps)
        make(0, 1)
        pass_on(2)
        run_together(steps)

        x_load.wait()
        gain = gains[0:1, :width]
        slab = 128
        gain_own[...] = jnp.zeros_like(gain_own)

        def unit_of(at):
            inverse = x_scale[at, :1]
            return x[at, :].astype(f32) * inverse, inverse

        for i in range(length // slab):
            at = slice(i * slab, (i + 1) * slab)
            unit, _ = unit_of(at)
            d_normed = d_own[at, :]
            share = jnp.sum(d_normed * gain * unit, -1, keepdims=True)
            moment[:, at] = jnp.broadcast_to(share, (slab, 128)).T[:8]
            gain_own[:8] += jnp.sum((d_normed * unit).reshape(slab // 8, 8, width), 0)
        sends = [
            net.send(moment, moments.at[bits - 1], (mo_s, mo_r), bits - 1, (net.flip(bits), net.c))
            for bits in range(1, n_rows)
        ]
        gain_own[8:] = gain_two[...]
        twin = net.send(gain_own, gain_twin, (gt_s, gt_r), 0, net.twin)
        next(w_steps)
        make(0, 2)
        for copy in sends:
            copy.wait_recv()
        whole = moment[...] + moments[0] + moments[1] + moments[2]
        for i in range(length // slab):
            at = slice(i * slab, (i + 1) * slab)
            unit, inverse = unit_of(at)
            mean = jnp.broadcast_to(whole[:1, at], (128, slab)).T[:, :1] / model
            grad_in[at, :] = d_resid[at, :] + inverse * (d_own[at, :] * gain - unit * mean)
        twin.wait_recv()
        mine = net.r * ring + net.z
        gain_sums[mine] = gain_own[...] + gain_twin[...]
        sends = [
            net.send(gain_sums.at[mine], gain_sums.at[mine], (ga_s, ga_r), number, device)
            for number, (hops, bits, device) in enumerate(others)
        ]
        make(0, 3)
        next(w_steps)
        make(1, 0)
        next(y_steps)
        make(1, 1)
        for load in router_loads:
            load.wait()
        for s in range(ring):
            d_gates = jnp.concatenate([gates_q[s], jnp.zeros((128 - experts, rows_dev), f32)], 0).T
            d_logits = probs_q[s] * (d_gates - jnp.sum(probs_q[s] * d_gates, -1, keepdims=True))
            high = d_logits.astype(bf16)
            low = (d_logits - high.astype(f32)).astype(bf16)
            part = matmul_tn(x_q[s], high) + matmul_tn(x_q[s], low)
            for core in range(2):
                rows = part[core * col_width : (core + 1) * col_width]
                router_part[core] = rows if s == 0 else router_part[core] + rows
        router_twin = net.send(router_part.at[1 - net.k], router_got.at[0], (ro_s, ro_r), 0, net.twin)
        make(1, 2)
        router_twin.wait_recv()
        router_sum[0] = router_part[net.k] + router_got[0]
        router_x = net.send(router_sum.at[0], router_got.at[1], (ro_s, ro_r), 1, net.x)
        proj_load.wait()
        next(y_steps)
        make(1, 3)
        for load in late:
            load.start()
        router_x.wait_recv()
        router_sum[1] = router_sum[0] + router_got[1]
        router_y = net.send(router_sum.at[1], router_got.at[2], (ro_s, ro_r), 2, net.y)
        run_together(y_steps, w_steps)
        for load in late:
            load.wait()
        for j in range(n_rows):
            make(2, j)
        for store in stores.values():
            store.wait()
        for copy in sends:
            copy.wait_recv()
        router_y.wait_recv()
        router_out[...] = router_sum[1] + router_got[2]
        total = gain_sums[net.z * ring]
        for i in range(1, ring):
            total = total + gain_sums[net.z * ring + i]
        gain_out[0:1] = jnp.sum(total[:8], 0, keepdims=True)
        gain_out[1:2] = jnp.sum(total[8:], 0, keepdims=True)
        gain_out[2:8] = jnp.zeros((6, width), f32)
        run_together(w_steps)
        net.finish()

    vmem = pltpu.VMEM
    return remote_call(
        kernel,
        "last_phase",
        7,
        [
            shape((length, width), bf16),
            shape((length, width), f32),
            shape((8, width), f32),
            shape((col_width, in_width), f32),
            shape((col_width, 128), f32),
            shape((model, half), f32),
            shape((model, half), f32),
            shape((half, model), f32),
        ],
        [
            vmem((length, width), f32),
            vmem((model, in_width), bf16),
            vmem((8, length), f32),
            vmem((n_rows - 1, 8, length), f32),
            vmem((16, width), f32),
            vmem((16, width), f32),
            vmem((chips, 16, width), f32),
            vmem((length, width), bf16),
            vmem((length, width), bf16),
            vmem((2 * n_slots, model), bf16),
            vmem((2 * n_slots, half), bf16),
            vmem((2 * n_slots, half), bf16),
            vmem((2, width, half), f32),
            vmem((1, half, width), f32),
            vmem((ring, rows_dev, width), bf16),
            vmem((ring, rows_dev, 128), f32),
            vmem((ring, experts, rows_dev), f32),
            vmem((2, col_width, 128), f32),
            vmem((3, col_width, 128), f32),
            vmem((2, col_width, 128), f32),
            vmem((ring - 2, length, width), bf16),
            vmem((ring - 2, length, width), bf16),
        ]
        + scatter_scratch(pieces, piece, width, resident=True)
        + scatter_scratch(1, length, width)
        + scatter_columns_scratch(ring, col_width, in_width)
        + pair_sems(n_rows - 1)
        + pair_sems(chips - 1)
        + pair_sems(1)
        + [pltpu.SemaphoreType.DMA((16,))]
        + pair_sems(3)
        + [pltpu.SemaphoreType.DMA((ring, 3))]
        + pair_sems(ring - 2),
        (
            d_first.reshape(pieces, piece, model), d_proj, normed, parts, part_sum, x, proj, d_resid,
            gains, gain_part, x_scale, *expert_rows, *twin_rows, *router_rows,
        ),
        in_vmem=(0, 1, 2, 4, 7, 8, 9, 10),
        out_vmem=(0, 1, 2, 3, 4),
    )


def add_bf16(left, right):
    return (left.astype(jnp.float32) + right.astype(jnp.float32)).astype(jnp.bfloat16)


class Exchange:
    def __init__(self):
        self.n_rows = lax.axis_size("rows")
        self.n_cols = lax.axis_size("cols")
        self.ring = self.n_cols // 2
        self.r = lax.axis_index("rows")
        self.c = lax.axis_index("cols")
        self.z = self.c // 2
        self.k = self.c % 2

    def move(self, values, target):
        pairs = []
        for r in range(self.n_rows):
            for c in range(self.n_cols):
                to_r, to_c = target(r, c)
                pairs.append((r * self.n_cols + c, to_r * self.n_cols + to_c))
        return lax.ppermute(values, ("rows", "cols"), pairs)

    def along_x(self, values):
        return self.move(values, lambda r, c: (r ^ 1, c))

    def along_y(self, values):
        return self.move(values, lambda r, c: (r ^ 2, c))

    def along_z(self, values, hops=1):
        return self.move(values, lambda r, c: (r, (c + 2 * hops) % self.n_cols))

    def across_z(self, values, bit):
        return self.move(values, lambda r, c: (r, c ^ (2 * bit)))

    def sibling(self, values):
        return self.move(values, lambda r, c: (r, c ^ 1))

    def chip(self, hops):
        return (self.z - hops + self.ring) % self.ring

    def place(self, hops):
        return self.r ^ self.chip(hops)

    def mixed(self, values, axis):
        width = values.shape[axis] // self.n_rows

        def branch(row):
            return lambda whole: jnp.concatenate(
                [
                    lax.slice_in_dim(whole, (row ^ j) * width, ((row ^ j) + 1) * width, axis=axis)
                    for j in range(self.n_rows)
                ],
                axis,
            )

        return lax.switch(self.r, [branch(row) for row in range(self.n_rows)], values)

    def rows_gather(self, block):
        half = block.shape[0] // 2
        from_x = self.along_x(block)
        from_y = self.along_y(block)
        first = self.along_y(from_x[:half])
        second = self.along_x(from_y[half:])
        return [block, from_x, from_y, jnp.concatenate([first, second], 0)]

    def rows_scatter(self, blocks):
        half = blocks[0].shape[0] // 2
        upper = [block[:half] for block in blocks]
        lower = [block[half:] for block in blocks]
        sent = self.along_x(jnp.stack([upper[1], upper[3]]))
        forward = add_bf16(upper[2], sent[1])
        upper_sum = upper[0].astype(jnp.float32) + sent[0].astype(jnp.float32)
        upper_sum = upper_sum + self.along_y(forward).astype(jnp.float32)
        sent = self.along_y(jnp.stack([lower[2], lower[3]]))
        forward = add_bf16(lower[1], sent[1])
        lower_sum = lower[0].astype(jnp.float32) + sent[0].astype(jnp.float32)
        lower_sum = lower_sum + self.along_x(forward).astype(jnp.float32)
        return jnp.concatenate([upper_sum, lower_sum], 0)

    def cols_gather(self, block, place):
        shape = (self.ring, 2) + block.shape
        whole = jnp.zeros(shape, block.dtype)
        rest = (0,) * block.ndim
        for hops in range(self.ring):
            twin = self.sibling(block)
            spot = place(hops)
            whole = lax.dynamic_update_slice(whole, block[None, None], (spot, self.k) + rest)
            whole = lax.dynamic_update_slice(whole, twin[None, None], (spot, 1 - self.k) + rest)
            if hops < self.ring - 1:
                block = self.along_z(block)
        return whole

    def pair_sum(self, parts):
        mine = lax.dynamic_index_in_dim(parts, self.k, 1, False)
        other = lax.dynamic_index_in_dim(parts, 1 - self.k, 1, False)
        return add_bf16(mine, self.sibling(other))

    def cols_scatter(self, parts, place):
        summed = self.pair_sum(parts)
        pick = lambda hops: lax.dynamic_index_in_dim(summed, place(hops), 0, False)
        run = pick(1)
        for hops in range(2, self.ring):
            run = add_bf16(self.along_z(run), pick(hops))
        return self.along_z(run).astype(jnp.float32) + pick(0).astype(jnp.float32)


def split_terms(values):
    high = lax.reduce_precision(values, 8, 7)
    return high.astype(jnp.bfloat16), (values - high).astype(jnp.bfloat16)


def gathered_layer(
    layer_in,
    norm1_gain,
    w_query,
    key_matrix,
    value_matrix,
    w_out,
    norm2_gain,
    w_router,
    shared_gate,
    shared_up,
    shared_down,
    expert_gate,
    expert_up,
    expert_down,
    routes,
    cotangent,
):
    net = Exchange()
    n_rows, ring = net.n_rows, net.ring
    r, c, z, k = net.r, net.c, net.z, net.k
    length, row_width = layer_in.shape[1:]
    rows_dev, top_k = routes.shape[2:]
    experts = w_router.shape[1]
    model_width = row_width * n_rows
    col_width = w_query.shape[0]
    q_width = w_query.shape[1]
    q_heads = q_width // HEAD_DIM
    kv_width = key_matrix.shape[1]
    shared_hidden = shared_gate.shape[1] // ring
    half_hidden = expert_gate.shape[2]
    slots = -(-2 * max(1, 5 * rows_dev * top_k // (8 * experts)) // 16) * 16
    index = lax.dynamic_index_in_dim

    expert_ids = jnp.arange(experts, dtype=jnp.int32)
    hot = jnp.sum(
        (routes.reshape(rows_dev, top_k)[:, :, None] == expert_ids).astype(jnp.float32), 1
    )
    earlier = jnp.tril(jnp.ones((rows_dev, rows_dev), jnp.float32), -1)
    rank = jnp.dot(earlier, hot, precision=PRECISE)
    slot_map = jnp.where(hot > 0, rank, -1.0).T

    small = jnp.concatenate([w_router, norm1_gain[:, None], norm2_gain[:, None]], 1)
    small = jnp.pad(small, ((0, 0), (0, 128 - small.shape[1])))
    pad_to = -(-shared_hidden // 128) * 128
    padded = lambda w: jnp.pad(
        w.reshape(col_width, ring, shared_hidden), ((0, 0), (0, 0), (0, pad_to - shared_hidden))
    )
    packed = jnp.concatenate([padded(shared_gate), padded(shared_up), padded(shared_down.T)], 2)
    packed = jnp.swapaxes(packed, 0, 1)
    experts_w = []
    for own in (expert_gate[0], expert_up[0], expert_down[0]):
        experts_w += [own, net.sibling(own)]
    positions = c * length + jnp.arange(length, dtype=jnp.int32)
    cosine_table, sine_table = rope_tables(positions, HEAD_DIM)
    tables = (
        jnp.concatenate([cosine_table, cosine_table], 1),
        jnp.concatenate([-sine_table, sine_table], 1),
    )

    (
        token_input, first_normed, weights_in, small, queries, kv_all, attn_f32, log_total,
        weights_out_t, grad_rows, second_normed, slot_maps, shared_w, attn_proj, gains,
        first_scale,
    ) = first_phase(
        n_rows, net.n_cols, layer_in[0], cotangent[0],
        jnp.concatenate([w_query, key_matrix, value_matrix], 1), small, w_out.T, packed, slot_map,
        tables,
    )
    joined = lambda whole: whole.reshape(-1, whole.shape[-1])
    attn_proj = joined(attn_proj)
    (
        d_block, rows_all, out_rows, slot_rows, d_part, e_act, d_e_gate, d_e_up, s_act, d_shared,
        gate_probs, d_gate_all,
    ) = experts_phase(
        n_rows, net.n_cols, second_normed, grad_rows, slot_maps, experts_w, shared_w, small, slots
    )
    expert_rows = [joined(part) for part in (slot_rows, d_part, e_act, d_e_gate, d_e_up)]
    d_projected, d_first, part_sum, g_out, d_resid, gain_part, *twin_rows = attention_back(
        n_rows, net.n_cols, d_block, index(d_gate_all, z, 1, False)[:, 0], gate_probs, small,
        (token_input, attn_proj, grad_rows), gains, weights_out_t, weights_in, queries, kv_all,
        attn_f32, log_total, tables, out_rows, expert_rows,
    )
    layer_out, grad_in, gain_grads, g_in, g_router, *g_experts = last_phase(
        n_rows, net.n_cols, d_first, d_projected, first_normed, out_rows, part_sum, token_input,
        attn_proj, d_resid, gains, gain_part, first_scale,
        expert_rows, twin_rows, (rows_all, gate_probs, d_gate_all),
    )
    gain_grads = index(gain_grads[:2].reshape(2, 2, col_width), k, 1, False)

    column_parts = lambda whole: whole.astype(jnp.bfloat16).reshape(ring, 2, col_width, -1)
    shared_parts = jnp.concatenate(
        [
            matmul_tn(joined(rows_all), joined(d_shared)),
            matmul_tn(joined(grad_rows), joined(s_act)),
        ],
        1,
    )
    shared_parts = net.pair_sum(column_parts(shared_parts))
    g_shared = jnp.zeros(shared_parts.shape, jnp.bfloat16)
    for hops in range(ring):
        piece = index(shared_parts, net.place(-hops), 0, False)
        piece = net.along_z(piece, hops) if hops else piece
        g_shared = lax.dynamic_update_slice(g_shared, piece[None], (net.chip(hops), 0, 0))
    g_shared = g_shared.astype(jnp.float32)
    shared_cols = lambda n: jnp.swapaxes(
        g_shared[:, :, n * pad_to : n * pad_to + shared_hidden], 0, 1
    ).reshape(col_width, -1)

    return (
        layer_out[None],
        grad_in[None],
        gain_grads[0],
        g_in[:, :q_width],
        g_in[:, q_width : q_width + kv_width],
        g_in[:, q_width + kv_width :],
        g_out.T,
        gain_grads[1],
        g_router[:, :experts],
        shared_cols(0),
        shared_cols(1),
        shared_cols(2).T,
        g_experts[0][None],
        g_experts[1][None],
        g_experts[2][None],
    )


def per_device(layer_in, *others):
    routes = others[13]
    w_router = others[6]
    n_rows, n_cols = lax.axis_size("rows"), lax.axis_size("cols")
    experts, top_k = w_router.shape[1], routes.shape[3]
    gathers = (
        experts <= 4 * top_k
        and layer_in.shape[0] == 1
        and n_rows == 4
        and n_cols == 2 * n_rows
        and 2 * experts == n_rows * n_cols
    )
    return (gathered_layer if gathers else routed_layer)(layer_in, *others)


def solution(mesh):
    placed = (
        P(None, "cols", "rows"),
        P("cols"),
        P("cols", "rows"),
        P("cols", "rows"),
        P("cols", "rows"),
        P("rows", "cols"),
        P("cols"),
        P("cols", None),
        P("cols", "rows"),
        P("cols", "rows"),
        P("rows", "cols"),
        P(("rows", "cols"), None, None),
        P(("rows", "cols"), None, None),
        P(("rows", "cols"), None, None),
        P("cols", "rows", None, None),
        P(None, "cols", "rows"),
    )
    return jax.shard_map(
        per_device,
        mesh=mesh,
        in_specs=placed,
        out_specs=(
            P(None, "cols", "rows"),
            P(None, "cols", "rows"),
            P("cols"),
            P("cols", "rows"),
            P("cols", "rows"),
            P("cols", "rows"),
            P("rows", "cols"),
            P("cols"),
            P("cols", None),
            P("cols", "rows"),
            P("cols", "rows"),
            P("rows", "cols"),
            P(("rows", "cols"), None, None),
            P(("rows", "cols"), None, None),
            P(("rows", "cols"), None, None),
        ),
        check_vma=False,
    )
```

```python
import math

import jax
import jax.numpy as jnp
from jax import lax
from jax.experimental import pallas as pl
from jax.experimental.pallas import tpu as pltpu
from jax.sharding import PartitionSpec as P

HEAD_DIM = 128


NORM_EPS = 1e-05
ROPE_BASE = 500000.0
NEG_LARGE = -1e30
PRECISE = lax.Precision.HIGHEST


def rope_tables(positions, head_size):
    half_size = head_size // 2
    inv_freq = ROPE_BASE ** (-(2.0 * jnp.arange(half_size, dtype=jnp.float32)) / head_size)
    angles = positions.astype(jnp.float32)[:, None] * inv_freq[None, :]
    return (jnp.cos(angles), jnp.sin(angles))


def apply_rotary(values, cosine_table, sine_table):
    half_size = values.shape[-1] // 2
    first_half = values[..., :half_size]
    second = values[..., half_size:]
    cos_b = cosine_table[:, None, :]
    sin_b = sine_table[:, None, :]
    return jnp.concatenate(
        [first_half * cos_b - second * sin_b, second * cos_b + first_half * sin_b], -1
    )


def matmul(left_op, right_op):
    return jnp.dot(left_op, right_op, preferred_element_type=jnp.float32)


def matmul_tn(left_op, right_op):
    return lax.dot_general(
        left_op, right_op, (((0,), (0,)), ((), ())), preferred_element_type=jnp.float32
    )


def matmul_nt(left_op, right_op):
    return lax.dot_general(
        left_op, right_op, (((1,), (1,)), ((), ())), preferred_element_type=jnp.float32
    )


def silu_parts(pre_act):
    sigma = jax.nn.sigmoid(pre_act)
    return (pre_act * sigma, sigma * (1.0 + pre_act * (1.0 - sigma)))


def keep_same(carry_in):
    return carry_in


def routed_layer(
    layer_in,
    norm1_gain,
    w_query,
    key_matrix,
    value_matrix,
    w_out,
    norm2_gain,
    w_router,
    shared_gate,
    shared_up,
    shared_down,
    expert_gate,
    expert_up,
    expert_down,
    routes,
    cotangent,
):
    n_rows = lax.axis_size("rows")
    n_cols = lax.axis_size("cols")
    row_idx = lax.axis_index("rows")
    col_idx = lax.axis_index("cols")
    sequence_count, len_dev, row_width = layer_in.shape
    tok_dev = sequence_count * len_dev
    rows_dev = routes.shape[2]
    top_k = routes.shape[3]
    experts = w_router.shape[1]
    devices = n_rows * n_cols
    capacity = 2 * max(1, 5 * rows_dev * top_k // (8 * experts))
    full_in = lax.all_gather(layer_in, "rows", axis=2, tiled=True)
    (
        gain_one,
        wq_full,
        wk_full,
        wv_full,
        wo_full,
        gain_two,
        router_full,
        sg_full,
        su_full,
        sd_full,
    ) = (
        lax.all_gather(norm1_gain, "cols", axis=0, tiled=True),
        lax.all_gather(w_query, "cols", axis=0, tiled=True),
        lax.all_gather(key_matrix, "cols", axis=0, tiled=True),
        lax.all_gather(value_matrix, "cols", axis=0, tiled=True),
        lax.all_gather(w_out, "cols", axis=1, tiled=True),
        lax.all_gather(norm2_gain, "cols", axis=0, tiled=True),
        lax.all_gather(w_router, "cols", axis=0, tiled=True),
        lax.all_gather(shared_gate, "cols", axis=0, tiled=True),
        lax.all_gather(shared_up, "cols", axis=0, tiled=True),
        lax.all_gather(shared_down, "cols", axis=1, tiled=True),
    )
    model_width = full_in.shape[2]
    token_input = full_in.reshape(tok_dev, model_width).astype(jnp.float32)
    first_inverse_deviation = lax.rsqrt(
        jnp.mean(token_input * token_input, -1, keepdims=True) + NORM_EPS
    )
    first_unit_rows = token_input * first_inverse_deviation
    first_gain_float = gain_one.astype(jnp.float32)
    first_normed = (first_unit_rows * first_gain_float).astype(jnp.bfloat16)
    q_pre = matmul(first_normed, wq_full)
    key_unrotated = matmul(first_normed, wk_full)
    value_projected = matmul(first_normed, wv_full).astype(jnp.bfloat16)
    q_heads = q_pre.shape[1] // HEAD_DIM
    positions = col_idx * len_dev + jnp.arange(len_dev, dtype=jnp.int32)
    cosine_table, sine_table = rope_tables(positions, HEAD_DIM)
    rotated_queries = apply_rotary(
        q_pre.reshape(sequence_count, len_dev, q_heads, HEAD_DIM), cosine_table, sine_table
    ).astype(jnp.bfloat16)
    rotated_keys = apply_rotary(
        key_unrotated.reshape(sequence_count, len_dev, 1, HEAD_DIM), cosine_table, sine_table
    ).astype(jnp.bfloat16)
    kv_local = jnp.concatenate(
        [
            rotated_keys.reshape(sequence_count, len_dev, HEAD_DIM),
            value_projected.reshape(sequence_count, len_dev, HEAD_DIM),
        ],
        -1,
    )
    kv_local = jnp.swapaxes(kv_local, 0, 1)
    query_t = jnp.transpose(rotated_queries, (0, 2, 1, 3))
    score_scale = 1.0 / math.sqrt(HEAD_DIM)
    q_last = col_idx * len_dev + len_dev - 1

    def online_update(carry_in, key_part, k_start):
        run_max, run_sum, run_acc = carry_in
        block_len = key_part.shape[0]
        scores = (
            jnp.einsum(
                "shqd,bsd->shqb",
                query_t,
                key_part[:, :, :HEAD_DIM],
                preferred_element_type=jnp.float32,
            )
            * score_scale
        )
        key_pos = k_start + jnp.arange(block_len, dtype=jnp.int32)
        causal = positions[:, None] >= key_pos[None, :]
        scores = jnp.where(causal, scores, NEG_LARGE)
        new_max = jnp.maximum(run_max, jnp.max(scores, -1))
        prob_vals = jnp.where(causal, jnp.exp(scores - new_max[..., None]), 0.0)
        rescale = jnp.exp(run_max - new_max)
        run_sum = run_sum * rescale + jnp.sum(prob_vals, -1)
        run_acc = run_acc * rescale[..., None] + jnp.einsum(
            "shqb,bsd->shqd",
            prob_vals.astype(jnp.bfloat16),
            key_part[:, :, HEAD_DIM:],
            preferred_element_type=jnp.float32,
        )
        return (new_max, run_sum, run_acc)

    fold_start = (
        jnp.full((sequence_count, q_heads, len_dev), NEG_LARGE, jnp.float32),
        jnp.zeros((sequence_count, q_heads, len_dev), jnp.float32),
        jnp.zeros((sequence_count, q_heads, len_dev, HEAD_DIM), jnp.float32),
    )
    carry_in = fold_start
    piece = lax.all_gather(kv_local, "cols", axis=0, tiled=True)
    start = jnp.int32(0)
    piece_len = piece.shape[0]
    step_len = min(512, piece_len)
    for offset in range(0, piece_len, step_len):
        key_part = piece[offset : offset + step_len]
        k_start = start + offset

        def updated(state_in, key_part=key_part, k_start=k_start):
            return online_update(state_in, key_part, k_start)

        carry_in = lax.cond(k_start <= q_last, updated, keep_same, carry_in)
    run_max, run_sum, run_acc = carry_in
    attn_f32 = run_acc / run_sum[..., None]
    log_total = run_max + jnp.log(run_sum)
    attn_bf = attn_f32.astype(jnp.bfloat16)
    attn_rows = jnp.transpose(attn_bf, (0, 2, 1, 3)).reshape(tok_dev, q_heads * HEAD_DIM)
    attn_proj = lax.psum(matmul(attn_rows, wo_full).astype(jnp.bfloat16), "rows").astype(
        jnp.float32
    )
    residual_stream = token_input + attn_proj
    second_inverse_deviation = lax.rsqrt(
        jnp.mean(residual_stream * residual_stream, -1, keepdims=True) + NORM_EPS
    )
    second_unit_rows = residual_stream * second_inverse_deviation
    second_gain_float = gain_two.astype(jnp.float32)
    second_normed = (second_unit_rows * second_gain_float).astype(jnp.bfloat16)
    gate_pre = matmul(second_normed, sg_full)
    up_pre = matmul(second_normed, su_full)
    silu_gate, silu_slope = silu_parts(gate_pre)
    shared_act = (silu_gate * up_pre).astype(jnp.bfloat16)
    ffn_part = matmul(shared_act, sd_full)
    my_rows = row_idx * rows_dev
    normed_mine = lax.dynamic_slice_in_dim(second_normed, my_rows, rows_dev, 0)
    route_mine = routes.reshape(rows_dev, top_k)
    logits = matmul(normed_mine, router_full)
    expert_ids = jnp.arange(experts, dtype=jnp.int32)
    chosen_hot = (route_mine[:, :, None] == expert_ids[None, None, :]).astype(jnp.float32)
    chosen = jnp.sum(chosen_hot * logits[:, None, :], -1)
    gate_probs = jax.nn.softmax(chosen, -1)
    assign_count = rows_dev * top_k
    flat_routes = route_mine.reshape(assign_count)
    assign_hot = (flat_routes[:, None] == expert_ids[None, :]).astype(jnp.int32)
    rank_in = jnp.sum((jnp.cumsum(assign_hot, 0) - assign_hot) * assign_hot, 1)
    slot_of = flat_routes * capacity + rank_in
    assign_of_slot = (
        jnp.zeros((experts * capacity,), jnp.int32)
        .at[slot_of]
        .set(jnp.arange(assign_count, dtype=jnp.int32))
    )
    slot_used = jnp.zeros((experts * capacity,), jnp.int32).at[slot_of].set(1)
    slot_row = assign_of_slot // top_k

    def send_rows(slot_vals):
        slot_vals = slot_vals.reshape(experts, capacity, model_width)
        outgoing = jnp.broadcast_to(
            slot_vals[:, None], (experts, 2, capacity, model_width)
        ).reshape(devices, capacity, model_width)
        received = lax.all_to_all(
            outgoing, ("rows", "cols"), split_axis=0, concat_axis=0, tiled=True
        )
        return received.reshape(devices * capacity, model_width)

    def return_rows(slot_vals):
        returned = lax.all_to_all(
            slot_vals.reshape(devices, capacity, model_width),
            ("rows", "cols"),
            split_axis=0,
            concat_axis=0,
            tiled=True,
        )
        returned = returned.reshape(experts, 2, capacity, model_width).astype(jnp.float32)
        summed = (returned[:, 0] + returned[:, 1]).astype(jnp.bfloat16)
        return summed.reshape(experts * capacity, model_width).astype(jnp.float32)

    slot_inputs = jnp.where(slot_used[:, None] > 0, normed_mine[slot_row], 0)
    expert_rows = send_rows(slot_inputs)
    eg_mat = expert_gate.reshape(model_width, -1)
    eu_mat = expert_up.reshape(model_width, -1)
    ed_mat = expert_down.reshape(-1, model_width)
    e_gate = matmul(expert_rows, eg_mat)
    e_up = matmul(expert_rows, eu_mat)
    e_silu, e_slope = silu_parts(e_gate)
    e_act = (e_silu * e_up).astype(jnp.bfloat16)
    e_out = matmul(e_act, ed_mat).astype(jnp.bfloat16)
    expert_sum = return_rows(e_out)
    picked = expert_sum[slot_of].reshape(rows_dev, top_k, model_width)
    routed = jnp.sum(gate_probs[:, :, None] * picked, 1)
    ffn_full = lax.dynamic_update_slice_in_dim(
        ffn_part, lax.dynamic_slice_in_dim(ffn_part, my_rows, rows_dev, 0) + routed, my_rows, 0
    )
    ffn_mine = lax.psum_scatter(
        ffn_full.reshape(sequence_count, len_dev, model_width).astype(jnp.bfloat16),
        "rows",
        scatter_dimension=2,
        tiled=True,
    ).astype(jnp.float32)
    resid_mine = lax.dynamic_slice_in_dim(
        residual_stream.reshape(sequence_count, len_dev, model_width),
        row_idx * row_width,
        row_width,
        2,
    )
    layer_out = (resid_mine + ffn_mine).astype(jnp.bfloat16)
    grad_full = lax.all_gather(cotangent, "rows", axis=2, tiled=True).reshape(tok_dev, model_width)
    d_shared_act = matmul_nt(grad_full, sd_full)
    grad_sd = matmul_tn(shared_act, grad_full)
    d_gate_pre = (d_shared_act * up_pre * silu_slope).astype(jnp.bfloat16)
    d_up_pre = (d_shared_act * silu_gate).astype(jnp.bfloat16)
    grad_sg = matmul_tn(second_normed, d_gate_pre)
    grad_su = matmul_tn(second_normed, d_up_pre)
    grad_second_normed = matmul_nt(d_gate_pre, sg_full) + matmul_nt(d_up_pre, su_full)
    grad_mine = lax.dynamic_slice_in_dim(grad_full, my_rows, rows_dev, 0).astype(jnp.float32)
    d_gates = jnp.sum(grad_mine[:, None, :] * picked, -1)
    to_experts = (
        (gate_probs[:, :, None] * grad_mine[:, None, :])
        .reshape(assign_count, model_width)
        .astype(jnp.bfloat16)
    )
    slot_grads = jnp.where(slot_used[:, None] > 0, to_experts[assign_of_slot], 0)
    d_expert_out = send_rows(slot_grads)
    grad_ed = matmul_tn(e_act, d_expert_out)
    d_e_act = matmul_nt(d_expert_out, ed_mat)
    d_e_gate = (d_e_act * e_up * e_slope).astype(jnp.bfloat16)
    d_e_up = (d_e_act * e_silu).astype(jnp.bfloat16)
    grad_eg = matmul_tn(expert_rows, d_e_gate)
    grad_eu = matmul_tn(expert_rows, d_e_up)
    d_rows = (matmul_nt(d_e_gate, eg_mat) + matmul_nt(d_e_up, eu_mat)).astype(jnp.bfloat16)
    d_assign = return_rows(d_rows)[slot_of].reshape(rows_dev, top_k, model_width)
    d_routed_in = jnp.sum(d_assign, 1)
    d_chosen = gate_probs * (d_gates - jnp.sum(gate_probs * d_gates, -1, keepdims=True))
    d_logits = jnp.sum(chosen_hot * d_chosen[:, :, None], 1)
    router_f = router_full.astype(jnp.float32)
    grad_router_part = jnp.dot(normed_mine.astype(jnp.float32).T, d_logits, precision=PRECISE)
    d_router_in = jnp.dot(d_logits, router_f.T, precision=PRECISE)
    d_mine = (
        lax.dynamic_slice_in_dim(grad_second_normed, my_rows, rows_dev, 0)
        + d_routed_in
        + d_router_in
    )
    grad_second_normed = lax.dynamic_update_slice_in_dim(grad_second_normed, d_mine, my_rows, 0)
    grad_second_normed, grad_router = (
        lax.psum(grad_second_normed.astype(jnp.bfloat16), "rows").astype(jnp.float32),
        lax.psum(grad_router_part.astype(jnp.bfloat16), "rows").astype(jnp.float32),
    )
    grad_second_unit = grad_second_normed * second_gain_float
    second_gain_gradient = jnp.sum(grad_second_normed * second_unit_rows, 0)
    d_resid = grad_full.astype(jnp.float32) + second_inverse_deviation * (
        grad_second_unit
        - second_unit_rows * jnp.mean(grad_second_unit * second_unit_rows, -1, keepdims=True)
    )
    d_attn = d_resid.astype(jnp.bfloat16)
    grad_wo = matmul_tn(attn_rows, d_attn)
    d_heads = matmul_nt(d_attn, wo_full).astype(jnp.bfloat16)
    d_heads_t = jnp.transpose(
        d_heads.reshape(sequence_count, len_dev, q_heads, HEAD_DIM), (0, 2, 1, 3)
    )
    delta_rows = jnp.sum(d_heads_t.astype(jnp.float32) * attn_f32, -1)
    kv_all = lax.all_gather(kv_local, "cols", axis=0, tiled=True)
    seq_len = kv_all.shape[0]
    key_block = min(512, seq_len)

    def key_step(block_no, carry_in):
        k_start = block_no * key_block
        key_part = lax.dynamic_slice_in_dim(kv_all, k_start, key_block, 0)

        def contribute(state_in):
            d_query_in, d_kv_in = state_in
            keys_bf = key_part[:, :, :HEAD_DIM]
            values_bf = key_part[:, :, HEAD_DIM:]
            scores = (
                jnp.einsum("shqd,bsd->shqb", query_t, keys_bf, preferred_element_type=jnp.float32)
                * score_scale
            )
            key_pos = k_start + jnp.arange(key_block, dtype=jnp.int32)
            causal = positions[:, None] >= key_pos[None, :]
            prob_vals = jnp.where(causal, jnp.exp(scores - log_total[..., None]), 0.0)
            d_prob = jnp.einsum(
                "shqd,bsd->shqb", d_heads_t, values_bf, preferred_element_type=jnp.float32
            )
            d_scores = (prob_vals * (d_prob - delta_rows[..., None])).astype(jnp.bfloat16)
            d_query_in = (
                d_query_in
                + jnp.einsum(
                    "shqb,bsd->shqd", d_scores, keys_bf, preferred_element_type=jnp.float32
                )
                * score_scale
            )
            d_key = (
                jnp.einsum("shqb,shqd->bsd", d_scores, query_t, preferred_element_type=jnp.float32)
                * score_scale
            )
            d_value = jnp.einsum(
                "shqb,shqd->bsd",
                prob_vals.astype(jnp.bfloat16),
                d_heads_t,
                preferred_element_type=jnp.float32,
            )
            d_kv_in = lax.dynamic_update_slice_in_dim(
                d_kv_in, jnp.concatenate([d_key, d_value], -1), k_start, 0
            )
            return (d_query_in, d_kv_in)

        return lax.cond(k_start <= q_last, contribute, keep_same, carry_in)

    grad_start = (
        jnp.zeros((sequence_count, q_heads, len_dev, HEAD_DIM), jnp.float32),
        jnp.zeros((seq_len, sequence_count, 2 * HEAD_DIM), jnp.float32),
    )
    d_query, d_kv_all = lax.fori_loop(0, seq_len // key_block, key_step, grad_start)
    d_kv = lax.psum_scatter(
        d_kv_all.astype(jnp.bfloat16), "cols", scatter_dimension=0, tiled=True
    ).astype(jnp.float32)
    d_query_rows = (
        apply_rotary(jnp.transpose(d_query, (0, 2, 1, 3)), cosine_table, -sine_table)
        .reshape(tok_dev, q_heads * HEAD_DIM)
        .astype(jnp.bfloat16)
    )
    d_kv_t = jnp.swapaxes(d_kv, 0, 1)
    d_key_rows = (
        apply_rotary(
            d_kv_t[:, :, :HEAD_DIM].reshape(sequence_count, len_dev, 1, HEAD_DIM),
            cosine_table,
            -sine_table,
        )
        .reshape(tok_dev, HEAD_DIM)
        .astype(jnp.bfloat16)
    )
    d_value_rows = d_kv_t[:, :, HEAD_DIM:].reshape(tok_dev, HEAD_DIM).astype(jnp.bfloat16)
    grad_wq = matmul_tn(first_normed, d_query_rows)
    grad_wk = matmul_tn(first_normed, d_key_rows)
    grad_wv = matmul_tn(first_normed, d_value_rows)
    grad_first_normed = (
        matmul_nt(d_query_rows, wq_full)
        + matmul_nt(d_key_rows, wk_full)
        + matmul_nt(d_value_rows, wv_full)
    )
    grad_first_normed = lax.psum(grad_first_normed.astype(jnp.bfloat16), "rows").astype(jnp.float32)
    grad_first_unit = grad_first_normed * first_gain_float
    first_gain_gradient = jnp.sum(grad_first_normed * first_unit_rows, 0)
    d_input = d_resid + first_inverse_deviation * (
        grad_first_unit
        - first_unit_rows * jnp.mean(grad_first_unit * first_unit_rows, -1, keepdims=True)
    )
    grad_in = lax.dynamic_slice_in_dim(
        d_input.reshape(sequence_count, len_dev, model_width), row_idx * row_width, row_width, 2
    )
    g_gain_one, g_wq, g_wk, g_wv, g_wo, g_gain_two, g_router, g_sg, g_su, g_sd = (
        lax.psum_scatter(
            first_gain_gradient.astype(jnp.bfloat16), "cols", scatter_dimension=0, tiled=True
        ).astype(jnp.float32),
        lax.psum_scatter(
            grad_wq.astype(jnp.bfloat16), "cols", scatter_dimension=0, tiled=True
        ).astype(jnp.float32),
        lax.psum_scatter(
            grad_wk.astype(jnp.bfloat16), "cols", scatter_dimension=0, tiled=True
        ).astype(jnp.float32),
        lax.psum_scatter(
            grad_wv.astype(jnp.bfloat16), "cols", scatter_dimension=0, tiled=True
        ).astype(jnp.float32),
        lax.psum_scatter(
            grad_wo.astype(jnp.bfloat16), "cols", scatter_dimension=1, tiled=True
        ).astype(jnp.float32),
        lax.psum_scatter(
            second_gain_gradient.astype(jnp.bfloat16), "cols", scatter_dimension=0, tiled=True
        ).astype(jnp.float32),
        lax.psum_scatter(
            grad_router.astype(jnp.bfloat16), "cols", scatter_dimension=0, tiled=True
        ).astype(jnp.float32),
        lax.psum_scatter(
            grad_sg.astype(jnp.bfloat16), "cols", scatter_dimension=0, tiled=True
        ).astype(jnp.float32),
        lax.psum_scatter(
            grad_su.astype(jnp.bfloat16), "cols", scatter_dimension=0, tiled=True
        ).astype(jnp.float32),
        lax.psum_scatter(
            grad_sd.astype(jnp.bfloat16), "cols", scatter_dimension=1, tiled=True
        ).astype(jnp.float32),
    )
    return (
        layer_out,
        grad_in,
        g_gain_one,
        g_wq,
        g_wk,
        g_wv,
        g_wo,
        g_gain_two,
        g_router,
        g_sg,
        g_su,
        g_sd,
        grad_eg.reshape(expert_gate.shape),
        grad_eu.reshape(expert_up.shape),
        grad_ed.reshape(expert_down.shape),
    )


def scores_of(keys, queries, scale):
    return matmul_nt(keys, queries) * scale


def causal_mask(scores):
    key_pos = lax.broadcasted_iota(jnp.int32, scores.shape, 0)
    query_pos = lax.broadcasted_iota(jnp.int32, scores.shape, 1)
    return query_pos >= key_pos


MESH_ID = pl.DeviceIdType.MESH
MIB = 1024 * 1024


class Links:
    def __init__(self, n_rows, n_cols):
        self.n_rows, self.n_cols, self.ring = n_rows, n_cols, n_cols // 2
        self.r = lax.axis_index("rows")
        self.c = lax.axis_index("cols")
        self.z = lax.div(self.c, 2)
        self.k = lax.rem(self.c, 2)
        self.x = (self.flip(1), self.c)
        self.y = (self.flip(2), self.c)
        self.up = (self.r, lax.rem(self.c + 2, n_cols))
        self.down = (self.r, lax.rem(self.c + n_cols - 2, n_cols))
        self.twin = (self.r, self.c + 1 - 2 * self.k)
        self.started = []

    def flip(self, bits):
        low, high = lax.rem(self.r, 2), lax.div(self.r, 2)
        low = 1 - low if bits & 1 else low
        high = 1 - high if bits & 2 else high
        return low + 2 * high

    def chip(self, hops):
        return lax.rem(self.z + (2 * self.ring - hops), self.ring)

    def place(self, hops):
        other = self.chip(hops)
        low = lax.rem(lax.rem(self.r, 2) + lax.rem(other, 2), 2)
        high = lax.rem(lax.div(self.r, 2) + lax.div(other, 2), 2)
        return low + 2 * high

    def spread_partners(self):
        return [
            (hops, bits, (self.flip(bits), lax.rem(self.c + 2 * hops, self.n_cols)))
            for hops in range(self.ring)
            for bits in range(self.n_rows)
            if hops or bits
        ]

    def greet(self, partners):
        barrier = pltpu.get_barrier_semaphore()
        for partner in partners:
            pl.semaphore_signal(barrier, inc=1, device_id=partner, device_id_type=MESH_ID)
        pl.semaphore_wait(barrier, len(partners))

    def send(self, src, dst, sems, number, partner):
        copy = pltpu.make_async_remote_copy(
            src_ref=src,
            dst_ref=dst,
            send_sem=sems[0].at[number],
            recv_sem=sems[1].at[number],
            device_id=partner,
            device_id_type=MESH_ID,
        )
        copy.start()
        self.started.append(copy)
        return copy

    def settle(self, copies):
        for copy in copies:
            copy.wait_send()
            self.started = [other for other in self.started if other is not copy]

    def finish(self):
        for copy in self.started:
            copy.wait_send()


def run_together(*steps):
    live = list(steps)
    while live:
        live = [step for step in live if next(step, True) is None]


def pair_sems(count):
    return [pltpu.SemaphoreType.DMA((count,)), pltpu.SemaphoreType.DMA((count,))]


class SquareGather:
    def __init__(self, net, src, out, sems, local_sem, chunks, known=None):
        self.net, self.src, self.out, self.sems, self.chunks = net, src, out, sems, chunks
        self.rows, self.width = src.shape
        if known is None:
            self.own = pltpu.make_async_copy(src, self.block(0, 0), local_sem)
        else:
            self.own = pltpu.make_async_copy(known, out.at[0], local_sem)
        self.own.start()
        self.ups, self.xs, self.ys, self.lasts = {}, {}, {}, {}

    def block(self, s, j, part=None):
        columns = pl.ds(j * self.width, self.width)
        if part is None:
            return self.out.at[s, :, columns]
        half = self.rows // 2
        return self.out.at[s, pl.ds(part * half, half), columns]

    def up(self, s):
        if s:
            self.ups[s].wait_recv()
        if s < self.chunks - 1:
            whole = self.src if s == 0 else self.block(s, 0)
            self.ups[s + 1] = self.net.send(
                whole, self.block(s + 1, 0), self.sems, 7 * s, self.net.up
            )

    def across(self, s):
        half = self.rows // 2
        part_of = lambda p: (
            self.src.at[pl.ds(p * half, half), :] if s == 0 else self.block(s, 0, p)
        )
        send = self.net.send
        self.xs[s] = {
            p: send(part_of(p), self.block(s, 1, p), self.sems, 7 * s + 1 + p, self.net.x)
            for p in (0, 1)
        }
        self.ys[s] = {
            p: send(part_of(p), self.block(s, 2, p), self.sems, 7 * s + 3 + p, self.net.y)
            for p in (1, 0)
        }

    def forward(self, s):
        block, send = self.block, self.net.send
        self.xs[s][0].wait_recv()
        one = send(block(s, 1, 0), block(s, 3, 0), self.sems, 7 * s + 5, self.net.y)
        self.ys[s][1].wait_recv()
        two = send(block(s, 2, 1), block(s, 3, 1), self.sems, 7 * s + 6, self.net.x)
        self.lasts[s] = [one, two]

    def complete(self, s):
        self.xs[s][1].wait_recv()
        self.ys[s][0].wait_recv()
        for copy in self.lasts[s]:
            copy.wait_recv()


def gather_square(net, src, out, sems, local_sem, chunks):
    gather = SquareGather(net, src, out, sems, local_sem, chunks)
    gather.across(0)
    yield
    if chunks > 1:
        gather.up(0)
        yield
    gather.forward(0)
    yield
    for s in range(1, chunks):
        gather.up(s)
        gather.across(s)
        yield
        gather.forward(s)
        yield
    gather.own.wait()
    for s in range(chunks):
        gather.complete(s)


def gather_columns(net, src, spot, sems, local_sem=None):
    if local_sem is not None:
        own = pltpu.make_async_copy(src, spot(0, net.k), local_sem)
        own.start()
    twins = []
    for hops in range(net.ring):
        if hops:
            up.wait_recv()
        here = src if hops == 0 else spot(hops, net.k)
        if hops < net.ring - 1:
            up = net.send(here, spot(hops, net.k), sems, hops, net.up)
        twins.append(net.send(here, spot(hops, net.k), sems, net.ring + hops, net.twin))
        yield
    if local_sem is not None:
        own.wait()
    for copy in twins:
        copy.wait_recv()


def add_slabs(target, terms, slab=64):
    rows = target.shape[0]

    @pl.loop(0, rows // slab)
    def _(i):
        at = pl.ds(pl.multiple_of(i * slab, slab), slab)
        total = terms[0](at)
        for term in terms[1:]:
            total = total + term(at)
        target[at, :] = total.astype(target.dtype)


def part_reader(ref, *lead, columns=None):
    def read(at):
        values = ref[(*lead, at, slice(None) if columns is None else columns)]
        return values.astype(jnp.float32)

    return read


def scatter_scratch(chunks, rows, width, resident=False):
    half = rows // 2
    kept = (1, 2, 16, 128) if resident else (chunks, 2, half, width)
    return [
        pltpu.VMEM(kept, jnp.bfloat16),
        pltpu.VMEM(kept[:1] + kept[2:] if resident else (chunks, half, 2 * width), jnp.bfloat16),
        pltpu.VMEM((chunks, 2, half, width), jnp.bfloat16),
        pltpu.VMEM((chunks, half, 2 * width), jnp.bfloat16),
        pltpu.VMEM((chunks, 2, half, width), jnp.bfloat16),
        pltpu.VMEM((chunks, 2, half, width), jnp.bfloat16),
        pltpu.SemaphoreType.DMA((chunks, 3)),
    ] + pair_sems(6 * chunks)


class SquareScatter:
    def __init__(self, net, scratch, resident=False):
        self.net, self.resident = net, resident
        self.my_up, self.my_low, self.got_x, self.got_y, self.got_last = scratch[:5]
        self.stage, self.load_sems, *self.sems = scratch[5:]
        self.half, self.width = self.got_x.shape[2:]
        self.src, self.loads, self.sent = {}, {}, {}
        self.left, self.right = pl.ds(0, self.width), pl.ds(self.width, self.width)

    def part(self, i, part, j, count=1):
        rows = pl.ds(part * self.half, self.half)
        return self.src[i].at[rows, pl.ds(j * self.width, count * self.width)]

    def mine(self, i, part, j):
        if self.resident:
            return part_reader(self.part(i, part, j))
        if part == 0:
            return part_reader(self.my_up, i, j // 2)
        return part_reader(self.my_low, i, columns=(self.left, self.right)[j])

    def give(self, i, src, j):
        self.src[i] = src
        net, sems = self.net, self.sems
        sent = self.sent.setdefault(i, {})
        if j & 1:
            sent["x", j] = net.send(
                self.part(i, 0, j), self.got_x.at[i, j // 2], sems, 6 * i + j // 2, net.x
            )
        if j & 2:
            columns = pl.ds((j - 2) * self.width, self.width)
            sent["y", j] = net.send(
                self.part(i, 1, j), self.got_y.at[i, :, columns], sems, 6 * i + j, net.y
            )

    def first(self, i, src):
        for j in (3, 1, 2):
            self.give(i, src, j)
        if not self.resident:
            load = pltpu.make_async_copy
            self.loads[i] = [
                load(self.part(i, 0, 0), self.my_up.at[i, 0], self.load_sems.at[i, 0]),
                load(self.part(i, 0, 2), self.my_up.at[i, 1], self.load_sems.at[i, 1]),
                load(self.part(i, 1, 0, 2), self.my_low.at[i], self.load_sems.at[i, 2]),
            ]
            for copy in self.loads[i]:
                copy.start()

    def second(self, i):
        net, sent, sems = self.net, self.sent[i], self.sems
        for copy in self.loads.get(i, []):
            copy.wait()
        sent["x", 3].wait_recv()
        add_slabs(self.stage.at[i, 0], [self.mine(i, 0, 2), part_reader(self.got_x, i, 1)])
        sent["up"] = net.send(self.stage.at[i, 0], self.got_last.at[i, 0], sems, 6 * i + 4, net.y)
        sent["y", 3].wait_recv()
        add_slabs(
            self.stage.at[i, 1],
            [self.mine(i, 1, 1), part_reader(self.got_y, i, columns=self.right)],
        )
        sent["low"] = net.send(self.stage.at[i, 1], self.got_last.at[i, 1], sems, 6 * i + 5, net.x)

    def third(self, i):
        for key in (("x", 1), ("y", 2), "up", "low"):
            self.sent[i][key].wait_recv()
        upper = [
            self.mine(i, 0, 0), part_reader(self.got_x, i, 0), part_reader(self.got_last, i, 0)
        ]
        lower = [
            self.mine(i, 1, 0),
            part_reader(self.got_y, i, columns=self.left),
            part_reader(self.got_last, i, 1),
        ]
        return upper, lower

    def release(self, i):
        self.net.settle([self.sent[i][key] for key in (("x", 3), ("y", 3), ("x", 1), ("y", 2))])


def scatter_square(net, src, scratch, order, finish, resident=False):
    scatter = SquareScatter(net, scratch, resident)
    for i in range(len(order) + 2):
        if i < len(order):
            scatter.first(i, src.at[order[i]])
            yield
        if 0 <= i - 1 < len(order):
            scatter.second(i - 1)
            yield
        if 0 <= i - 2:
            finish(order[i - 2], *scatter.third(i - 2))
            yield


def ring_scratch(ring, rows, width):
    return [
        pltpu.VMEM((ring - 1, rows, width), jnp.bfloat16),
        pltpu.VMEM((ring - 1, rows, width), jnp.bfloat16),
    ] + pair_sems(ring - 1)


def ring_finish(net, scratch, target, copies):
    landed, leaving, *sems = scratch
    rows = landed.shape[1]

    def finish(s, upper, lower):
        turn = (s - 1) % net.ring
        for part, terms in ((0, upper), (1, lower)):
            at = pl.ds(part * (rows // 2), rows // 2)
            if turn and not part:
                copies[turn - 1].wait_recv()
            if turn:
                terms = terms + [part_reader(landed.at[turn - 1, at, :])]
            goal = target.at[at, :] if s == 0 else leaving.at[turn, at, :]
            add_slabs(goal, terms)
        if s:
            copies.append(net.send(leaving.at[turn], landed.at[turn], sems, turn, net.up))

    return finish


def scatter_columns(net, part, out, scratch):
    got_twin, landed, leaving, twin_send, twin_recv, *sems = scratch
    twins, copies = {}, []
    order = list(range(1, net.ring)) + [0]
    for hops in order:
        twins[hops] = net.send(
            part(hops, 1 - net.k), got_twin.at[hops], (twin_send, twin_recv), hops, net.twin
        )
    yield
    for turn, hops in enumerate(order):
        twins[hops].wait_recv()
        terms = [part_reader(part(hops, net.k)), part_reader(got_twin, hops)]
        if turn:
            copies[turn - 1].wait_recv()
            terms.append(part_reader(landed, turn - 1))
        add_slabs(leaving.at[turn] if hops else out, terms, 32)
        if hops:
            copies.append(net.send(leaving.at[turn], landed.at[turn], sems, turn, net.up))
        yield


def scatter_columns_scratch(ring, rows, width):
    return [
        pltpu.VMEM((ring, rows, width), jnp.bfloat16),
        pltpu.VMEM((ring - 1, rows, width), jnp.bfloat16),
        pltpu.VMEM((ring - 1, rows, width), jnp.bfloat16),
    ] + pair_sems(ring) + pair_sems(ring - 1)


def remote_call(kernel, name, collective_id, out_shape, scratch, operands, in_vmem=(), out_vmem=(), cost=None):
    anywhere = pl.BlockSpec(memory_space=pl.ANY)
    vmem = pl.BlockSpec(memory_space=pltpu.VMEM)
    return pl.pallas_call(
        kernel,
        out_shape=out_shape,
        in_specs=[vmem if i in in_vmem else anywhere for i in range(len(operands))],
        out_specs=[vmem if i in out_vmem else anywhere for i in range(len(out_shape))],
        scratch_shapes=scratch,
        compiler_params=pltpu.CompilerParams(
            collective_id=collective_id, has_side_effects=True, vmem_limit_bytes=63 * MIB
        ),
        cost_estimate=cost,
        name=name,
    )(*operands)


def spread_columns(net, packed, spot, sems, local_sem):
    own = pltpu.make_async_copy(packed.at[net.chip(0)], spot(0, net.k), local_sem)
    own.start()
    pieces = []
    for hops in range(1, net.ring):
        target = (net.r, lax.rem(net.c + 2 * hops, net.n_cols))
        pieces.append(
            net.send(packed.at[net.chip(-hops)], spot_at(spot, net, hops), sems, hops, target)
        )
    yield
    own.wait()
    twins = [net.send(spot(0, net.k), spot(0, net.k), sems, net.ring, net.twin)]
    yield
    for hops in range(1, net.ring):
        pieces[hops - 1].wait_recv()
        here = spot(hops, net.k)
        twins.append(net.send(here, here, sems, net.ring + hops, net.twin))
        yield
    for copy in twins:
        copy.wait_recv()


def spot_at(spot, net, hops):
    return spot(0, net.k)


def first_phase(n_rows, n_cols, block, grads, weights, small, weights_out, packed, slot_map, tables):
    ring = n_cols // 2
    length, row_width = block.shape
    model = n_rows * row_width
    col_width, in_width = weights.shape
    q_width = weights_out.shape[1]
    heads = q_width // HEAD_DIM
    small_width = small.shape[1]
    experts = slot_map.shape[0]
    scale = 1.0 / math.sqrt(HEAD_DIM)
    pieces = 2
    piece = length // pieces
    bf16, f32 = jnp.bfloat16, jnp.float32
    shape = jax.ShapeDtypeStruct

    def kernel(
        x_in, g_in, w_in, small_in, wo_in, packed_in, map_in, cosine, sine,
        x_out, normed_out, w_out, small_out, q, kv_out, out, lse, wo_out, g_out, second, map_out,
        shared_out, sum_out, gains_out, scale_out,
        x, normed, w, small_all, kv, wo, proj, proj_sum, result, projected, top, total, acc,
        *sems,
    ):
        scratch, sems = list(sems[:9]), list(sems[9:])
        pairs = lambda: (sems.pop(0), sems.pop(0))
        x_sems, g_sems, w_sems, small_sems, wo_sems, kv_sems = [pairs() for _ in range(6)]
        map_sems, shared_sems, sum_sems, sum_sems_two, u_sems = [pairs() for _ in range(5)]
        local = sems.pop(0)
        net = Links(n_rows, n_cols)
        others = net.spread_partners()
        net.greet([device for _, _, device in others] + [net.twin])
        by_place = lambda ref, columns=slice(None): lambda hops, core: ref.at[
            pl.ds((net.place(hops) * 2 + core) * col_width, col_width), columns
        ]
        for_q, for_kv = pl.ds(0, q_width), pl.ds(q_width, 2 * HEAD_DIM)

        x_steps = gather_square(net, x_in, x, x_sems, local.at[0], 1)
        small_steps = gather_columns(net, small_in, by_place(small_all), small_sems, local.at[1])
        w_steps = gather_columns(net, w_in.at[:, for_q], by_place(w, for_q), w_sems, local.at[2])
        u_steps = gather_columns(net, w_in.at[:, for_kv], by_place(w, for_kv), u_sems, local.at[18])
        wo_steps = gather_columns(net, wo_in, by_place(wo), wo_sems, local.at[3])
        g_steps = gather_square(net, g_in, g_out, g_sems, local.at[4], ring)
        saves = []

        def save(src, dst):
            copy = pltpu.make_async_copy(src, dst, local.at[8 + len(saves)])
            copy.start()
            saves.append(copy)

        next(small_steps)
        next(u_steps)
        next(x_steps)
        next(w_steps)
        maps = []
        for number, (hops, bits, device) in enumerate(others):
            maps.append(net.send(map_in, map_out.at[hops, net.r], map_sems, number, device))
        own_map = pltpu.make_async_copy(map_in, map_out.at[0, net.r], local.at[5])
        own_map.start()
        next(small_steps)
        next(u_steps)
        next(w_steps)
        next(x_steps)
        next(g_steps)
        next(small_steps)
        next(u_steps)
        next(small_steps)
        next(u_steps)
        next(w_steps)
        run_together(x_steps, small_steps)
        save(x.at[0], x_out)
        save(small_all, small_out)
        gains = small_all[...].astype(f32).T
        gains_out[...] = gains[experts : experts + 8]
        first_gain = gains[experts : experts + 1]
        second_gain = gains[experts + 1 : experts + 2]

        @pl.loop(0, length // 64)
        def _(i):
            at = pl.ds(pl.multiple_of(i * 64, 64), 64)
            values = x[0, at, :].astype(f32)
            inverse = lax.rsqrt(jnp.mean(values * values, -1, keepdims=True) + NORM_EPS)
            normed[at, :] = (values * inverse * first_gain).astype(bf16)
            scale_out[at, :] = jnp.broadcast_to(inverse, (64, 128))

        save(normed, normed_out)
        def rotate(columns):
            values = projected[:, columns]
            turned = pltpu.roll(values, HEAD_DIM // 2, 1)
            return (values * cosine[...] + turned * sine[...]).astype(bf16)

        run_together(u_steps)
        projected[:, for_kv] = matmul(normed[...], w[:, for_kv])
        kv[net.c, :, :HEAD_DIM] = rotate(slice(q_width, q_width + HEAD_DIM))
        kv[net.c, :, HEAD_DIM:] = projected[:, q_width + HEAD_DIM :].astype(bf16)
        kv_steps = gather_columns(
            net, kv.at[net.c], lambda hops, core: kv.at[2 * net.chip(hops) + core], kv_sems
        )
        next(kv_steps)
        next(w_steps)
        next(kv_steps)
        run_together(w_steps)
        save(w, w_out)
        next(wo_steps)
        next(g_steps)
        projected[:, for_q] = matmul(normed[...], w[:, for_q])
        for head in range(heads):
            columns = slice(head * HEAD_DIM, (head + 1) * HEAD_DIM)
            q[:, columns] = rotate(columns)
        next(kv_steps)
        next(g_steps)
        next(kv_steps)
        next(wo_steps)
        run_together(kv_steps)
        save(kv, kv_out)
        next(wo_steps)
        next(g_steps)

        for head in range(heads):
            columns = slice(head * HEAD_DIM, (head + 1) * HEAD_DIM)
            queries = q[:, columns]

            def part(number):
                return scores_of(kv[number, :, :HEAD_DIM], queries, scale), kv[number, :, HEAD_DIM:]

            scores, values = part(net.c)
            scores = jnp.where(causal_mask(scores), scores, NEG_LARGE)
            high = jnp.max(scores, 0, keepdims=True)
            probs = jnp.exp(scores - high)
            top[...] = high
            total[...] = jnp.sum(probs, 0, keepdims=True)
            acc[...] = matmul_tn(values, probs.astype(bf16))

            @pl.loop(0, net.c)
            def _(number):
                scores, values = part(number)
                high = jnp.maximum(top[...], jnp.max(scores, 0, keepdims=True))
                probs = jnp.exp(scores - high)
                shrink = jnp.exp(top[...] - high)
                top[...] = high
                total[...] = total[...] * shrink + jnp.sum(probs, 0, keepdims=True)
                acc[...] = acc[...] * shrink + matmul_tn(values, probs.astype(bf16))

            out[:, columns] = (acc[...] / total[...]).T
            lse[head] = top[...] + jnp.log(total[...])
            if head == 0:
                next(g_steps)
            if head == 2:
                next(wo_steps)
            if head == 3:
                next(g_steps)

        run_together(wo_steps)
        save(wo, wo_out)
        heads_out = out[...].astype(bf16)
        for s in range(pieces):
            for j in range(n_rows):
                at = slice(j * row_width, (j + 1) * row_width)
                proj[s, :, at] = matmul_nt(
                    heads_out[s * piece : (s + 1) * piece], wo[at, :]
                ).astype(bf16)
        gathers = []

        def finish(s, upper, lower):
            add_slabs(result.at[s, pl.ds(0, piece // 2), :], upper)
            add_slabs(result.at[s, pl.ds(piece // 2, piece // 2), :], lower)
            steps = gather_square(
                net, result.at[s], proj_sum.at[pl.ds(s, 1)], (sum_sems, sum_sems_two)[s],
                local.at[6 + s], 1,
            )
            next(steps)
            gathers.append(steps)

        shared_steps = spread_columns(
            net, packed_in, by_place(shared_out), shared_sems, local.at[8 + 8]
        )
        sum_steps = scatter_square(net, proj, scratch, list(range(pieces)), finish, resident=True)
        next(sum_steps)
        next(shared_steps)
        next(sum_steps)
        run_together(sum_steps)
        next(shared_steps)

        def second_norm(s):
            @pl.loop(0, piece // 64)
            def _(i):
                at = pl.ds(pl.multiple_of(i * 64, 64), 64)
                there = pl.ds(pl.multiple_of(s * piece + i * 64, 64), 64)
                values = x[0, there, :].astype(f32) + proj_sum[s, at, :].astype(f32)
                inverse = lax.rsqrt(jnp.mean(values * values, -1, keepdims=True) + NORM_EPS)
                second[there, :] = (values * inverse * second_gain).astype(bf16)

        for s in range(pieces):
            run_together(gathers[s])
            second_norm(s)
        save(proj_sum, sum_out)
        run_together(g_steps, shared_steps)
        own_map.wait()
        for copy in maps:
            copy.wait_recv()
        for copy in saves:
            copy.wait()
        net.finish()

    partners = n_rows * ring - 1
    vmem = pltpu.VMEM
    return remote_call(
        kernel,
        "first_phase",
        1,
        [
            shape((length, model), bf16),
            shape((length, model), bf16),
            shape((model, in_width), bf16),
            shape((model, small_width), bf16),
            shape((length, q_width), bf16),
            shape((n_cols, length, 2 * HEAD_DIM), bf16),
            shape((length, q_width), f32),
            shape((heads, 1, length), f32),
            shape((model, q_width), bf16),
            shape((ring, length, model), bf16),
            shape((length, model), bf16),
            shape((ring, n_rows, *slot_map.shape), f32),
            shape((model, packed.shape[2]), bf16),
            shape((pieces, piece, model), bf16),
            shape((8, model), f32),
            shape((length, 128), f32),
        ],
        [
            vmem((1, length, model), bf16),
            vmem((length, model), bf16),
            vmem((model, in_width), bf16),
            vmem((model, small_width), bf16),
            vmem((n_cols, length, 2 * HEAD_DIM), bf16),
            vmem((model, q_width), bf16),
            vmem((pieces, piece, model), bf16),
            vmem((pieces, piece, model), bf16),
            vmem((pieces, piece, row_width), bf16),
            vmem((length, in_width), f32),
            vmem((1, length), f32),
            vmem((1, length), f32),
            vmem((HEAD_DIM, length), f32),
        ]
        + scatter_scratch(pieces, piece, row_width, resident=True)
        + pair_sems(7)
        + pair_sems(7 * ring)
        + pair_sems(2 * ring)
        + pair_sems(2 * ring)
        + pair_sems(2 * ring)
        + pair_sems(2 * ring)
        + pair_sems(partners)
        + pair_sems(2 * ring)
        + pair_sems(7)
        + pair_sems(7)
        + pair_sems(2 * ring)
        + [pltpu.SemaphoreType.DMA((19,))],
        (block, grads, weights, small, weights_out, packed, slot_map, *tables),
        in_vmem=(7, 8),
        out_vmem=(4, 6, 7, 10, 14, 15),
    )


def experts_phase(n_rows, n_cols, second, grads, maps, experts_w, shared, router, slots):
    ring = n_cols // 2
    tokens, model = second.shape
    width = model // n_rows
    experts = n_rows * ring
    half_hidden = experts_w[0].shape[1]
    hidden = 2 * half_hidden
    pad = shared.shape[1] // 3
    blocks, _, block_rows = maps.shape[1:]
    n_slots = blocks * slots
    bf16, f32 = jnp.bfloat16, jnp.float32
    shape = jax.ShapeDtypeStruct

    def kernel(
        known, g_in, maps, gate_own, gate_twin, up_own, up_twin, down_own, down_twin, shared_in,
        router_in,
        result, rows_out, y_out, slot_out, d_part_out, act_out, d_gate_out, d_up_out, s_act_out,
        d_shared_out, probs_out, gate_out,
        w_gate, w_up, w_down, shared, router, x, g, slot_rows, part, e_act, d_gate, d_up, s_act,
        d_shared, probs, d_x, d_gates, *rest,
    ):
        scratch, (landed, leaving, ring_s, ring_r) = rest[:9], rest[9:13]
        xs, xr, ms, mr, local, w_sems, out_sems = rest[13:]
        net = Links(n_rows, n_cols)
        others = net.spread_partners()
        net.greet([device for _, _, device in others])
        mine = net.r * ring + net.z
        gather = SquareGather(
            net, known.at[:, pl.ds(0, width)], rows_out, (xs, xr), local.at[0], ring, known=known
        )
        gather.up(0)
        x_load = lambda s: pltpu.make_async_copy(
            known if s == 0 else rows_out.at[s], x, local.at[1]
        )
        g_load = lambda s: pltpu.make_async_copy(g_in.at[s], g, local.at[2])
        x_load(0).start()
        g_load(0).start()
        shared_load = pltpu.make_async_copy(shared_in, shared, local.at[3])
        shared_load.start()
        router_load = pltpu.make_async_copy(router_in, router, local.at[4])
        router_load.start()
        weights = []
        for j in range(n_rows):
            there = pl.ds(pl.multiple_of(net.flip(j) * width, width), width)
            here = pl.ds(j * width, width)
            for h, sources in enumerate(((gate_own, up_own, down_own), (gate_twin, up_twin, down_twin))):
                cols = pl.ds(h * half_hidden, half_hidden)
                number = 6 * j + 3 * h
                weights += [
                    pltpu.make_async_copy(
                        sources[0].at[there, :], w_gate.at[here, cols], w_sems.at[number]
                    ),
                    pltpu.make_async_copy(
                        sources[1].at[there, :], w_up.at[here, cols], w_sems.at[number + 1]
                    ),
                    pltpu.make_async_copy(
                        sources[2].at[:, there], w_down.at[cols, here], w_sems.at[number + 2]
                    ),
                ]
        scatter = SquareScatter(net, scratch, resident=True)
        ring_copies, stores = {}, {}
        kept = {
            "slot": (slot_rows, slot_out), "part": (part, d_part_out), "act": (e_act, act_out),
            "d_gate": (d_gate, d_gate_out), "d_up": (d_up, d_up_out), "s_act": (s_act, s_act_out),
            "d_shared": (d_shared, d_shared_out), "probs": (probs, probs_out), "y": (g, y_out),
        }

        def store(s, *names):
            for name in names:
                source, target = kept[name]
                number = list(kept).index(name)
                stores[name] = pltpu.make_async_copy(source, target.at[s], out_sems.at[number])
                stores[name].start()

        def stored(*names):
            for name in names:
                if name in stores:
                    stores.pop(name).wait()

        def pass_on(s):
            turn = s - 1
            for p, terms in enumerate(scatter.third(s)):
                at = pl.ds(p * (tokens // 2), tokens // 2)
                if s == 0:
                    add_slabs(result.at[at, :], terms)
                    continue
                if turn:
                    ring_copies[turn - 1, p].wait_recv()
                    terms = terms + [part_reader(landed.at[turn - 1, at, :])]
                if turn > 1:
                    net.settle([ring_copies[turn - 2, p]])
                add_slabs(leaving.at[turn % 2, at, :], terms)
                ring_copies[turn, p] = net.send(
                    leaving.at[turn % 2, at, :], landed.at[turn, at, :], (ring_s, ring_r),
                    2 * turn + p, net.up,
                )

        def in_lanes(column):
            high = column.astype(bf16)
            rest = column - high.astype(f32)
            middle = rest.astype(bf16)
            low = (rest - middle.astype(f32)).astype(bf16)
            lane = lax.broadcasted_iota(jnp.int32, (column.shape[0], 128), 1)
            terms = jnp.where(lane == 0, high.astype(f32), 0.0)
            terms = jnp.where(lane == 1, middle.astype(f32), terms)
            return jnp.where(lane == 2, low.astype(f32), terms).astype(bf16)

        tile = 512

        def compute(s, ticks):
            def tick(name):
                for step in ticks.get(name, []):
                    step()

            lanes = lax.broadcasted_iota(jnp.int32, (1, 128), 1)
            mine_hot = (lanes == mine).astype(f32)
            slot_row, slot_column, chosen = [], [], []
            for b in range(blocks):
                own_map = jnp.where(
                    lax.broadcasted_iota(jnp.int32, (experts, block_rows), 0) == mine, maps[s, b], 0.0
                )
                own_map = jnp.sum(own_map, 0, keepdims=True)
                slot_row.append(jnp.where(own_map >= 0, own_map + b * slots, -1.0))
                filled = jnp.concatenate(
                    [maps[s, b], jnp.full((128 - experts, block_rows), -1.0, f32)], 0
                ).T
                chosen.append(filled)
                own_map = jnp.sum(filled * mine_hot, -1, keepdims=True)
                slot_column.append(jnp.where(own_map >= 0, own_map + b * slots, -1.0))
            slot_row, chosen = jnp.concatenate(slot_row, 1), jnp.concatenate(chosen, 0)
            slot_column = jnp.concatenate(slot_column, 0)
            numbers = lambda dims, axis: lax.broadcasted_iota(jnp.int32, dims, axis).astype(f32)
            pick = (numbers((n_slots, tokens), 0) == slot_row).astype(f32).astype(bf16)
            pick_t = (numbers((tokens, n_slots), 1) == slot_column).astype(f32).astype(bf16)

            stored("probs", "s_act", "d_shared", "y")
            if s:
                g_load(s).start()
            x_load(s).wait()
            if s == 0:
                router_load.wait()
                shared_load.wait()
                g_load(0).wait()
                for copy in weights:
                    copy.start()
            logits = matmul(x[...], router[...])
            logits = jnp.where(chosen >= 0, logits, NEG_LARGE)
            logits = jnp.exp(logits - jnp.max(logits, -1, keepdims=True))
            gate_probs = logits / jnp.sum(logits, -1, keepdims=True)
            probs[...] = gate_probs
            my_gate = jnp.sum(gate_probs * mine_hot, -1, keepdims=True)
            slot_gate = jnp.sum(matmul(pick, in_lanes(my_gate)), -1, keepdims=True)
            s_gate = matmul(x[...], shared[:, :pad])
            s_up = matmul(x[...], shared[:, pad : 2 * pad])
            if s:
                g_load(s).wait()
            through = matmul(g[...], shared[:, 2 * pad :])
            s_silu, s_slope = silu_parts(s_gate)
            s_act[...] = (s_silu * s_up).astype(bf16)
            d_shared[:, :pad] = (through * s_up * s_slope).astype(bf16)
            d_shared[:, pad:] = (through * s_silu).astype(bf16)
            store(s, "probs", "s_act", "d_shared")
            tick("shared")

            stored("slot", "part", "act", "d_gate", "d_up")
            for t in range(model // tile):
                at = slice(t * tile, (t + 1) * tile)
                slot_rows[:, at] = matmul(pick, x[:, at]).astype(bf16)
                part[:, at] = matmul(pick, g[:, at]).astype(bf16)
            if s == 0:
                for copy in weights:
                    copy.wait()
            tick("picked")

            step = half_hidden // 3

            def hidden_tile(t, total):
                at = pl.ds(pl.multiple_of(t * step, step), step)
                e_gate = matmul(slot_rows[...], w_gate[:, at])
                e_up = matmul(slot_rows[...], w_up[:, at])
                through = matmul_nt(part[...], w_down[at, :])
                e_silu, e_slope = silu_parts(e_gate)
                act = e_silu * e_up
                d_act = through * slot_gate
                e_act[:, at] = act.astype(bf16)
                d_gate[:, at] = (d_act * e_up * e_slope).astype(bf16)
                d_up[:, at] = (d_act * e_silu).astype(bf16)
                return total + jnp.sum(act * through, -1, keepdims=True)

            d_slot_gate = lax.fori_loop(0, 3, hidden_tile, jnp.zeros((n_slots, 1), f32))
            tick("half")
            d_slot_gate = lax.fori_loop(3, 6, hidden_tile, d_slot_gate)
            d_gates[net.chip(s)] = jnp.sum(
                matmul_tn(in_lanes(d_slot_gate), pick), 0, keepdims=True
            )
            part[...] = (part[...].astype(f32) * slot_gate).astype(bf16)
            store(s, "slot", "part", "act", "d_gate", "d_up")
            tick("hidden")

            d_chunk = d_x.at[s % 2]
            if s >= 2:
                scatter.release(s - 2)
            def out_tile(t):
                at = pl.ds(pl.multiple_of(t * tile, tile), tile)
                d_slot = matmul_nt(d_gate[...], w_gate[at, :]) + matmul_nt(d_up[...], w_up[at, :])
                d_chunk[:, at] = (
                    matmul(pick_t, d_slot.astype(bf16))
                    + matmul_nt(d_shared[...], shared[at, : 2 * pad])
                ).astype(bf16)
                out = (matmul(e_act[...], w_down[:, at]) * slot_gate).astype(bf16)
                g[:, at] = (
                    matmul(pick_t, out) + matmul_nt(s_act[...], shared[at, 2 * pad :])
                ).astype(bf16)

            pl.loop(2, 5)(out_tile)
            tick("right")
            scatter.give(s, d_chunk, 3)
            scatter.give(s, d_chunk, 2)
            pl.loop(0, 2)(out_tile)
            scatter.give(s, d_chunk, 1)
            store(s, "y")
            tick("left")

        def arrive(s):
            def step():
                gather.up(s)
                gather.across(s)

            return step

        def take(s):
            def step():
                gather.complete(s)
                x_load(s).start()

            return step

        pass_x = lambda s: lambda: gather.forward(s)
        second_of = lambda s: lambda: scatter.second(s)
        third_of = lambda s: lambda: pass_on(s)
        compute(0, {"hidden": [arrive(1)], "right": [pass_x(1)], "left": [arrive(2), take(1)]})
        compute(
            1,
            {
                "half": [pass_x(2), arrive(3)],
                "hidden": [second_of(0)],
                "left": [third_of(0), take(2)],
            },
        )
        compute(2, {"picked": [pass_x(3)], "hidden": [second_of(1)], "left": [third_of(1), take(3)]})
        compute(3, {"hidden": [second_of(2)], "left": [third_of(2)]})
        copies = []
        own = pltpu.make_async_copy(d_gates, gate_out.at[mine], local.at[5])
        own.start()
        for number, (hops, bits, device) in enumerate(others):
            copies.append(net.send(d_gates, gate_out.at[mine], (ms, mr), number, device))
        scatter.second(3)
        pass_on(3)
        for p in range(2):
            at = pl.ds(p * (tokens // 2), tokens // 2)
            ring_copies[ring - 2, p].wait_recv()
            add_slabs(
                result.at[at, :], [part_reader(result.at[at, :]), part_reader(landed.at[ring - 2, at, :])]
            )
        stored(*kept)
        own.wait()
        gather.own.wait()
        for copy in copies:
            copy.wait_recv()
        net.finish()

    vmem = pltpu.VMEM
    by_chunk = lambda dtype, *dims: shape((ring, *dims), dtype)
    return remote_call(
        kernel,
        "experts_phase",
        5,
        [
            shape((tokens, width), bf16),
            by_chunk(bf16, tokens, model),
            by_chunk(bf16, tokens, model),
            by_chunk(bf16, n_slots, model),
            by_chunk(bf16, n_slots, model),
            by_chunk(bf16, n_slots, hidden),
            by_chunk(bf16, n_slots, hidden),
            by_chunk(bf16, n_slots, hidden),
            by_chunk(bf16, tokens, pad),
            by_chunk(bf16, tokens, 2 * pad),
            by_chunk(f32, tokens, 128),
            shape((experts, ring, 1, tokens), f32),
        ],
        [
            vmem((model, hidden), bf16),
            vmem((model, hidden), bf16),
            vmem((hidden, model), bf16),
            vmem(shared.shape, bf16),
            vmem(router.shape, bf16),
            vmem((tokens, model), bf16),
            vmem((tokens, model), bf16),
            vmem((n_slots, model), bf16),
            vmem((n_slots, model), bf16),
            vmem((n_slots, hidden), bf16),
            vmem((n_slots, hidden), bf16),
            vmem((n_slots, hidden), bf16),
            vmem((tokens, pad), bf16),
            vmem((tokens, 2 * pad), bf16),
            vmem((tokens, 128), f32),
            vmem((2, tokens, model), bf16),
            vmem((ring, 1, tokens), f32),
        ]
        + scatter_scratch(ring, tokens, width, resident=True)
        + [vmem((ring - 1, tokens, width), bf16), vmem((2, tokens, width), bf16)]
        + pair_sems(2 * (ring - 1))
        + pair_sems(7 * ring)
        + pair_sems(experts - 1)
        + [
            pltpu.SemaphoreType.DMA((6,)),
            pltpu.SemaphoreType.DMA((24,)),
            pltpu.SemaphoreType.DMA((9,)),
        ],
        (second, grads, maps, *experts_w, shared, router),
        in_vmem=(2,),
        out_vmem=(0,),
    )


def attention_back(
    n_rows, n_cols, d_block, d_gates, probs, router, token_rows, gains, weights_out, weights_in,
    queries, kv, heads_out, lse, tables, parts, expert_rows,
):
    ring = n_cols // 2
    length, model = token_rows[0].shape
    experts = n_rows * ring
    q_width = weights_out.shape[1]
    in_width = weights_in.shape[1]
    col_width = model // n_cols
    width = model // n_rows
    heads = q_width // HEAD_DIM
    scale = 1.0 / math.sqrt(HEAD_DIM)
    half = expert_rows[2].shape[1] // 2
    n_slots = expert_rows[2].shape[0]
    bf16, f32 = jnp.bfloat16, jnp.float32
    shape = jax.ShapeDtypeStruct

    def kernel(
        block, gates, probs_in, router, x_in, proj_in, g_in, gains, wo_in, w_in, q, kv, out, lse, cosine,
        sine, y_in, xr_in, dp_in, act_in, dg_in, du_in,
        d_proj, d_first, y_out, wo_out, d_resid, gain_out, xr_out, dp_out, act_out, dg_out, du_out,
        second, proj, g, probs, high_ref, low_ref,
        wo, w, go, delta, dqt, dkv, dkv_own, wo_part, y_hold, y_landed, *rest,
    ):
        scratch, kv_parts, wo_parts = rest[:9], rest[9:16], rest[16:23]
        gs, gr, yr_s, yr_r, es, er, local = rest[23:]
        net = Links(n_rows, n_cols)
        net.greet([net.x, net.y, net.up, net.down, net.twin])
        gather = gather_square(net, block, second, (gs, gr), local.at[1], 1)
        next(gather)
        others = pl.ds(half, half)
        twins = [
            net.send(source, target, (es, er), number, net.twin)
            for number, (source, target) in enumerate(
                (
                    (xr_in, xr_out), (dg_in.at[:, others], dg_out), (du_in.at[:, others], du_out),
                    (act_in.at[:, others], act_out), (dp_in, dp_out),
                )
            )
        ]
        x, d_attn = d_first, proj
        loads = [
            pltpu.make_async_copy(a, b, local.at[2 + i])
            for i, (a, b) in enumerate(((x_in, x), (proj_in, proj), (g_in.at[0], g)))
        ]
        probs_load = pltpu.make_async_copy(probs_in.at[0], probs, local.at[6])
        probs_load.start()
        for load in loads:
            load.start()
        wo_load = pltpu.make_async_copy(wo_in, wo, local.at[5])
        wo_load.start()
        w_load = pltpu.make_async_copy(w_in, w, local.at[0])
        w_load.start()
        d_gates = jnp.concatenate(
            [gates[...].reshape(experts, length), jnp.zeros((128 - experts, length), f32)], 0
        ).T
        probs_load.wait()
        d_logits = probs[...] * (d_gates - jnp.sum(probs[...] * d_gates, -1, keepdims=True))
        high = d_logits.astype(bf16)
        high_ref[...] = high
        low_ref[...] = (d_logits - high.astype(f32)).astype(bf16)
        for load in loads:
            load.wait()

        hop = []

        def keep_sum(s, upper, lower):
            half = length // 2
            target = y_hold if s == 1 else y_out.at[s - 1]
            add_slabs(target.at[pl.ds(0, half), :], upper)
            add_slabs(target.at[pl.ds(half, half), :], lower)
            if s == 1:
                hop.append(net.send(y_hold, y_landed, (yr_s, yr_r), 0, net.up))

        y_steps = scatter_square(net, y_in, scratch, list(range(1, ring)), keep_sum)
        by_place = lambda ref: lambda hops, core: ref.at[
            pl.ds((net.place(hops) * 2 + core) * col_width, col_width), :
        ]

        run_together(gather)
        next(y_steps)
        next(y_steps)
        gain = gains[1:2]
        gain_out[...] = jnp.zeros_like(gain_out)

        @pl.loop(0, length // 128)
        def _(i):
            at = pl.ds(pl.multiple_of(i * 128, 128), 128)
            values = x[at, :].astype(f32) + proj[at, :].astype(f32)
            inverse = lax.rsqrt(jnp.mean(values * values, -1, keepdims=True) + NORM_EPS)
            unit = values * inverse
            d_second = second[0, at, :].astype(f32)
            d_second = d_second + matmul_nt(high_ref[at, :], router[...])
            d_second = d_second + matmul_nt(low_ref[at, :], router[...])
            d_unit = d_second * gain
            moment = jnp.mean(d_unit * unit, -1, keepdims=True)
            resid = g[at, :].astype(f32) + inverse * (d_unit - unit * moment)
            d_attn[at, :] = resid.astype(bf16)
            d_resid[at, :] = resid[:, :width]
            along = (d_second[:, :width] * unit[:, :width]).reshape(16, 8, width)
            gain_out[...] += jnp.sum(along, 0)

        wo_load.wait()
        go[...] = matmul(d_attn[...], wo[...]).astype(bf16)
        wo_part[...] = matmul_tn(d_attn[...], out[...].astype(bf16)).astype(bf16)
        wo_steps = scatter_columns(net, by_place(wo_part), wo_out, wo_parts)
        next(wo_steps)
        for head in range(heads):
            columns = slice(head * HEAD_DIM, (head + 1) * HEAD_DIM)
            product = (go[:, columns].astype(f32) * out[:, columns]).T
            delta[head] = jnp.sum(product, 0, keepdims=True)
        dqt[...] = jnp.zeros_like(dqt)
        dkv[...] = jnp.zeros_like(dkv)
        next(wo_steps)
        next(y_steps)
        next(y_steps)

        def one_block(number, masked):
            keys = kv[number, :, :HEAD_DIM]
            values = kv[number, :, HEAD_DIM:]
            keys_t = keys.T
            d_key = jnp.zeros((length, HEAD_DIM), f32)
            d_value = jnp.zeros((length, HEAD_DIM), f32)
            for head in range(heads):
                columns = slice(head * HEAD_DIM, (head + 1) * HEAD_DIM)
                queries = q[:, columns]
                grads = go[:, columns]
                probs = jnp.exp(scores_of(keys, queries, scale) - lse[head])
                if masked:
                    probs = jnp.where(causal_mask(probs), probs, 0.0)
                d_probs = matmul_nt(values, grads)
                d_scores = (probs * (d_probs - delta[head])).astype(bf16)
                d_value = d_value + matmul(probs.astype(bf16), grads)
                d_key = d_key + matmul(d_scores, queries)
                dqt[head] = dqt[head] + matmul(keys_t, d_scores)
            dkv[number, :, :HEAD_DIM] = (d_key * scale).astype(bf16)
            dkv[number, :, HEAD_DIM:] = d_value.astype(bf16)

        one_block(net.c, True)
        middle = lax.div(net.c, 2)

        @pl.loop(0, middle)
        def _(number):
            one_block(number, False)

        next(y_steps)
        next(y_steps)
        next(wo_steps)

        @pl.loop(middle, net.c)
        def _(number):
            one_block(number, False)

        next(wo_steps)
        kv_steps = scatter_columns(
            net, lambda hops, core: dkv.at[2 * net.chip(hops) + core], dkv_own, kv_parts
        )
        next(kv_steps)
        next(kv_steps)
        next(y_steps)

        def turned_back(values):
            return (values * cosine[...] - pltpu.roll(values, HEAD_DIM // 2, 1) * sine[...]).astype(bf16)

        for head in range(heads):
            columns = slice(head * HEAD_DIM, (head + 1) * HEAD_DIM)
            d_proj[:, columns] = turned_back((dqt[head] * scale).T)
        next(kv_steps)
        next(y_steps)
        next(kv_steps)
        next(wo_steps)
        run_together(kv_steps)
        next(y_steps, None)
        d_proj[:, q_width : q_width + HEAD_DIM] = turned_back(dkv_own[:, :HEAD_DIM])
        d_proj[:, q_width + HEAD_DIM :] = dkv_own[:, HEAD_DIM:].astype(bf16)
        w_load.wait()
        for j in range(n_rows):
            at = slice(j * width, (j + 1) * width)
            d_first[:, at] = matmul_nt(d_proj[...], w[at, :]).astype(bf16)
        run_together(y_steps, wo_steps)
        hop[0].wait_recv()
        y_out[0] = y_landed[...]
        for copy in twins:
            copy.wait_recv()
        net.finish()

    vmem = pltpu.VMEM
    return remote_call(
        kernel,
        "attention_back",
        6,
        [
            shape((length, in_width), bf16),
            shape((length, model), bf16),
            shape((ring - 1, length, width), bf16),
            shape((col_width, q_width), f32),
            shape((length, width), f32),
            shape((8, width), f32),
            shape((n_slots, model), bf16),
            shape((n_slots, model), bf16),
            shape((n_slots, half), bf16),
            shape((n_slots, half), bf16),
            shape((n_slots, half), bf16),
        ],
        [
            vmem((1, length, model), bf16),
            vmem((length, model), bf16),
            vmem((length, model), bf16),
            vmem((length, 128), f32),
            vmem((length, 128), bf16),
            vmem((length, 128), bf16),
            vmem((model, q_width), bf16),
            vmem((model, in_width), bf16),
            vmem((length, q_width), bf16),
            vmem((heads, 1, length), f32),
            vmem((heads, HEAD_DIM, length), f32),
            vmem((n_cols, length, 2 * HEAD_DIM), bf16),
            vmem((length, 2 * HEAD_DIM), f32),
            vmem((model, q_width), bf16),
            vmem((length, width), bf16),
            vmem((length, width), bf16),
        ]
        + scatter_scratch(ring - 1, length, width)
        + scatter_columns_scratch(ring, length, 2 * HEAD_DIM)
        + scatter_columns_scratch(ring, col_width, q_width)
        + pair_sems(7)
        + pair_sems(1)
        + pair_sems(5)
        + [pltpu.SemaphoreType.DMA((7,))],
        (
            d_block, d_gates, probs, router, *token_rows, gains, weights_out, weights_in, queries, kv,
            heads_out, lse, *tables, parts, *expert_rows,
        ),
        in_vmem=(1, 3, 7, 10, 11, 12, 13, 14, 15),
        out_vmem=(0, 1, 2, 3, 4, 5),
    )


def last_phase(
    n_rows, n_cols, d_first, d_proj, normed, parts, part_sum, x, proj, d_resid, gains, gain_part,
    x_scale, expert_rows, twin_rows, router_rows,
):
    ring = n_cols // 2
    length, model = d_first.shape
    width = model // n_rows
    in_width = d_proj.shape[1]
    col_width = model // n_cols
    pieces = 2
    piece = length // pieces
    bf16, f32 = jnp.bfloat16, jnp.float32
    shape = jax.ShapeDtypeStruct
    chips = n_rows * ring
    slot_rows, d_part, e_act, d_gate, d_up = expert_rows
    n_slots, hidden = e_act.shape
    half = hidden // 2
    experts = router_rows[2].shape[0]
    rows_dev = length // n_rows

    def kernel(
        d_first, d_proj, normed, y_in, y_sum, x_in, proj_in, d_resid, gains, gain_two, x_scale,
        xr_in, dp_in, act_in, dg_in, du_in, xr_twin, dp_twin, act_twin, dg_twin, du_twin,
        rows_in, probs_in, gates_in,
        layer_out, grad_in, gain_out, w_out, router_out, out_g, out_u, out_d,
        d_own, w_part, moment, moments, gain_own, gain_twin, gain_sums, proj, x,
        xr, dg, du, full_a, full_b,
        x_q, probs_q, gates_q, router_part, router_got, router_sum, y_landed, y_leaving, *rest,
    ):
        scratch, y_scratch = rest[:9], rest[9:18]
        w_parts = rest[18:25]
        mo_s, mo_r, ga_s, ga_r, gt_s, gt_r, sem, ro_s, ro_r, router_sems, yr_s, yr_r = rest[25:]
        full = (full_a, full_b)
        net = Links(n_rows, n_cols)
        others = net.spread_partners()
        net.greet([device for _, _, device in others] + [net.twin])

        def finish(s, upper, lower):
            at = lambda p: pl.ds(s * piece + p * (piece // 2), piece // 2)
            add_slabs(d_own.at[at(0), :], upper)
            add_slabs(d_own.at[at(1), :], lower)

        ring_copies = []

        def pass_on(turn):
            if turn == 1:
                before = part_reader(y_sum, 0)
            else:
                ring_copies[turn - 2].wait_recv()
                before = part_reader(y_landed, turn - 2)
            add_slabs(y_leaving.at[turn - 1], [part_reader(y_sum, turn), before])
            ring_copies.append(
                net.send(
                    y_leaving.at[turn - 1], y_landed.at[turn - 1], (yr_s, yr_r), turn - 1, net.up
                )
            )

        pass_on(1)

        def finish_out(s, upper, lower):
            ring_copies[-1].wait_recv()
            for part, terms in ((0, upper), (1, lower)):
                at = pl.ds(part * (length // 2), length // 2)
                extra = [
                    part_reader(y_landed.at[ring - 3, at, :]),
                    part_reader(x.at[at, :]),
                    part_reader(proj.at[at, :]),
                ]
                add_slabs(layer_out.at[at, :], terms + extra)

        steps = scatter_square(net, d_first, scratch, list(range(pieces)), finish, resident=True)
        y_steps = scatter_square(net, y_in, y_scratch, [0], finish_out)
        next(steps)
        next(steps)
        ours, mine, twins = pl.ds(0, half), pl.ds(0, n_slots), pl.ds(n_slots, n_slots)
        loads = [
            pltpu.make_async_copy(a, b, sem.at[i])
            for i, (a, b) in enumerate(
                (
                    (xr_in, xr.at[mine]), (xr_twin, xr.at[twins]),
                    (dg_in.at[:, ours], dg.at[mine]), (dg_twin, dg.at[twins]),
                    (du_in.at[:, ours], du.at[mine]), (du_twin, du.at[twins]),
                    (act_in.at[:, ours], dg.at[mine]), (act_twin, dg.at[twins]),
                    (dp_in, xr.at[mine]), (dp_twin, xr.at[twins]),
                )
            )
        ]
        early, late = loads[:6], loads[6:]
        for load in early:
            load.start()
        stores = {}

        def make(kind, j):
            group, slot = kind // 2, j % 2 if kind < 2 else 0
            columns = slice(j * width, (j + 1) * width)
            at = pl.ds(pl.multiple_of(net.flip(j) * width, width), width)
            if (group, slot) in stores:
                stores[group, slot].wait()
            if kind < 2:
                full[group][slot] = matmul_tn(xr[:, columns], (dg, du)[kind][...])
                target = (out_g, out_u)[kind].at[at, :]
            else:
                full[group][slot] = matmul_tn(dg[...], xr[:, columns])
                target = out_d.at[:, at]
            store = pltpu.make_async_copy(full[group].at[slot], target, sem.at[12 + 2 * group + slot])
            store.start()
            stores[group, slot] = store

        proj_load = pltpu.make_async_copy(proj_in.at[:, pl.ds(0, width)], proj, sem.at[10])
        proj_load.start()
        x_load = pltpu.make_async_copy(x_in.at[:, pl.ds(0, width)], x, sem.at[11])
        x_load.start()
        quarter = pl.ds(pl.multiple_of(net.r * rows_dev, rows_dev), rows_dev)
        column = pl.ds(pl.multiple_of(net.place(0) * width, width), width)
        router_loads = []
        for s in range(ring):
            router_loads += [
                pltpu.make_async_copy(
                    rows_in.at[s, quarter, column], x_q.at[s], router_sems.at[s, 0]
                ),
                pltpu.make_async_copy(probs_in.at[s, quarter, :], probs_q.at[s], router_sems.at[s, 1]),
                pltpu.make_async_copy(
                    gates_in.at[:, net.chip(s), 0, quarter], gates_q.at[s], router_sems.at[s, 2]
                ),
            ]
        for load in router_loads:
            load.start()
        w_part[...] = matmul_tn(normed[...], d_proj[...]).astype(bf16)
        by_place = lambda hops, core: w_part.at[
            pl.ds((net.place(hops) * 2 + core) * col_width, col_width), :
        ]
        w_steps = scatter_columns(net, by_place, w_out, w_parts)
        next(w_steps)
        next(steps)
        for load in early:
            load.wait()
        make(0, 0)
        next(w_steps)
        next(steps)
        next(y_steps)
        make(0, 1)
        pass_on(2)
        run_together(steps)

        x_load.wait()
        gain = gains[0:1, :width]
        slab = 128
        gain_own[...] = jnp.zeros_like(gain_own)

        def unit_of(at):
            inverse = x_scale[at, :1]
            return x[at, :].astype(f32) * inverse, inverse

        for i in range(length // slab):
            at = slice(i * slab, (i + 1) * slab)
            unit, _ = unit_of(at)
            d_normed = d_own[at, :]
            share = jnp.sum(d_normed * gain * unit, -1, keepdims=True)
            moment[:, at] = jnp.broadcast_to(share, (slab, 128)).T[:8]
            gain_own[:8] += jnp.sum((d_normed * unit).reshape(slab // 8, 8, width), 0)
        sends = [
            net.send(moment, moments.at[bits - 1], (mo_s, mo_r), bits - 1, (net.flip(bits), net.c))
            for bits in range(1, n_rows)
        ]
        gain_own[8:] = gain_two[...]
        twin = net.send(gain_own, gain_twin, (gt_s, gt_r), 0, net.twin)
        next(w_steps)
        make(0, 2)
        for copy in sends:
            copy.wait_recv()
        whole = moment[...] + moments[0] + moments[1] + moments[2]
        for i in range(length // slab):
            at = slice(i * slab, (i + 1) * slab)
            unit, inverse = unit_of(at)
            mean = jnp.broadcast_to(whole[:1, at], (128, slab)).T[:, :1] / model
            grad_in[at, :] = d_resid[at, :] + inverse * (d_own[at, :] * gain - unit * mean)
        twin.wait_recv()
        mine = net.r * ring + net.z
        gain_sums[mine] = gain_own[...] + gain_twin[...]
        sends = [
            net.send(gain_sums.at[mine], gain_sums.at[mine], (ga_s, ga_r), number, device)
            for number, (hops, bits, device) in enumerate(others)
        ]
        make(0, 3)
        next(w_steps)
        make(1, 0)
        next(y_steps)
        make(1, 1)
        for load in router_loads:
            load.wait()
        for s in range(ring):
            d_gates = jnp.concatenate([gates_q[s], jnp.zeros((128 - experts, rows_dev), f32)], 0).T
            d_logits = probs_q[s] * (d_gates - jnp.sum(probs_q[s] * d_gates, -1, keepdims=True))
            high = d_logits.astype(bf16)
            low = (d_logits - high.astype(f32)).astype(bf16)
            part = matmul_tn(x_q[s], high) + matmul_tn(x_q[s], low)
            for core in range(2):
                rows = part[core * col_width : (core + 1) * col_width]
                router_part[core] = rows if s == 0 else router_part[core] + rows
        router_twin = net.send(router_part.at[1 - net.k], router_got.at[0], (ro_s, ro_r), 0, net.twin)
        make(1, 2)
        router_twin.wait_recv()
        router_sum[0] = router_part[net.k] + router_got[0]
        router_x = net.send(router_sum.at[0], router_got.at[1], (ro_s, ro_r), 1, net.x)
        proj_load.wait()
        next(y_steps)
        make(1, 3)
        for load in late:
            load.start()
        router_x.wait_recv()
        router_sum[1] = router_sum[0] + router_got[1]
        router_y = net.send(router_sum.at[1], router_got.at[2], (ro_s, ro_r), 2, net.y)
        run_together(y_steps, w_steps)
        for load in late:
            load.wait()
        for j in range(n_rows):
            make(2, j)
        for store in stores.values():
            store.wait()
        for copy in sends:
            copy.wait_recv()
        router_y.wait_recv()
        router_out[...] = router_sum[1] + router_got[2]
        total = gain_sums[net.z * ring]
        for i in range(1, ring):
            total = total + gain_sums[net.z * ring + i]
        gain_out[0:1] = jnp.sum(total[:8], 0, keepdims=True)
        gain_out[1:2] = jnp.sum(total[8:], 0, keepdims=True)
        gain_out[2:8] = jnp.zeros((6, width), f32)
        run_together(w_steps)
        net.finish()

    vmem = pltpu.VMEM
    return remote_call(
        kernel,
        "last_phase",
        7,
        [
            shape((length, width), bf16),
            shape((length, width), f32),
            shape((8, width), f32),
            shape((col_width, in_width), f32),
            shape((col_width, 128), f32),
            shape((model, half), f32),
            shape((model, half), f32),
            shape((half, model), f32),
        ],
        [
            vmem((length, width), f32),
            vmem((model, in_width), bf16),
            vmem((8, length), f32),
            vmem((n_rows - 1, 8, length), f32),
            vmem((16, width), f32),
            vmem((16, width), f32),
            vmem((chips, 16, width), f32),
            vmem((length, width), bf16),
            vmem((length, width), bf16),
            vmem((2 * n_slots, model), bf16),
            vmem((2 * n_slots, half), bf16),
            vmem((2 * n_slots, half), bf16),
            vmem((2, width, half), f32),
            vmem((1, half, width), f32),
            vmem((ring, rows_dev, width), bf16),
            vmem((ring, rows_dev, 128), f32),
            vmem((ring, experts, rows_dev), f32),
            vmem((2, col_width, 128), f32),
            vmem((3, col_width, 128), f32),
            vmem((2, col_width, 128), f32),
            vmem((ring - 2, length, width), bf16),
            vmem((ring - 2, length, width), bf16),
        ]
        + scatter_scratch(pieces, piece, width, resident=True)
        + scatter_scratch(1, length, width)
        + scatter_columns_scratch(ring, col_width, in_width)
        + pair_sems(n_rows - 1)
        + pair_sems(chips - 1)
        + pair_sems(1)
        + [pltpu.SemaphoreType.DMA((16,))]
        + pair_sems(3)
        + [pltpu.SemaphoreType.DMA((ring, 3))]
        + pair_sems(ring - 2),
        (
            d_first.reshape(pieces, piece, model), d_proj, normed, parts, part_sum, x, proj, d_resid,
            gains, gain_part, x_scale, *expert_rows, *twin_rows, *router_rows,
        ),
        in_vmem=(0, 1, 2, 4, 7, 8, 9, 10),
        out_vmem=(0, 1, 2, 3, 4),
    )


def add_bf16(left, right):
    return (left.astype(jnp.float32) + right.astype(jnp.float32)).astype(jnp.bfloat16)


class Exchange:
    def __init__(self):
        self.n_rows = lax.axis_size("rows")
        self.n_cols = lax.axis_size("cols")
        self.ring = self.n_cols // 2
        self.r = lax.axis_index("rows")
        self.c = lax.axis_index("cols")
        self.z = self.c // 2
        self.k = self.c % 2

    def move(self, values, target):
        pairs = []
        for r in range(self.n_rows):
            for c in range(self.n_cols):
                to_r, to_c = target(r, c)
                pairs.append((r * self.n_cols + c, to_r * self.n_cols + to_c))
        return lax.ppermute(values, ("rows", "cols"), pairs)

    def along_x(self, values):
        return self.move(values, lambda r, c: (r ^ 1, c))

    def along_y(self, values):
        return self.move(values, lambda r, c: (r ^ 2, c))

    def along_z(self, values, hops=1):
        return self.move(values, lambda r, c: (r, (c + 2 * hops) % self.n_cols))

    def across_z(self, values, bit):
        return self.move(values, lambda r, c: (r, c ^ (2 * bit)))

    def sibling(self, values):
        return self.move(values, lambda r, c: (r, c ^ 1))

    def chip(self, hops):
        return (self.z - hops + self.ring) % self.ring

    def place(self, hops):
        return self.r ^ self.chip(hops)

    def mixed(self, values, axis):
        width = values.shape[axis] // self.n_rows

        def branch(row):
            return lambda whole: jnp.concatenate(
                [
                    lax.slice_in_dim(whole, (row ^ j) * width, ((row ^ j) + 1) * width, axis=axis)
                    for j in range(self.n_rows)
                ],
                axis,
            )

        return lax.switch(self.r, [branch(row) for row in range(self.n_rows)], values)

    def rows_gather(self, block):
        half = block.shape[0] // 2
        from_x = self.along_x(block)
        from_y = self.along_y(block)
        first = self.along_y(from_x[:half])
        second = self.along_x(from_y[half:])
        return [block, from_x, from_y, jnp.concatenate([first, second], 0)]

    def rows_scatter(self, blocks):
        half = blocks[0].shape[0] // 2
        upper = [block[:half] for block in blocks]
        lower = [block[half:] for block in blocks]
        sent = self.along_x(jnp.stack([upper[1], upper[3]]))
        forward = add_bf16(upper[2], sent[1])
        upper_sum = upper[0].astype(jnp.float32) + sent[0].astype(jnp.float32)
        upper_sum = upper_sum + self.along_y(forward).astype(jnp.float32)
        sent = self.along_y(jnp.stack([lower[2], lower[3]]))
        forward = add_bf16(lower[1], sent[1])
        lower_sum = lower[0].astype(jnp.float32) + sent[0].astype(jnp.float32)
        lower_sum = lower_sum + self.along_x(forward).astype(jnp.float32)
        return jnp.concatenate([upper_sum, lower_sum], 0)

    def cols_gather(self, block, place):
        shape = (self.ring, 2) + block.shape
        whole = jnp.zeros(shape, block.dtype)
        rest = (0,) * block.ndim
        for hops in range(self.ring):
            twin = self.sibling(block)
            spot = place(hops)
            whole = lax.dynamic_update_slice(whole, block[None, None], (spot, self.k) + rest)
            whole = lax.dynamic_update_slice(whole, twin[None, None], (spot, 1 - self.k) + rest)
            if hops < self.ring - 1:
                block = self.along_z(block)
        return whole

    def pair_sum(self, parts):
        mine = lax.dynamic_index_in_dim(parts, self.k, 1, False)
        other = lax.dynamic_index_in_dim(parts, 1 - self.k, 1, False)
        return add_bf16(mine, self.sibling(other))

    def cols_scatter(self, parts, place):
        summed = self.pair_sum(parts)
        pick = lambda hops: lax.dynamic_index_in_dim(summed, place(hops), 0, False)
        run = pick(1)
        for hops in range(2, self.ring):
            run = add_bf16(self.along_z(run), pick(hops))
        return self.along_z(run).astype(jnp.float32) + pick(0).astype(jnp.float32)


def split_terms(values):
    high = lax.reduce_precision(values, 8, 7)
    return high.astype(jnp.bfloat16), (values - high).astype(jnp.bfloat16)


def gathered_layer(
    layer_in,
    norm1_gain,
    w_query,
    key_matrix,
    value_matrix,
    w_out,
    norm2_gain,
    w_router,
    shared_gate,
    shared_up,
    shared_down,
    expert_gate,
    expert_up,
    expert_down,
    routes,
    cotangent,
):
    net = Exchange()
    n_rows, ring = net.n_rows, net.ring
    r, c, z, k = net.r, net.c, net.z, net.k
    length, row_width = layer_in.shape[1:]
    rows_dev, top_k = routes.shape[2:]
    experts = w_router.shape[1]
    model_width = row_width * n_rows
    col_width = w_query.shape[0]
    q_width = w_query.shape[1]
    q_heads = q_width // HEAD_DIM
    kv_width = key_matrix.shape[1]
    shared_hidden = shared_gate.shape[1] // ring
    half_hidden = expert_gate.shape[2]
    slots = -(-2 * max(1, 5 * rows_dev * top_k // (8 * experts)) // 16) * 16
    index = lax.dynamic_index_in_dim

    expert_ids = jnp.arange(experts, dtype=jnp.int32)
    hot = jnp.sum(
        (routes.reshape(rows_dev, top_k)[:, :, None] == expert_ids).astype(jnp.float32), 1
    )
    earlier = jnp.tril(jnp.ones((rows_dev, rows_dev), jnp.float32), -1)
    rank = jnp.dot(earlier, hot, precision=PRECISE)
    slot_map = jnp.where(hot > 0, rank, -1.0).T

    small = jnp.concatenate([w_router, norm1_gain[:, None], norm2_gain[:, None]], 1)
    small = jnp.pad(small, ((0, 0), (0, 128 - small.shape[1])))
    pad_to = -(-shared_hidden // 128) * 128
    padded = lambda w: jnp.pad(
        w.reshape(col_width, ring, shared_hidden), ((0, 0), (0, 0), (0, pad_to - shared_hidden))
    )
    packed = jnp.concatenate([padded(shared_gate), padded(shared_up), padded(shared_down.T)], 2)
    packed = jnp.swapaxes(packed, 0, 1)
    experts_w = []
    for own in (expert_gate[0], expert_up[0], expert_down[0]):
        experts_w += [own, net.sibling(own)]
    positions = c * length + jnp.arange(length, dtype=jnp.int32)
    cosine_table, sine_table = rope_tables(positions, HEAD_DIM)
    tables = (
        jnp.concatenate([cosine_table, cosine_table], 1),
        jnp.concatenate([-sine_table, sine_table], 1),
    )

    (
        token_input, first_normed, weights_in, small, queries, kv_all, attn_f32, log_total,
        weights_out_t, grad_rows, second_normed, slot_maps, shared_w, attn_proj, gains,
        first_scale,
    ) = first_phase(
        n_rows, net.n_cols, layer_in[0], cotangent[0],
        jnp.concatenate([w_query, key_matrix, value_matrix], 1), small, w_out.T, packed, slot_map,
        tables,
    )
    joined = lambda whole: whole.reshape(-1, whole.shape[-1])
    attn_proj = joined(attn_proj)
    (
        d_block, rows_all, out_rows, slot_rows, d_part, e_act, d_e_gate, d_e_up, s_act, d_shared,
        gate_probs, d_gate_all,
    ) = experts_phase(
        n_rows, net.n_cols, second_normed, grad_rows, slot_maps, experts_w, shared_w, small, slots
    )
    expert_rows = [joined(part) for part in (slot_rows, d_part, e_act, d_e_gate, d_e_up)]
    d_projected, d_first, part_sum, g_out, d_resid, gain_part, *twin_rows = attention_back(
        n_rows, net.n_cols, d_block, index(d_gate_all, z, 1, False)[:, 0], gate_probs, small,
        (token_input, attn_proj, grad_rows), gains, weights_out_t, weights_in, queries, kv_all,
        attn_f32, log_total, tables, out_rows, expert_rows,
    )
    layer_out, grad_in, gain_grads, g_in, g_router, *g_experts = last_phase(
        n_rows, net.n_cols, d_first, d_projected, first_normed, out_rows, part_sum, token_input,
        attn_proj, d_resid, gains, gain_part, first_scale,
        expert_rows, twin_rows, (rows_all, gate_probs, d_gate_all),
    )
    gain_grads = index(gain_grads[:2].reshape(2, 2, col_width), k, 1, False)

    column_parts = lambda whole: whole.astype(jnp.bfloat16).reshape(ring, 2, col_width, -1)
    shared_parts = jnp.concatenate(
        [
            matmul_tn(joined(rows_all), joined(d_shared)),
            matmul_tn(joined(grad_rows), joined(s_act)),
        ],
        1,
    )
    shared_parts = net.pair_sum(column_parts(shared_parts))
    g_shared = jnp.zeros(shared_parts.shape, jnp.bfloat16)
    for hops in range(ring):
        piece = index(shared_parts, net.place(-hops), 0, False)
        piece = net.along_z(piece, hops) if hops else piece
        g_shared = lax.dynamic_update_slice(g_shared, piece[None], (net.chip(hops), 0, 0))
    g_shared = g_shared.astype(jnp.float32)
    shared_cols = lambda n: jnp.swapaxes(
        g_shared[:, :, n * pad_to : n * pad_to + shared_hidden], 0, 1
    ).reshape(col_width, -1)

    return (
        layer_out[None],
        grad_in[None],
        gain_grads[0],
        g_in[:, :q_width],
        g_in[:, q_width : q_width + kv_width],
        g_in[:, q_width + kv_width :],
        g_out.T,
        gain_grads[1],
        g_router[:, :experts],
        shared_cols(0),
        shared_cols(1),
        shared_cols(2).T,
        g_experts[0][None],
        g_experts[1][None],
        g_experts[2][None],
    )


def per_device(layer_in, *others):
    routes = others[13]
    w_router = others[6]
    n_rows, n_cols = lax.axis_size("rows"), lax.axis_size("cols")
    experts, top_k = w_router.shape[1], routes.shape[3]
    gathers = (
        experts <= 4 * top_k
        and layer_in.shape[0] == 1
        and n_rows == 4
        and n_cols == 2 * n_rows
        and 2 * experts == n_rows * n_cols
    )
    return (gathered_layer if gathers else routed_layer)(layer_in, *others)


def solution(mesh):
    placed = (
        P(None, "cols", "rows"),
        P("cols"),
        P("cols", "rows"),
        P("cols", "rows"),
        P("cols", "rows"),
        P("rows", "cols"),
        P("cols"),
        P("cols", None),
        P("cols", "rows"),
        P("cols", "rows"),
        P("rows", "cols"),
        P(("rows", "cols"), None, None),
        P(("rows", "cols"), None, None),
        P(("rows", "cols"), None, None),
        P("cols", "rows", None, None),
        P(None, "cols", "rows"),
    )
    return jax.shard_map(
        per_device,
        mesh=mesh,
        in_specs=placed,
        out_specs=(
            P(None, "cols", "rows"),
            P(None, "cols", "rows"),
            P("cols"),
            P("cols", "rows"),
            P("cols", "rows"),
            P("cols", "rows"),
            P("rows", "cols"),
            P("cols"),
            P("cols", None),
            P("cols", "rows"),
            P("cols", "rows"),
            P("rows", "cols"),
            P(("rows", "cols"), None, None),
            P(("rows", "cols"), None, None),
            P(("rows", "cols"), None, None),
        ),
        check_vma=False,
    )
```
